256 devices in a mesh: px: 16 (over y_lo, x, core), py: 16 (over z, y_hi).
Axes of the slice: x: 4, y: 4 (y_hi: 2, y_lo: 2; y = y_hi * 2 + y_lo), z: 8, core: 2. Of those that a mesh axis runs over, the one named last changes fastest.
Arguments:
- electric: float32 [3, 256, 256, 128], P(None, 'px', 'py'), may hold values from -4 to 4
- magnetic: float32 [3, 256, 256, 128], P(None, 'px', 'py'), may hold values from -4 to 4
- material: int32 [256, 256, 128], P('px', 'py'), may hold values from 0 to 7
- permittivity: float32 [8], replicated, may hold values from 1 to 4.5
- conductivity: float32 [8], replicated, may hold values from 0.002 to 0.05
Outputs:
- electric_next: float32 [3, 256, 256, 128], P(None, 'px', 'py')
- magnetic_next: float32 [3, 256, 256, 128], P(None, 'px', 'py')
The draws below stay inside these ranges and needn't reach their ends.
All inputs are finite; a program needn't handle non-finite values.
Results may differ from the reference program's by a relative error of at most 0.005.
Values sent between devices are 32-bit elements; how exact they have to be, the bound alone decides.
No kernel may reach another device: no remote copies, remote signals or barrier semaphores. Data moves between devices by JAX's collectives and lax.ppermute only.
A program may use at most 64 MiB of HBM per device.

```python
import math
import jax
import jax.numpy as jnp
from jax import lax

NZ = 128
MATERIALS = 8
NX = 256
NY = 256


def place_ends(result, stream_key, smallest, high):
    place = [jax.random.randint(jax.random.fold_in(stream_key, axis), (), 0, length) for axis, length in enumerate(result.shape)]
    main_axis = result.shape.index(max(result.shape))
    next_to = place[:main_axis] + [(place[main_axis] + 1) % result.shape[main_axis]] + place[main_axis + 1:]
    return result.at[tuple(place)].set(smallest).at[tuple(next_to)].set(high)


def block_scale(stream_key, extent, split, smallest, top_value):
    factor_of = 1.0
    for dim, parts in split:
        steps = jax.random.uniform(jax.random.fold_in(jax.random.fold_in(stream_key, 6), dim), (parts,), jnp.float32, smallest / len(split), top_value / len(split))
        factor_of = factor_of * jnp.repeat(jnp.exp(steps), extent[dim] // parts).reshape((-1,) + (1,) * (len(extent) - 1 - dim))
    return factor_of


def bell_draw(rng, shape, deviation, reach, pieces=(), kind=jnp.bfloat16):
    result = jax.random.normal(rng, shape, jnp.float32) * deviation
    if len(pieces) > 0:
        result = block_scale(rng, shape, pieces, -0.22, 0.18) * result
    return jnp.clip(result, min=-reach, max=reach).astype(kind)


def setup_inputs(seed: int = 0) -> dict:
    keys = jax.random.split(jax.random.key(seed), 6)
    return {
        "electric": bell_draw(keys[0], (3, NX, NY, NZ), 0.5, 4.0, ((1, 16), (2, 16)), jnp.float32),
        "magnetic": bell_draw(keys[1], (3, NX, NY, NZ), 0.5, 4.0, ((1, 16), (2, 16)), jnp.float32),
        "material": place_ends(jax.random.randint(keys[2], (NX, NY, NZ), 0, MATERIALS), jax.random.fold_in(keys[2], 1), 0, MATERIALS - 1).astype(jnp.int32),
        "permittivity": jnp.clip(jnp.exp(jax.random.uniform(keys[3], (MATERIALS,), jnp.float32, math.log(1.0), math.log(4.5))), 1.0, 4.5),
        "conductivity": jnp.clip(jnp.exp(jax.random.uniform(keys[4], (MATERIALS,), jnp.float32, math.log(0.002), math.log(0.05))), 0.002, 0.05),
    }


half_step = 32.0


def from_before(values, stride, direction, filler):
    length = values.shape[direction]
    widths = [(0, 0)] * values.ndim
    widths[direction] = (stride, 0)
    padded = jnp.pad(values, widths, constant_values=filler)
    return lax.slice_in_dim(padded, 0, length, axis=direction)


def from_after(values, stride, direction, filler):
    length = values.shape[direction]
    widths = [(0, 0)] * values.ndim
    widths[direction] = (0, stride)
    padded = jnp.pad(values, widths, constant_values=filler)
    return lax.slice_in_dim(padded, stride, stride + length, axis=direction)


def reduce_lines(lower_band, middle, upper_band, sources, direction):
    length = middle.shape[direction]
    stride = 1
    while stride < length:
        left_ratio = lower_band / from_before(middle, stride, direction, 1.0)
        right_ratio = upper_band / from_after(middle, stride, direction, 1.0)
        new_middle = middle - from_before(upper_band, stride, direction, 0.0) * left_ratio - from_after(lower_band, stride, direction, 0.0) * right_ratio
        lower_band = -from_before(lower_band, stride, direction, 0.0) * left_ratio
        upper_band = -from_after(upper_band, stride, direction, 0.0) * right_ratio
        sources = tuple(column - from_before(column, stride, direction, 0.0) * left_ratio - from_after(column, stride, direction, 0.0) * right_ratio for column in sources)
        middle = new_middle
        stride = stride * 2
    return tuple(column / middle for column in sources)


def line_system(line_rate, first_row, final_row):
    zero_band = jnp.zeros_like(line_rate)
    lower_band = jnp.where(first_row, zero_band, -line_rate)
    upper_band = jnp.where(final_row, zero_band, -line_rate)
    middle = 1.0 + 2.0 * line_rate - jnp.where(first_row, line_rate, zero_band)
    return lower_band, middle, upper_band


def solve_whole(line_rate, source, direction):
    length = line_rate.shape[direction]
    dims_shape = [1] * line_rate.ndim
    dims_shape[direction] = length
    position = lax.broadcasted_iota(jnp.int32, tuple(dims_shape), direction)
    lower_band, middle, upper_band = line_system(line_rate, position == 0, position == length - 1)
    return reduce_lines(lower_band, middle, upper_band, (source,), direction)[0]


def ahead(values, direction):
    return from_after(values, 1, direction, 0.0) - values


def behind(values, direction):
    return values - from_before(values, 1, direction, 0.0)


def reference(electric, magnetic, material, permittivity, conductivity):
    perm_cell = permittivity[material]
    cond_cell = conductivity[material]
    denominator = perm_cell / half_step + 0.5 * cond_cell
    retain = (perm_cell / half_step - 0.5 * cond_cell) / denominator
    driving = 1.0 / denominator
    line_rate = half_step * driving
    elec_x, elec_y, elec_z = electric[0], electric[1], electric[2]
    magn_x, magn_y, magn_z = magnetic[0], magnetic[1], magnetic[2]
    source_x = retain * elec_x + driving * (behind(magn_z, 1) - behind(magn_y, 2)) - line_rate * behind(ahead(elec_y, 0), 1)
    half_x = solve_whole(line_rate, source_x, 1)
    source_y = retain * elec_y + driving * (behind(magn_x, 2) - behind(magn_z, 0)) - line_rate * behind(ahead(elec_z, 1), 2)
    half_y = solve_whole(line_rate, source_y, 2)
    source_z = retain * elec_z + driving * (behind(magn_y, 0) - behind(magn_x, 1)) - line_rate * behind(ahead(elec_x, 2), 0)
    half_z = solve_whole(line_rate, source_z, 0)
    hold_x = magn_x - half_step * ahead(elec_z, 1) + half_step * ahead(half_y, 2)
    hold_y = magn_y - half_step * ahead(elec_x, 2) + half_step * ahead(half_z, 0)
    hold_z = magn_z - half_step * ahead(elec_y, 0) + half_step * ahead(half_x, 1)
    source_x2 = retain * half_x + driving * (behind(hold_z, 1) - behind(hold_y, 2)) - line_rate * behind(ahead(half_z, 0), 2)
    full_x = solve_whole(line_rate, source_x2, 2)
    source_y2 = retain * half_y + driving * (behind(hold_x, 2) - behind(hold_z, 0)) - line_rate * behind(ahead(half_x, 1), 0)
    full_y = solve_whole(line_rate, source_y2, 0)
    source_z2 = retain * half_z + driving * (behind(hold_y, 0) - behind(hold_x, 1)) - line_rate * behind(ahead(half_y, 2), 1)
    full_z = solve_whole(line_rate, source_z2, 1)
    new_x = hold_x - half_step * ahead(full_z, 1) + half_step * ahead(half_y, 2)
    new_y = hold_y - half_step * ahead(full_x, 2) + half_step * ahead(half_z, 0)
    new_z = hold_z - half_step * ahead(full_y, 0) + half_step * ahead(half_x, 1)
    return jnp.stack([full_x, full_y, full_z], axis=0), jnp.stack([new_x, new_y, new_z], axis=0)
```

```python
import functools

import jax
import jax.numpy as jnp
from jax import lax
from jax.experimental import pallas as pl
from jax.experimental.pallas import tpu as pltpu
from jax.sharding import PartitionSpec as P

h = 32.0
B = 16
F32 = jnp.float32


def plane(i):
    return pl.ds(i * B, B)


def strided(j):
    return pl.ds(j, B, stride=B)


def lanes(v):
    return lax.broadcasted_iota(jnp.int32, v.shape, 1)


def behind_z(v):
    return v - jnp.where(lanes(v) == 0, 0.0, pltpu.roll(v, 1, 1))


def ahead_z(v):
    n = v.shape[1]
    return jnp.where(lanes(v) == n - 1, 0.0, pltpu.roll(v, n - 1, 1)) - v


def factor(w_of, first_block, p, u, v):
    d = None
    y = []
    for j in range(B):
        w = w_of(j)
        e = w + (jnp.where(first_block, 0.0, 1.0) if j == 0 else d)
        inv = 1.0 / (1.0 + e)
        d = e * inv
        p[plane(j)] = inv
        y.append(jnp.ones_like(inv) if j == 0 else y[-1] * last)
        last = inv
    uj = y[B - 1] * last
    vj = last
    u[plane(B - 1)] = uj
    v[plane(B - 1)] = vj
    for j in range(B - 2, -1, -1):
        inv = p[plane(j)]
        uj = inv * (y[j] + uj)
        vj = inv * vj
        u[plane(j)] = uj
        v[plane(j)] = vj


def eliminate(source_of, p, g):
    y = source_of(0)
    ys = [y]
    for j in range(1, B):
        y = source_of(j) + p[plane(j - 1)] * y
        ys.append(y)
    x = y * p[plane(B - 1)]
    end = x
    g[plane(B - 1)] = x
    for j in range(B - 2, -1, -1):
        x = p[plane(j)] * (ys[j] + x)
        g[plane(j)] = x
    return x, end


def boundary(me, n, rows_of, coef_of):
    zero = jnp.zeros_like(coef_of(0)[0])
    alpha, beta, gamma, delta = zero, zero, zero, zero
    for s in range(n - 1):
        gf, dl = rows_of(s)
        ff, fl, ll = coef_of(s)
        t = fl / (1.0 - ff * beta)
        on = s < me
        alpha, beta = (
            jnp.where(on, dl + t * (alpha + beta * gf), alpha),
            jnp.where(on, ll + t * beta * fl, beta),
        )
        m = n - 1 - s
        gf, dl = rows_of(m)
        ff, fl, ll = coef_of(m)
        t = fl / (1.0 - ll * delta)
        on = m > me
        gamma, delta = (
            jnp.where(on, gf + t * (gamma + delta * dl), gamma),
            jnp.where(on, ff + t * delta * fl, delta),
        )
    gf, dl = rows_of(me)
    ff, fl, ll = coef_of(me)
    t = fl / (1.0 - ll * delta)
    gamma_here = gf + t * (gamma + delta * dl)
    delta_here = ff + t * delta * fl
    before = (alpha + beta * gamma_here) / (1.0 - beta * delta_here)
    after = (gamma + delta * (dl + fl * before)) / (1.0 - delta * ll)
    return before, after


def solve_z(r, w):
    n = r.shape[1]
    lane = lanes(r)
    e = jnp.where(lane == n - 1, 0.0, 1.0)
    l = jnp.where(lane == 0, 0.0, 1.0)
    s = w + jnp.where(lane == n - 1, 1.0, 0.0)
    step = 1
    while step < n:
        inv = 1.0 / (s + (l + e))
        kl = l * pltpu.roll(inv, step, 1)
        kr = e * pltpu.roll(inv, n - step, 1)
        r = r + (kl * pltpu.roll(r, step, 1) + kr * pltpu.roll(r, n - step, 1))
        s = s + (kl * pltpu.roll(s, step, 1) + kr * pltpu.roll(s, n - step, 1))
        l = kl * pltpu.roll(l, step, 1)
        e = kr * pltpu.roll(e, n - step, 1)
        step *= 2
    return r / s


def tables_kernel(me, eps, sig, material, w, c, p, u, v):
    ws = [eps[m] * (1.0 / (h * h)) + sig[m] * (0.5 / h) for m in range(eps.shape[0])]
    cs = [eps[m] * (1.0 / (h * h)) - sig[m] * (0.5 / h) for m in range(eps.shape[0])]
    for i in range(B):
        ids = material[plane(i)]
        wi = jnp.full(ids.shape, ws[0], F32)
        ci = jnp.full(ids.shape, cs[0], F32)
        for m in range(1, len(ws)):
            wi = jnp.where(ids == m, ws[m], wi)
            ci = jnp.where(ids == m, cs[m], ci)
        w[plane(i)] = wi
        c[plane(i)] = ci
    factor(lambda j: w[strided(j)], me[1] == 0, p, u, v)


def first_y_kernel(n, elec, magn, ey_next, c, p, u, v, flux, g, msg):
    for i in range(B):
        ahead = elec[1, plane(i + 1)] if i < B - 1 else ey_next[...]
        flux[plane(i)] = magn[2, plane(i)] * (1.0 / h) - (ahead - elec[1, plane(i)])

    def source(j):
        f = flux[strided(j)]
        if j > 0:
            f = f - flux[strided(j - 1)]
        own = c[strided(j)] * elec.at[0][strided(j)]
        return own + (f - behind_z(magn.at[1][strided(j)]) * (1.0 / h))

    first, last = eliminate(source, p, g)
    last = last - flux[strided(B - 1)]
    for m in range(n):
        msg[m, plane(0)] = first
        msg[m, plane(1)] = last
        msg[m, plane(2)] = u[plane(0)]
        msg[m, plane(3)] = v[plane(0)]
        msg[m, plane(4)] = v[plane(B - 1)]


def first_x_kernel(me, elec, magn, hx_prev, w, c, p, u, v, flux, g, ends):
    factor(lambda i: w[plane(i)], me[0] == 0, p, u, v)
    row = lax.broadcasted_iota(jnp.int32, (B, w.shape[1]), 0)

    def source(i):
        q = magn[1, plane(i)] * (1.0 / h) - ahead_z(elec[0, plane(i)])
        flux[plane(i)] = q
        if i > 0:
            q = q - flux[plane(i - 1)]
        hx = magn[0, plane(i)]
        before = jnp.where(row == 0, hx_prev[pl.ds(i, 1)], pltpu.roll(hx, 1, 0))
        return c[plane(i)] * elec[2, plane(i)] + (q - (hx - before) * (1.0 / h))

    first, last = eliminate(source, p, g)
    ends[plane(0)] = first
    ends[plane(1)] = last - flux[plane(B - 1)]


def first_z_kernel(elec, magn, ez_next, hz_prev, w, c, fy, curl, flux):
    row = lax.broadcasted_iota(jnp.int32, (B, w.shape[1]), 0)
    for i in range(B):
        ez = elec[2, plane(i)]
        after = jnp.where(row == B - 1, ez_next[pl.ds(i, 1)], pltpu.roll(ez, B - 1, 0))
        r = magn[0, plane(i)] * (1.0 / h) - (after - ez)
        hz = magn[2, plane(i)]
        before = magn[2, plane(i - 1)] if i > 0 else hz_prev[...]
        ci = c[plane(i)]
        v = solve_z(ci * elec[1, plane(i)] + (behind_z(r) - (hz - before) * (1.0 / h)), w[plane(i)])
        rise = ahead_z(v)
        mx = r + rise
        fy[plane(i)] = v
        curl[plane(i)] = ci * v + behind_z(mx)
        flux[plane(i)] = -(mx + rise)


def second_x_kernel(n, me, got, g, u, v, flux, c, curl, p_x, u_x, v_x, ends, part, flux2, g2, msg, fx):
    my = me[1]
    before, after = boundary(
        my,
        n[1],
        lambda m: (got[m, plane(0)], got[m, plane(1)]),
        lambda m: (got[m, plane(2)], got[m, plane(3)], got[m, plane(4)]),
    )
    for j in range(B):
        fx[plane(j)] = g[plane(j)] + (u[plane(j)] * before + v[plane(j)] * after)
    mz_before = jnp.where(my == 0, 0.0, fx[plane(0)] - before)
    for j in range(B):
        here = fx[plane(j)]
        rise = (fx[plane(j + 1)] if j < B - 1 else after) - here
        mz = flux[strided(j)] + rise
        part[strided(j)] = c[strided(j)] * here + (mz - mz_before)
        flux2[strided(j)] = -(mz + rise)
        mz_before = mz

    def source(i):
        f = flux2[plane(i)]
        if i > 0:
            f = f - flux2[plane(i - 1)]
        return curl[plane(i)] + f

    first, last = eliminate(source, p_x, g2)
    last = last - flux2[plane(B - 1)]
    for m in range(n[0]):
        msg[m, plane(0)] = first
        msg[m, plane(1)] = last
        msg[m, plane(2)] = ends[plane(0)]
        msg[m, plane(3)] = ends[plane(1)]
        msg[m, plane(4)] = u_x[plane(0)]
        msg[m, plane(5)] = v_x[plane(0)]
        msg[m, plane(6)] = v_x[plane(B - 1)]


def second_y_kernel(
    n, me, got, g, g2, u, v, flux, flux2, c, flux_y, p_y, full_y, new_z, rise_y, part, g3, msg, fz
):
    mx = me[0]
    coef = lambda m: (got[m, plane(4)], got[m, plane(5)], got[m, plane(6)])
    before, after = boundary(mx, n[0], lambda m: (got[m, plane(0)], got[m, plane(1)]), coef)
    for i in range(B):
        full_y[plane(i)] = g2[plane(i)] + (u[plane(i)] * before + v[plane(i)] * after)
    for i in range(B):
        rise = (full_y[plane(i + 1)] if i < B - 1 else after) - full_y[plane(i)]
        new_z[plane(i)] = -h * (flux2[plane(i)] + rise)
    before, after = boundary(mx, n[0], lambda m: (got[m, plane(2)], got[m, plane(3)]), coef)
    for i in range(B):
        fz[plane(i)] = g[plane(i)] + (u[plane(i)] * before + v[plane(i)] * after)
    my_before = jnp.where(mx == 0, 0.0, fz[plane(0)] - before)
    for i in range(B):
        here = fz[plane(i)]
        rise = (fz[plane(i + 1)] if i < B - 1 else after) - here
        my = flux[plane(i)] + rise
        rise_y[plane(i)] = my + rise
        part[plane(i)] = c[plane(i)] * here + (my - my_before)
        my_before = my

    def source(j):
        f = flux_y[strided(j)]
        if j > 0:
            f = f - flux_y[strided(j - 1)]
        return part[strided(j)] + f

    first, last = eliminate(source, p_y, g3)
    last = last - flux_y[strided(B - 1)]
    for m in range(n[1]):
        msg[m, plane(0)] = first
        msg[m, plane(1)] = last


def second_z_kernel(part, rise_y, w, full_x, new_y):
    for i in range(B):
        a = rise_y[plane(i)]
        v = solve_z(part[plane(i)] - behind_z(a), w[plane(i)])
        full_x[plane(i)] = v
        new_y[plane(i)] = h * (a - ahead_z(v))


def last_kernel(n, me, coefs, got, g, u, v, flux_y, full_x, full_y, new_y, new_z, elec, magn):
    before, after = boundary(
        me[1],
        n[1],
        lambda m: (got[m, plane(0)], got[m, plane(1)]),
        lambda m: (coefs[m, plane(2)], coefs[m, plane(3)], coefs[m, plane(4)]),
    )
    elec[0] = full_x[...]
    elec[1] = full_y[...]
    magn[1] = new_y[...]
    magn[2] = new_z[...]
    ez, hx = elec.at[2], magn.at[0]
    here = None
    for j in range(B):
        ahead = g[plane(j)] + (u[plane(j)] * before + v[plane(j)] * after)
        ez[strided(j)] = ahead
        if j > 0:
            hx[strided(j - 1)] = -h * (flux_y[strided(j - 1)] + (ahead - here))
        here = ahead
    hx[strided(B - 1)] = -h * (flux_y[strided(B - 1)] + (after - here))


VMEM = pl.BlockSpec(memory_space=pltpu.VMEM)
SMEM = pl.BlockSpec(memory_space=pltpu.SMEM)


def call(kernel, ins, outs, scalars=0, scratch=(), flops=2_000_000):
    shapes = [jax.ShapeDtypeStruct(s, F32) for s in outs]
    size = sum(4 * x.size for x in ins) + sum(4 * s.size for s in shapes)
    return pl.pallas_call(
        kernel,
        out_shape=shapes,
        in_specs=[SMEM] * scalars + [VMEM] * (len(ins) - scalars),
        out_specs=[VMEM] * len(outs),
        scratch_shapes=[pltpu.VMEM(s, F32) for s in scratch],
        compiler_params=pltpu.CompilerParams(vmem_limit_bytes=40 * 1024 * 1024),
        cost_estimate=pl.CostEstimate(flops=flops, bytes_accessed=size, transcendentals=0),
    )(*ins)


def local(electric, magnetic, material, permittivity, conductivity):
    nx, ny = lax.axis_size("px"), lax.axis_size("py")
    nz = material.shape[2]
    cells, edge = (B * B, nz), (B, nz)
    me = jnp.stack([lax.axis_index("px"), lax.axis_index("py")]).astype(jnp.int32)
    elec = electric.reshape(3, *cells)
    magn = magnetic.reshape(3, *cells)
    ids = material.reshape(cells)

    down = lambda n: [(i + 1, i) for i in range(n - 1)]
    up = lambda n: [(i, i + 1) for i in range(n - 1)]
    ey_next = lax.ppermute(electric[1, 0], "px", down(nx))
    hx_prev = lax.ppermute(magnetic[0, :, B - 1], "py", up(ny))
    ez_next = lax.ppermute(electric[2, :, 0], "py", down(ny))
    hz_prev = lax.ppermute(magnetic[2, B - 1], "px", up(nx))

    w, c, p_y, u_y, v_y = call(
        tables_kernel, [me, permittivity, conductivity, ids], [cells] * 5, scalars=3
    )
    flux_a, g_a, msg = call(
        functools.partial(first_y_kernel, ny),
        [elec, magn, ey_next, c, p_y, u_y, v_y],
        [cells, cells, (ny, 5 * B, nz)],
    )
    got_y = lax.all_to_all(msg, "py", 0, 0, tiled=True)
    p_x, u_x, v_x, flux_b, g_b, ends_b = call(
        first_x_kernel, [me, elec, magn, hx_prev, w, c], [cells] * 5 + [(2 * B, nz)], scalars=1
    )
    fy, curl, flux_y = call(
        first_z_kernel, [elec, magn, ez_next, hz_prev, w, c], [cells] * 3, flops=8_000_000
    )
    part_x, flux2, g_a2, msg = call(
        functools.partial(second_x_kernel, (nx, ny)),
        [me, got_y, g_a, u_y, v_y, flux_a, c, curl, p_x, u_x, v_x, ends_b],
        [cells] * 3 + [(nx, 7 * B, nz)],
        scalars=1,
        scratch=[cells],
    )
    got_x = lax.all_to_all(msg, "px", 0, 0, tiled=True)
    full_y, new_z, rise_y, part_z, g_b2, msg = call(
        functools.partial(second_y_kernel, (nx, ny)),
        [me, got_x, g_b, g_a2, u_x, v_x, flux_b, flux2, c, flux_y, p_y],
        [cells] * 5 + [(ny, 2 * B, nz)],
        scalars=1,
        scratch=[cells],
    )
    got = lax.all_to_all(msg, "py", 0, 0, tiled=True)
    full_x, new_y = call(second_z_kernel, [part_x, rise_y, w], [cells] * 2, flops=8_000_000)
    out = call(
        functools.partial(last_kernel, (nx, ny)),
        [me, got_y, got, g_b2, u_y, v_y, flux_y, full_x, full_y, new_y, new_z],
        [(3, *cells)] * 2,
        scalars=1,
    )
    return tuple(a.reshape(3, B, B, nz) for a in out)


def solution(mesh):
    placed = (P(None, "px", "py", None), P(None, "px", "py", None), P("px", "py", None), P(), P())
    return jax.shard_map(
        local,
        mesh=mesh,
        in_specs=placed,
        out_specs=(P(None, "px", "py", None), P(None, "px", "py", None)),
        check_vma=False,
    )
```

```python
import functools

import jax
import jax.numpy as jnp
from jax import lax
from jax.experimental import pallas as pl
from jax.experimental.pallas import tpu as pltpu
from jax.sharding import PartitionSpec as P

h = 32.0
B = 16
F32 = jnp.float32


def plane(i):
    return pl.ds(i * B, B)


def strided(j):
    return pl.ds(j, B, stride=B)


def lanes(v):
    return lax.broadcasted_iota(jnp.int32, v.shape, 1)


def behind_z(v):
    return v - jnp.where(lanes(v) == 0, 0.0, pltpu.roll(v, 1, 1))


def ahead_z(v):
    n = v.shape[1]
    return jnp.where(lanes(v) == n - 1, 0.0, pltpu.roll(v, n - 1, 1)) - v


def factor(w_of, first_block, p, u, v):
    d = None
    y = []
    for j in range(B):
        w = w_of(j)
        e = w + (jnp.where(first_block, 0.0, 1.0) if j == 0 else d)
        inv = 1.0 / (1.0 + e)
        d = e * inv
        p[plane(j)] = inv
        y.append(jnp.ones_like(inv) if j == 0 else y[-1] * last)
        last = inv
    uj = y[B - 1] * last
    vj = last
    u[plane(B - 1)] = uj
    v[plane(B - 1)] = vj
    for j in range(B - 2, -1, -1):
        inv = p[plane(j)]
        uj = inv * (y[j] + uj)
        vj = inv * vj
        u[plane(j)] = uj
        v[plane(j)] = vj


def eliminate(source_of, p, g):
    y = source_of(0)
    ys = [y]
    for j in range(1, B):
        y = source_of(j) + p[plane(j - 1)] * y
        ys.append(y)
    x = y * p[plane(B - 1)]
    end = x
    g[plane(B - 1)] = x
    for j in range(B - 2, -1, -1):
        x = p[plane(j)] * (ys[j] + x)
        g[plane(j)] = x
    return x, end


def boundary(me, n, rows_of, coef_of, outer):
    left = [a for a, _ in outer]
    right = [b for _, b in outer]
    beta = delta = jnp.zeros_like(left[0])
    for s in range(n - 1):
        ff, fl, ll = coef_of(s)
        t = fl / (1.0 - ff * beta)
        on = s < me
        left = [
            jnp.where(on, dl + t * (a + beta * gf), a) for a, (gf, dl) in zip(left, rows_of(s))
        ]
        beta = jnp.where(on, ll + t * beta * fl, beta)
        m = n - 1 - s
        ff, fl, ll = coef_of(m)
        t = fl / (1.0 - ll * delta)
        on = m > me
        right = [
            jnp.where(on, gf + t * (b + delta * dl), b) for b, (gf, dl) in zip(right, rows_of(m))
        ]
        delta = jnp.where(on, ff + t * delta * fl, delta)
    ff, fl, ll = coef_of(me)
    after_scale = 1.0 / (1.0 - delta * ll)
    t = fl * after_scale
    before_scale = 1.0 / (1.0 - beta * (ff + t * delta * fl))
    ends = []
    for a, b, (gf, dl) in zip(left, right, rows_of(me)):
        before = (a + beta * (gf + t * (b + delta * dl))) * before_scale
        ends.append((before, (b + delta * (dl + fl * before)) * after_scale))
    return ends


def merge(one, two):
    (ff1, fl1, ll1), rows1 = one
    (ff2, fl2, ll2), rows2 = two
    d = 1.0 / (1.0 - ll1 * ff2)
    t1, t2 = fl1 * d, fl2 * d
    rows = [
        (gf1 + t1 * (gf2 + ff2 * dl1), dl2 + t2 * (dl1 + ll1 * gf2))
        for (gf1, dl1), (gf2, dl2) in zip(rows1, rows2)
    ]
    return (ff1 + t1 * fl1 * ff2, t1 * fl2, ll2 + t2 * fl2 * ll1), rows


def solve_z(r, w):
    n = r.shape[1]
    lane = lanes(r)
    e = jnp.where(lane == n - 1, 0.0, 1.0)
    l = jnp.where(lane == 0, 0.0, 1.0)
    s = w + jnp.where(lane == n - 1, 1.0, 0.0)
    step = 1
    while step < n:
        inv = 1.0 / (s + (l + e))
        kl = l * pltpu.roll(inv, step, 1)
        kr = e * pltpu.roll(inv, n - step, 1)
        r = r + (kl * pltpu.roll(r, step, 1) + kr * pltpu.roll(r, n - step, 1))
        s = s + (kl * pltpu.roll(s, step, 1) + kr * pltpu.roll(s, n - step, 1))
        l = kl * pltpu.roll(l, step, 1)
        e = kr * pltpu.roll(e, n - step, 1)
        step *= 2
    return r / s


def tables_kernel(
    me, eps, sig, material, elec, magn, w, c, p, u, v, flux, part, ids, ex, ez, hx, hy, sems
):
    loads = [(material, ids), (elec.at[0], ex), (magn.at[1], hy), (elec.at[2], ez), (magn.at[0], hx)]
    loads = [pltpu.make_async_copy(a, b, sems.at[k]) for k, (a, b) in enumerate(loads)]
    for load in loads:
        load.start()
    ws = [eps[m] * (1.0 / (h * h)) + sig[m] * (0.5 / h) for m in range(eps.shape[0])]
    cs = [eps[m] * (1.0 / (h * h)) - sig[m] * (0.5 / h) for m in range(eps.shape[0])]
    loads[0].wait()
    for i in range(B):
        cell = ids[plane(i)]
        wi = jnp.full(cell.shape, ws[0], F32)
        ci = jnp.full(cell.shape, cs[0], F32)
        for m in range(1, len(ws)):
            wi = jnp.where(cell == m, ws[m], wi)
            ci = jnp.where(cell == m, cs[m], ci)
        w[plane(i)] = wi
        c[plane(i)] = ci
    factor(lambda i: w[plane(i)], me[0] == 0, p, u, v)
    for load in loads[1:]:
        load.wait()
    row = lax.broadcasted_iota(jnp.int32, (B, w.shape[1]), 0)
    for i in range(B):
        q = hy[plane(i)] * (1.0 / h) - ahead_z(ex[plane(i)])
        flux[plane(i)] = q
        if i > 0:
            q = q - flux[plane(i - 1)]
        here = hx[plane(i)]
        before = jnp.where(row == 0, 0.0, pltpu.roll(here, 1, 0))
        part[plane(i)] = c[plane(i)] * ez[plane(i)] + (q - (here - before) * (1.0 / h))


def first_x_kernel(n, part, hx_prev, ey_first, hz_last, flux, p, u, v, g, msg):
    row = lax.broadcasted_iota(jnp.int32, hx_prev.shape, 0)

    def source(i):
        return part[plane(i)] + jnp.where(row == 0, hx_prev[pl.ds(i, 1)] * (1.0 / h), 0.0)

    first, last = eliminate(source, p, g)
    last = last - flux[plane(B - 1)]
    sent = [first, last, u[plane(0)], v[plane(0)], v[plane(B - 1)], ey_first[...], hz_last[...]]
    for m in range(n):
        for k, value in enumerate(sent):
            msg[m, plane(k)] = value


def first_z_kernel(me, elec, magn, ez_next, w, c, p, u, v, r, curl, flux_y, flux_a, part_a, fy):
    factor(lambda j: w[strided(j)], me[1] == 0, p, u, v)
    row = lax.broadcasted_iota(jnp.int32, (B, w.shape[1]), 0)
    for i in range(B):
        ez = elec[2, plane(i)]
        after = jnp.where(row == B - 1, ez_next[pl.ds(i, 1)], pltpu.roll(ez, B - 1, 0))
        ri = magn[0, plane(i)] * (1.0 / h) - (after - ez)
        r[plane(i)] = ri
        if i > 0:
            gain = (magn[2, plane(i)] - magn[2, plane(i - 1)]) * (1.0 / h)
            fy[plane(i)] = c[plane(i)] * elec[1, plane(i)] + (behind_z(ri) - gain)
        here = c[plane(i)] * elec[0, plane(i)]
        part_a[plane(i)] = here - behind_z(magn[1, plane(i)]) * (1.0 / h)
        if i < B - 1:
            rise = elec[1, plane(i + 1)] - elec[1, plane(i)]
            flux_a[plane(i)] = magn[2, plane(i)] * (1.0 / h) - rise
    flux_a[plane(B - 1)] = magn[2, plane(B - 1)] * (1.0 / h) + elec[1, plane(B - 1)]
    fy[plane(0)] = jnp.zeros((B, w.shape[1]), F32)

    def solve(k, carry):
        rows = pl.ds(k * (4 * B), 4 * B)
        x = solve_z(fy[rows], w[rows])
        rise = ahead_z(x)
        mx = r[rows] + rise
        curl[rows] = c[rows] * x + behind_z(mx)
        flux_y[rows] = -(mx + rise)
        return carry

    lax.fori_loop(0, B // 4, solve, 0)


def both_y_kernel(
    n, near, me, got, elec, magn, g_b, u_x, v_x, flux_b, w, c, r, curl_in, flux_y_in, flux_a_in, part_a,
    p_y, u_y, v_y, rise_y, curl, flux_y, flux_a, g_a, g_c, msg, part, fz
):
    me_x = me[0]
    top, bottom = plane(0), plane(B - 1)
    ahead = jnp.where(me_x == n - 1, 0.0, got[jnp.minimum(me_x + 1, n - 1), plane(5)])
    before = jnp.where(me_x == 0, 0.0, got[jnp.maximum(me_x - 1, 0), plane(6)])
    flux_a[...] = flux_a_in[...]
    flux_a[bottom] = flux_a_in[bottom] - ahead
    curl[...] = curl_in[...]
    flux_y[...] = flux_y_in[...]
    hz = (magn[2, top] - before) * (1.0 / h)
    x = solve_z(c[top] * elec[1, top] + (behind_z(r[top]) - hz), w[top])
    rise = ahead_z(x)
    mx = r[top] + rise
    curl[top] = c[top] * x + behind_z(mx)
    flux_y[top] = -(mx + rise)

    def source_a(j):
        f = flux_a[strided(j)]
        if j > 0:
            f = f - flux_a[strided(j - 1)]
        return part_a[strided(j)] + f

    first_a, last_a = eliminate(source_a, p_y, g_a)
    last_a = last_a - flux_a[strided(B - 1)]

    zero = jnp.zeros_like(ahead)
    ((before, after),) = boundary(
        me_x,
        n,
        lambda m: [(got[m, plane(0)], got[m, plane(1)])],
        lambda m: (got[m, plane(2)], got[m, plane(3)], got[m, plane(4)]),
        [(zero, zero)],
    )
    for i in range(B):
        fz[plane(i)] = g_b[plane(i)] + (u_x[plane(i)] * before + v_x[plane(i)] * after)
    my_before = jnp.where(me_x == 0, 0.0, fz[top] - before)
    for i in range(B):
        here = fz[plane(i)]
        rise = (fz[plane(i + 1)] if i < B - 1 else after) - here
        my = flux_b[plane(i)] + rise
        rise_y[plane(i)] = my + rise
        part[plane(i)] = c[plane(i)] * here + (my - my_before)
        my_before = my

    def source_c(j):
        f = flux_y[strided(j)]
        if j > 0:
            f = f - flux_y[strided(j - 1)]
        return part[strided(j)] + f

    first_c, last_c = eliminate(source_c, p_y, g_c)
    last_c = last_c - flux_y[strided(B - 1)]
    sent = [first_a, last_a, first_c, last_c, u_y[plane(0)], v_y[plane(0)], v_y[plane(B - 1)]]
    for m in range(near):
        for k, value in enumerate(sent):
            msg[m, plane(k)] = value


def y_rows(got):
    return lambda m: [(got[m, plane(0)], got[m, plane(1)]), (got[m, plane(2)], got[m, plane(3)])]


def y_coefs(got):
    return lambda m: (got[m, plane(4)], got[m, plane(5)], got[m, plane(6)])


def merge_kernel(near, far, got, msg):
    blocks = [(y_coefs(got)(m), y_rows(got)(m)) for m in range(near)]
    while len(blocks) > 1:
        blocks = [merge(a, b) for a, b in zip(blocks[::2], blocks[1::2])]
    coefs, rows = blocks[0]
    sent = [value for pair in rows for value in pair] + list(coefs)
    for m in range(far):
        for k, value in enumerate(sent):
            msg[m, plane(k)] = value


def second_x_kernel(
    n, near, far, me, got_near, got_far, g_a, g_c, u, v, flux_a, flux_y, c, curl, p_x, part, flux2, g2, full_z, new_x,
    msg, fx
):
    my = me[1]
    zero = jnp.zeros((B, c.shape[1]), F32)
    outer = boundary(lax.div(my, near), far, y_rows(got_far), y_coefs(got_far), [(zero, zero)] * 2)
    (before, after), (before_c, after_c) = boundary(
        lax.rem(my, near), near, y_rows(got_near), y_coefs(got_near), outer
    )
    for j in range(B):
        fx[plane(j)] = g_a[plane(j)] + (u[plane(j)] * before + v[plane(j)] * after)
    mz_before = jnp.where(my == 0, 0.0, fx[plane(0)] - before)
    for j in range(B):
        here = fx[plane(j)]
        rise = (fx[plane(j + 1)] if j < B - 1 else after) - here
        mz = flux_a[strided(j)] + rise
        part[strided(j)] = c[strided(j)] * here + (mz - mz_before)
        flux2[strided(j)] = -(mz + rise)
        mz_before = mz

    def source(i):
        f = flux2[plane(i)]
        if i > 0:
            f = f - flux2[plane(i - 1)]
        return curl[plane(i)] + f

    first, last = eliminate(source, p_x, g2)
    last = last - flux2[plane(B - 1)]
    for m in range(n):
        msg[m, plane(0)] = first
        msg[m, plane(1)] = last
    here = None
    for j in range(B):
        ahead = g_c[plane(j)] + (u[plane(j)] * before_c + v[plane(j)] * after_c)
        full_z[strided(j)] = ahead
        if j > 0:
            new_x[strided(j - 1)] = -h * (flux_y[strided(j - 1)] + (ahead - here))
        here = ahead
    new_x[strided(B - 1)] = -h * (flux_y[strided(B - 1)] + (after_c - here))


def second_z_kernel(part, rise_y, w, full_x, new_y):
    def solve(k, carry):
        rows = pl.ds(k * (4 * B), 4 * B)
        a = rise_y[rows]
        x = solve_z(part[rows] - behind_z(a), w[rows])
        full_x[rows] = x
        new_y[rows] = h * (a - ahead_z(x))
        return carry

    lax.fori_loop(0, B // 4, solve, 0)


def last_kernel(n, me, coefs, got, g, u, v, flux2, full_x, full_z, new_x, new_y, elec, magn):
    elec[0] = full_x[...]
    elec[2] = full_z[...]
    magn[0] = new_x[...]
    magn[1] = new_y[...]
    zero = jnp.zeros_like(got[0, plane(0)])
    ((before, after),) = boundary(
        me[0],
        n,
        lambda m: [(got[m, plane(0)], got[m, plane(1)])],
        lambda m: (coefs[m, plane(2)], coefs[m, plane(3)], coefs[m, plane(4)]),
        [(zero, zero)],
    )
    here = None
    for i in range(B):
        ahead = g[plane(i)] + (u[plane(i)] * before + v[plane(i)] * after)
        elec[1, plane(i)] = ahead
        if i > 0:
            magn[2, plane(i - 1)] = -h * (flux2[plane(i - 1)] + (ahead - here))
        here = ahead
    magn[2, plane(B - 1)] = -h * (flux2[plane(B - 1)] + (after - here))


VMEM = pl.BlockSpec(memory_space=pltpu.VMEM)
SMEM = pl.BlockSpec(memory_space=pltpu.SMEM)
HBM = pl.BlockSpec(memory_space=pltpu.HBM)


def call(kernel, ins, outs, scalars=0, specs=None, scratch=(), flops=2_000_000):
    shapes = [jax.ShapeDtypeStruct(s, F32) for s in outs]
    size = sum(4 * x.size for x in ins) + sum(4 * s.size for s in shapes)
    return pl.pallas_call(
        kernel,
        out_shape=shapes,
        in_specs=specs or [SMEM] * scalars + [VMEM] * (len(ins) - scalars),
        out_specs=[VMEM] * len(outs),
        scratch_shapes=[s if not isinstance(s, tuple) else pltpu.VMEM(s, F32) for s in scratch],
        compiler_params=pltpu.CompilerParams(vmem_limit_bytes=32 * 1024 * 1024),
        cost_estimate=pl.CostEstimate(flops=flops, bytes_accessed=size, transcendentals=0),
    )(*ins)


def local(electric, magnetic, material, permittivity, conductivity):
    nx, ny = lax.axis_size("px"), lax.axis_size("py")
    near = 1 << (ny.bit_length() // 2)
    far = ny // near
    nz = material.shape[2]
    cells = (B * B, nz)
    me = jnp.stack([lax.axis_index("px"), lax.axis_index("py")]).astype(jnp.int32)
    elec = electric.reshape(3, *cells)
    magn = magnetic.reshape(3, *cells)
    ids = material.reshape(cells)

    hx_prev = lax.ppermute(magnetic[0, :, B - 1], "py", [(i, i + 1) for i in range(ny - 1)])
    w, c, p_x, u_x, v_x, flux_b, part_b = call(
        tables_kernel,
        [me, permittivity, conductivity, ids, elec, magn],
        [cells] * 7,
        specs=[SMEM] * 3 + [HBM] * 3,
        scratch=[pltpu.VMEM(cells, jnp.int32)] + [cells] * 4 + [pltpu.SemaphoreType.DMA((5,))],
    )
    g_b, msg = call(
        functools.partial(first_x_kernel, nx),
        [part_b, hx_prev, electric[1, 0], magnetic[2, B - 1], flux_b, p_x, u_x, v_x],
        [cells, (nx, 7 * B, nz)],
    )
    got_x = lax.all_to_all(msg, "px", 0, 0, tiled=True)
    ez_next = lax.ppermute(electric[2, :, 0], "py", [(i + 1, i) for i in range(ny - 1)])
    p_y, u_y, v_y, r, curl, flux_y, flux_a, part_a = call(
        first_z_kernel,
        [me, elec, magn, ez_next, w, c],
        [cells] * 8,
        scalars=1,
        scratch=[cells],
        flops=8_000_000,
    )
    rise_y, curl, flux_y, flux_a, g_a, g_c, msg = call(
        functools.partial(both_y_kernel, nx, near),
        [me, got_x, elec, magn, g_b, u_x, v_x, flux_b, w, c, r, curl, flux_y, flux_a, part_a, p_y, u_y, v_y],
        [cells] * 6 + [(near, 7 * B, nz)],
        scalars=1,
        scratch=[cells] * 2,
    )
    groups = [[q * near + k for k in range(near)] for q in range(far)]
    got_near = lax.all_to_all(msg, "py", 0, 0, axis_index_groups=groups, tiled=True)
    (msg,) = call(functools.partial(merge_kernel, near, far), [got_near], [(far, 7 * B, nz)])
    groups = [[q * near + k for q in range(far)] for k in range(near)]
    got_far = lax.all_to_all(msg, "py", 0, 0, axis_index_groups=groups, tiled=True)
    part_x, flux2, g2, full_z, new_x, msg = call(
        functools.partial(second_x_kernel, nx, near, far),
        [me, got_near, got_far, g_a, g_c, u_y, v_y, flux_a, flux_y, c, curl, p_x],
        [cells] * 5 + [(nx, 2 * B, nz)],
        scalars=1,
        scratch=[cells],
    )
    got = lax.all_to_all(msg, "px", 0, 0, tiled=True)
    full_x, new_y = call(second_z_kernel, [part_x, rise_y, w], [cells] * 2, flops=8_000_000)
    out = call(
        functools.partial(last_kernel, nx),
        [me, got_x, got, g2, u_x, v_x, flux2, full_x, full_z, new_x, new_y],
        [(3, *cells)] * 2,
        scalars=1,
    )
    return tuple(a.reshape(3, B, B, nz) for a in out)


def solution(mesh):
    placed = (P(None, "px", "py", None), P(None, "px", "py", None), P("px", "py", None), P(), P())
    return jax.shard_map(
        local,
        mesh=mesh,
        in_specs=placed,
        out_specs=(P(None, "px", "py", None), P(None, "px", "py", None)),
        check_vma=False,
    )
```

```python
import functools

import jax
import jax.numpy as jnp
from jax import lax
from jax.experimental import pallas as pl
from jax.experimental.pallas import tpu as pltpu
from jax.sharding import PartitionSpec as P

h = 32.0
B = 16
F32 = jnp.float32


def plane(i):
    return pl.ds(i * B, B)


def strided(j):
    return pl.ds(j, B, stride=B)


def lanes(v):
    return lax.broadcasted_iota(jnp.int32, v.shape, 1)


def behind_z(v):
    return v - jnp.where(lanes(v) == 0, 0.0, pltpu.roll(v, 1, 1))


def ahead_z(v):
    n = v.shape[1]
    return jnp.where(lanes(v) == n - 1, 0.0, pltpu.roll(v, n - 1, 1)) - v


def factor(w_of, first_block, p, u, v):
    d = None
    y = []
    for j in range(B):
        w = w_of(j)
        e = w + (jnp.where(first_block, 0.0, 1.0) if j == 0 else d)
        inv = 1.0 / (1.0 + e)
        d = e * inv
        p[plane(j)] = inv
        y.append(jnp.ones_like(inv) if j == 0 else y[-1] * last)
        last = inv
    uj = y[B - 1] * last
    vj = last
    u[plane(B - 1)] = uj
    v[plane(B - 1)] = vj
    for j in range(B - 2, -1, -1):
        inv = p[plane(j)]
        uj = inv * (y[j] + uj)
        vj = inv * vj
        u[plane(j)] = uj
        v[plane(j)] = vj


def eliminate(source_of, p, g):
    y = source_of(0)
    ys = [y]
    for j in range(1, B):
        y = source_of(j) + p[plane(j - 1)] * y
        ys.append(y)
    x = y * p[plane(B - 1)]
    end = x
    g[plane(B - 1)] = x
    for j in range(B - 2, -1, -1):
        x = p[plane(j)] * (ys[j] + x)
        g[plane(j)] = x
    return x, end


def boundary(me, n, rows_of, coef_of, outer):
    left = [a for a, _ in outer]
    right = [b for _, b in outer]
    beta = delta = jnp.zeros_like(left[0])
    for s in range(n - 1):
        ff, fl, ll = coef_of(s)
        t = fl / (1.0 - ff * beta)
        on = s < me
        left = [
            jnp.where(on, dl + t * (a + beta * gf), a) for a, (gf, dl) in zip(left, rows_of(s))
        ]
        beta = jnp.where(on, ll + t * beta * fl, beta)
        m = n - 1 - s
        ff, fl, ll = coef_of(m)
        t = fl / (1.0 - ll * delta)
        on = m > me
        right = [
            jnp.where(on, gf + t * (b + delta * dl), b) for b, (gf, dl) in zip(right, rows_of(m))
        ]
        delta = jnp.where(on, ff + t * delta * fl, delta)
    ff, fl, ll = coef_of(me)
    after_scale = 1.0 / (1.0 - delta * ll)
    t = fl * after_scale
    before_scale = 1.0 / (1.0 - beta * (ff + t * delta * fl))
    ends = []
    for a, b, (gf, dl) in zip(left, right, rows_of(me)):
        before = (a + beta * (gf + t * (b + delta * dl))) * before_scale
        ends.append((before, (b + delta * (dl + fl * before)) * after_scale))
    return ends


def merge(one, two):
    (ff1, fl1, ll1), rows1 = one
    (ff2, fl2, ll2), rows2 = two
    d = 1.0 / (1.0 - ll1 * ff2)
    t1, t2 = fl1 * d, fl2 * d
    rows = [
        (gf1 + t1 * (gf2 + ff2 * dl1), dl2 + t2 * (dl1 + ll1 * gf2))
        for (gf1, dl1), (gf2, dl2) in zip(rows1, rows2)
    ]
    return (ff1 + t1 * fl1 * ff2, t1 * fl2, ll2 + t2 * fl2 * ll1), rows


def solve_z(r, w):
    n = r.shape[1]
    lane = lanes(r)
    e = jnp.where(lane == n - 1, 0.0, 1.0)
    l = jnp.where(lane == 0, 0.0, 1.0)
    s = w + jnp.where(lane == n - 1, 1.0, 0.0)
    step = 1
    while step < n:
        inv = 1.0 / (s + (l + e))
        kl = l * pltpu.roll(inv, step, 1)
        kr = e * pltpu.roll(inv, n - step, 1)
        r = r + (kl * pltpu.roll(r, step, 1) + kr * pltpu.roll(r, n - step, 1))
        s = s + (kl * pltpu.roll(s, step, 1) + kr * pltpu.roll(s, n - step, 1))
        l = kl * pltpu.roll(l, step, 1)
        e = kr * pltpu.roll(e, n - step, 1)
        step *= 2
    return r / s


def collect(r, own, others, got):
    got[r] = own[...]
    for s, other in enumerate(others, 1):
        got[lax.bitwise_xor(r, s)] = other[...]


def rows_in(got, sources):
    return lambda m: [(got[m, plane(2 * k)], got[m, plane(2 * k + 1)]) for k in range(sources)]


def coefs_in(got, at):
    return lambda m: tuple(got[m, plane(at + k)] for k in range(3))


def tables_kernel(
    me, eps, sig, material, elec, magn, w, c, p, u, v, flux, part, ids, ex, ez, hx, hy, sems
):
    loads = [(material, ids), (elec.at[0], ex), (magn.at[1], hy), (elec.at[2], ez), (magn.at[0], hx)]
    loads = [pltpu.make_async_copy(a, b, sems.at[k]) for k, (a, b) in enumerate(loads)]
    for load in loads:
        load.start()
    ws = [eps[m] * (1.0 / (h * h)) + sig[m] * (0.5 / h) for m in range(eps.shape[0])]
    cs = [eps[m] * (1.0 / (h * h)) - sig[m] * (0.5 / h) for m in range(eps.shape[0])]
    loads[0].wait()
    for i in range(B):
        cell = ids[plane(i)]
        wi = jnp.full(cell.shape, ws[0], F32)
        ci = jnp.full(cell.shape, cs[0], F32)
        for m in range(1, len(ws)):
            wi = jnp.where(cell == m, ws[m], wi)
            ci = jnp.where(cell == m, cs[m], ci)
        w[plane(i)] = wi
        c[plane(i)] = ci
    factor(lambda i: w[plane(i)], me[0] == 0, p, u, v)
    for load in loads[1:]:
        load.wait()
    row = lax.broadcasted_iota(jnp.int32, (B, w.shape[1]), 0)
    for i in range(B):
        q = hy[plane(i)] * (1.0 / h) - ahead_z(ex[plane(i)])
        flux[plane(i)] = q
        if i > 0:
            q = q - flux[plane(i - 1)]
        here = hx[plane(i)]
        before = jnp.where(row == 0, 0.0, pltpu.roll(here, 1, 0))
        part[plane(i)] = c[plane(i)] * ez[plane(i)] + (q - (here - before) * (1.0 / h))


def first_x_kernel(part, hx_prev, flux, p, u, v, g, msg):
    row = lax.broadcasted_iota(jnp.int32, hx_prev.shape, 0)

    def source(i):
        return part[plane(i)] + jnp.where(row == 0, hx_prev[pl.ds(i, 1)] * (1.0 / h), 0.0)

    first, last = eliminate(source, p, g)
    msg[plane(0)] = first
    msg[plane(1)] = last - flux[plane(B - 1)]
    msg[plane(2)] = u[plane(0)]
    msg[plane(3)] = v[plane(0)]
    msg[plane(4)] = v[plane(B - 1)]


def merge_kernel(axis, near, sources, me, *refs):
    got, msg = refs[-2:]
    collect(lax.rem(me[axis], near), refs[0], refs[1:near], got)
    rows_of, coef_of = rows_in(got, sources), coefs_in(got, 2 * sources)
    blocks = [(coef_of(m), rows_of(m)) for m in range(near)]
    while len(blocks) > 1:
        blocks = [merge(a, b) for a, b in zip(blocks[::2], blocks[1::2])]
    coefs, rows = blocks[0]
    for k, value in enumerate([v for pair in rows for v in pair] + list(coefs)):
        msg[plane(k)] = value


def merge_rows_kernel(axis, near, me, coefs, *refs):
    got, msg = refs[-2:]
    collect(lax.rem(me[axis], near), refs[0], refs[1:near], got)
    rows_of, coef_of = rows_in(got, 1), coefs_in(coefs, 2)
    blocks = [(coef_of(m), rows_of(m)) for m in range(near)]
    while len(blocks) > 1:
        blocks = [merge(a, b) for a, b in zip(blocks[::2], blocks[1::2])]
    msg[plane(0)], msg[plane(1)] = blocks[0][1][0]


def solved_ends(here, near, far, sources, got_near, got_far, coefs_near, coefs_far):
    zero = jnp.zeros_like(got_near[0, plane(0)])
    outer = boundary(
        lax.div(here, near), far, rows_in(got_far, sources), coefs_far, [(zero, zero)] * sources
    )
    return boundary(lax.rem(here, near), near, rows_in(got_near, sources), coefs_near, outer)


def first_z_kernel(me, elec, magn, w, c, p, u, v, r2, src2, curl, flux_y, flux_a, part_a, src, r, ef, mf, sems):
    loads = [pltpu.make_async_copy(elec, ef, sems.at[0]), pltpu.make_async_copy(magn, mf, sems.at[1])]
    for load in loads:
        load.start()
    factor(lambda j: w[strided(j)], me[1] == 0, p, u, v)
    for load in loads:
        load.wait()
    row = lax.broadcasted_iota(jnp.int32, (B, w.shape[1]), 0)
    for i in range(B):
        ez = ef[2, plane(i)]
        after = jnp.where(row == B - 1, 0.0, pltpu.roll(ez, B - 1, 0))
        ri = mf[0, plane(i)] * (1.0 / h) - (after - ez)
        r[plane(i)] = ri
        gain = mf[2, plane(i)]
        if i > 0:
            gain = gain - mf[2, plane(i - 1)]
        src[plane(i)] = c[plane(i)] * ef[1, plane(i)] + (behind_z(ri) - gain * (1.0 / h))
        part_a[plane(i)] = c[plane(i)] * ef[0, plane(i)] - behind_z(mf[1, plane(i)]) * (1.0 / h)
        if i < B - 1:
            rise = ef[1, plane(i + 1)] - ef[1, plane(i)]
            flux_a[plane(i)] = mf[2, plane(i)] * (1.0 / h) - rise
    flux_a[plane(B - 1)] = mf[2, plane(B - 1)] * (1.0 / h) + ef[1, plane(B - 1)]
    for two, of in ((r2, r), (src2, src)):
        two[plane(0)] = of[plane(0)]
        two[plane(1)] = of[strided(B - 1)]

    def solve(k, carry):
        rows = pl.ds(k * (4 * B), 4 * B)
        x = solve_z(src[rows], w[rows])
        rise = ahead_z(x)
        mx = r[rows] + rise
        curl[rows] = c[rows] * x + behind_z(mx)
        flux_y[rows] = -(mx + rise)
        return carry

    lax.fori_loop(0, B // 4, solve, 0)


def both_y_kernel(near, far, me, got_near, *refs):
    others, refs = refs[:far], refs[far:]
    (ey_next, ez_next, hz_prev, g_b, u_x, v_x, flux_b, w, c, r2, src2, curl_in, flux_y_in, flux_a_in, part_a, p_y, u_y, v_y) = refs[:18]
    got_far, rise_y, curl, flux_y, flux_a, g_a, g_c, msg, part, fz = refs[18:]
    me_x = me[0]
    top, corner = plane(0), strided(B - 1)
    collect(lax.div(me_x, near), others[0], others[1:], got_far)

    curl[...] = curl_in[...]
    flux_y[...] = flux_y_in[...]
    flux_a[...] = flux_a_in[...]

    last = lax.broadcasted_iota(jnp.int32, ez_next.shape, 0) == B - 1
    ez = ez_next[...]
    ez_top = jnp.where(last, ez[0:1], 0.0)
    rr = jnp.concatenate([r2[plane(0)] - ez_top, r2[plane(1)] - ez])
    ss = jnp.concatenate(
        [src2[plane(0)] + (hz_prev[...] * (1.0 / h) - behind_z(ez_top)), src2[plane(1)] - behind_z(ez)]
    )
    x = solve_z(ss, jnp.concatenate([w[top], w[corner]]))
    rise = ahead_z(x)
    mx = rr + rise
    cc = jnp.concatenate([c[top], c[corner]]) * x + behind_z(mx)
    ff = -(mx + rise)
    curl[corner] = cc[B:]
    flux_y[corner] = ff[B:]
    curl[top] = cc[:B]
    flux_y[top] = ff[:B]

    flux_a[plane(B - 1)] = flux_a[plane(B - 1)] - ey_next[...]

    def source_a(j):
        f = flux_a[strided(j)]
        if j > 0:
            f = f - flux_a[strided(j - 1)]
        return part_a[strided(j)] + f

    first_a, last_a = eliminate(source_a, p_y, g_a)
    last_a = last_a - flux_a[strided(B - 1)]

    ((before, after),) = solved_ends(
        me_x, near, far, 1, got_near, got_far, coefs_in(got_near, 2), coefs_in(got_far, 2)
    )
    for i in range(B):
        fz[plane(i)] = g_b[plane(i)] + (u_x[plane(i)] * before + v_x[plane(i)] * after)
    my_before = jnp.where(me_x == 0, 0.0, fz[top] - before)
    for i in range(B):
        here = fz[plane(i)]
        rise = (fz[plane(i + 1)] if i < B - 1 else after) - here
        my = flux_b[plane(i)] + rise
        rise_y[plane(i)] = my + rise
        part[plane(i)] = c[plane(i)] * here + (my - my_before)
        my_before = my

    def source_c(j):
        f = flux_y[strided(j)]
        if j > 0:
            f = f - flux_y[strided(j - 1)]
        return part[strided(j)] + f

    first_c, last_c = eliminate(source_c, p_y, g_c)
    last_c = last_c - flux_y[strided(B - 1)]
    sent = [first_a, last_a, first_c, last_c, u_y[plane(0)], v_y[plane(0)], v_y[plane(B - 1)]]
    for k, value in enumerate(sent):
        msg[plane(k)] = value


def second_x_kernel(near, far, me, got_near, *refs):
    others, refs = refs[:far], refs[far:]
    g_a, u, v, flux_a, c, curl, p_x, part, flux2, g2, ends_c, msg, got_far, fx = refs
    my = me[1]
    collect(lax.div(my, near), others[0], others[1:], got_far)
    (before, after), (before_c, after_c) = solved_ends(
        my, near, far, 2, got_near, got_far, coefs_in(got_near, 4), coefs_in(got_far, 4)
    )
    ends_c[plane(0)] = before_c
    ends_c[plane(1)] = after_c
    for j in range(B):
        fx[plane(j)] = g_a[plane(j)] + (u[plane(j)] * before + v[plane(j)] * after)
    mz_before = jnp.where(my == 0, 0.0, fx[plane(0)] - before)
    for j in range(B):
        here = fx[plane(j)]
        rise = (fx[plane(j + 1)] if j < B - 1 else after) - here
        mz = flux_a[strided(j)] + rise
        part[strided(j)] = c[strided(j)] * here + (mz - mz_before)
        flux2[strided(j)] = -(mz + rise)
        mz_before = mz

    def source(i):
        f = flux2[plane(i)]
        if i > 0:
            f = f - flux2[plane(i - 1)]
        return curl[plane(i)] + f

    first, last = eliminate(source, p_x, g2)
    msg[plane(0)] = first
    msg[plane(1)] = last - flux2[plane(B - 1)]


def second_z_kernel(
    part, rise_y, w, ends_c, g_c, u, v, flux_y, elec, magn, full_x, full_z, new_x, new_y, sems
):
    before, after = ends_c[plane(0)], ends_c[plane(1)]
    here = None
    for j in range(B):
        ahead = g_c[plane(j)] + (u[plane(j)] * before + v[plane(j)] * after)
        full_z[strided(j)] = ahead
        if j > 0:
            new_x[strided(j - 1)] = -h * (flux_y[strided(j - 1)] + (ahead - here))
        here = ahead
    new_x[strided(B - 1)] = -h * (flux_y[strided(B - 1)] + (after - here))
    stores = [(full_z, elec.at[2]), (new_x, magn.at[0]), (full_x, elec.at[0]), (new_y, magn.at[1])]
    stores = [pltpu.make_async_copy(a, b, sems.at[k]) for k, (a, b) in enumerate(stores)]
    stores[0].start()
    stores[1].start()

    def solve(k, carry):
        rows = pl.ds(k * (4 * B), 4 * B)
        a = rise_y[rows]
        x = solve_z(part[rows] - behind_z(a), w[rows])
        full_x[rows] = x
        new_y[rows] = h * (a - ahead_z(x))
        return carry

    lax.fori_loop(0, B // 4, solve, 0)
    stores[2].start()
    stores[3].start()
    for store in stores:
        store.wait()


def last_kernel(near, far, me, coefs_near, coefs_far, got_near, *refs):
    others, refs = refs[:far], refs[far:]
    g, u, v, flux2, _, _, elec, magn, got_far, full_y, new_z, sems = refs
    collect(lax.div(me[0], near), others[0], others[1:], got_far)
    ((before, after),) = solved_ends(
        me[0], near, far, 1, got_near, got_far, coefs_in(coefs_near, 2), coefs_in(coefs_far, 2)
    )
    here = None
    for i in range(B):
        ahead = g[plane(i)] + (u[plane(i)] * before + v[plane(i)] * after)
        full_y[plane(i)] = ahead
        if i > 0:
            new_z[plane(i - 1)] = -h * (flux2[plane(i - 1)] + (ahead - here))
        here = ahead
    new_z[plane(B - 1)] = -h * (flux2[plane(B - 1)] + (after - here))
    stores = [(full_y, elec.at[1]), (new_z, magn.at[2])]
    stores = [pltpu.make_async_copy(a, b, sems.at[k]) for k, (a, b) in enumerate(stores)]
    for store in stores:
        store.start()
    for store in stores:
        store.wait()


VMEM = pl.BlockSpec(memory_space=pltpu.VMEM)
SMEM = pl.BlockSpec(memory_space=pltpu.SMEM)
HBM = pl.BlockSpec(memory_space=pltpu.HBM)


def call(kernel, ins, outs, specs=None, out_specs=None, scratch=(), aliases=None, flops=1_000_000):
    shapes = [pltpu.HBM(s, F32) if out_specs else jax.ShapeDtypeStruct(s, F32) for s in outs]
    return pl.pallas_call(
        kernel,
        out_shape=shapes,
        in_specs=specs or [SMEM] + [VMEM] * (len(ins) - 1),
        out_specs=out_specs or [VMEM] * len(outs),
        scratch_shapes=[pltpu.VMEM(s, F32) if isinstance(s, tuple) else s for s in scratch],
        input_output_aliases=aliases or {},
        compiler_params=pltpu.CompilerParams(vmem_limit_bytes=24 * 1024 * 1024),
        cost_estimate=pl.CostEstimate(flops=flops, bytes_accessed=1_000_000, transcendentals=0),
    )(*ins)


def shared(value, axis, n, step, count):
    others = [
        lax.ppermute(value, axis, [(i, i ^ (step * s)) for i in range(n)]) for s in range(1, count)
    ]
    return [value] + others


def split(n):
    near = 1 << (n.bit_length() // 2)
    return near, n // near


def local(electric, magnetic, material, permittivity, conductivity):
    nx, ny = lax.axis_size("px"), lax.axis_size("py")
    near_x, far_x = split(nx)
    near_y, far_y = split(ny)
    nz = material.shape[2]
    cells = (B * B, nz)
    me = jnp.stack([lax.axis_index("px"), lax.axis_index("py")]).astype(jnp.int32)
    in_hbm = lambda a: pltpu.with_memory_space_constraint(a, pltpu.HBM)
    elec = in_hbm(electric.reshape(3, *cells))
    magn = in_hbm(magnetic.reshape(3, *cells))
    ids = in_hbm(material.reshape(cells))
    dma = pltpu.SemaphoreType.DMA
    down = lambda n: [(i + 1, i) for i in range(n - 1)]
    up = lambda n: [(i, i + 1) for i in range(n - 1)]

    hx_prev = lax.ppermute(magnetic[0, :, B - 1], "py", up(ny))
    w, c, p_x, u_x, v_x, flux_b, part_b = call(
        tables_kernel,
        [me, permittivity, conductivity, ids, elec, magn],
        [cells] * 7,
        specs=[SMEM] * 3 + [HBM] * 3,
        scratch=[pltpu.VMEM(cells, jnp.int32)] + [cells] * 4 + [dma((5,))],
    )
    g_b, msg = call(
        first_x_kernel, [part_b, hx_prev, flux_b, p_x, u_x, v_x], [cells, (5 * B, nz)], specs=[VMEM] * 6
    )
    ins = shared(msg, "px", nx, 1, near_x)
    ey_next = lax.ppermute(electric[1, 0], "px", down(nx))
    hz_prev = lax.ppermute(magnetic[2, B - 1], "px", up(nx))
    ez_next = lax.ppermute(electric[2, :, 0], "py", down(ny))
    near_b, msg = call(
        functools.partial(merge_kernel, 0, near_x, 1), [me] + ins, [(near_x, 5 * B, nz), (5 * B, nz)]
    )
    ins = shared(msg, "px", nx, near_x, far_x)
    p_y, u_y, v_y, r2, src2, curl, flux_y, flux_a, part_a = call(
        first_z_kernel,
        [me, elec, magn, w, c],
        [cells] * 3 + [(2 * B, nz)] * 2 + [cells] * 4,
        specs=[SMEM, HBM, HBM, VMEM, VMEM],
        scratch=[cells] * 2 + [(3, *cells)] * 2 + [dma((2,))],
        flops=8_000_000,
    )
    ins = [me, near_b] + ins + [ey_next, ez_next, hz_prev, g_b, u_x, v_x, flux_b, w, c, r2, src2]
    far_b, rise_y, curl, flux_y, flux_a, g_a, g_c, msg = call(
        functools.partial(both_y_kernel, near_x, far_x),
        ins + [curl, flux_y, flux_a, part_a, p_y, u_y, v_y],
        [(far_x, 5 * B, nz)] + [cells] * 6 + [(7 * B, nz)],
        scratch=[cells] * 2,
    )
    ins = shared(msg, "py", ny, 1, near_y)
    near_ac, msg = call(
        functools.partial(merge_kernel, 1, near_y, 2), [me] + ins, [(near_y, 7 * B, nz), (7 * B, nz)]
    )
    ins = shared(msg, "py", ny, near_y, far_y)
    part_x, flux2, g2, ends_c, msg = call(
        functools.partial(second_x_kernel, near_y, far_y),
        [me, near_ac] + ins + [g_a, u_y, v_y, flux_a, c, curl, p_x],
        [cells] * 3 + [(2 * B, nz)] * 2,
        scratch=[(far_y, 7 * B, nz), cells],
    )
    ins = shared(msg, "px", nx, 1, near_x)
    near_a, msg = call(
        functools.partial(merge_rows_kernel, 0, near_x),
        [me, near_b] + ins,
        [(near_x, 2 * B, nz), (2 * B, nz)],
    )
    ins = shared(msg, "px", nx, near_x, far_x)
    elec, magn = call(
        second_z_kernel,
        [part_x, rise_y, w, ends_c, g_c, u_y, v_y, flux_y],
        [(3, *cells)] * 2,
        specs=[VMEM] * 8,
        out_specs=[HBM] * 2,
        scratch=[cells] * 4 + [dma((4,))],
        flops=8_000_000,
    )
    ins = [me, near_b, far_b, near_a] + ins + [g2, u_x, v_x, flux2]
    at = len(ins)
    out = call(
        functools.partial(last_kernel, near_x, far_x),
        ins + [elec, magn],
        [(3, *cells)] * 2,
        specs=[SMEM] + [VMEM] * (at - 1) + [HBM] * 2,
        out_specs=[HBM] * 2,
        scratch=[(far_x, 2 * B, nz), cells, cells, dma((2,))],
        aliases={at: 0, at + 1: 1},
    )
    return tuple(a.reshape(3, B, B, nz) for a in out)


def solution(mesh):
    placed = (P(None, "px", "py", None), P(None, "px", "py", None), P("px", "py", None), P(), P())
    return jax.shard_map(
        local,
        mesh=mesh,
        in_specs=placed,
        out_specs=(P(None, "px", "py", None), P(None, "px", "py", None)),
        check_vma=False,
    )
```

```python
import functools

import jax
import jax.numpy as jnp
from jax import lax
from jax.experimental import pallas as pl
from jax.experimental.pallas import tpu as pltpu
from jax.sharding import PartitionSpec as P

h = 32.0
B = 16
F32 = jnp.float32


def plane(i):
    return pl.ds(i * B, B)


def strided(j):
    return pl.ds(j, B, stride=B)


def lanes(v):
    return lax.broadcasted_iota(jnp.int32, v.shape, 1)


def behind_z(v):
    return v - jnp.where(lanes(v) == 0, 0.0, pltpu.roll(v, 1, 1))


def ahead_z(v):
    n = v.shape[1]
    return jnp.where(lanes(v) == n - 1, 0.0, pltpu.roll(v, n - 1, 1)) - v


def factor(w_of, first_block, p, u, v):
    d = None
    y = []
    for j in range(B):
        w = w_of(j)
        e = w + (jnp.where(first_block, 0.0, 1.0) if j == 0 else d)
        inv = 1.0 / (1.0 + e)
        d = e * inv
        p[plane(j)] = inv
        y.append(jnp.ones_like(inv) if j == 0 else y[-1] * last)
        last = inv
    uj = y[B - 1] * last
    vj = last
    u[plane(B - 1)] = uj
    v[plane(B - 1)] = vj
    for j in range(B - 2, -1, -1):
        inv = p[plane(j)]
        uj = inv * (y[j] + uj)
        vj = inv * vj
        u[plane(j)] = uj
        v[plane(j)] = vj


def eliminate(source_of, p, g):
    y = source_of(0)
    ys = [y]
    for j in range(1, B):
        y = source_of(j) + p[plane(j - 1)] * y
        ys.append(y)
    x = y * p[plane(B - 1)]
    end = x
    g[plane(B - 1)] = x
    for j in range(B - 2, -1, -1):
        x = p[plane(j)] * (ys[j] + x)
        g[plane(j)] = x
    return x, end


def boundary(me, n, rows_of, coef_of, outer):
    left = [a for a, _ in outer]
    right = [b for _, b in outer]
    beta = delta = jnp.zeros_like(left[0])
    for s in range(n - 1):
        ff, fl, ll = coef_of(s)
        t = fl / (1.0 - ff * beta)
        on = s < me
        left = [
            jnp.where(on, dl + t * (a + beta * gf), a) for a, (gf, dl) in zip(left, rows_of(s))
        ]
        beta = jnp.where(on, ll + t * beta * fl, beta)
        m = n - 1 - s
        ff, fl, ll = coef_of(m)
        t = fl / (1.0 - ll * delta)
        on = m > me
        right = [
            jnp.where(on, gf + t * (b + delta * dl), b) for b, (gf, dl) in zip(right, rows_of(m))
        ]
        delta = jnp.where(on, ff + t * delta * fl, delta)
    ff, fl, ll = coef_of(me)
    after_scale = 1.0 / (1.0 - delta * ll)
    t = fl * after_scale
    before_scale = 1.0 / (1.0 - beta * (ff + t * delta * fl))
    ends = []
    for a, b, (gf, dl) in zip(left, right, rows_of(me)):
        before = (a + beta * (gf + t * (b + delta * dl))) * before_scale
        ends.append((before, (b + delta * (dl + fl * before)) * after_scale))
    return ends


def merge(one, two):
    (ff1, fl1, ll1), rows1 = one
    (ff2, fl2, ll2), rows2 = two
    d = 1.0 / (1.0 - ll1 * ff2)
    t1, t2 = fl1 * d, fl2 * d
    rows = [
        (gf1 + t1 * (gf2 + ff2 * dl1), dl2 + t2 * (dl1 + ll1 * gf2))
        for (gf1, dl1), (gf2, dl2) in zip(rows1, rows2)
    ]
    return (ff1 + t1 * fl1 * ff2, t1 * fl2, ll2 + t2 * fl2 * ll1), rows


def solve_z(r, w):
    n = r.shape[1]
    lane = lanes(r)
    e = jnp.where(lane == n - 1, 0.0, 1.0)
    l = jnp.where(lane == 0, 0.0, 1.0)
    s = w + jnp.where(lane == n - 1, 1.0, 0.0)
    step = 1
    while step < n:
        inv = 1.0 / (s + (l + e))
        a, b = e * inv, l * inv
        r = r + (pltpu.roll(a * r, step, 1) + pltpu.roll(b * r, n - step, 1))
        s = s + (pltpu.roll(a * s, step, 1) + pltpu.roll(b * s, n - step, 1))
        g = a * l
        if 2 * step < n:
            e, l = pltpu.roll(g, n - step, 1), pltpu.roll(g, step, 1)
        step *= 2
    return r / s


def collect(r, own, others, got):
    got[r] = own[...]
    for s, other in enumerate(others, 1):
        got[lax.bitwise_xor(r, s)] = other[...]


def rows_in(got, sources):
    return lambda m: [(got[m, plane(2 * k)], got[m, plane(2 * k + 1)]) for k in range(sources)]


def coefs_in(got, at):
    return lambda m: tuple(got[m, plane(at + k)] for k in range(3))


def tables_kernel(
    me, eps_in, sig_in, material, elec_in, magn_in, w, c, p, u, v, flux, part, elec, magn, ez_first, ids, eps, sig, sems
):
    loads = [(eps_in, eps), (sig_in, sig), (material, ids)]
    for field, to, k in ((elec_in, elec, 0), (magn_in, magn, 1), (elec_in, elec, 2), (magn_in, magn, 0)):
        loads.append((field.at[k], to.at[k]))
    loads += [(elec_in.at[1], elec.at[1]), (magn_in.at[2], magn.at[2])]
    loads = [pltpu.make_async_copy(a, b, sems.at[k]) for k, (a, b) in enumerate(loads)]
    for load in loads:
        load.start()
    for load in loads[:3]:
        load.wait()
    ws = [eps[m] * (1.0 / (h * h)) + sig[m] * (0.5 / h) for m in range(eps.shape[0])]
    cs = [eps[m] * (1.0 / (h * h)) - sig[m] * (0.5 / h) for m in range(eps.shape[0])]
    for i in range(B):
        cell = ids[plane(i)]
        wi = jnp.full(cell.shape, ws[0], F32)
        ci = jnp.full(cell.shape, cs[0], F32)
        for m in range(1, len(ws)):
            wi = jnp.where(cell == m, ws[m], wi)
            ci = jnp.where(cell == m, cs[m], ci)
        w[plane(i)] = wi
        c[plane(i)] = ci
    factor(lambda i: w[plane(i)], me[0] == 0, p, u, v)
    for load in loads[3:7]:
        load.wait()
    row = lax.broadcasted_iota(jnp.int32, (B, w.shape[1]), 0)
    for i in range(B):
        q = magn[1, plane(i)] * (1.0 / h) - ahead_z(elec[0, plane(i)])
        flux[plane(i)] = q
        if i > 0:
            q = q - flux[plane(i - 1)]
        here = magn[0, plane(i)]
        before = jnp.where(row == 0, 0.0, pltpu.roll(here, 1, 0))
        part[plane(i)] = c[plane(i)] * elec[2, plane(i)] + (q - (here - before) * (1.0 / h))
    ez_first[...] = elec.at[2][strided(0)]
    for load in loads[7:]:
        load.wait()


def first_x_kernel(part, hx_prev, flux, p, u, v, elec, magn, g, msg):
    row = lax.broadcasted_iota(jnp.int32, hx_prev.shape, 0)

    def source(i):
        return part[plane(i)] + jnp.where(row == 0, hx_prev[pl.ds(i, 1)] * (1.0 / h), 0.0)

    first, last = eliminate(source, p, g)
    msg[plane(0)] = first
    msg[plane(1)] = last - flux[plane(B - 1)]
    msg[plane(2)] = u[plane(0)]
    msg[plane(3)] = v[plane(0)]
    msg[plane(4)] = v[plane(B - 1)]
    msg[plane(5)] = elec[1, plane(0)]
    msg[plane(6)] = magn[2, plane(B - 1)]


def merge_kernel(axis, near, sources, halos, me, *refs):
    got, msg = refs[-2:]
    collect(lax.rem(me[axis], near), refs[0], refs[1:near], got)
    rows_of, coef_of = rows_in(got, sources), coefs_in(got, 2 * sources)
    blocks = [(coef_of(m), rows_of(m)) for m in range(near)]
    while len(blocks) > 1:
        blocks = [merge(a, b) for a, b in zip(blocks[::2], blocks[1::2])]
    coefs, rows = blocks[0]
    for k, value in enumerate([v for pair in rows for v in pair] + list(coefs)):
        msg[plane(k)] = value
    if halos:
        msg[plane(5)] = got[0, plane(5)]
        msg[plane(6)] = got[near - 1, plane(6)]


def merge_rows_kernel(axis, near, me, coefs, *refs):
    got, msg = refs[-2:]
    collect(lax.rem(me[axis], near), refs[0], refs[1:near], got)
    rows_of, coef_of = rows_in(got, 1), coefs_in(coefs, 2)
    blocks = [(coef_of(m), rows_of(m)) for m in range(near)]
    while len(blocks) > 1:
        blocks = [merge(a, b) for a, b in zip(blocks[::2], blocks[1::2])]
    msg[plane(0)], msg[plane(1)] = blocks[0][1][0]


def solved_ends(here, near, far, sources, got_near, got_far, coefs_near, coefs_far):
    zero = jnp.zeros_like(got_near[0, plane(0)])
    outer = boundary(
        lax.div(here, near), far, rows_in(got_far, sources), coefs_far, [(zero, zero)] * sources
    )
    return boundary(lax.rem(here, near), near, rows_in(got_near, sources), coefs_near, outer)


def first_z_kernel(me, ef, mf, w, c, p, u, v, r2, src2, curl, flux_y, flux_a, part_a, src, r):
    factor(lambda j: w[strided(j)], me[1] == 0, p, u, v)
    row = lax.broadcasted_iota(jnp.int32, (B, w.shape[1]), 0)
    for i in range(B):
        ez = ef[2, plane(i)]
        after = jnp.where(row == B - 1, 0.0, pltpu.roll(ez, B - 1, 0))
        ri = mf[0, plane(i)] * (1.0 / h) - (after - ez)
        r[plane(i)] = ri
        gain = mf[2, plane(i)]
        if i > 0:
            gain = gain - mf[2, plane(i - 1)]
        src[plane(i)] = c[plane(i)] * ef[1, plane(i)] + (behind_z(ri) - gain * (1.0 / h))
        part_a[plane(i)] = c[plane(i)] * ef[0, plane(i)] - behind_z(mf[1, plane(i)]) * (1.0 / h)
        if i < B - 1:
            rise = ef[1, plane(i + 1)] - ef[1, plane(i)]
            flux_a[plane(i)] = mf[2, plane(i)] * (1.0 / h) - rise
    flux_a[plane(B - 1)] = mf[2, plane(B - 1)] * (1.0 / h) + ef[1, plane(B - 1)]
    for two, of in ((r2, r), (src2, src)):
        two[plane(0)] = of[plane(0)]
        two[plane(1)] = of[strided(B - 1)]

    x = solve_z(src[...], w[...])
    rise = ahead_z(x)
    mx = r[...] + rise
    curl[...] = c[...] * x + behind_z(mx)
    flux_y[...] = -(mx + rise)


def both_y_kernel(near, far, me, got_near, *refs):
    others, refs = refs[:far], refs[far:]
    (ez_next, g_b, u_x, v_x, flux_b, w, c, r2, src2, curl_in, flux_y_in, flux_a_in, part_a, p_y, u_y, v_y) = refs[:16]
    got_far, rise_y, curl, flux_y, flux_a, g_a, g_c, msg, part, fz = refs[16:]
    me_x = me[0]
    top, corner = plane(0), strided(B - 1)
    q, r = lax.div(me_x, near), lax.rem(me_x, near)
    collect(q, others[0], others[1:], got_far)
    ey_next = jnp.where(
        r < near - 1,
        got_near[jnp.minimum(r + 1, near - 1), plane(5)],
        jnp.where(q < far - 1, got_far[jnp.minimum(q + 1, far - 1), plane(5)], 0.0),
    )
    hz_prev = jnp.where(
        r > 0,
        got_near[jnp.maximum(r - 1, 0), plane(6)],
        jnp.where(q > 0, got_far[jnp.maximum(q - 1, 0), plane(6)], 0.0),
    )
    curl[...] = curl_in[...]
    flux_y[...] = flux_y_in[...]
    flux_a[...] = flux_a_in[...]

    last = lax.broadcasted_iota(jnp.int32, ez_next.shape, 0) == B - 1
    ez = ez_next[...]
    ez_top = jnp.where(last, ez[0:1], 0.0)
    rr = jnp.concatenate([r2[plane(0)] - ez_top, r2[plane(1)] - ez])
    ss = jnp.concatenate(
        [src2[plane(0)] + (hz_prev * (1.0 / h) - behind_z(ez_top)), src2[plane(1)] - behind_z(ez)]
    )
    x = solve_z(ss, jnp.concatenate([w[top], w[corner]]))
    rise = ahead_z(x)
    mx = rr + rise
    cc = jnp.concatenate([c[top], c[corner]]) * x + behind_z(mx)
    ff = -(mx + rise)
    curl[corner] = cc[B:]
    flux_y[corner] = ff[B:]
    curl[top] = cc[:B]
    flux_y[top] = ff[:B]

    flux_a[plane(B - 1)] = flux_a[plane(B - 1)] - ey_next

    def source_a(j):
        f = flux_a[strided(j)]
        if j > 0:
            f = f - flux_a[strided(j - 1)]
        return part_a[strided(j)] + f

    first_a, last_a = eliminate(source_a, p_y, g_a)
    last_a = last_a - flux_a[strided(B - 1)]

    ((before, after),) = solved_ends(
        me_x, near, far, 1, got_near, got_far, coefs_in(got_near, 2), coefs_in(got_far, 2)
    )
    for i in range(B):
        fz[plane(i)] = g_b[plane(i)] + (u_x[plane(i)] * before + v_x[plane(i)] * after)
    my_before = jnp.where(me_x == 0, 0.0, fz[top] - before)
    for i in range(B):
        here = fz[plane(i)]
        rise = (fz[plane(i + 1)] if i < B - 1 else after) - here
        my = flux_b[plane(i)] + rise
        rise_y[plane(i)] = my + rise
        part[plane(i)] = c[plane(i)] * here + (my - my_before)
        my_before = my

    def source_c(j):
        f = flux_y[strided(j)]
        if j > 0:
            f = f - flux_y[strided(j - 1)]
        return part[strided(j)] + f

    first_c, last_c = eliminate(source_c, p_y, g_c)
    last_c = last_c - flux_y[strided(B - 1)]
    sent = [first_a, last_a, first_c, last_c, u_y[plane(0)], v_y[plane(0)], v_y[plane(B - 1)]]
    for k, value in enumerate(sent):
        msg[plane(k)] = value


def second_x_kernel(near, far, me, got_near, *refs):
    others, refs = refs[:far], refs[far:]
    g_a, u, v, flux_a, c, curl, p_x, part, flux2, g2, ends_c, msg, got_far, fx = refs
    my = me[1]
    collect(lax.div(my, near), others[0], others[1:], got_far)
    (before, after), (before_c, after_c) = solved_ends(
        my, near, far, 2, got_near, got_far, coefs_in(got_near, 4), coefs_in(got_far, 4)
    )
    ends_c[plane(0)] = before_c
    ends_c[plane(1)] = after_c
    for j in range(B):
        fx[plane(j)] = g_a[plane(j)] + (u[plane(j)] * before + v[plane(j)] * after)
    mz_before = jnp.where(my == 0, 0.0, fx[plane(0)] - before)
    for j in range(B):
        here = fx[plane(j)]
        rise = (fx[plane(j + 1)] if j < B - 1 else after) - here
        mz = flux_a[strided(j)] + rise
        part[strided(j)] = c[strided(j)] * here + (mz - mz_before)
        flux2[strided(j)] = -(mz + rise)
        mz_before = mz

    def source(i):
        f = flux2[plane(i)]
        if i > 0:
            f = f - flux2[plane(i - 1)]
        return curl[plane(i)] + f

    first, last = eliminate(source, p_x, g2)
    msg[plane(0)] = first
    msg[plane(1)] = last - flux2[plane(B - 1)]


def second_z_kernel(
    part, rise_y, w, ends_c, g_c, u, v, flux_y, elec, magn, full_x, full_z, new_x, new_y, sems
):
    before, after = ends_c[plane(0)], ends_c[plane(1)]
    here = None
    for j in range(B):
        ahead = g_c[plane(j)] + (u[plane(j)] * before + v[plane(j)] * after)
        full_z[strided(j)] = ahead
        if j > 0:
            new_x[strided(j - 1)] = -h * (flux_y[strided(j - 1)] + (ahead - here))
        here = ahead
    new_x[strided(B - 1)] = -h * (flux_y[strided(B - 1)] + (after - here))
    stores = [(full_z, elec.at[2]), (new_x, magn.at[0]), (full_x, elec.at[0]), (new_y, magn.at[1])]
    stores = [pltpu.make_async_copy(a, b, sems.at[k]) for k, (a, b) in enumerate(stores)]
    stores[0].start()
    stores[1].start()

    a = rise_y[...]
    x = solve_z(part[...] - behind_z(a), w[...])
    full_x[...] = x
    new_y[...] = h * (a - ahead_z(x))
    stores[2].start()
    stores[3].start()
    for store in stores:
        store.wait()


def last_kernel(near, far, me, coefs_near, coefs_far, got_near, *refs):
    others, refs = refs[:far], refs[far:]
    g, u, v, flux2, _, _, elec, magn, got_far, full_y, new_z, sems = refs
    collect(lax.div(me[0], near), others[0], others[1:], got_far)
    ((before, after),) = solved_ends(
        me[0], near, far, 1, got_near, got_far, coefs_in(coefs_near, 2), coefs_in(coefs_far, 2)
    )
    stores = [(full_y, elec.at[1]), (new_z, magn.at[2])]
    stores = [pltpu.make_async_copy(a, b, sems.at[k]) for k, (a, b) in enumerate(stores)]
    for i in range(B):
        full_y[plane(i)] = g[plane(i)] + (u[plane(i)] * before + v[plane(i)] * after)
    stores[0].start()
    for i in range(B):
        rise = (full_y[plane(i + 1)] if i < B - 1 else after) - full_y[plane(i)]
        new_z[plane(i)] = -h * (flux2[plane(i)] + rise)
    stores[1].start()
    for store in stores:
        store.wait()


VMEM = pl.BlockSpec(memory_space=pltpu.VMEM)
SMEM = pl.BlockSpec(memory_space=pltpu.SMEM)
HBM = pl.BlockSpec(memory_space=pltpu.HBM)


def call(kernel, ins, outs, specs=None, out_specs=None, scratch=(), aliases=None, flops=1_000_000):
    shapes = [pltpu.HBM(s, F32) if out_specs else jax.ShapeDtypeStruct(s, F32) for s in outs]
    return pl.pallas_call(
        kernel,
        out_shape=shapes,
        in_specs=specs or [SMEM] + [VMEM] * (len(ins) - 1),
        out_specs=out_specs or [VMEM] * len(outs),
        scratch_shapes=[pltpu.VMEM(s, F32) if isinstance(s, tuple) else s for s in scratch],
        input_output_aliases=aliases or {},
        compiler_params=pltpu.CompilerParams(vmem_limit_bytes=24 * 1024 * 1024),
        cost_estimate=pl.CostEstimate(flops=flops, bytes_accessed=1_000_000, transcendentals=0),
    )(*ins)


def shared(value, axis, n, step, count, order):
    got = {
        s: lax.ppermute(value, axis, [(i, i ^ (step * s)) for i in range(n)]) for s in order if s < count
    }
    return [value] + [got[s] for s in range(1, count)]


def split(n):
    near = 1 << (n.bit_length() // 2)
    return near, n // near


def local(electric, magnetic, material, permittivity, conductivity):
    nx, ny = lax.axis_size("px"), lax.axis_size("py")
    near_x, far_x = split(nx)
    near_y, far_y = split(ny)
    nz = material.shape[2]
    cells = (B * B, nz)
    me = jnp.stack([lax.axis_index("px"), lax.axis_index("py")]).astype(jnp.int32)
    in_hbm = lambda a: pltpu.with_memory_space_constraint(a, pltpu.HBM)
    elec = in_hbm(electric.reshape(3, *cells))
    magn = in_hbm(magnetic.reshape(3, *cells))
    ids = in_hbm(material.reshape(cells))
    dma = pltpu.SemaphoreType.DMA
    px_near, px_far, py_near, py_far = (1, 2, 3), (2, 1, 3), (2, 3, 1), (1, 3, 2)

    hx_prev = lax.ppermute(magnetic[0, :, B - 1], "py", [(i, i + 1) for i in range(ny - 1)])
    w, c, p_x, u_x, v_x, flux_b, part_b, ef, mf, ez_first = call(
        tables_kernel,
        [me, in_hbm(permittivity), in_hbm(conductivity), ids, elec, magn],
        [cells] * 7 + [(3, *cells)] * 2 + [(B, nz)],
        specs=[SMEM] + [HBM] * 5,
        scratch=[pltpu.VMEM(cells, jnp.int32)] + [pltpu.SMEM(permittivity.shape, F32)] * 2 + [dma((9,))],
    )
    g_b, msg = call(
        first_x_kernel,
        [part_b, hx_prev, flux_b, p_x, u_x, v_x, ef, mf],
        [cells, (7 * B, nz)],
        specs=[VMEM] * 8,
    )
    ins = shared(msg, "px", nx, 1, near_x, px_near)
    ez_next = lax.ppermute(ez_first, "py", [(i + 1, i) for i in range(ny - 1)])
    near_b, msg = call(
        functools.partial(merge_kernel, 0, near_x, 1, True),
        [me] + ins,
        [(near_x, 7 * B, nz), (7 * B, nz)],
    )
    ins = shared(msg, "px", nx, near_x, far_x, px_far)
    p_y, u_y, v_y, r2, src2, curl, flux_y, flux_a, part_a = call(
        first_z_kernel,
        [me, ef, mf, w, c],
        [cells] * 3 + [(2 * B, nz)] * 2 + [cells] * 4,
        scratch=[cells] * 2,
        flops=8_000_000,
    )
    ins = [me, near_b] + ins + [ez_next, g_b, u_x, v_x, flux_b, w, c, r2, src2]
    far_b, rise_y, curl, flux_y, flux_a, g_a, g_c, msg = call(
        functools.partial(both_y_kernel, near_x, far_x),
        ins + [curl, flux_y, flux_a, part_a, p_y, u_y, v_y],
        [(far_x, 7 * B, nz)] + [cells] * 6 + [(7 * B, nz)],
        scratch=[cells] * 2,
    )
    ins = shared(msg, "py", ny, 1, near_y, py_near)
    near_ac, msg = call(
        functools.partial(merge_kernel, 1, near_y, 2, False), [me] + ins, [(near_y, 7 * B, nz), (7 * B, nz)]
    )
    ins = shared(msg, "py", ny, near_y, far_y, py_far)
    part_x, flux2, g2, ends_c, msg = call(
        functools.partial(second_x_kernel, near_y, far_y),
        [me, near_ac] + ins + [g_a, u_y, v_y, flux_a, c, curl, p_x],
        [cells] * 3 + [(2 * B, nz)] * 2,
        scratch=[(far_y, 7 * B, nz), cells],
    )
    ins = shared(msg, "px", nx, 1, near_x, px_near)
    near_a, msg = call(
        functools.partial(merge_rows_kernel, 0, near_x),
        [me, near_b] + ins,
        [(near_x, 2 * B, nz), (2 * B, nz)],
    )
    ins = shared(msg, "px", nx, near_x, far_x, px_far)
    elec, magn = call(
        second_z_kernel,
        [part_x, rise_y, w, ends_c, g_c, u_y, v_y, flux_y],
        [(3, *cells)] * 2,
        specs=[VMEM] * 8,
        out_specs=[HBM] * 2,
        scratch=[cells] * 4 + [dma((4,))],
        flops=8_000_000,
    )
    ins = [me, near_b, far_b, near_a] + ins + [g2, u_x, v_x, flux2]
    at = len(ins)
    out = call(
        functools.partial(last_kernel, near_x, far_x),
        ins + [elec, magn],
        [(3, *cells)] * 2,
        specs=[SMEM] + [VMEM] * (at - 1) + [HBM] * 2,
        out_specs=[HBM] * 2,
        scratch=[(far_x, 2 * B, nz), cells, cells, dma((2,))],
        aliases={at: 0, at + 1: 1},
    )
    return tuple(a.reshape(3, B, B, nz) for a in out)


def solution(mesh):
    placed = (P(None, "px", "py", None), P(None, "px", "py", None), P("px", "py", None), P(), P())
    return jax.shard_map(
        local,
        mesh=mesh,
        in_specs=placed,
        out_specs=(P(None, "px", "py", None), P(None, "px", "py", None)),
        check_vma=False,
    )
```

```python
import functools

import jax
import jax.numpy as jnp
from jax import lax
from jax.experimental import pallas as pl
from jax.experimental.pallas import tpu as pltpu
from jax.sharding import PartitionSpec as P

h = 32.0
B = 16
F32 = jnp.float32


def plane(i):
    return pl.ds(i * B, B)


def strided(j):
    return pl.ds(j, B, stride=B)


def lanes(v):
    return lax.broadcasted_iota(jnp.int32, v.shape, 1)


def behind_z(v):
    return v - jnp.where(lanes(v) == 0, 0.0, pltpu.roll(v, 1, 1))


def ahead_z(v):
    n = v.shape[1]
    return jnp.where(lanes(v) == n - 1, 0.0, pltpu.roll(v, n - 1, 1)) - v


def factor(w_of, first_block, p, u, v):
    d = None
    y = []
    for j in range(B):
        w = w_of(j)
        e = w + (jnp.where(first_block, 0.0, 1.0) if j == 0 else d)
        inv = 1.0 / (1.0 + e)
        d = e * inv
        p[plane(j)] = inv
        y.append(jnp.ones_like(inv) if j == 0 else y[-1] * last)
        last = inv
    uj = y[B - 1] * last
    vj = last
    u[plane(B - 1)] = uj
    v[plane(B - 1)] = vj
    for j in range(B - 2, -1, -1):
        inv = p[plane(j)]
        uj = inv * (y[j] + uj)
        vj = inv * vj
        u[plane(j)] = uj
        v[plane(j)] = vj


def eliminate(source_of, p, g):
    y = source_of(0)
    ys = [y]
    for j in range(1, B):
        y = source_of(j) + p[plane(j - 1)] * y
        ys.append(y)
    x = y * p[plane(B - 1)]
    end = x
    g[plane(B - 1)] = x
    for j in range(B - 2, -1, -1):
        x = p[plane(j)] * (ys[j] + x)
        g[plane(j)] = x
    return x, end


def boundary(me, n, rows_of, coef_of, outer):
    left = [a for a, _ in outer]
    right = [b for _, b in outer]
    beta = delta = jnp.zeros_like(left[0])
    for s in range(n - 1):
        ff, fl, ll = coef_of(s)
        t = fl / (1.0 - ff * beta)
        on = s < me
        left = [
            jnp.where(on, dl + t * (a + beta * gf), a) for a, (gf, dl) in zip(left, rows_of(s))
        ]
        beta = jnp.where(on, ll + t * beta * fl, beta)
        m = n - 1 - s
        ff, fl, ll = coef_of(m)
        t = fl / (1.0 - ll * delta)
        on = m > me
        right = [
            jnp.where(on, gf + t * (b + delta * dl), b) for b, (gf, dl) in zip(right, rows_of(m))
        ]
        delta = jnp.where(on, ff + t * delta * fl, delta)
    ff, fl, ll = coef_of(me)
    after_scale = 1.0 / (1.0 - delta * ll)
    t = fl * after_scale
    before_scale = 1.0 / (1.0 - beta * (ff + t * delta * fl))
    ends = []
    for a, b, (gf, dl) in zip(left, right, rows_of(me)):
        before = (a + beta * (gf + t * (b + delta * dl))) * before_scale
        ends.append((before, (b + delta * (dl + fl * before)) * after_scale))
    return ends


def merge(one, two):
    (ff1, fl1, ll1), rows1 = one
    (ff2, fl2, ll2), rows2 = two
    d = 1.0 / (1.0 - ll1 * ff2)
    t1, t2 = fl1 * d, fl2 * d
    rows = [
        (gf1 + t1 * (gf2 + ff2 * dl1), dl2 + t2 * (dl1 + ll1 * gf2))
        for (gf1, dl1), (gf2, dl2) in zip(rows1, rows2)
    ]
    return (ff1 + t1 * fl1 * ff2, t1 * fl2, ll2 + t2 * fl2 * ll1), rows


def solve_z(r, w):
    n = r.shape[1]
    lane = lanes(r)
    e = jnp.where(lane == n - 1, 0.0, 1.0)
    l = jnp.where(lane == 0, 0.0, 1.0)
    s = w + jnp.where(lane == n - 1, 1.0, 0.0)
    step = 1
    while step < n:
        inv = 1.0 / (s + (l + e))
        a, b = e * inv, l * inv
        r = r + (pltpu.roll(a * r, step, 1) + pltpu.roll(b * r, n - step, 1))
        s = s + (pltpu.roll(a * s, step, 1) + pltpu.roll(b * s, n - step, 1))
        g = a * l
        if 2 * step < n:
            e, l = pltpu.roll(g, n - step, 1), pltpu.roll(g, step, 1)
        step *= 2
    return r / s


def collect(r, order, own, others, got):
    got[r] = own[...]
    for s, other in zip(order, others):
        got[lax.bitwise_xor(r, s)] = other[...]


def rows_in(got, sources):
    return lambda m: [(got[m, plane(2 * k)], got[m, plane(2 * k + 1)]) for k in range(sources)]


def coefs_in(got, at):
    return lambda m: tuple(got[m, plane(at + k)] for k in range(3))


def tables_kernel(
    me, eps_in, sig_in, material, elec_in, magn_in, w, c, p, u, v, flux, part, elec, magn, ez_first, ids, eps, sig, sems
):
    loads = [(eps_in, eps), (sig_in, sig), (material, ids)]
    for field, to, k in ((elec_in, elec, 0), (magn_in, magn, 1), (elec_in, elec, 2), (magn_in, magn, 0)):
        loads.append((field.at[k], to.at[k]))
    loads += [(elec_in.at[1], elec.at[1]), (magn_in.at[2], magn.at[2])]
    loads = [pltpu.make_async_copy(a, b, sems.at[k]) for k, (a, b) in enumerate(loads)]
    for load in loads:
        load.start()
    for load in loads[:3]:
        load.wait()
    ws = [eps[m] * (1.0 / (h * h)) + sig[m] * (0.5 / h) for m in range(eps.shape[0])]
    cs = [eps[m] * (1.0 / (h * h)) - sig[m] * (0.5 / h) for m in range(eps.shape[0])]
    for i in range(B):
        cell = ids[plane(i)]
        wi = jnp.full(cell.shape, ws[0], F32)
        ci = jnp.full(cell.shape, cs[0], F32)
        for m in range(1, len(ws)):
            wi = jnp.where(cell == m, ws[m], wi)
            ci = jnp.where(cell == m, cs[m], ci)
        w[plane(i)] = wi
        c[plane(i)] = ci
    factor(lambda i: w[plane(i)], me[0] == 0, p, u, v)
    for load in loads[3:7]:
        load.wait()
    row = lax.broadcasted_iota(jnp.int32, (B, w.shape[1]), 0)
    for i in range(B):
        q = magn[1, plane(i)] * (1.0 / h) - ahead_z(elec[0, plane(i)])
        flux[plane(i)] = q
        if i > 0:
            q = q - flux[plane(i - 1)]
        here = magn[0, plane(i)]
        before = jnp.where(row == 0, 0.0, pltpu.roll(here, 1, 0))
        part[plane(i)] = c[plane(i)] * elec[2, plane(i)] + (q - (here - before) * (1.0 / h))
    ez_first[...] = elec.at[2][strided(0)]
    for load in loads[7:]:
        load.wait()


def first_x_kernel(part, hx_prev, flux, p, u, v, elec, magn, g, msg):
    row = lax.broadcasted_iota(jnp.int32, hx_prev.shape, 0)

    def source(i):
        return part[plane(i)] + jnp.where(row == 0, hx_prev[pl.ds(i, 1)] * (1.0 / h), 0.0)

    first, last = eliminate(source, p, g)
    msg[plane(0)] = first
    msg[plane(1)] = last - flux[plane(B - 1)]
    msg[plane(2)] = u[plane(0)]
    msg[plane(3)] = v[plane(0)]
    msg[plane(4)] = v[plane(B - 1)]
    msg[plane(5)] = elec[1, plane(0)]
    msg[plane(6)] = magn[2, plane(B - 1)]


def merge_kernel(axis, near, order, sources, halos, me, *refs):
    got, msg = refs[-2:]
    collect(lax.rem(me[axis], near), order, refs[0], refs[1:near], got)
    rows_of, coef_of = rows_in(got, sources), coefs_in(got, 2 * sources)
    blocks = [(coef_of(m), rows_of(m)) for m in range(near)]
    while len(blocks) > 1:
        blocks = [merge(a, b) for a, b in zip(blocks[::2], blocks[1::2])]
    coefs, rows = blocks[0]
    for k, value in enumerate([v for pair in rows for v in pair] + list(coefs)):
        msg[plane(k)] = value
    if halos:
        msg[plane(5)] = got[0, plane(5)]
        msg[plane(6)] = got[near - 1, plane(6)]


def merge_rows_kernel(axis, near, order, me, coefs, *refs):
    got, msg = refs[-2:]
    collect(lax.rem(me[axis], near), order, refs[0], refs[1:near], got)
    rows_of, coef_of = rows_in(got, 1), coefs_in(coefs, 2)
    blocks = [(coef_of(m), rows_of(m)) for m in range(near)]
    while len(blocks) > 1:
        blocks = [merge(a, b) for a, b in zip(blocks[::2], blocks[1::2])]
    msg[plane(0)], msg[plane(1)] = blocks[0][1][0]


def solved_ends(here, near, far, sources, got_near, got_far, coefs_near, coefs_far):
    zero = jnp.zeros_like(got_near[0, plane(0)])
    outer = boundary(
        lax.div(here, near), far, rows_in(got_far, sources), coefs_far, [(zero, zero)] * sources
    )
    return boundary(lax.rem(here, near), near, rows_in(got_near, sources), coefs_near, outer)


def first_z_kernel(me, ef, mf, w, c, p, u, v, r2, src2, curl, flux_y, flux_a, part_a, src, r):
    factor(lambda j: w[strided(j)], me[1] == 0, p, u, v)
    row = lax.broadcasted_iota(jnp.int32, (B, w.shape[1]), 0)
    for i in range(B):
        ez = ef[2, plane(i)]
        after = jnp.where(row == B - 1, 0.0, pltpu.roll(ez, B - 1, 0))
        ri = mf[0, plane(i)] * (1.0 / h) - (after - ez)
        r[plane(i)] = ri
        gain = mf[2, plane(i)]
        if i > 0:
            gain = gain - mf[2, plane(i - 1)]
        src[plane(i)] = c[plane(i)] * ef[1, plane(i)] + (behind_z(ri) - gain * (1.0 / h))
        part_a[plane(i)] = c[plane(i)] * ef[0, plane(i)] - behind_z(mf[1, plane(i)]) * (1.0 / h)
        if i < B - 1:
            rise = ef[1, plane(i + 1)] - ef[1, plane(i)]
            flux_a[plane(i)] = mf[2, plane(i)] * (1.0 / h) - rise
    flux_a[plane(B - 1)] = mf[2, plane(B - 1)] * (1.0 / h) + ef[1, plane(B - 1)]
    for two, of in ((r2, r), (src2, src)):
        two[plane(0)] = of[plane(0)]
        two[plane(1)] = of[strided(B - 1)]

    x = solve_z(src[...], w[...])
    rise = ahead_z(x)
    mx = r[...] + rise
    curl[...] = c[...] * x + behind_z(mx)
    flux_y[...] = -(mx + rise)


def both_y_kernel(near, far, order, me, got_near, *refs):
    others, refs = refs[:far], refs[far:]
    (ez_next, g_b, u_x, v_x, flux_b, w, c, r2, src2, curl_in, flux_y_in, flux_a_in, part_a, p_y, u_y, v_y) = refs[:16]
    got_far, rise_y, curl, flux_y, flux_a, g_a, g_c, msg, part, fz = refs[16:]
    me_x = me[0]
    top, corner = plane(0), strided(B - 1)
    q, r = lax.div(me_x, near), lax.rem(me_x, near)
    collect(q, order, others[0], others[1:], got_far)
    ey_next = jnp.where(
        r < near - 1,
        got_near[jnp.minimum(r + 1, near - 1), plane(5)],
        jnp.where(q < far - 1, got_far[jnp.minimum(q + 1, far - 1), plane(5)], 0.0),
    )
    hz_prev = jnp.where(
        r > 0,
        got_near[jnp.maximum(r - 1, 0), plane(6)],
        jnp.where(q > 0, got_far[jnp.maximum(q - 1, 0), plane(6)], 0.0),
    )
    curl[...] = curl_in[...]
    flux_y[...] = flux_y_in[...]
    flux_a[...] = flux_a_in[...]

    last = lax.broadcasted_iota(jnp.int32, ez_next.shape, 0) == B - 1
    ez = ez_next[...]
    ez_top = jnp.where(last, ez[0:1], 0.0)
    rr = jnp.concatenate([r2[plane(0)] - ez_top, r2[plane(1)] - ez])
    ss = jnp.concatenate(
        [src2[plane(0)] + (hz_prev * (1.0 / h) - behind_z(ez_top)), src2[plane(1)] - behind_z(ez)]
    )
    x = solve_z(ss, jnp.concatenate([w[top], w[corner]]))
    rise = ahead_z(x)
    mx = rr + rise
    cc = jnp.concatenate([c[top], c[corner]]) * x + behind_z(mx)
    ff = -(mx + rise)
    curl[corner] = cc[B:]
    flux_y[corner] = ff[B:]
    curl[top] = cc[:B]
    flux_y[top] = ff[:B]

    flux_a[plane(B - 1)] = flux_a[plane(B - 1)] - ey_next

    def source_a(j):
        f = flux_a[strided(j)]
        if j > 0:
            f = f - flux_a[strided(j - 1)]
        return part_a[strided(j)] + f

    first_a, last_a = eliminate(source_a, p_y, g_a)
    last_a = last_a - flux_a[strided(B - 1)]

    ((before, after),) = solved_ends(
        me_x, near, far, 1, got_near, got_far, coefs_in(got_near, 2), coefs_in(got_far, 2)
    )
    for i in range(B):
        fz[plane(i)] = g_b[plane(i)] + (u_x[plane(i)] * before + v_x[plane(i)] * after)
    my_before = jnp.where(me_x == 0, 0.0, fz[top] - before)
    for i in range(B):
        here = fz[plane(i)]
        rise = (fz[plane(i + 1)] if i < B - 1 else after) - here
        my = flux_b[plane(i)] + rise
        rise_y[plane(i)] = my + rise
        part[plane(i)] = c[plane(i)] * here + (my - my_before)
        my_before = my

    def source_c(j):
        f = flux_y[strided(j)]
        if j > 0:
            f = f - flux_y[strided(j - 1)]
        return part[strided(j)] + f

    first_c, last_c = eliminate(source_c, p_y, g_c)
    last_c = last_c - flux_y[strided(B - 1)]
    sent = [first_a, last_a, first_c, last_c, u_y[plane(0)], v_y[plane(0)], v_y[plane(B - 1)]]
    for k, value in enumerate(sent):
        msg[plane(k)] = value


def second_x_kernel(near, far, order, me, got_near, *refs):
    others, refs = refs[:far], refs[far:]
    g_a, u, v, flux_a, c, curl, p_x, part, flux2, g2, ends_c, msg, got_far, fx = refs
    my = me[1]
    collect(lax.div(my, near), order, others[0], others[1:], got_far)
    (before, after), (before_c, after_c) = solved_ends(
        my, near, far, 2, got_near, got_far, coefs_in(got_near, 4), coefs_in(got_far, 4)
    )
    ends_c[plane(0)] = before_c
    ends_c[plane(1)] = after_c
    for j in range(B):
        fx[plane(j)] = g_a[plane(j)] + (u[plane(j)] * before + v[plane(j)] * after)
    mz_before = jnp.where(my == 0, 0.0, fx[plane(0)] - before)
    for j in range(B):
        here = fx[plane(j)]
        rise = (fx[plane(j + 1)] if j < B - 1 else after) - here
        mz = flux_a[strided(j)] + rise
        part[strided(j)] = c[strided(j)] * here + (mz - mz_before)
        flux2[strided(j)] = -(mz + rise)
        mz_before = mz

    def source(i):
        f = flux2[plane(i)]
        if i > 0:
            f = f - flux2[plane(i - 1)]
        return curl[plane(i)] + f

    first, last = eliminate(source, p_x, g2)
    msg[plane(0)] = first
    msg[plane(1)] = last - flux2[plane(B - 1)]


def second_y_kernel(ends_c, g_c, u, v, flux_y, elec, magn, full_z, new_x, sems):
    stores = [(full_z, elec.at[2]), (new_x, magn.at[0])]
    stores = [pltpu.make_async_copy(a, b, sems.at[k]) for k, (a, b) in enumerate(stores)]
    before, after = ends_c[plane(0)], ends_c[plane(1)]
    here = None
    for j in range(B):
        ahead = g_c[plane(j)] + (u[plane(j)] * before + v[plane(j)] * after)
        full_z[strided(j)] = ahead
        if j > 0:
            new_x[strided(j - 1)] = -h * (flux_y[strided(j - 1)] + (ahead - here))
        here = ahead
    new_x[strided(B - 1)] = -h * (flux_y[strided(B - 1)] + (after - here))
    for store in stores:
        store.start()
    for store in stores:
        store.wait()


def second_z_kernel(part, rise_y, w, _, __, elec, magn, full_x, new_y, sems):
    stores = [(full_x, elec.at[0]), (new_y, magn.at[1])]
    stores = [pltpu.make_async_copy(a, b, sems.at[k]) for k, (a, b) in enumerate(stores)]
    a = rise_y[...]
    x = solve_z(part[...] - behind_z(a), w[...])
    full_x[...] = x
    stores[0].start()
    new_y[...] = h * (a - ahead_z(x))
    stores[1].start()
    for store in stores:
        store.wait()


def last_kernel(near, far, order, me, coefs_near, coefs_far, got_near, *refs):
    others, refs = refs[:far], refs[far:]
    g, u, v, flux2, _, _, elec, magn, got_far, full_y, new_z, sems = refs
    collect(lax.div(me[0], near), order, others[0], others[1:], got_far)
    ((before, after),) = solved_ends(
        me[0], near, far, 1, got_near, got_far, coefs_in(coefs_near, 2), coefs_in(coefs_far, 2)
    )
    stores = [(full_y, elec.at[1]), (new_z, magn.at[2])]
    stores = [pltpu.make_async_copy(a, b, sems.at[k]) for k, (a, b) in enumerate(stores)]
    for i in range(B):
        full_y[plane(i)] = g[plane(i)] + (u[plane(i)] * before + v[plane(i)] * after)
    stores[0].start()
    for i in range(B):
        rise = (full_y[plane(i + 1)] if i < B - 1 else after) - full_y[plane(i)]
        new_z[plane(i)] = -h * (flux2[plane(i)] + rise)
    stores[1].start()
    for store in stores:
        store.wait()


VMEM = pl.BlockSpec(memory_space=pltpu.VMEM)
SMEM = pl.BlockSpec(memory_space=pltpu.SMEM)
HBM = pl.BlockSpec(memory_space=pltpu.HBM)


def call(kernel, ins, outs, specs=None, out_specs=None, scratch=(), aliases=None, flops=1_000_000):
    shapes = [pltpu.HBM(s, F32) if out_specs else jax.ShapeDtypeStruct(s, F32) for s in outs]
    return pl.pallas_call(
        kernel,
        out_shape=shapes,
        in_specs=specs or [SMEM] + [VMEM] * (len(ins) - 1),
        out_specs=out_specs or [VMEM] * len(outs),
        scratch_shapes=[pltpu.VMEM(s, F32) if isinstance(s, tuple) else s for s in scratch],
        input_output_aliases=aliases or {},
        compiler_params=pltpu.CompilerParams(vmem_limit_bytes=24 * 1024 * 1024),
        cost_estimate=pl.CostEstimate(flops=flops, bytes_accessed=1_000_000, transcendentals=0),
    )(*ins)


def shared(value, axis, n, step, order):
    return [value] + [lax.ppermute(value, axis, [(i, i ^ (step * s)) for i in range(n)]) for s in order]


def split(n):
    near = 1 << (n.bit_length() // 2)
    return near, n // near


def local(electric, magnetic, material, permittivity, conductivity):
    nx, ny = lax.axis_size("px"), lax.axis_size("py")
    near_x, far_x = split(nx)
    near_y, far_y = split(ny)
    nz = material.shape[2]
    cells = (B * B, nz)
    me = jnp.stack([lax.axis_index("px"), lax.axis_index("py")]).astype(jnp.int32)
    in_hbm = lambda a: pltpu.with_memory_space_constraint(a, pltpu.HBM)
    elec = in_hbm(electric.reshape(3, *cells))
    magn = in_hbm(magnetic.reshape(3, *cells))
    ids = in_hbm(material.reshape(cells))
    dma = pltpu.SemaphoreType.DMA
    orders = [(1, 2, 3), (2, 1, 3), (2, 3, 1), (1, 3, 2)]
    counts = (near_x, far_x, near_y, far_y)
    px_near, px_far, py_near, py_far = [
        tuple(s for s in order if s < count) for order, count in zip(orders, counts)
    ]

    hx_prev = lax.ppermute(magnetic[0, :, B - 1], "py", [(i, i + 1) for i in range(ny - 1)])
    w, c, p_x, u_x, v_x, flux_b, part_b, ef, mf, ez_first = call(
        tables_kernel,
        [me, in_hbm(permittivity), in_hbm(conductivity), ids, elec, magn],
        [cells] * 7 + [(3, *cells)] * 2 + [(B, nz)],
        specs=[SMEM] + [HBM] * 5,
        scratch=[pltpu.VMEM(cells, jnp.int32)] + [pltpu.SMEM(permittivity.shape, F32)] * 2 + [dma((9,))],
    )
    g_b, msg = call(
        first_x_kernel,
        [part_b, hx_prev, flux_b, p_x, u_x, v_x, ef, mf],
        [cells, (7 * B, nz)],
        specs=[VMEM] * 8,
    )
    ins = shared(msg, "px", nx, 1, px_near)
    ez_next = lax.ppermute(ez_first, "py", [(i + 1, i) for i in range(ny - 1)])
    near_b, msg = call(
        functools.partial(merge_kernel, 0, near_x, px_near, 1, True),
        [me] + ins,
        [(near_x, 7 * B, nz), (7 * B, nz)],
    )
    msg, ez_next = lax.optimization_barrier((msg, ez_next))
    ins = shared(msg, "px", nx, near_x, px_far)
    p_y, u_y, v_y, r2, src2, curl, flux_y, flux_a, part_a = call(
        first_z_kernel,
        [me, ef, mf, w, c],
        [cells] * 3 + [(2 * B, nz)] * 2 + [cells] * 4,
        scratch=[cells] * 2,
        flops=8_000_000,
    )
    ins = [me, near_b] + ins + [ez_next, g_b, u_x, v_x, flux_b, w, c, r2, src2]
    far_b, rise_y, curl, flux_y, flux_a, g_a, g_c, msg = call(
        functools.partial(both_y_kernel, near_x, far_x, px_far),
        ins + [curl, flux_y, flux_a, part_a, p_y, u_y, v_y],
        [(far_x, 7 * B, nz)] + [cells] * 6 + [(7 * B, nz)],
        scratch=[cells] * 2,
    )
    ins = shared(msg, "py", ny, 1, py_near)
    near_ac, msg = call(
        functools.partial(merge_kernel, 1, near_y, py_near, 2, False), [me] + ins, [(near_y, 7 * B, nz), (7 * B, nz)]
    )
    ins = shared(msg, "py", ny, near_y, py_far)
    part_x, flux2, g2, ends_c, msg = call(
        functools.partial(second_x_kernel, near_y, far_y, py_far),
        [me, near_ac] + ins + [g_a, u_y, v_y, flux_a, c, curl, p_x],
        [cells] * 3 + [(2 * B, nz)] * 2,
        scratch=[(far_y, 7 * B, nz), cells],
    )
    ins = shared(msg, "px", nx, 1, px_near)
    elec, magn = call(
        second_y_kernel,
        [ends_c, g_c, u_y, v_y, flux_y],
        [(3, *cells)] * 2,
        specs=[VMEM] * 5,
        out_specs=[HBM] * 2,
        scratch=[cells] * 2 + [dma((2,))],
    )
    near_a, msg = call(
        functools.partial(merge_rows_kernel, 0, near_x, px_near),
        [me, near_b] + ins,
        [(near_x, 2 * B, nz), (2 * B, nz)],
    )
    msg, elec = lax.optimization_barrier((msg, elec))
    ins = shared(msg, "px", nx, near_x, px_far)
    elec, magn = call(
        second_z_kernel,
        [part_x, rise_y, w, elec, magn],
        [(3, *cells)] * 2,
        specs=[VMEM] * 3 + [HBM] * 2,
        out_specs=[HBM] * 2,
        scratch=[cells] * 2 + [dma((2,))],
        aliases={3: 0, 4: 1},
        flops=8_000_000,
    )
    ins = [me, near_b, far_b, near_a] + ins + [g2, u_x, v_x, flux2]
    at = len(ins)
    out = call(
        functools.partial(last_kernel, near_x, far_x, px_far),
        ins + [elec, magn],
        [(3, *cells)] * 2,
        specs=[SMEM] + [VMEM] * (at - 1) + [HBM] * 2,
        out_specs=[HBM] * 2,
        scratch=[(far_x, 2 * B, nz), cells, cells, dma((2,))],
        aliases={at: 0, at + 1: 1},
    )
    return tuple(a.reshape(3, B, B, nz) for a in out)


def solution(mesh):
    placed = (P(None, "px", "py", None), P(None, "px", "py", None), P("px", "py", None), P(), P())
    return jax.shard_map(
        local,
        mesh=mesh,
        in_specs=placed,
        out_specs=(P(None, "px", "py", None), P(None, "px", "py", None)),
        check_vma=False,
    )
```

```python
import functools

import jax
import jax.numpy as jnp
from jax import lax
from jax.experimental import pallas as pl
from jax.experimental.pallas import tpu as pltpu
from jax.sharding import PartitionSpec as P

h = 32.0
B = 16
F32 = jnp.float32


def plane(i):
    return pl.ds(i * B, B)


def strided(j):
    return pl.ds(j, B, stride=B)


def lanes(v):
    return lax.broadcasted_iota(jnp.int32, v.shape, 1)


def behind_z(v):
    return v - jnp.where(lanes(v) == 0, 0.0, pltpu.roll(v, 1, 1))


def ahead_z(v):
    n = v.shape[1]
    return jnp.where(lanes(v) == n - 1, 0.0, pltpu.roll(v, n - 1, 1)) - v


def factor(w_of, first_block, p, u, v):
    d = None
    y = []
    for j in range(B):
        w = w_of(j)
        e = w + (jnp.where(first_block, 0.0, 1.0) if j == 0 else d)
        inv = 1.0 / (1.0 + e)
        d = e * inv
        p[plane(j)] = inv
        y.append(jnp.ones_like(inv) if j == 0 else y[-1] * last)
        last = inv
    uj = y[B - 1] * last
    vj = last
    u[plane(B - 1)] = uj
    v[plane(B - 1)] = vj
    for j in range(B - 2, -1, -1):
        inv = p[plane(j)]
        uj = inv * (y[j] + uj)
        vj = inv * vj
        u[plane(j)] = uj
        v[plane(j)] = vj


def eliminate(source_of, p, g):
    y = source_of(0)
    ys = [y]
    for j in range(1, B):
        y = source_of(j) + p[plane(j - 1)] * y
        ys.append(y)
    x = y * p[plane(B - 1)]
    end = x
    g[plane(B - 1)] = x
    for j in range(B - 2, -1, -1):
        x = p[plane(j)] * (ys[j] + x)
        g[plane(j)] = x
    return x, end


def boundary(me, rows, coefs, here, coef_here, outer):
    n = len(rows)
    left = [a for a, _ in outer]
    right = [b for _, b in outer]
    beta = delta = jnp.zeros_like(left[0])
    for s in range(n - 1):
        ff, fl, ll = coefs[s]
        t = fl / (1.0 - ff * beta)
        on = s < me
        left = [jnp.where(on, dl + t * (a + beta * gf), a) for a, (gf, dl) in zip(left, rows[s])]
        beta = jnp.where(on, ll + t * beta * fl, beta)
        m = n - 1 - s
        ff, fl, ll = coefs[m]
        t = fl / (1.0 - ll * delta)
        on = m > me
        right = [jnp.where(on, gf + t * (b + delta * dl), b) for b, (gf, dl) in zip(right, rows[m])]
        delta = jnp.where(on, ff + t * delta * fl, delta)
    ff, fl, ll = coef_here
    after_scale = 1.0 / (1.0 - delta * ll)
    t = fl * after_scale
    before_scale = 1.0 / (1.0 - beta * (ff + t * delta * fl))
    ends = []
    for a, b, (gf, dl) in zip(left, right, here):
        before = (a + beta * (gf + t * (b + delta * dl))) * before_scale
        ends.append((before, (b + delta * (dl + fl * before)) * after_scale))
    return ends


def merge(one, two):
    (ff1, fl1, ll1), rows1 = one
    (ff2, fl2, ll2), rows2 = two
    d = 1.0 / (1.0 - ll1 * ff2)
    t1, t2 = fl1 * d, fl2 * d
    rows = [
        (gf1 + t1 * (gf2 + ff2 * dl1), dl2 + t2 * (dl1 + ll1 * gf2))
        for (gf1, dl1), (gf2, dl2) in zip(rows1, rows2)
    ]
    return (ff1 + t1 * fl1 * ff2, t1 * fl2, ll2 + t2 * fl2 * ll1), rows


def solve_z(r, w):
    n = r.shape[1]
    lane = lanes(r)
    e = jnp.where(lane == n - 1, 0.0, 1.0)
    l = jnp.where(lane == 0, 0.0, 1.0)
    s = w + jnp.where(lane == n - 1, 1.0, 0.0)
    step = 1
    while step < n:
        inv = 1.0 / (s + (l + e))
        a, b = e * inv, l * inv
        r = r + (pltpu.roll(a * r, step, 1) + pltpu.roll(b * r, n - step, 1))
        s = s + (pltpu.roll(a * s, step, 1) + pltpu.roll(b * s, n - step, 1))
        g = a * l
        if 2 * step < n:
            e, l = pltpu.roll(g, n - step, 1), pltpu.roll(g, step, 1)
        step *= 2
    return r / s


def collect(r, order, own, others, got):
    refs = [own] + [others[order.index(s)] for s in range(1, len(order) + 1)]
    count = len(refs)
    blocks = [[] for _ in refs]
    for k in range(own.shape[0] // B):
        values = [ref[plane(k)] for ref in refs]
        bit = 1
        while bit < count:
            swap = lax.bitwise_and(r, bit) != 0
            values = [jnp.where(swap, values[m ^ bit], values[m]) for m in range(count)]
            bit *= 2
        for m, value in enumerate(values):
            got[m, plane(k)] = value
            blocks[m].append(value)
    return blocks


def rows_of(block, sources):
    return [(block[2 * k], block[2 * k + 1]) for k in range(sources)]


def stored(got, m, planes):
    return [got[plane(k)] if m is None else got[m, plane(k)] for k in planes]


def tables_kernel(
    me, eps_in, sig_in, material, elec_in, magn_in, w, c, p, u, v, flux, part, elec, magn, ez_first, ids, eps, sig, sems
):
    loads = [(eps_in, eps), (sig_in, sig), (material, ids)]
    for field, to, k in ((elec_in, elec, 0), (magn_in, magn, 1), (elec_in, elec, 2), (magn_in, magn, 0)):
        loads.append((field.at[k], to.at[k]))
    loads += [(elec_in.at[1], elec.at[1]), (magn_in.at[2], magn.at[2])]
    loads = [pltpu.make_async_copy(a, b, sems.at[k]) for k, (a, b) in enumerate(loads)]
    for load in loads:
        load.start()
    for load in loads[:3]:
        load.wait()
    ws = [eps[m] * (1.0 / (h * h)) + sig[m] * (0.5 / h) for m in range(eps.shape[0])]
    cs = [eps[m] * (1.0 / (h * h)) - sig[m] * (0.5 / h) for m in range(eps.shape[0])]
    for i in range(B):
        cell = ids[plane(i)]
        wi = jnp.full(cell.shape, ws[0], F32)
        ci = jnp.full(cell.shape, cs[0], F32)
        for m in range(1, len(ws)):
            wi = jnp.where(cell == m, ws[m], wi)
            ci = jnp.where(cell == m, cs[m], ci)
        w[plane(i)] = wi
        c[plane(i)] = ci
    factor(lambda i: w[plane(i)], me[0] == 0, p, u, v)
    for load in loads[3:7]:
        load.wait()
    row = lax.broadcasted_iota(jnp.int32, (B, w.shape[1]), 0)
    for i in range(B):
        q = magn[1, plane(i)] * (1.0 / h) - ahead_z(elec[0, plane(i)])
        flux[plane(i)] = q
        if i > 0:
            q = q - flux[plane(i - 1)]
        here = magn[0, plane(i)]
        before = jnp.where(row == 0, 0.0, pltpu.roll(here, 1, 0))
        part[plane(i)] = c[plane(i)] * elec[2, plane(i)] + (q - (here - before) * (1.0 / h))
    for k in range(ez_first.shape[0] // B):
        ez_first[plane(k)] = elec.at[2][strided(0)]
    for load in loads[7:]:
        load.wait()


def first_x_kernel(me, part, hx_prev, flux, p, u, v, elec, magn, g, msg):
    row = lax.broadcasted_iota(jnp.int32, hx_prev.shape, 0)
    scale = jnp.where(me[1] == 0, 0.0, jnp.where(row == 0, 1.0 / h, 0.0))

    def source(i):
        return part[plane(i)] + hx_prev[pl.ds(i, 1)] * scale

    first, last = eliminate(source, p, g)
    msg[plane(0)] = first
    msg[plane(1)] = last - flux[plane(B - 1)]
    msg[plane(2)] = u[plane(0)]
    msg[plane(3)] = v[plane(0)]
    msg[plane(4)] = v[plane(B - 1)]
    msg[plane(5)] = elec[1, plane(0)]
    msg[plane(6)] = magn[2, plane(B - 1)]


def merged(blocks):
    while len(blocks) > 1:
        blocks = [merge(a, b) for a, b in zip(blocks[::2], blocks[1::2])]
    return blocks[0]


def merge_kernel(axis, near, order, sources, halos, me, *refs):
    got, msg = refs[-2:]
    blocks = collect(lax.rem(me[axis], near), order, refs[0], refs[1:near], got)
    at = 2 * sources
    coefs, rows = merged([(b[at : at + 3], rows_of(b, sources)) for b in blocks])
    for k, value in enumerate([v for pair in rows for v in pair] + list(coefs)):
        msg[plane(k)] = value
    if halos:
        msg[plane(5)] = blocks[0][5]
        msg[plane(6)] = blocks[-1][6]


def merge_rows_kernel(axis, near, order, me, coefs, *refs):
    got, msg = refs[-2:]
    blocks = collect(lax.rem(me[axis], near), order, refs[0], refs[1:near], got)
    _, rows = merged([(stored(coefs, m, (2, 3, 4)), rows_of(b, 1)) for m, b in enumerate(blocks)])
    msg[plane(0)], msg[plane(1)] = rows[0]


def solved_ends(here, near, sources, near_rows, near_coefs, far_rows, far_coefs, own_near, own_far):
    zero = jnp.zeros_like(far_coefs[0][0])
    outer = boundary(lax.div(here, near), far_rows, far_coefs, *own_far, [(zero, zero)] * sources)
    return boundary(lax.rem(here, near), near_rows, near_coefs, *own_near, outer)


def first_z_kernel(n, me, ef, mf, ez_next, w, c, p, u, v, r_top, src_top, curl, flux_y, flux_a, part_a, src, r):
    factor(lambda j: w[strided(j)], me[1] == 0, p, u, v)
    inside = jnp.where(me[1] == n - 1, 0.0, 1.0)
    row = lax.broadcasted_iota(jnp.int32, (B, w.shape[1]), 0)
    for i in range(B):
        ez = ef[2, plane(i)]
        after = jnp.where(row == B - 1, ez_next[pl.ds(i, 1)] * inside, pltpu.roll(ez, B - 1, 0))
        ri = mf[0, plane(i)] * (1.0 / h) - (after - ez)
        r[plane(i)] = ri
        gain = mf[2, plane(i)]
        if i > 0:
            gain = gain - mf[2, plane(i - 1)]
        src[plane(i)] = c[plane(i)] * ef[1, plane(i)] + (behind_z(ri) - gain * (1.0 / h))
        part_a[plane(i)] = c[plane(i)] * ef[0, plane(i)] - behind_z(mf[1, plane(i)]) * (1.0 / h)
        if i < B - 1:
            rise = ef[1, plane(i + 1)] - ef[1, plane(i)]
            flux_a[plane(i)] = mf[2, plane(i)] * (1.0 / h) - rise
    flux_a[plane(B - 1)] = mf[2, plane(B - 1)] * (1.0 / h) + ef[1, plane(B - 1)]
    r_top[...] = r[plane(0)]
    src_top[...] = src[plane(0)]
    x = solve_z(src[...], w[...])
    rise = ahead_z(x)
    mx = r[...] + rise
    curl[...] = c[...] * x + behind_z(mx)
    flux_y[...] = -(mx + rise)


def both_y_kernel(near, far, order, me, got_near, *refs):
    others, refs = refs[:far], refs[far:]
    (g_b, u_x, v_x, flux_b, w, c, r_top, src_top, curl_in, flux_y_in, flux_a_in, part_a, p_y, u_y, v_y) = refs[:15]
    got_far, rise_y, curl, flux_y, flux_a, g_a, g_c, msg, part, fz = refs[15:]
    me_x = me[0]
    top = plane(0)
    q, r = lax.div(me_x, near), lax.rem(me_x, near)
    far_blocks = collect(q, order, others[0], others[1:], got_far)
    near_blocks = [stored(got_near, m, range(5)) for m in range(near)]
    ey_next = jnp.where(
        r < near - 1,
        got_near[jnp.minimum(r + 1, near - 1), plane(5)],
        jnp.where(q < far - 1, got_far[jnp.minimum(q + 1, far - 1), plane(5)], 0.0),
    )
    hz_prev = jnp.where(
        r > 0,
        got_near[jnp.maximum(r - 1, 0), plane(6)],
        jnp.where(q > 0, got_far[jnp.maximum(q - 1, 0), plane(6)], 0.0),
    )
    curl[...] = curl_in[...]
    flux_y[...] = flux_y_in[...]
    flux_a[...] = flux_a_in[...]

    x = solve_z(src_top[...] + hz_prev * (1.0 / h), w[top])
    rise = ahead_z(x)
    mx = r_top[...] + rise
    curl[top] = c[top] * x + behind_z(mx)
    flux_y[top] = -(mx + rise)

    flux_a[plane(B - 1)] = flux_a[plane(B - 1)] - ey_next

    def source_a(j):
        f = flux_a[strided(j)]
        if j > 0:
            f = f - flux_a[strided(j - 1)]
        return part_a[strided(j)] + f

    first_a, last_a = eliminate(source_a, p_y, g_a)
    last_a = last_a - flux_a[strided(B - 1)]

    own_near, own_far = stored(got_near, r, range(5)), stored(others[0], None, range(5))
    ((before, after),) = solved_ends(
        me_x,
        near,
        1,
        [rows_of(b, 1) for b in near_blocks],
        [b[2:5] for b in near_blocks],
        [rows_of(b, 1) for b in far_blocks],
        [b[2:5] for b in far_blocks],
        (rows_of(own_near, 1), own_near[2:5]),
        (rows_of(own_far, 1), own_far[2:5]),
    )
    for i in range(B):
        fz[plane(i)] = g_b[plane(i)] + (u_x[plane(i)] * before + v_x[plane(i)] * after)
    my_before = jnp.where(me_x == 0, 0.0, fz[top] - before)
    for i in range(B):
        here = fz[plane(i)]
        rise = (fz[plane(i + 1)] if i < B - 1 else after) - here
        my = flux_b[plane(i)] + rise
        rise_y[plane(i)] = my + rise
        part[plane(i)] = c[plane(i)] * here + (my - my_before)
        my_before = my

    def source_c(j):
        f = flux_y[strided(j)]
        if j > 0:
            f = f - flux_y[strided(j - 1)]
        return part[strided(j)] + f

    first_c, last_c = eliminate(source_c, p_y, g_c)
    last_c = last_c - flux_y[strided(B - 1)]
    sent = [first_a, last_a, first_c, last_c, u_y[plane(0)], v_y[plane(0)], v_y[plane(B - 1)]]
    for k, value in enumerate(sent):
        msg[plane(k)] = value


def second_x_kernel(near, far, order, me, got_near, *refs):
    others, refs = refs[:far], refs[far:]
    g_a, u, v, flux_a, c, curl, p_x, part, flux2, g2, ends_c, msg, got_far, fx = refs
    my = me[1]
    far_blocks = collect(lax.div(my, near), order, others[0], others[1:], got_far)
    near_blocks = [stored(got_near, m, range(7)) for m in range(near)]
    own_near, own_far = stored(got_near, lax.rem(my, near), range(7)), stored(others[0], None, range(7))
    (before, after), (before_c, after_c) = solved_ends(
        my,
        near,
        2,
        [rows_of(b, 2) for b in near_blocks],
        [b[4:7] for b in near_blocks],
        [rows_of(b, 2) for b in far_blocks],
        [b[4:7] for b in far_blocks],
        (rows_of(own_near, 2), own_near[4:7]),
        (rows_of(own_far, 2), own_far[4:7]),
    )
    ends_c[plane(0)] = before_c
    ends_c[plane(1)] = after_c
    for j in range(B):
        fx[plane(j)] = g_a[plane(j)] + (u[plane(j)] * before + v[plane(j)] * after)
    mz_before = jnp.where(my == 0, 0.0, fx[plane(0)] - before)
    for j in range(B):
        here = fx[plane(j)]
        rise = (fx[plane(j + 1)] if j < B - 1 else after) - here
        mz = flux_a[strided(j)] + rise
        part[strided(j)] = c[strided(j)] * here + (mz - mz_before)
        flux2[strided(j)] = -(mz + rise)
        mz_before = mz

    def source(i):
        f = flux2[plane(i)]
        if i > 0:
            f = f - flux2[plane(i - 1)]
        return curl[plane(i)] + f

    first, last = eliminate(source, p_x, g2)
    msg[plane(0)] = first
    msg[plane(1)] = last - flux2[plane(B - 1)]


def second_y_kernel(ends_c, g_c, u, v, flux_y, elec, magn, full_z, new_x, sems):
    stores = [(full_z, elec.at[2]), (new_x, magn.at[0])]
    stores = [pltpu.make_async_copy(a, b, sems.at[k]) for k, (a, b) in enumerate(stores)]
    before, after = ends_c[plane(0)], ends_c[plane(1)]
    here = None
    for j in range(B):
        ahead = g_c[plane(j)] + (u[plane(j)] * before + v[plane(j)] * after)
        full_z[strided(j)] = ahead
        if j > 0:
            new_x[strided(j - 1)] = -h * (flux_y[strided(j - 1)] + (ahead - here))
        here = ahead
    new_x[strided(B - 1)] = -h * (flux_y[strided(B - 1)] + (after - here))
    for store in stores:
        store.start()
    for store in stores:
        store.wait()


def second_z_kernel(part, rise_y, w, _, __, elec, magn, full_x, new_y, sems):
    stores = [(full_x, elec.at[0]), (new_y, magn.at[1])]
    stores = [pltpu.make_async_copy(a, b, sems.at[k]) for k, (a, b) in enumerate(stores)]
    a = rise_y[...]
    x = solve_z(part[...] - behind_z(a), w[...])
    full_x[...] = x
    stores[0].start()
    new_y[...] = h * (a - ahead_z(x))
    stores[1].start()
    for store in stores:
        store.wait()


def last_kernel(near, far, order, me, coefs_near, coefs_far, got_near, *refs):
    others, refs = refs[:far], refs[far:]
    g, u, v, flux2, _, _, elec, magn, got_far, full_y, new_z, sems = refs
    q, r = lax.div(me[0], near), lax.rem(me[0], near)
    far_blocks = collect(q, order, others[0], others[1:], got_far)
    ((before, after),) = solved_ends(
        me[0],
        near,
        1,
        [rows_of(stored(got_near, m, range(2)), 1) for m in range(near)],
        [stored(coefs_near, m, (2, 3, 4)) for m in range(near)],
        [rows_of(b, 1) for b in far_blocks],
        [stored(coefs_far, m, (2, 3, 4)) for m in range(far)],
        (rows_of(stored(got_near, r, range(2)), 1), stored(coefs_near, r, (2, 3, 4))),
        (rows_of(stored(others[0], None, range(2)), 1), stored(coefs_far, q, (2, 3, 4))),
    )
    stores = [(full_y, elec.at[1]), (new_z, magn.at[2])]
    stores = [pltpu.make_async_copy(a, b, sems.at[k]) for k, (a, b) in enumerate(stores)]
    for i in range(B):
        full_y[plane(i)] = g[plane(i)] + (u[plane(i)] * before + v[plane(i)] * after)
    stores[0].start()
    for i in range(B):
        rise = (full_y[plane(i + 1)] if i < B - 1 else after) - full_y[plane(i)]
        new_z[plane(i)] = -h * (flux2[plane(i)] + rise)
    stores[1].start()
    for store in stores:
        store.wait()


VMEM = pl.BlockSpec(memory_space=pltpu.VMEM)
SMEM = pl.BlockSpec(memory_space=pltpu.SMEM)
HBM = pl.BlockSpec(memory_space=pltpu.HBM)


def call(kernel, ins, outs, specs=None, out_specs=None, scratch=(), aliases=None, flops=1_000_000):
    shapes = [pltpu.HBM(s, F32) if out_specs else jax.ShapeDtypeStruct(s, F32) for s in outs]
    return pl.pallas_call(
        kernel,
        out_shape=shapes,
        in_specs=specs or [SMEM] + [VMEM] * (len(ins) - 1),
        out_specs=out_specs or [VMEM] * len(outs),
        scratch_shapes=[pltpu.VMEM(s, F32) if isinstance(s, tuple) else s for s in scratch],
        input_output_aliases=aliases or {},
        compiler_params=pltpu.CompilerParams(vmem_limit_bytes=24 * 1024 * 1024),
        cost_estimate=pl.CostEstimate(flops=flops, bytes_accessed=1_000_000, transcendentals=0),
    )(*ins)


def shared(value, axis, n, step, order):
    return [value] + [lax.ppermute(value, axis, [(i, i ^ (step * s)) for i in range(n)]) for s in order]


def split(n):
    near = 1 << (n.bit_length() // 2)
    return near, n // near


def local(electric, magnetic, material, permittivity, conductivity):
    nx, ny = lax.axis_size("px"), lax.axis_size("py")
    near_x, far_x = split(nx)
    near_y, far_y = split(ny)
    nz = material.shape[2]
    cells = (B * B, nz)
    me = jnp.stack([lax.axis_index("px"), lax.axis_index("py")]).astype(jnp.int32)
    in_hbm = lambda a: pltpu.with_memory_space_constraint(a, pltpu.HBM)
    elec = in_hbm(electric.reshape(3, *cells))
    magn = in_hbm(magnetic.reshape(3, *cells))
    ids = in_hbm(material.reshape(cells))
    dma = pltpu.SemaphoreType.DMA
    orders = [(1, 2, 3), (2, 1, 3), (2, 3, 1), (1, 3, 2)]
    counts = (near_x, far_x, near_y, far_y)
    px_near, px_far, py_near, py_far = [
        tuple(s for s in order if s < count) for order, count in zip(orders, counts)
    ]

    hx_prev = lax.ppermute(magnetic[0, :, B - 1], "py", [(i, (i + 1) % ny) for i in range(ny)])
    w, c, p_x, u_x, v_x, flux_b, part_b, ef, mf, ez_first = call(
        tables_kernel,
        [me, in_hbm(permittivity), in_hbm(conductivity), ids, elec, magn],
        [cells] * 7 + [(3, *cells)] * 2 + [(8 * B, nz)],
        specs=[SMEM] + [HBM] * 5,
        scratch=[pltpu.VMEM(cells, jnp.int32)] + [pltpu.SMEM(permittivity.shape, F32)] * 2 + [dma((9,))],
    )
    g_b, msg = call(
        first_x_kernel,
        [me, part_b, hx_prev, flux_b, p_x, u_x, v_x, ef, mf],
        [cells, (7 * B, nz)],
    )
    ins = shared(msg, "px", nx, 1, px_near)
    ez_next = lax.ppermute(ez_first, "py", [((i + 1) % ny, i) for i in range(ny)])
    near_b, msg = call(
        functools.partial(merge_kernel, 0, near_x, px_near, 1, True),
        [me] + ins,
        [(near_x, 7 * B, nz), (7 * B, nz)],
    )
    ins = shared(msg, "px", nx, near_x, px_far)
    p_y, u_y, v_y, r_top, src_top, curl, flux_y, flux_a, part_a = call(
        functools.partial(first_z_kernel, ny),
        [me, ef, mf, ez_next, w, c],
        [cells] * 3 + [(B, nz)] * 2 + [cells] * 4,
        scratch=[cells] * 2,
        flops=8_000_000,
    )
    ins = [me, near_b] + ins + [g_b, u_x, v_x, flux_b, w, c, r_top, src_top]
    far_b, rise_y, curl, flux_y, flux_a, g_a, g_c, msg = call(
        functools.partial(both_y_kernel, near_x, far_x, px_far),
        ins + [curl, flux_y, flux_a, part_a, p_y, u_y, v_y],
        [(far_x, 7 * B, nz)] + [cells] * 6 + [(7 * B, nz)],
        scratch=[cells] * 2,
    )
    ins = shared(msg, "py", ny, 1, py_near)
    near_ac, msg = call(
        functools.partial(merge_kernel, 1, near_y, py_near, 2, False), [me] + ins, [(near_y, 7 * B, nz), (7 * B, nz)]
    )
    ins = shared(msg, "py", ny, near_y, py_far)
    part_x, flux2, g2, ends_c, msg = call(
        functools.partial(second_x_kernel, near_y, far_y, py_far),
        [me, near_ac] + ins + [g_a, u_y, v_y, flux_a, c, curl, p_x],
        [cells] * 3 + [(2 * B, nz)] * 2,
        scratch=[(far_y, 7 * B, nz), cells],
    )
    ins = shared(msg, "px", nx, 1, px_near)
    elec, magn = call(
        second_y_kernel,
        [ends_c, g_c, u_y, v_y, flux_y],
        [(3, *cells)] * 2,
        specs=[VMEM] * 5,
        out_specs=[HBM] * 2,
        scratch=[cells] * 2 + [dma((2,))],
    )
    near_a, msg = call(
        functools.partial(merge_rows_kernel, 0, near_x, px_near),
        [me, near_b] + ins,
        [(near_x, 2 * B, nz), (2 * B, nz)],
    )
    msg, elec = lax.optimization_barrier((msg, elec))
    ins = shared(msg, "px", nx, near_x, px_far)
    elec, magn = call(
        second_z_kernel,
        [part_x, rise_y, w, elec, magn],
        [(3, *cells)] * 2,
        specs=[VMEM] * 3 + [HBM] * 2,
        out_specs=[HBM] * 2,
        scratch=[cells] * 2 + [dma((2,))],
        aliases={3: 0, 4: 1},
        flops=8_000_000,
    )
    ins = [me, near_b, far_b, near_a] + ins + [g2, u_x, v_x, flux2]
    at = len(ins)
    out = call(
        functools.partial(last_kernel, near_x, far_x, px_far),
        ins + [elec, magn],
        [(3, *cells)] * 2,
        specs=[SMEM] + [VMEM] * (at - 1) + [HBM] * 2,
        out_specs=[HBM] * 2,
        scratch=[(far_x, 2 * B, nz), cells, cells, dma((2,))],
        aliases={at: 0, at + 1: 1},
    )
    return tuple(a.reshape(3, B, B, nz) for a in out)


def solution(mesh):
    placed = (P(None, "px", "py", None), P(None, "px", "py", None), P("px", "py", None), P(), P())
    return jax.shard_map(
        local,
        mesh=mesh,
        in_specs=placed,
        out_specs=(P(None, "px", "py", None), P(None, "px", "py", None)),
        check_vma=False,
    )
```

```python
import functools

import jax
import jax.numpy as jnp
from jax import lax
from jax.experimental import pallas as pl
from jax.experimental.pallas import tpu as pltpu
from jax.sharding import PartitionSpec as P

h = 32.0
B = 16
F32 = jnp.float32


def plane(i):
    return pl.ds(i * B, B)


def strided(j):
    return pl.ds(j, B, stride=B)


def lanes(v):
    return lax.broadcasted_iota(jnp.int32, v.shape, 1)


def behind_z(v):
    return v - jnp.where(lanes(v) == 0, 0.0, pltpu.roll(v, 1, 1))


def ahead_z(v):
    n = v.shape[1]
    return jnp.where(lanes(v) == n - 1, 0.0, pltpu.roll(v, n - 1, 1)) - v


def factor(w_of, first_block, p, u, v):
    d = None
    y = []
    for j in range(B):
        w = w_of(j)
        e = w + (jnp.where(first_block, 0.0, 1.0) if j == 0 else d)
        inv = 1.0 / (1.0 + e)
        d = e * inv
        p[plane(j)] = inv
        y.append(jnp.ones_like(inv) if j == 0 else y[-1] * last)
        last = inv
    uj = y[B - 1] * last
    vj = last
    u[plane(B - 1)] = uj
    v[plane(B - 1)] = vj
    for j in range(B - 2, -1, -1):
        inv = p[plane(j)]
        uj = inv * (y[j] + uj)
        vj = inv * vj
        u[plane(j)] = uj
        v[plane(j)] = vj


def eliminate(source_of, p, g):
    y = source_of(0)
    ys = [y]
    for j in range(1, B):
        y = source_of(j) + p[plane(j - 1)] * y
        ys.append(y)
    x = y * p[plane(B - 1)]
    end = x
    g[plane(B - 1)] = x
    for j in range(B - 2, -1, -1):
        x = p[plane(j)] * (ys[j] + x)
        g[plane(j)] = x
    return x, end


def boundary(me, rows, coefs, here, coef_here, outer):
    n = len(rows)
    left = [a for a, _ in outer]
    right = [b for _, b in outer]
    beta = delta = jnp.zeros_like(left[0])
    for s in range(n - 1):
        ff, fl, ll = coefs[s]
        t = fl / (1.0 - ff * beta)
        on = s < me
        left = [jnp.where(on, dl + t * (a + beta * gf), a) for a, (gf, dl) in zip(left, rows[s])]
        beta = jnp.where(on, ll + t * beta * fl, beta)
        m = n - 1 - s
        ff, fl, ll = coefs[m]
        t = fl / (1.0 - ll * delta)
        on = m > me
        right = [jnp.where(on, gf + t * (b + delta * dl), b) for b, (gf, dl) in zip(right, rows[m])]
        delta = jnp.where(on, ff + t * delta * fl, delta)
    ff, fl, ll = coef_here
    after_scale = 1.0 / (1.0 - delta * ll)
    t = fl * after_scale
    before_scale = 1.0 / (1.0 - beta * (ff + t * delta * fl))
    ends = []
    for a, b, (gf, dl) in zip(left, right, here):
        before = (a + beta * (gf + t * (b + delta * dl))) * before_scale
        ends.append((before, (b + delta * (dl + fl * before)) * after_scale))
    return ends


def merge(one, two):
    (ff1, fl1, ll1), rows1 = one
    (ff2, fl2, ll2), rows2 = two
    d = 1.0 / (1.0 - ll1 * ff2)
    t1, t2 = fl1 * d, fl2 * d
    rows = [
        (gf1 + t1 * (gf2 + ff2 * dl1), dl2 + t2 * (dl1 + ll1 * gf2))
        for (gf1, dl1), (gf2, dl2) in zip(rows1, rows2)
    ]
    return (ff1 + t1 * fl1 * ff2, t1 * fl2, ll2 + t2 * fl2 * ll1), rows


def solve_z(r, w):
    n = r.shape[1]
    lane = lanes(r)
    e = jnp.where(lane == n - 1, 0.0, 1.0)
    l = jnp.where(lane == 0, 0.0, 1.0)
    s = w + jnp.where(lane == n - 1, 1.0, 0.0)
    step = 1
    while step < n:
        inv = 1.0 / (s + (l + e))
        a, b = e * inv, l * inv
        r = r + (pltpu.roll(a * r, step, 1) + pltpu.roll(b * r, n - step, 1))
        s = s + (pltpu.roll(a * s, step, 1) + pltpu.roll(b * s, n - step, 1))
        g = a * l
        if 2 * step < n:
            e, l = pltpu.roll(g, n - step, 1), pltpu.roll(g, step, 1)
        step *= 2
    return r / s


def collect(r, order, own, others, got):
    refs = [own] + [others[order.index(s)] for s in range(1, len(order) + 1)]
    count = len(refs)
    blocks = [[] for _ in refs]
    for k in range(own.shape[0] // B):
        values = [ref[plane(k)] for ref in refs]
        bit = 1
        while bit < count:
            swap = lax.bitwise_and(r, bit) != 0
            values = [jnp.where(swap, values[m ^ bit], values[m]) for m in range(count)]
            bit *= 2
        for m, value in enumerate(values):
            got[m, plane(k)] = value
            blocks[m].append(value)
    return blocks


def rows_of(block, sources):
    return [(block[2 * k], block[2 * k + 1]) for k in range(sources)]


def stored(got, m, planes):
    return [got[m, plane(k)] for k in planes]


def loaded(msg, planes):
    return [msg[plane(k)] for k in planes]


def pick(values, index):
    out = values[0]
    for k in range(1, len(values)):
        out = jnp.where(index == k, values[k], out)
    return out


def place(pos, axis, near):
    here = pos[plane(axis)]
    return lax.shift_right_logical(here, near.bit_length() - 1), lax.bitwise_and(here, near - 1)


def tables_kernel(
    me, eps_in, sig_in, material, elec_in, magn_in, w, c, p, u, v, flux, part, elec, magn, ez_first, pos, ids, eps, sig, sems
):
    loads = [(eps_in, eps), (sig_in, sig), (material, ids)]
    for field, to, k in ((elec_in, elec, 0), (magn_in, magn, 1), (elec_in, elec, 2), (magn_in, magn, 0)):
        loads.append((field.at[k], to.at[k]))
    loads += [(elec_in.at[1], elec.at[1]), (magn_in.at[2], magn.at[2])]
    loads = [pltpu.make_async_copy(a, b, sems.at[k]) for k, (a, b) in enumerate(loads)]
    for load in loads:
        load.start()
    for axis in range(2):
        pos[plane(axis)] = jnp.full((B, w.shape[1]), me[axis], jnp.int32)
    for load in loads[:3]:
        load.wait()
    ws = [eps[m] * (1.0 / (h * h)) + sig[m] * (0.5 / h) for m in range(eps.shape[0])]
    cs = [eps[m] * (1.0 / (h * h)) - sig[m] * (0.5 / h) for m in range(eps.shape[0])]
    for i in range(B):
        cell = ids[plane(i)]
        wi = jnp.full(cell.shape, ws[0], F32)
        ci = jnp.full(cell.shape, cs[0], F32)
        for m in range(1, len(ws)):
            wi = jnp.where(cell == m, ws[m], wi)
            ci = jnp.where(cell == m, cs[m], ci)
        w[plane(i)] = wi
        c[plane(i)] = ci
    factor(lambda i: w[plane(i)], me[0] == 0, p, u, v)
    for load in loads[3:7]:
        load.wait()
    row = lax.broadcasted_iota(jnp.int32, (B, w.shape[1]), 0)
    for i in range(B):
        q = magn[1, plane(i)] * (1.0 / h) - ahead_z(elec[0, plane(i)])
        flux[plane(i)] = q
        if i > 0:
            q = q - flux[plane(i - 1)]
        here = magn[0, plane(i)]
        before = jnp.where(row == 0, 0.0, pltpu.roll(here, 1, 0))
        part[plane(i)] = c[plane(i)] * elec[2, plane(i)] + (q - (here - before) * (1.0 / h))
    for k in range(ez_first.shape[0] // B):
        ez_first[plane(k)] = elec.at[2][strided(0)]
    for load in loads[7:]:
        load.wait()


def first_x_kernel(pos, part, hx_prev, flux, p, u, v, elec, magn, g, msg):
    row = lax.broadcasted_iota(jnp.int32, hx_prev.shape, 0)
    scale = jnp.where(pos[plane(1)] == 0, 0.0, jnp.where(row == 0, 1.0 / h, 0.0))

    def source(i):
        return part[plane(i)] + hx_prev[pl.ds(i, 1)] * scale

    first, last = eliminate(source, p, g)
    msg[plane(0)] = first
    msg[plane(1)] = last - flux[plane(B - 1)]
    msg[plane(2)] = u[plane(0)]
    msg[plane(3)] = v[plane(0)]
    msg[plane(4)] = v[plane(B - 1)]
    msg[plane(5)] = elec[1, plane(0)]
    msg[plane(6)] = magn[2, plane(B - 1)]


def merged(blocks):
    while len(blocks) > 1:
        blocks = [merge(a, b) for a, b in zip(blocks[::2], blocks[1::2])]
    return blocks[0]


def merge_kernel(axis, near, order, sources, halos, pos, *refs):
    got, msg = refs[-2:]
    blocks = collect(place(pos, axis, near)[1], order, refs[0], refs[1:near], got)
    at = 2 * sources
    coefs, rows = merged([(b[at : at + 3], rows_of(b, sources)) for b in blocks])
    for k, value in enumerate([v for pair in rows for v in pair] + list(coefs)):
        msg[plane(k)] = value
    if halos:
        msg[plane(5)] = blocks[0][5]
        msg[plane(6)] = blocks[-1][6]


def merge_rows_kernel(axis, near, order, pos, coefs, *refs):
    got, msg = refs[-2:]
    blocks = collect(place(pos, axis, near)[1], order, refs[0], refs[1:near], got)
    _, rows = merged([(stored(coefs, m, (2, 3, 4)), rows_of(b, 1)) for m, b in enumerate(blocks)])
    msg[plane(0)], msg[plane(1)] = rows[0]


def solved_ends(q, r, sources, near_rows, near_coefs, far_rows, far_coefs, own_near, own_far):
    zero = jnp.zeros_like(far_coefs[0][0])
    outer = boundary(q, far_rows, far_coefs, *own_far, [(zero, zero)] * sources)
    return boundary(r, near_rows, near_coefs, *own_near, outer)


def first_z_kernel(n, pos, ef, mf, ez_next, w, c, p, u, v, r_top, src_top, curl, flux_y, flux_a, part_a, src, r):
    factor(lambda j: w[strided(j)], pos[plane(1)] == 0, p, u, v)
    inside = jnp.where(pos[pl.ds(B, 1)] == n - 1, 0.0, 1.0)
    row = lax.broadcasted_iota(jnp.int32, (B, w.shape[1]), 0)
    for i in range(B):
        ez = ef[2, plane(i)]
        after = jnp.where(row == B - 1, ez_next[pl.ds(i, 1)] * inside, pltpu.roll(ez, B - 1, 0))
        ri = mf[0, plane(i)] * (1.0 / h) - (after - ez)
        r[plane(i)] = ri
        gain = mf[2, plane(i)]
        if i > 0:
            gain = gain - mf[2, plane(i - 1)]
        src[plane(i)] = c[plane(i)] * ef[1, plane(i)] + (behind_z(ri) - gain * (1.0 / h))
        part_a[plane(i)] = c[plane(i)] * ef[0, plane(i)] - behind_z(mf[1, plane(i)]) * (1.0 / h)
        if i < B - 1:
            rise = ef[1, plane(i + 1)] - ef[1, plane(i)]
            flux_a[plane(i)] = mf[2, plane(i)] * (1.0 / h) - rise
    flux_a[plane(B - 1)] = mf[2, plane(B - 1)] * (1.0 / h) + ef[1, plane(B - 1)]
    r_top[...] = r[plane(0)]
    src_top[...] = src[plane(0)]
    x = solve_z(src[...], w[...])
    rise = ahead_z(x)
    mx = r[...] + rise
    curl[...] = c[...] * x + behind_z(mx)
    flux_y[...] = -(mx + rise)


def both_y_kernel(near, far, order, pos, got_near, own_near, *refs):
    others, refs = refs[:far], refs[far:]
    (g_b, u_x, v_x, flux_b, w, c, r_top, src_top, curl_in, flux_y_in, flux_a_in, part_a, p_y, u_y, v_y) = refs[:15]
    got_far, rise_y, curl, flux_y, flux_a, g_a, g_c, msg, part, fz = refs[15:]
    top = plane(0)
    q, r = place(pos, 0, near)
    far_blocks = collect(q, order, others[0], others[1:], got_far)
    near_blocks = [stored(got_near, m, range(7)) for m in range(near)]
    after_group = jnp.where(q < far - 1, pick([b[5] for b in far_blocks], q + 1), 0.0)
    ey_next = jnp.where(r < near - 1, pick([b[5] for b in near_blocks], r + 1), after_group)
    before_group = jnp.where(q > 0, pick([b[6] for b in far_blocks], q - 1), 0.0)
    hz_prev = jnp.where(r > 0, pick([b[6] for b in near_blocks], r - 1), before_group)
    curl[...] = curl_in[...]
    flux_y[...] = flux_y_in[...]
    flux_a[...] = flux_a_in[...]

    x = solve_z(src_top[...] + hz_prev * (1.0 / h), w[top])
    rise = ahead_z(x)
    mx = r_top[...] + rise
    curl[top] = c[top] * x + behind_z(mx)
    flux_y[top] = -(mx + rise)

    flux_a[plane(B - 1)] = flux_a[plane(B - 1)] - ey_next

    def source_a(j):
        f = flux_a[strided(j)]
        if j > 0:
            f = f - flux_a[strided(j - 1)]
        return part_a[strided(j)] + f

    first_a, last_a = eliminate(source_a, p_y, g_a)
    last_a = last_a - flux_a[strided(B - 1)]

    own, own_group = loaded(own_near, range(5)), loaded(others[0], range(5))
    ((before, after),) = solved_ends(
        q,
        r,
        1,
        [rows_of(b, 1) for b in near_blocks],
        [b[2:5] for b in near_blocks],
        [rows_of(b, 1) for b in far_blocks],
        [b[2:5] for b in far_blocks],
        (rows_of(own, 1), own[2:5]),
        (rows_of(own_group, 1), own_group[2:5]),
    )
    for i in range(B):
        fz[plane(i)] = g_b[plane(i)] + (u_x[plane(i)] * before + v_x[plane(i)] * after)
    my_before = jnp.where(pos[plane(0)] == 0, 0.0, fz[top] - before)
    for i in range(B):
        here = fz[plane(i)]
        rise = (fz[plane(i + 1)] if i < B - 1 else after) - here
        my = flux_b[plane(i)] + rise
        rise_y[plane(i)] = my + rise
        part[plane(i)] = c[plane(i)] * here + (my - my_before)
        my_before = my

    def source_c(j):
        f = flux_y[strided(j)]
        if j > 0:
            f = f - flux_y[strided(j - 1)]
        return part[strided(j)] + f

    first_c, last_c = eliminate(source_c, p_y, g_c)
    last_c = last_c - flux_y[strided(B - 1)]
    sent = [first_a, last_a, first_c, last_c, u_y[plane(0)], v_y[plane(0)], v_y[plane(B - 1)]]
    for k, value in enumerate(sent):
        msg[plane(k)] = value


def second_x_kernel(near, far, order, pos, got_near, own_near, *refs):
    others, refs = refs[:far], refs[far:]
    g_a, u, v, flux_a, c, curl, p_x, part, flux2, g2, ends_c, msg, got_far, fx = refs
    q, r = place(pos, 1, near)
    far_blocks = collect(q, order, others[0], others[1:], got_far)
    near_blocks = [stored(got_near, m, range(7)) for m in range(near)]
    own, own_group = loaded(own_near, range(7)), loaded(others[0], range(7))
    (before, after), (before_c, after_c) = solved_ends(
        q,
        r,
        2,
        [rows_of(b, 2) for b in near_blocks],
        [b[4:7] for b in near_blocks],
        [rows_of(b, 2) for b in far_blocks],
        [b[4:7] for b in far_blocks],
        (rows_of(own, 2), own[4:7]),
        (rows_of(own_group, 2), own_group[4:7]),
    )
    ends_c[plane(0)] = before_c
    ends_c[plane(1)] = after_c
    for j in range(B):
        fx[plane(j)] = g_a[plane(j)] + (u[plane(j)] * before + v[plane(j)] * after)
    mz_before = jnp.where(pos[plane(1)] == 0, 0.0, fx[plane(0)] - before)
    for j in range(B):
        here = fx[plane(j)]
        rise = (fx[plane(j + 1)] if j < B - 1 else after) - here
        mz = flux_a[strided(j)] + rise
        part[strided(j)] = c[strided(j)] * here + (mz - mz_before)
        flux2[strided(j)] = -(mz + rise)
        mz_before = mz

    def source(i):
        f = flux2[plane(i)]
        if i > 0:
            f = f - flux2[plane(i - 1)]
        return curl[plane(i)] + f

    first, last = eliminate(source, p_x, g2)
    msg[plane(0)] = first
    msg[plane(1)] = last - flux2[plane(B - 1)]


def second_y_kernel(ends_c, g_c, u, v, flux_y, part, rise_y, w, elec, magn, full_x, new_y, full_z, new_x, sems):
    stores = [(full_z, elec.at[2]), (new_x, magn.at[0])]
    stores = [pltpu.make_async_copy(a, b, sems.at[k]) for k, (a, b) in enumerate(stores)]
    before, after = ends_c[plane(0)], ends_c[plane(1)]
    here = None
    for j in range(B):
        ahead = g_c[plane(j)] + (u[plane(j)] * before + v[plane(j)] * after)
        full_z[strided(j)] = ahead
        if j > 0:
            new_x[strided(j - 1)] = -h * (flux_y[strided(j - 1)] + (ahead - here))
        here = ahead
    new_x[strided(B - 1)] = -h * (flux_y[strided(B - 1)] + (after - here))
    for store in stores:
        store.start()
    rows = pl.ds(0, w.shape[0] // 2)
    a = rise_y[rows]
    x = solve_z(part[rows] - behind_z(a), w[rows])
    full_x[...] = x
    new_y[...] = h * (a - ahead_z(x))
    for store in stores:
        store.wait()


def second_z_kernel(part, rise_y, w, x_half, y_half, _, __, elec, magn, full_x, new_y, sems):
    size = w.shape[0] // 2
    rows = [pl.ds(0, size), pl.ds(size, size)]
    stores = [(x_half, 0, elec, 0), (y_half, 0, magn, 1), (full_x, 1, elec, 0), (new_y, 1, magn, 1)]
    stores = [
        pltpu.make_async_copy(a, b.at[k, rows[at]], sems.at[i]) for i, (a, at, b, k) in enumerate(stores)
    ]
    stores[0].start()
    stores[1].start()
    a = rise_y[rows[1]]
    x = solve_z(part[rows[1]] - behind_z(a), w[rows[1]])
    full_x[...] = x
    stores[2].start()
    new_y[...] = h * (a - ahead_z(x))
    stores[3].start()
    for store in stores:
        store.wait()


def last_kernel(near, far, order, pos, coefs_near, coefs_far, own_b, group_b, got_near, own_near, *refs):
    others, refs = refs[:far], refs[far:]
    g, u, v, flux2, _, _, elec, magn, got_far, full_y, new_z, sems = refs
    q, r = place(pos, 0, near)
    far_blocks = collect(q, order, others[0], others[1:], got_far)
    ((before, after),) = solved_ends(
        q,
        r,
        1,
        [rows_of(stored(got_near, m, range(2)), 1) for m in range(near)],
        [stored(coefs_near, m, (2, 3, 4)) for m in range(near)],
        [rows_of(b, 1) for b in far_blocks],
        [stored(coefs_far, m, (2, 3, 4)) for m in range(far)],
        (rows_of(loaded(own_near, range(2)), 1), loaded(own_b, (2, 3, 4))),
        (rows_of(loaded(others[0], range(2)), 1), loaded(group_b, (2, 3, 4))),
    )
    stores = [(full_y, elec.at[1]), (new_z, magn.at[2])]
    stores = [pltpu.make_async_copy(a, b, sems.at[k]) for k, (a, b) in enumerate(stores)]
    for i in range(B):
        full_y[plane(i)] = g[plane(i)] + (u[plane(i)] * before + v[plane(i)] * after)
    stores[0].start()
    for i in range(B):
        rise = (full_y[plane(i + 1)] if i < B - 1 else after) - full_y[plane(i)]
        new_z[plane(i)] = -h * (flux2[plane(i)] + rise)
    stores[1].start()
    for store in stores:
        store.wait()


VMEM = pl.BlockSpec(memory_space=pltpu.VMEM)
SMEM = pl.BlockSpec(memory_space=pltpu.SMEM)
HBM = pl.BlockSpec(memory_space=pltpu.HBM)


def call(kernel, ins, outs, specs=None, out_specs=None, scratch=(), aliases=None, flops=1_000_000):
    shapes = [jax.ShapeDtypeStruct(s, F32) if isinstance(s, tuple) else s for s in outs]
    return pl.pallas_call(
        kernel,
        out_shape=shapes,
        in_specs=specs or [VMEM] * len(ins),
        out_specs=out_specs or [VMEM] * len(outs),
        scratch_shapes=[pltpu.VMEM(s, F32) if isinstance(s, tuple) else s for s in scratch],
        input_output_aliases=aliases or {},
        compiler_params=pltpu.CompilerParams(vmem_limit_bytes=24 * 1024 * 1024),
        cost_estimate=pl.CostEstimate(flops=flops, bytes_accessed=1_000_000, transcendentals=0),
    )(*ins)


def shared(value, axis, n, step, order):
    return [value] + [lax.ppermute(value, axis, [(i, i ^ (step * s)) for i in range(n)]) for s in order]


def split(n):
    near = 1 << (n.bit_length() // 2)
    return near, n // near


def local(electric, magnetic, material, permittivity, conductivity):
    nx, ny = lax.axis_size("px"), lax.axis_size("py")
    near_x, far_x = split(nx)
    near_y, far_y = split(ny)
    nz = material.shape[2]
    cells = (B * B, nz)
    me = jnp.stack([lax.axis_index("px"), lax.axis_index("py")]).astype(jnp.int32)
    in_hbm = lambda a: pltpu.with_memory_space_constraint(a, pltpu.HBM)
    elec = in_hbm(electric.reshape(3, *cells))
    magn = in_hbm(magnetic.reshape(3, *cells))
    ids = in_hbm(material.reshape(cells))
    dma = pltpu.SemaphoreType.DMA
    orders = [(1, 2, 3), (2, 1, 3), (2, 3, 1), (1, 3, 2)]
    counts = (near_x, far_x, near_y, far_y)
    px_near, px_far, py_near, py_far = [
        tuple(s for s in order if s < count) for order, count in zip(orders, counts)
    ]

    hx_prev = lax.ppermute(magnetic[0, :, B - 1], "py", [(i, (i + 1) % ny) for i in range(ny)])
    w, c, p_x, u_x, v_x, flux_b, part_b, ef, mf, ez_first, pos = call(
        tables_kernel,
        [me, in_hbm(permittivity), in_hbm(conductivity), ids, elec, magn],
        [cells] * 7 + [(3, *cells)] * 2 + [(8 * B, nz), jax.ShapeDtypeStruct((2 * B, nz), jnp.int32)],
        specs=[SMEM] + [HBM] * 5,
        scratch=[pltpu.VMEM(cells, jnp.int32)] + [pltpu.SMEM(permittivity.shape, F32)] * 2 + [dma((9,))],
    )
    g_b, own_b = call(
        first_x_kernel,
        [pos, part_b, hx_prev, flux_b, p_x, u_x, v_x, ef, mf],
        [cells, (7 * B, nz)],
    )
    ins = shared(own_b, "px", nx, 1, px_near)
    ez_next = lax.ppermute(ez_first, "py", [((i + 1) % ny, i) for i in range(ny)])
    near_b, group_b = call(
        functools.partial(merge_kernel, 0, near_x, px_near, 1, True),
        [pos] + ins,
        [(near_x, 7 * B, nz), (7 * B, nz)],
    )
    ins = shared(group_b, "px", nx, near_x, px_far)
    p_y, u_y, v_y, r_top, src_top, curl, flux_y, flux_a, part_a = call(
        functools.partial(first_z_kernel, ny),
        [pos, ef, mf, ez_next, w, c],
        [cells] * 3 + [(B, nz)] * 2 + [cells] * 4,
        scratch=[cells] * 2,
        flops=8_000_000,
    )
    ins = [pos, near_b, own_b] + ins + [g_b, u_x, v_x, flux_b, w, c, r_top, src_top]
    far_b, rise_y, curl, flux_y, flux_a, g_a, g_c, own_ac = call(
        functools.partial(both_y_kernel, near_x, far_x, px_far),
        ins + [curl, flux_y, flux_a, part_a, p_y, u_y, v_y],
        [(far_x, 7 * B, nz)] + [cells] * 6 + [(7 * B, nz)],
        scratch=[cells] * 2,
    )
    ins = shared(own_ac, "py", ny, 1, py_near)
    near_ac, msg = call(
        functools.partial(merge_kernel, 1, near_y, py_near, 2, False), [pos] + ins, [(near_y, 7 * B, nz), (7 * B, nz)]
    )
    ins = shared(msg, "py", ny, near_y, py_far)
    part_x, flux2, g2, ends_c, own_a = call(
        functools.partial(second_x_kernel, near_y, far_y, py_far),
        [pos, near_ac, own_ac] + ins + [g_a, u_y, v_y, flux_a, c, curl, p_x],
        [cells] * 3 + [(2 * B, nz)] * 2,
        scratch=[(far_y, 7 * B, nz), cells],
    )
    ins = shared(own_a, "px", nx, 1, px_near)
    half, whole = (B * B // 2, nz), pltpu.HBM((3, *cells), F32)
    elec, magn, x_half, y_half = call(
        second_y_kernel,
        [ends_c, g_c, u_y, v_y, flux_y, part_x, rise_y, w],
        [whole, whole, half, half],
        out_specs=[HBM] * 2 + [VMEM] * 2,
        scratch=[cells] * 2 + [dma((2,))],
        flops=4_000_000,
    )
    near_a, msg = call(
        functools.partial(merge_rows_kernel, 0, near_x, px_near),
        [pos, near_b] + ins,
        [(near_x, 2 * B, nz), (2 * B, nz)],
    )
    msg, elec = lax.optimization_barrier((msg, elec))
    ins = shared(msg, "px", nx, near_x, px_far)
    elec, magn = call(
        second_z_kernel,
        [part_x, rise_y, w, x_half, y_half, elec, magn],
        [whole] * 2,
        specs=[VMEM] * 5 + [HBM] * 2,
        out_specs=[HBM] * 2,
        scratch=[half] * 2 + [dma((4,))],
        aliases={5: 0, 6: 1},
        flops=4_000_000,
    )
    ins = [pos, near_b, far_b, own_b, group_b, near_a, own_a] + ins + [g2, u_x, v_x, flux2]
    at = len(ins)
    out = call(
        functools.partial(last_kernel, near_x, far_x, px_far),
        ins + [elec, magn],
        [whole] * 2,
        specs=[VMEM] * at + [HBM] * 2,
        out_specs=[HBM] * 2,
        scratch=[(far_x, 2 * B, nz), cells, cells, dma((2,))],
        aliases={at: 0, at + 1: 1},
    )
    return tuple(a.reshape(3, B, B, nz) for a in out)


def solution(mesh):
    placed = (P(None, "px", "py", None), P(None, "px", "py", None), P("px", "py", None), P(), P())
    return jax.shard_map(
        local,
        mesh=mesh,
        in_specs=placed,
        out_specs=(P(None, "px", "py", None), P(None, "px", "py", None)),
        check_vma=False,
    )
```

```python
import functools

import jax
import jax.numpy as jnp
from jax import lax
from jax.experimental import pallas as pl
from jax.experimental.pallas import tpu as pltpu
from jax.sharding import PartitionSpec as P

h = 32.0
B = 16
F32 = jnp.float32


def plane(i):
    return pl.ds(i * B, B)


def strided(j):
    return pl.ds(j, B, stride=B)


def lanes(v):
    return lax.broadcasted_iota(jnp.int32, v.shape, 1)


def behind_z(v):
    return v - jnp.where(lanes(v) == 0, 0.0, pltpu.roll(v, 1, 1))


def ahead_z(v):
    n = v.shape[1]
    return jnp.where(lanes(v) == n - 1, 0.0, pltpu.roll(v, n - 1, 1)) - v


def factor(w_of, first_block, p, u, v):
    d = None
    y = []
    for j in range(B):
        w = w_of(j)
        e = w + (jnp.where(first_block, 0.0, 1.0) if j == 0 else d)
        inv = 1.0 / (1.0 + e)
        d = e * inv
        p[plane(j)] = inv
        y.append(jnp.ones_like(inv) if j == 0 else y[-1] * last)
        last = inv
    uj = y[B - 1] * last
    vj = last
    u[plane(B - 1)] = uj
    v[plane(B - 1)] = vj
    for j in range(B - 2, -1, -1):
        inv = p[plane(j)]
        uj = inv * (y[j] + uj)
        vj = inv * vj
        u[plane(j)] = uj
        v[plane(j)] = vj


def eliminate(source_of, p, g):
    y = source_of(0)
    ys = [y]
    for j in range(1, B):
        y = source_of(j) + p[plane(j - 1)] * y
        ys.append(y)
    x = y * p[plane(B - 1)]
    end = x
    g[plane(B - 1)] = x
    for j in range(B - 2, -1, -1):
        x = p[plane(j)] * (ys[j] + x)
        g[plane(j)] = x
    return x, end


def boundary(me, rows, coefs, here, coef_here, outer):
    n = len(rows)
    left = [a for a, _ in outer]
    right = [b for _, b in outer]
    beta = delta = jnp.zeros_like(left[0])
    for s in range(n - 1):
        ff, fl, ll = coefs[s]
        t = fl / (1.0 - ff * beta)
        on = s < me
        left = [jnp.where(on, dl + t * (a + beta * gf), a) for a, (gf, dl) in zip(left, rows[s])]
        beta = jnp.where(on, ll + t * beta * fl, beta)
        m = n - 1 - s
        ff, fl, ll = coefs[m]
        t = fl / (1.0 - ll * delta)
        on = m > me
        right = [jnp.where(on, gf + t * (b + delta * dl), b) for b, (gf, dl) in zip(right, rows[m])]
        delta = jnp.where(on, ff + t * delta * fl, delta)
    ff, fl, ll = coef_here
    after_scale = 1.0 / (1.0 - delta * ll)
    t = fl * after_scale
    before_scale = 1.0 / (1.0 - beta * (ff + t * delta * fl))
    ends = []
    for a, b, (gf, dl) in zip(left, right, here):
        before = (a + beta * (gf + t * (b + delta * dl))) * before_scale
        ends.append((before, (b + delta * (dl + fl * before)) * after_scale))
    return ends


def merge(one, two):
    (ff1, fl1, ll1), rows1 = one
    (ff2, fl2, ll2), rows2 = two
    d = 1.0 / (1.0 - ll1 * ff2)
    t1, t2 = fl1 * d, fl2 * d
    rows = [
        (gf1 + t1 * (gf2 + ff2 * dl1), dl2 + t2 * (dl1 + ll1 * gf2))
        for (gf1, dl1), (gf2, dl2) in zip(rows1, rows2)
    ]
    return (ff1 + t1 * fl1 * ff2, t1 * fl2, ll2 + t2 * fl2 * ll1), rows


def solve_z(r, w):
    n = r.shape[1]
    lane = lanes(r)
    e = jnp.where(lane == n - 1, 0.0, 1.0)
    l = jnp.where(lane == 0, 0.0, 1.0)
    s = w + jnp.where(lane == n - 1, 1.0, 0.0)
    step = 1
    while step < n:
        inv = 1.0 / (s + (l + e))
        a, b = e * inv, l * inv
        r = r + (pltpu.roll(a * r, step, 1) + pltpu.roll(b * r, n - step, 1))
        s = s + (pltpu.roll(a * s, step, 1) + pltpu.roll(b * s, n - step, 1))
        g = a * l
        if 2 * step < n:
            e, l = pltpu.roll(g, n - step, 1), pltpu.roll(g, step, 1)
        step *= 2
    return r / s


def factors_kernel(w_in, a_out, b_out, scale):
    w = w_in[...]
    n = w.shape[1]
    lane = lanes(w)
    e = jnp.where(lane == n - 1, 0.0, 1.0)
    l = jnp.where(lane == 0, 0.0, 1.0)
    s = w + jnp.where(lane == n - 1, 1.0, 0.0)
    for k in range(a_out.shape[0]):
        step = 1 << k
        inv = 1.0 / (s + (l + e))
        a, b = e * inv, l * inv
        a_out[k] = a
        b_out[k] = b
        s = s + (pltpu.roll(a * s, step, 1) + pltpu.roll(b * s, n - step, 1))
        g = a * l
        e, l = pltpu.roll(g, n - step, 1), pltpu.roll(g, step, 1)
    scale[...] = 1.0 / s


def solve_factored(r, a, b, scale):
    n = r.shape[1]
    for k in range(a.shape[0]):
        step = 1 << k
        r = r + (pltpu.roll(a[k] * r, step, 1) + pltpu.roll(b[k] * r, n - step, 1))
    return r * scale[...]


def collect(r, order, own, others, got):
    refs = [own] + [others[order.index(s)] for s in range(1, len(order) + 1)]
    count = len(refs)
    blocks = [[] for _ in refs]
    for k in range(own.shape[0] // B):
        values = [ref[plane(k)] for ref in refs]
        bit = 1
        while bit < count:
            swap = lax.bitwise_and(r, bit) != 0
            values = [jnp.where(swap, values[m ^ bit], values[m]) for m in range(count)]
            bit *= 2
        for m, value in enumerate(values):
            got[m, plane(k)] = value
            blocks[m].append(value)
    return blocks


def rows_of(block, sources):
    return [(block[2 * k], block[2 * k + 1]) for k in range(sources)]


def stored(got, m, planes):
    return [got[m, plane(k)] for k in planes]


def loaded(msg, planes):
    return [msg[plane(k)] for k in planes]


def pick(values, index):
    out = values[0]
    for k in range(1, len(values)):
        out = jnp.where(index == k, values[k], out)
    return out


def place(pos, axis, near):
    here = pos[plane(axis)]
    return lax.shift_right_logical(here, near.bit_length() - 1), lax.bitwise_and(here, near - 1)


def tables_kernel(
    me, eps_in, sig_in, material, elec_in, magn_in, w, c, p, u, v, flux, part, elec, magn, ez_first, pos, ids, eps, sig, sems
):
    loads = [(eps_in, eps), (sig_in, sig), (material, ids)]
    for field, to, k in ((elec_in, elec, 0), (magn_in, magn, 1), (elec_in, elec, 2), (magn_in, magn, 0)):
        loads.append((field.at[k], to.at[k]))
    loads += [(elec_in.at[1], elec.at[1]), (magn_in.at[2], magn.at[2])]
    loads = [pltpu.make_async_copy(a, b, sems.at[k]) for k, (a, b) in enumerate(loads)]
    for load in loads:
        load.start()
    for axis in range(2):
        pos[plane(axis)] = jnp.full((B, w.shape[1]), me[axis], jnp.int32)
    for load in loads[:3]:
        load.wait()
    ws = [eps[m] * (1.0 / (h * h)) + sig[m] * (0.5 / h) for m in range(eps.shape[0])]
    cs = [eps[m] * (1.0 / (h * h)) - sig[m] * (0.5 / h) for m in range(eps.shape[0])]
    for i in range(B):
        cell = ids[plane(i)]
        wi = jnp.full(cell.shape, ws[0], F32)
        ci = jnp.full(cell.shape, cs[0], F32)
        for m in range(1, len(ws)):
            wi = jnp.where(cell == m, ws[m], wi)
            ci = jnp.where(cell == m, cs[m], ci)
        w[plane(i)] = wi
        c[plane(i)] = ci
    factor(lambda i: w[plane(i)], me[0] == 0, p, u, v)
    for load in loads[3:7]:
        load.wait()
    row = lax.broadcasted_iota(jnp.int32, (B, w.shape[1]), 0)
    for i in range(B):
        q = magn[1, plane(i)] * (1.0 / h) - ahead_z(elec[0, plane(i)])
        flux[plane(i)] = q
        if i > 0:
            q = q - flux[plane(i - 1)]
        here = magn[0, plane(i)]
        before = jnp.where(row == 0, 0.0, pltpu.roll(here, 1, 0))
        part[plane(i)] = c[plane(i)] * elec[2, plane(i)] + (q - (here - before) * (1.0 / h))
    for k in range(ez_first.shape[0] // B):
        ez_first[plane(k)] = elec.at[2][strided(0)]
    for load in loads[7:]:
        load.wait()


def first_x_kernel(pos, part, hx_prev, flux, p, u, v, elec, magn, g, msg):
    row = lax.broadcasted_iota(jnp.int32, hx_prev.shape, 0)
    scale = jnp.where(pos[plane(1)] == 0, 0.0, jnp.where(row == 0, 1.0 / h, 0.0))

    def source(i):
        return part[plane(i)] + hx_prev[pl.ds(i, 1)] * scale

    first, last = eliminate(source, p, g)
    msg[plane(0)] = first
    msg[plane(1)] = last - flux[plane(B - 1)]
    msg[plane(2)] = u[plane(0)]
    msg[plane(3)] = v[plane(0)]
    msg[plane(4)] = v[plane(B - 1)]
    msg[plane(5)] = elec[1, plane(0)]
    msg[plane(6)] = magn[2, plane(B - 1)]


def merged(blocks):
    while len(blocks) > 1:
        blocks = [merge(a, b) for a, b in zip(blocks[::2], blocks[1::2])]
    return blocks[0]


def merge_kernel(axis, near, order, sources, halos, pos, *refs):
    got, msg = refs[-2:]
    blocks = collect(place(pos, axis, near)[1], order, refs[0], refs[1:near], got)
    at = 2 * sources
    coefs, rows = merged([(b[at : at + 3], rows_of(b, sources)) for b in blocks])
    for k, value in enumerate([v for pair in rows for v in pair] + list(coefs)):
        msg[plane(k)] = value
    if halos:
        msg[plane(5)] = blocks[0][5]
        msg[plane(6)] = blocks[-1][6]


def merge_rows_kernel(axis, near, order, pos, coefs, *refs):
    got, msg = refs[-2:]
    blocks = collect(place(pos, axis, near)[1], order, refs[0], refs[1:near], got)
    _, rows = merged([(stored(coefs, m, (2, 3, 4)), rows_of(b, 1)) for m, b in enumerate(blocks)])
    msg[plane(0)], msg[plane(1)] = rows[0]


def solved_ends(q, r, sources, near_rows, near_coefs, far_rows, far_coefs, own_near, own_far):
    zero = jnp.zeros_like(far_coefs[0][0])
    outer = boundary(q, far_rows, far_coefs, *own_far, [(zero, zero)] * sources)
    return boundary(r, near_rows, near_coefs, *own_near, outer)


def first_z_kernel(n, pos, ef, mf, ez_next, w, c, p, u, v, r_top, src_top, curl, flux_y, flux_a, part_a, src, r):
    factor(lambda j: w[strided(j)], pos[plane(1)] == 0, p, u, v)
    inside = jnp.where(pos[pl.ds(B, 1)] == n - 1, 0.0, 1.0)
    row = lax.broadcasted_iota(jnp.int32, (B, w.shape[1]), 0)
    for i in range(B):
        ez = ef[2, plane(i)]
        after = jnp.where(row == B - 1, ez_next[pl.ds(i, 1)] * inside, pltpu.roll(ez, B - 1, 0))
        ri = mf[0, plane(i)] * (1.0 / h) - (after - ez)
        r[plane(i)] = ri
        gain = mf[2, plane(i)]
        if i > 0:
            gain = gain - mf[2, plane(i - 1)]
        src[plane(i)] = c[plane(i)] * ef[1, plane(i)] + (behind_z(ri) - gain * (1.0 / h))
        part_a[plane(i)] = c[plane(i)] * ef[0, plane(i)] - behind_z(mf[1, plane(i)]) * (1.0 / h)
        if i < B - 1:
            rise = ef[1, plane(i + 1)] - ef[1, plane(i)]
            flux_a[plane(i)] = mf[2, plane(i)] * (1.0 / h) - rise
    flux_a[plane(B - 1)] = mf[2, plane(B - 1)] * (1.0 / h) + ef[1, plane(B - 1)]
    r_top[...] = r[plane(0)]
    src_top[...] = src[plane(0)]
    x = solve_z(src[...], w[...])
    rise = ahead_z(x)
    mx = r[...] + rise
    curl[...] = c[...] * x + behind_z(mx)
    flux_y[...] = -(mx + rise)


def both_y_kernel(near, far, order, pos, got_near, own_near, *refs):
    others, refs = refs[:far], refs[far:]
    (g_b, u_x, v_x, flux_b, w, c, r_top, src_top, curl_in, flux_y_in, flux_a_in, part_a, p_y, u_y, v_y) = refs[:15]
    got_far, rise_y, curl, flux_y, flux_a, g_a, g_c, msg, part, fz = refs[15:]
    top = plane(0)
    q, r = place(pos, 0, near)
    far_blocks = collect(q, order, others[0], others[1:], got_far)
    near_blocks = [stored(got_near, m, range(7)) for m in range(near)]
    after_group = jnp.where(q < far - 1, pick([b[5] for b in far_blocks], q + 1), 0.0)
    ey_next = jnp.where(r < near - 1, pick([b[5] for b in near_blocks], r + 1), after_group)
    before_group = jnp.where(q > 0, pick([b[6] for b in far_blocks], q - 1), 0.0)
    hz_prev = jnp.where(r > 0, pick([b[6] for b in near_blocks], r - 1), before_group)
    curl[...] = curl_in[...]
    flux_y[...] = flux_y_in[...]
    flux_a[...] = flux_a_in[...]

    x = solve_z(src_top[...] + hz_prev * (1.0 / h), w[top])
    rise = ahead_z(x)
    mx = r_top[...] + rise
    curl[top] = c[top] * x + behind_z(mx)
    flux_y[top] = -(mx + rise)

    flux_a[plane(B - 1)] = flux_a[plane(B - 1)] - ey_next

    def source_a(j):
        f = flux_a[strided(j)]
        if j > 0:
            f = f - flux_a[strided(j - 1)]
        return part_a[strided(j)] + f

    first_a, last_a = eliminate(source_a, p_y, g_a)
    last_a = last_a - flux_a[strided(B - 1)]

    own, own_group = loaded(own_near, range(5)), loaded(others[0], range(5))
    ((before, after),) = solved_ends(
        q,
        r,
        1,
        [rows_of(b, 1) for b in near_blocks],
        [b[2:5] for b in near_blocks],
        [rows_of(b, 1) for b in far_blocks],
        [b[2:5] for b in far_blocks],
        (rows_of(own, 1), own[2:5]),
        (rows_of(own_group, 1), own_group[2:5]),
    )
    for i in range(B):
        fz[plane(i)] = g_b[plane(i)] + (u_x[plane(i)] * before + v_x[plane(i)] * after)
    my_before = jnp.where(pos[plane(0)] == 0, 0.0, fz[top] - before)
    for i in range(B):
        here = fz[plane(i)]
        rise = (fz[plane(i + 1)] if i < B - 1 else after) - here
        my = flux_b[plane(i)] + rise
        rise_y[plane(i)] = my + rise
        part[plane(i)] = c[plane(i)] * here + (my - my_before)
        my_before = my

    def source_c(j):
        f = flux_y[strided(j)]
        if j > 0:
            f = f - flux_y[strided(j - 1)]
        return part[strided(j)] + f

    first_c, last_c = eliminate(source_c, p_y, g_c)
    last_c = last_c - flux_y[strided(B - 1)]
    sent = [first_a, last_a, first_c, last_c, u_y[plane(0)], v_y[plane(0)], v_y[plane(B - 1)]]
    for k, value in enumerate(sent):
        msg[plane(k)] = value


def second_x_kernel(near, far, order, pos, got_near, own_near, *refs):
    others, refs = refs[:far], refs[far:]
    g_a, u, v, flux_a, c, curl, p_x, part, flux2, g2, ends_c, msg, got_far, fx = refs
    q, r = place(pos, 1, near)
    far_blocks = collect(q, order, others[0], others[1:], got_far)
    near_blocks = [stored(got_near, m, range(7)) for m in range(near)]
    own, own_group = loaded(own_near, range(7)), loaded(others[0], range(7))
    (before, after), (before_c, after_c) = solved_ends(
        q,
        r,
        2,
        [rows_of(b, 2) for b in near_blocks],
        [b[4:7] for b in near_blocks],
        [rows_of(b, 2) for b in far_blocks],
        [b[4:7] for b in far_blocks],
        (rows_of(own, 2), own[4:7]),
        (rows_of(own_group, 2), own_group[4:7]),
    )
    ends_c[plane(0)] = before_c
    ends_c[plane(1)] = after_c
    for j in range(B):
        fx[plane(j)] = g_a[plane(j)] + (u[plane(j)] * before + v[plane(j)] * after)
    mz_before = jnp.where(pos[plane(1)] == 0, 0.0, fx[plane(0)] - before)
    for j in range(B):
        here = fx[plane(j)]
        rise = (fx[plane(j + 1)] if j < B - 1 else after) - here
        mz = flux_a[strided(j)] + rise
        part[strided(j)] = c[strided(j)] * here + (mz - mz_before)
        flux2[strided(j)] = -(mz + rise)
        mz_before = mz

    def source(i):
        f = flux2[plane(i)]
        if i > 0:
            f = f - flux2[plane(i - 1)]
        return curl[plane(i)] + f

    first, last = eliminate(source, p_x, g2)
    msg[plane(0)] = first
    msg[plane(1)] = last - flux2[plane(B - 1)]


def second_y_kernel(ends_c, g_c, u, v, flux_y, elec, magn, full_z, new_x, sems):
    stores = [(full_z, elec.at[2]), (new_x, magn.at[0])]
    stores = [pltpu.make_async_copy(a, b, sems.at[k]) for k, (a, b) in enumerate(stores)]
    before, after = ends_c[plane(0)], ends_c[plane(1)]
    here = None
    for j in range(B):
        ahead = g_c[plane(j)] + (u[plane(j)] * before + v[plane(j)] * after)
        full_z[strided(j)] = ahead
        if j > 0:
            new_x[strided(j - 1)] = -h * (flux_y[strided(j - 1)] + (ahead - here))
        here = ahead
    new_x[strided(B - 1)] = -h * (flux_y[strided(B - 1)] + (after - here))
    for store in stores:
        store.start()
    for store in stores:
        store.wait()


def second_z_kernel(part, rise_y, z_a, z_b, z_scale, _, __, elec, magn, full_x, new_y, sems):
    stores = [(full_x, elec.at[0]), (new_y, magn.at[1])]
    stores = [pltpu.make_async_copy(a, b, sems.at[k]) for k, (a, b) in enumerate(stores)]
    a = rise_y[...]
    x = solve_factored(part[...] - behind_z(a), z_a, z_b, z_scale)
    full_x[...] = x
    stores[0].start()
    new_y[...] = h * (a - ahead_z(x))
    stores[1].start()
    for store in stores:
        store.wait()


def last_kernel(near, far, order, pos, coefs_near, coefs_far, own_b, group_b, got_near, own_near, *refs):
    others, refs = refs[:far], refs[far:]
    g, u, v, flux2, _, _, elec, magn, got_far, full_y, new_z, sems = refs
    q, r = place(pos, 0, near)
    far_blocks = collect(q, order, others[0], others[1:], got_far)
    ((before, after),) = solved_ends(
        q,
        r,
        1,
        [rows_of(stored(got_near, m, range(2)), 1) for m in range(near)],
        [stored(coefs_near, m, (2, 3, 4)) for m in range(near)],
        [rows_of(b, 1) for b in far_blocks],
        [stored(coefs_far, m, (2, 3, 4)) for m in range(far)],
        (rows_of(loaded(own_near, range(2)), 1), loaded(own_b, (2, 3, 4))),
        (rows_of(loaded(others[0], range(2)), 1), loaded(group_b, (2, 3, 4))),
    )
    stores = [(full_y, elec.at[1]), (new_z, magn.at[2])]
    stores = [pltpu.make_async_copy(a, b, sems.at[k]) for k, (a, b) in enumerate(stores)]
    for i in range(B):
        full_y[plane(i)] = g[plane(i)] + (u[plane(i)] * before + v[plane(i)] * after)
    stores[0].start()
    for i in range(B):
        rise = (full_y[plane(i + 1)] if i < B - 1 else after) - full_y[plane(i)]
        new_z[plane(i)] = -h * (flux2[plane(i)] + rise)
    stores[1].start()
    for store in stores:
        store.wait()


VMEM = pl.BlockSpec(memory_space=pltpu.VMEM)
SMEM = pl.BlockSpec(memory_space=pltpu.SMEM)
HBM = pl.BlockSpec(memory_space=pltpu.HBM)


def call(kernel, ins, outs, specs=None, out_specs=None, scratch=(), aliases=None, flops=1_000_000):
    shapes = [jax.ShapeDtypeStruct(s, F32) if isinstance(s, tuple) else s for s in outs]
    return pl.pallas_call(
        kernel,
        out_shape=shapes,
        in_specs=specs or [VMEM] * len(ins),
        out_specs=out_specs or [VMEM] * len(outs),
        scratch_shapes=[pltpu.VMEM(s, F32) if isinstance(s, tuple) else s for s in scratch],
        input_output_aliases=aliases or {},
        compiler_params=pltpu.CompilerParams(vmem_limit_bytes=24 * 1024 * 1024),
        cost_estimate=pl.CostEstimate(flops=flops, bytes_accessed=1_000_000, transcendentals=0),
    )(*ins)


def shared(value, axis, n, order, near=1, bent=()):
    masks = [near * s + (near // 2 if s in bent else 0) for s in order]
    return [value] + [lax.ppermute(value, axis, [(i, i ^ mask) for i in range(n)]) for mask in masks]


def split(n):
    near = 1 << (n.bit_length() // 2)
    return near, n // near


def local(electric, magnetic, material, permittivity, conductivity):
    nx, ny = lax.axis_size("px"), lax.axis_size("py")
    near_x, far_x = split(nx)
    near_y, far_y = split(ny)
    nz = material.shape[2]
    cells = (B * B, nz)
    me = jnp.stack([lax.axis_index("px"), lax.axis_index("py")]).astype(jnp.int32)
    in_hbm = lambda a: pltpu.with_memory_space_constraint(a, pltpu.HBM)
    elec = in_hbm(electric.reshape(3, *cells))
    magn = in_hbm(magnetic.reshape(3, *cells))
    ids = in_hbm(material.reshape(cells))
    dma = pltpu.SemaphoreType.DMA
    orders = [(1, 2, 3), (2, 1, 3), (2, 3, 1), (1, 3, 2)]
    counts = (near_x, far_x, near_y, far_y)
    px_near, px_far, py_near, py_far = [
        tuple(s for s in order if s < count) for order, count in zip(orders, counts)
    ]

    hx_prev = lax.ppermute(magnetic[0, :, B - 1], "py", [(i, (i + 1) % ny) for i in range(ny)])
    w, c, p_x, u_x, v_x, flux_b, part_b, ef, mf, ez_first, pos = call(
        tables_kernel,
        [me, in_hbm(permittivity), in_hbm(conductivity), ids, elec, magn],
        [cells] * 7 + [(3, *cells)] * 2 + [(8 * B, nz), jax.ShapeDtypeStruct((2 * B, nz), jnp.int32)],
        specs=[SMEM] + [HBM] * 5,
        scratch=[pltpu.VMEM(cells, jnp.int32)] + [pltpu.SMEM(permittivity.shape, F32)] * 2 + [dma((9,))],
    )
    g_b, own_b = call(
        first_x_kernel,
        [pos, part_b, hx_prev, flux_b, p_x, u_x, v_x, ef, mf],
        [cells, (7 * B, nz)],
    )
    ins = shared(own_b, "px", nx, px_near)
    ez_next = lax.ppermute(ez_first, "py", [((i + 1) % ny, i) for i in range(ny)])
    near_b, group_b = call(
        functools.partial(merge_kernel, 0, near_x, px_near, 1, True),
        [pos] + ins,
        [(near_x, 7 * B, nz), (7 * B, nz)],
    )
    ins = shared(group_b, "px", nx, px_far, near_x, (1, 3))
    p_y, u_y, v_y, r_top, src_top, curl, flux_y, flux_a, part_a = call(
        functools.partial(first_z_kernel, ny),
        [pos, ef, mf, ez_next, w, c],
        [cells] * 3 + [(B, nz)] * 2 + [cells] * 4,
        scratch=[cells] * 2,
        flops=8_000_000,
    )
    ins = [pos, near_b, own_b] + ins + [g_b, u_x, v_x, flux_b, w, c, r_top, src_top]
    far_b, rise_y, curl, flux_y, flux_a, g_a, g_c, own_ac = call(
        functools.partial(both_y_kernel, near_x, far_x, px_far),
        ins + [curl, flux_y, flux_a, part_a, p_y, u_y, v_y],
        [(far_x, 7 * B, nz)] + [cells] * 6 + [(7 * B, nz)],
        scratch=[cells] * 2,
    )
    ins = shared(own_ac, "py", ny, py_near)
    near_ac, msg = call(
        functools.partial(merge_kernel, 1, near_y, py_near, 2, False), [pos] + ins, [(near_y, 7 * B, nz), (7 * B, nz)]
    )
    msg, w = lax.optimization_barrier((msg, w))
    ins = shared(msg, "py", ny, py_far, near_y, (2,))
    steps = (nz - 1).bit_length()
    z_factors = call(factors_kernel, [w], [(steps, *cells)] * 2 + [cells], flops=8_000_000)
    ins, z_factors = lax.optimization_barrier((ins, z_factors))
    part_x, flux2, g2, ends_c, own_a = call(
        functools.partial(second_x_kernel, near_y, far_y, py_far),
        [pos, near_ac, own_ac] + ins + [g_a, u_y, v_y, flux_a, c, curl, p_x],
        [cells] * 3 + [(2 * B, nz)] * 2,
        scratch=[(far_y, 7 * B, nz), cells],
    )
    ins = shared(own_a, "px", nx, px_near)
    whole = pltpu.HBM((3, *cells), F32)
    elec, magn = call(
        second_y_kernel,
        [ends_c, g_c, u_y, v_y, flux_y],
        [whole, whole],
        out_specs=[HBM] * 2,
        scratch=[cells] * 2 + [dma((2,))],
    )
    near_a, msg = call(
        functools.partial(merge_rows_kernel, 0, near_x, px_near),
        [pos, near_b] + ins,
        [(near_x, 2 * B, nz), (2 * B, nz)],
    )
    msg, elec = lax.optimization_barrier((msg, elec))
    ins = shared(msg, "px", nx, px_far, near_x, (1, 3))
    elec, magn = call(
        second_z_kernel,
        [part_x, rise_y, *z_factors, elec, magn],
        [whole] * 2,
        specs=[VMEM] * 5 + [HBM] * 2,
        out_specs=[HBM] * 2,
        scratch=[cells] * 2 + [dma((2,))],
        aliases={5: 0, 6: 1},
        flops=4_000_000,
    )
    ins = [pos, near_b, far_b, own_b, group_b, near_a, own_a] + ins + [g2, u_x, v_x, flux2]
    at = len(ins)
    out = call(
        functools.partial(last_kernel, near_x, far_x, px_far),
        ins + [elec, magn],
        [whole] * 2,
        specs=[VMEM] * at + [HBM] * 2,
        out_specs=[HBM] * 2,
        scratch=[(far_x, 2 * B, nz), cells, cells, dma((2,))],
        aliases={at: 0, at + 1: 1},
    )
    return tuple(a.reshape(3, B, B, nz) for a in out)


def solution(mesh):
    placed = (P(None, "px", "py", None), P(None, "px", "py", None), P("px", "py", None), P(), P())
    return jax.shard_map(
        local,
        mesh=mesh,
        in_specs=placed,
        out_specs=(P(None, "px", "py", None), P(None, "px", "py", None)),
        check_vma=False,
    )
```

```python
import functools

import jax
import jax.numpy as jnp
from jax import lax
from jax.experimental import pallas as pl
from jax.experimental.pallas import tpu as pltpu
from jax.sharding import PartitionSpec as P

h = 32.0
B = 16
F32 = jnp.float32


def plane(i):
    return pl.ds(i * B, B)


def strided(j):
    return pl.ds(j, B, stride=B)


def lanes(v):
    return lax.broadcasted_iota(jnp.int32, v.shape, 1)


def behind_z(v):
    return v - jnp.where(lanes(v) == 0, 0.0, pltpu.roll(v, 1, 1))


def ahead_z(v):
    n = v.shape[1]
    return jnp.where(lanes(v) == n - 1, 0.0, pltpu.roll(v, n - 1, 1)) - v


def factor(w_of, first_block, p, u, v):
    d = None
    y = []
    for j in range(B):
        w = w_of(j)
        e = w + (jnp.where(first_block, 0.0, 1.0) if j == 0 else d)
        inv = 1.0 / (1.0 + e)
        d = e * inv
        p[plane(j)] = inv
        y.append(jnp.ones_like(inv) if j == 0 else y[-1] * last)
        last = inv
    uj = y[B - 1] * last
    vj = last
    u[plane(B - 1)] = uj
    v[plane(B - 1)] = vj
    for j in range(B - 2, -1, -1):
        inv = p[plane(j)]
        uj = inv * (y[j] + uj)
        vj = inv * vj
        u[plane(j)] = uj
        v[plane(j)] = vj


def eliminate(source_of, p, g):
    y = source_of(0)
    ys = [y]
    for j in range(1, B):
        y = source_of(j) + p[plane(j - 1)] * y
        ys.append(y)
    x = y * p[plane(B - 1)]
    end = x
    g[plane(B - 1)] = x
    for j in range(B - 2, -1, -1):
        x = p[plane(j)] * (ys[j] + x)
        g[plane(j)] = x
    return x, end


def boundary(me, rows, coefs, here, coef_here, outer):
    n = len(rows)
    left = [a for a, _ in outer]
    right = [b for _, b in outer]
    beta = delta = jnp.zeros_like(left[0])
    for s in range(n - 1):
        ff, fl, ll = coefs[s]
        t = fl / (1.0 - ff * beta)
        on = s < me
        left = [jnp.where(on, dl + t * (a + beta * gf), a) for a, (gf, dl) in zip(left, rows[s])]
        beta = jnp.where(on, ll + t * beta * fl, beta)
        m = n - 1 - s
        ff, fl, ll = coefs[m]
        t = fl / (1.0 - ll * delta)
        on = m > me
        right = [jnp.where(on, gf + t * (b + delta * dl), b) for b, (gf, dl) in zip(right, rows[m])]
        delta = jnp.where(on, ff + t * delta * fl, delta)
    ff, fl, ll = coef_here
    after_scale = 1.0 / (1.0 - delta * ll)
    t = fl * after_scale
    before_scale = 1.0 / (1.0 - beta * (ff + t * delta * fl))
    ends = []
    for a, b, (gf, dl) in zip(left, right, here):
        before = (a + beta * (gf + t * (b + delta * dl))) * before_scale
        ends.append((before, (b + delta * (dl + fl * before)) * after_scale))
    return ends


def merge(one, two):
    (ff1, fl1, ll1), rows1 = one
    (ff2, fl2, ll2), rows2 = two
    d = 1.0 / (1.0 - ll1 * ff2)
    t1, t2 = fl1 * d, fl2 * d
    rows = [
        (gf1 + t1 * (gf2 + ff2 * dl1), dl2 + t2 * (dl1 + ll1 * gf2))
        for (gf1, dl1), (gf2, dl2) in zip(rows1, rows2)
    ]
    return (ff1 + t1 * fl1 * ff2, t1 * fl2, ll2 + t2 * fl2 * ll1), rows


def solve_z(r, w):
    n = r.shape[1]
    lane = lanes(r)
    e = jnp.where(lane == n - 1, 0.0, 1.0)
    l = jnp.where(lane == 0, 0.0, 1.0)
    s = w + jnp.where(lane == n - 1, 1.0, 0.0)
    step = 1
    while step < n:
        inv = 1.0 / (s + (l + e))
        a, b = e * inv, l * inv
        r = r + (pltpu.roll(a * r, step, 1) + pltpu.roll(b * r, n - step, 1))
        s = s + (pltpu.roll(a * s, step, 1) + pltpu.roll(b * s, n - step, 1))
        g = a * l
        if 2 * step < n:
            e, l = pltpu.roll(g, n - step, 1), pltpu.roll(g, step, 1)
        step *= 2
    return r / s


def collect(r, order, own, others, got):
    refs = [own] + [others[order.index(s)] for s in range(1, len(order) + 1)]
    count = len(refs)
    blocks = [[] for _ in refs]
    for k in range(own.shape[0] // B):
        values = [ref[plane(k)] for ref in refs]
        bit = 1
        while bit < count:
            swap = lax.bitwise_and(r, bit) != 0
            values = [jnp.where(swap, values[m ^ bit], values[m]) for m in range(count)]
            bit *= 2
        for m, value in enumerate(values):
            got[m, plane(k)] = value
            blocks[m].append(value)
    return blocks


def rows_of(block, sources):
    return [(block[2 * k], block[2 * k + 1]) for k in range(sources)]


def stored(got, m, planes):
    return [got[m, plane(k)] for k in planes]


def loaded(msg, planes):
    return [msg[plane(k)] for k in planes]


def pick(values, index):
    out = values[0]
    for k in range(1, len(values)):
        out = jnp.where(index == k, values[k], out)
    return out


def place(pos, axis, near):
    here = pos[plane(axis)]
    return lax.shift_right_logical(here, near.bit_length() - 1), lax.bitwise_and(here, near - 1)


def cut_kernel(magn, hx_last, sem):
    load = pltpu.make_async_copy(magn.at[0, :, B - 1], hx_last, sem)
    load.start()
    load.wait()


def tables_kernel(
    me, eps_in, sig_in, material, elec_in, magn_in, w, c, p, u, v, flux, part, elec, magn, ez_first, pos, ids, eps, sig, sems
):
    loads = [(eps_in, eps), (sig_in, sig), (material, ids)]
    for field, to, k in ((elec_in, elec, 0), (magn_in, magn, 1), (elec_in, elec, 2), (magn_in, magn, 0)):
        loads.append((field.at[k], to.at[k]))
    loads += [(elec_in.at[1], elec.at[1]), (magn_in.at[2], magn.at[2])]
    loads = [pltpu.make_async_copy(a, b, sems.at[k]) for k, (a, b) in enumerate(loads)]
    for load in loads:
        load.start()
    for axis in range(2):
        pos[plane(axis)] = jnp.full((B, w.shape[1]), me[axis], jnp.int32)
    for load in loads[:3]:
        load.wait()
    ws = [eps[m] * (1.0 / (h * h)) + sig[m] * (0.5 / h) for m in range(eps.shape[0])]
    cs = [eps[m] * (1.0 / (h * h)) - sig[m] * (0.5 / h) for m in range(eps.shape[0])]
    for i in range(B):
        cell = ids[plane(i)]
        wi = jnp.full(cell.shape, ws[0], F32)
        ci = jnp.full(cell.shape, cs[0], F32)
        for m in range(1, len(ws)):
            wi = jnp.where(cell == m, ws[m], wi)
            ci = jnp.where(cell == m, cs[m], ci)
        w[plane(i)] = wi
        c[plane(i)] = ci
    factor(lambda i: w[plane(i)], me[0] == 0, p, u, v)
    for load in loads[3:7]:
        load.wait()
    row = lax.broadcasted_iota(jnp.int32, (B, w.shape[1]), 0)
    for i in range(B):
        q = magn[1, plane(i)] * (1.0 / h) - ahead_z(elec[0, plane(i)])
        flux[plane(i)] = q
        if i > 0:
            q = q - flux[plane(i - 1)]
        here = magn[0, plane(i)]
        before = jnp.where(row == 0, 0.0, pltpu.roll(here, 1, 0))
        part[plane(i)] = c[plane(i)] * elec[2, plane(i)] + (q - (here - before) * (1.0 / h))
    for k in range(ez_first.shape[0] // B):
        ez_first[plane(k)] = elec.at[2][strided(0)]
    for load in loads[7:]:
        load.wait()


def first_x_kernel(pos, part, hx_prev, flux, p, u, v, elec, magn, g, msg):
    row = lax.broadcasted_iota(jnp.int32, hx_prev.shape, 0)
    scale = jnp.where(pos[plane(1)] == 0, 0.0, jnp.where(row == 0, 1.0 / h, 0.0))

    def source(i):
        return part[plane(i)] + hx_prev[pl.ds(i, 1)] * scale

    first, last = eliminate(source, p, g)
    msg[plane(0)] = first
    msg[plane(1)] = last - flux[plane(B - 1)]
    msg[plane(2)] = u[plane(0)]
    msg[plane(3)] = v[plane(0)]
    msg[plane(4)] = v[plane(B - 1)]
    msg[plane(5)] = elec[1, plane(0)]
    msg[plane(6)] = magn[2, plane(B - 1)]


def merged(blocks):
    while len(blocks) > 1:
        blocks = [merge(a, b) for a, b in zip(blocks[::2], blocks[1::2])]
    return blocks[0]


def merge_kernel(axis, near, order, sources, halos, pos, *refs):
    got, msg = refs[-2:]
    blocks = collect(place(pos, axis, near)[1], order, refs[0], refs[1:near], got)
    at = 2 * sources
    coefs, rows = merged([(b[at : at + 3], rows_of(b, sources)) for b in blocks])
    for k, value in enumerate([v for pair in rows for v in pair] + list(coefs)):
        msg[plane(k)] = value
    if halos:
        msg[plane(5)] = blocks[0][5]
        msg[plane(6)] = blocks[-1][6]


def solved_ends(q, r, sources, near_rows, near_coefs, far_rows, far_coefs, own_near, own_far):
    zero = jnp.zeros_like(far_coefs[0][0])
    outer = boundary(q, far_rows, far_coefs, *own_far, [(zero, zero)] * sources)
    return boundary(r, near_rows, near_coefs, *own_near, outer)


def first_z_kernel(n, pos, ef, mf, ez_next, w, c, p, u, v, r_top, src_top, curl, flux_y, flux_a, part_a, src, r):
    factor(lambda j: w[strided(j)], pos[plane(1)] == 0, p, u, v)
    inside = jnp.where(pos[pl.ds(B, 1)] == n - 1, 0.0, 1.0)
    row = lax.broadcasted_iota(jnp.int32, (B, w.shape[1]), 0)
    for i in range(B):
        ez = ef[2, plane(i)]
        after = jnp.where(row == B - 1, ez_next[pl.ds(i, 1)] * inside, pltpu.roll(ez, B - 1, 0))
        ri = mf[0, plane(i)] * (1.0 / h) - (after - ez)
        r[plane(i)] = ri
        gain = mf[2, plane(i)]
        if i > 0:
            gain = gain - mf[2, plane(i - 1)]
        src[plane(i)] = c[plane(i)] * ef[1, plane(i)] + (behind_z(ri) - gain * (1.0 / h))
        part_a[plane(i)] = c[plane(i)] * ef[0, plane(i)] - behind_z(mf[1, plane(i)]) * (1.0 / h)
        if i < B - 1:
            rise = ef[1, plane(i + 1)] - ef[1, plane(i)]
            flux_a[plane(i)] = mf[2, plane(i)] * (1.0 / h) - rise
    flux_a[plane(B - 1)] = mf[2, plane(B - 1)] * (1.0 / h) + ef[1, plane(B - 1)]
    r_top[...] = r[plane(0)]
    src_top[...] = src[plane(0)]
    x = solve_z(src[...], w[...])
    rise = ahead_z(x)
    mx = r[...] + rise
    curl[...] = c[...] * x + behind_z(mx)
    flux_y[...] = -(mx + rise)


def both_y_kernel(near, far, order, pos, got_near, own_near, *refs):
    others, refs = refs[:far], refs[far:]
    (g_b, u_x, v_x, flux_b, w, c, r_top, src_top, curl_in, flux_y_in, flux_a_in, part_a, p_y, u_y, v_y) = refs[:15]
    got_far, rise_y, curl, flux_y, flux_a, g_a, g_c, msg, part, fz = refs[15:]
    top = plane(0)
    q, r = place(pos, 0, near)
    far_blocks = collect(q, order, others[0], others[1:], got_far)
    near_blocks = [stored(got_near, m, range(7)) for m in range(near)]
    after_group = jnp.where(q < far - 1, pick([b[5] for b in far_blocks], q + 1), 0.0)
    ey_next = jnp.where(r < near - 1, pick([b[5] for b in near_blocks], r + 1), after_group)
    before_group = jnp.where(q > 0, pick([b[6] for b in far_blocks], q - 1), 0.0)
    hz_prev = jnp.where(r > 0, pick([b[6] for b in near_blocks], r - 1), before_group)
    curl[...] = curl_in[...]
    flux_y[...] = flux_y_in[...]
    flux_a[...] = flux_a_in[...]

    x = solve_z(src_top[...] + hz_prev * (1.0 / h), w[top])
    rise = ahead_z(x)
    mx = r_top[...] + rise
    curl[top] = c[top] * x + behind_z(mx)
    flux_y[top] = -(mx + rise)

    flux_a[plane(B - 1)] = flux_a[plane(B - 1)] - ey_next

    def source_a(j):
        f = flux_a[strided(j)]
        if j > 0:
            f = f - flux_a[strided(j - 1)]
        return part_a[strided(j)] + f

    first_a, last_a = eliminate(source_a, p_y, g_a)
    last_a = last_a - flux_a[strided(B - 1)]

    own, own_group = loaded(own_near, range(5)), loaded(others[0], range(5))
    ((before, after),) = solved_ends(
        q,
        r,
        1,
        [rows_of(b, 1) for b in near_blocks],
        [b[2:5] for b in near_blocks],
        [rows_of(b, 1) for b in far_blocks],
        [b[2:5] for b in far_blocks],
        (rows_of(own, 1), own[2:5]),
        (rows_of(own_group, 1), own_group[2:5]),
    )
    for i in range(B):
        fz[plane(i)] = g_b[plane(i)] + (u_x[plane(i)] * before + v_x[plane(i)] * after)
    my_before = jnp.where(pos[plane(0)] == 0, 0.0, fz[top] - before)
    for i in range(B):
        here = fz[plane(i)]
        rise = (fz[plane(i + 1)] if i < B - 1 else after) - here
        my = flux_b[plane(i)] + rise
        rise_y[plane(i)] = my + rise
        part[plane(i)] = c[plane(i)] * here + (my - my_before)
        my_before = my

    def source_c(j):
        f = flux_y[strided(j)]
        if j > 0:
            f = f - flux_y[strided(j - 1)]
        return part[strided(j)] + f

    first_c, last_c = eliminate(source_c, p_y, g_c)
    last_c = last_c - flux_y[strided(B - 1)]
    sent = [first_a, last_a, first_c, last_c, u_y[plane(0)], v_y[plane(0)], v_y[plane(B - 1)]]
    for k, value in enumerate(sent):
        msg[plane(k)] = value


def second_x_kernel(near, far, near_x, far_x, order, pos, got_near, own_near, *refs):
    others, refs = refs[:far], refs[far:]
    g_a, u, v, flux_a, c, curl, p_x, near_b, part, flux2, g2, ends_c, own_a, msg, got_far, fx = refs
    q, r = place(pos, 1, near)
    far_blocks = collect(q, order, others[0], others[1:], got_far)
    near_blocks = [stored(got_near, m, range(7)) for m in range(near)]
    own, own_group = loaded(own_near, range(7)), loaded(others[0], range(7))
    (before, after), (before_c, after_c) = solved_ends(
        q,
        r,
        2,
        [rows_of(b, 2) for b in near_blocks],
        [b[4:7] for b in near_blocks],
        [rows_of(b, 2) for b in far_blocks],
        [b[4:7] for b in far_blocks],
        (rows_of(own, 2), own[4:7]),
        (rows_of(own_group, 2), own_group[4:7]),
    )
    ends_c[plane(0)] = before_c
    ends_c[plane(1)] = after_c
    for j in range(B):
        fx[plane(j)] = g_a[plane(j)] + (u[plane(j)] * before + v[plane(j)] * after)
    mz_before = jnp.where(pos[plane(1)] == 0, 0.0, fx[plane(0)] - before)
    for j in range(B):
        here = fx[plane(j)]
        rise = (fx[plane(j + 1)] if j < B - 1 else after) - here
        mz = flux_a[strided(j)] + rise
        part[strided(j)] = c[strided(j)] * here + (mz - mz_before)
        flux2[strided(j)] = -(mz + rise)
        mz_before = mz

    def source(i):
        f = flux2[plane(i)]
        if i > 0:
            f = f - flux2[plane(i - 1)]
        return curl[plane(i)] + f

    first, last = eliminate(source, p_x, g2)
    own = [first, last - flux2[plane(B - 1)]]
    own_a[plane(0)], own_a[plane(1)] = own
    q, r = place(pos, 0, near_x)
    alone = [
        (stored(near_b, m, (2, 3, 4)), [[jnp.where(r == m, value, 0.0) for value in own]])
        for m in range(near_x)
    ]
    share = merged(alone)[1][0]
    for group in range(far_x):
        for k in range(2):
            value = jnp.where(q == group, own[k], share[k])
            for m in range(near_x):
                msg[group * near_x + m, plane(k)] = value


def second_yz_kernel(
    ends_c, g_c, u, v, flux_y, part, rise_y, w, elec, magn, full_z, new_x, full_x, new_y, sems
):
    stores = [(full_z, elec.at[2]), (new_x, magn.at[0]), (full_x, elec.at[0]), (new_y, magn.at[1])]
    stores = [pltpu.make_async_copy(a, b, sems.at[k]) for k, (a, b) in enumerate(stores)]
    before, after = ends_c[plane(0)], ends_c[plane(1)]
    here = None
    for j in range(B):
        ahead = g_c[plane(j)] + (u[plane(j)] * before + v[plane(j)] * after)
        full_z[strided(j)] = ahead
        if j > 0:
            new_x[strided(j - 1)] = -h * (flux_y[strided(j - 1)] + (ahead - here))
        here = ahead
    new_x[strided(B - 1)] = -h * (flux_y[strided(B - 1)] + (after - here))
    stores[0].start()
    stores[1].start()
    a = rise_y[...]
    x = solve_z(part[...] - behind_z(a), w[...])
    full_x[...] = x
    stores[2].start()
    new_y[...] = h * (a - ahead_z(x))
    stores[3].start()
    for store in stores:
        store.wait()


def last_kernel(near, far, pos, near_b, far_b, own_b, group_b, got, own_a, *refs):
    g, u, v, flux2, _, _, elec, magn, full_y, new_z, sems = refs
    q, r = place(pos, 0, near)
    blocks = [[stored(got, group * near + m, range(2)) for m in range(near)] for group in range(far)]
    near_rows = [
        rows_of([pick([blocks[group][m][k] for group in range(far)], q) for k in range(2)], 1)
        for m in range(near)
    ]
    near_coefs = [stored(near_b, m, (2, 3, 4)) for m in range(near)]
    own_rows = merged(list(zip(near_coefs, near_rows)))[1]
    far_rows = [rows_of([sum(block[k] for block in group) for k in range(2)], 1) for group in blocks]
    ((before, after),) = solved_ends(
        q,
        r,
        1,
        near_rows,
        near_coefs,
        far_rows,
        [stored(far_b, m, (2, 3, 4)) for m in range(far)],
        (rows_of(loaded(own_a, range(2)), 1), loaded(own_b, (2, 3, 4))),
        (own_rows, loaded(group_b, (2, 3, 4))),
    )
    stores = [(full_y, elec.at[1]), (new_z, magn.at[2])]
    stores = [pltpu.make_async_copy(a, b, sems.at[k]) for k, (a, b) in enumerate(stores)]
    for i in range(B):
        full_y[plane(i)] = g[plane(i)] + (u[plane(i)] * before + v[plane(i)] * after)
    stores[0].start()
    for i in range(B):
        rise = (full_y[plane(i + 1)] if i < B - 1 else after) - full_y[plane(i)]
        new_z[plane(i)] = -h * (flux2[plane(i)] + rise)
    stores[1].start()
    for store in stores:
        store.wait()


VMEM = pl.BlockSpec(memory_space=pltpu.VMEM)
SMEM = pl.BlockSpec(memory_space=pltpu.SMEM)
HBM = pl.BlockSpec(memory_space=pltpu.HBM)


def call(kernel, ins, outs, specs=None, out_specs=None, scratch=(), aliases=None, flops=1_000_000):
    shapes = [jax.ShapeDtypeStruct(s, F32) if isinstance(s, tuple) else s for s in outs]
    return pl.pallas_call(
        kernel,
        out_shape=shapes,
        in_specs=specs or [VMEM] * len(ins),
        out_specs=out_specs or [VMEM] * len(outs),
        scratch_shapes=[pltpu.VMEM(s, F32) if isinstance(s, tuple) else s for s in scratch],
        input_output_aliases=aliases or {},
        compiler_params=pltpu.CompilerParams(vmem_limit_bytes=24 * 1024 * 1024),
        cost_estimate=pl.CostEstimate(flops=flops, bytes_accessed=1_000_000, transcendentals=0),
    )(*ins)


def shared(value, axis, n, order, near=1, bent=()):
    masks = [near * s + (near // 2 if s in bent else 0) for s in order]
    return [value] + [lax.ppermute(value, axis, [(i, i ^ mask) for i in range(n)]) for mask in masks]


def split(n):
    near = 1 << (n.bit_length() // 2)
    return near, n // near


def local(electric, magnetic, material, permittivity, conductivity):
    nx, ny = lax.axis_size("px"), lax.axis_size("py")
    near_x, far_x = split(nx)
    near_y, far_y = split(ny)
    nz = material.shape[2]
    cells = (B * B, nz)
    me = jnp.stack([lax.axis_index("px"), lax.axis_index("py")]).astype(jnp.int32)
    in_hbm = lambda a: pltpu.with_memory_space_constraint(a, pltpu.HBM)
    elec = in_hbm(electric.reshape(3, *cells))
    magn = in_hbm(magnetic.reshape(3, *cells))
    ids = in_hbm(material.reshape(cells))
    dma = pltpu.SemaphoreType.DMA
    orders = [(1, 2, 3), (2, 1, 3), (2, 1, 3), (1, 3, 2)]
    counts = (near_x, far_x, near_y, far_y)
    px_near, px_far, py_near, py_far = [
        tuple(s for s in order if s < count) for order, count in zip(orders, counts)
    ]

    (hx_last,) = call(
        cut_kernel, [in_hbm(magnetic)], [(B, nz)], specs=[HBM], scratch=[dma(())], flops=1000
    )
    hx_prev = lax.ppermute(hx_last, "py", [(i, (i + 1) % ny) for i in range(ny)])
    w, c, p_x, u_x, v_x, flux_b, part_b, ef, mf, ez_first, pos = call(
        tables_kernel,
        [me, in_hbm(permittivity), in_hbm(conductivity), ids, elec, magn],
        [cells] * 7 + [(3, *cells)] * 2 + [(8 * B, nz), jax.ShapeDtypeStruct((2 * B, nz), jnp.int32)],
        specs=[SMEM] + [HBM] * 5,
        scratch=[pltpu.VMEM(cells, jnp.int32)] + [pltpu.SMEM(permittivity.shape, F32)] * 2 + [dma((9,))],
    )
    g_b, own_b = call(
        first_x_kernel,
        [pos, part_b, hx_prev, flux_b, p_x, u_x, v_x, ef, mf],
        [cells, (7 * B, nz)],
    )
    ins = shared(own_b, "px", nx, px_near)
    ez_next = lax.ppermute(ez_first, "py", [((i + 1) % ny, i) for i in range(ny)])
    near_b, group_b = call(
        functools.partial(merge_kernel, 0, near_x, px_near, 1, True),
        [pos] + ins,
        [(near_x, 7 * B, nz), (7 * B, nz)],
    )
    ins = shared(group_b, "px", nx, px_far, near_x, (1, 3))
    p_y, u_y, v_y, r_top, src_top, curl, flux_y, flux_a, part_a = call(
        functools.partial(first_z_kernel, ny),
        [pos, ef, mf, ez_next, w, c],
        [cells] * 3 + [(B, nz)] * 2 + [cells] * 4,
        scratch=[cells] * 2,
        flops=8_000_000,
    )
    ins = [pos, near_b, own_b] + ins + [g_b, u_x, v_x, flux_b, w, c, r_top, src_top]
    far_b, rise_y, curl, flux_y, flux_a, g_a, g_c, own_ac = call(
        functools.partial(both_y_kernel, near_x, far_x, px_far),
        ins + [curl, flux_y, flux_a, part_a, p_y, u_y, v_y],
        [(far_x, 7 * B, nz)] + [cells] * 6 + [(7 * B, nz)],
        scratch=[cells] * 2,
    )
    ins = shared(own_ac, "py", ny, py_near)
    near_ac, msg = call(
        functools.partial(merge_kernel, 1, near_y, py_near, 2, False), [pos] + ins, [(near_y, 7 * B, nz), (7 * B, nz)]
    )
    ins = shared(msg, "py", ny, py_far, near_y, (2,))
    part_x, flux2, g2, ends_c, own_a, msg = call(
        functools.partial(second_x_kernel, near_y, far_y, near_x, far_x, py_far),
        [pos, near_ac, own_ac] + ins + [g_a, u_y, v_y, flux_a, c, curl, p_x, near_b],
        [cells] * 3 + [(2 * B, nz)] * 2 + [(nx, 2 * B, nz)],
        scratch=[(far_y, 7 * B, nz), cells],
    )
    got = lax.all_to_all(msg, "px", 0, 0, tiled=True)
    whole = pltpu.HBM((3, *cells), F32)
    elec, magn = call(
        second_yz_kernel,
        [ends_c, g_c, u_y, v_y, flux_y, part_x, rise_y, w],
        [whole, whole],
        out_specs=[HBM] * 2,
        scratch=[cells] * 4 + [dma((4,))],
        flops=8_000_000,
    )
    ins = [pos, near_b, far_b, own_b, group_b, got, own_a, g2, u_x, v_x, flux2]
    at = len(ins)
    out = call(
        functools.partial(last_kernel, near_x, far_x),
        ins + [elec, magn],
        [whole] * 2,
        specs=[VMEM] * at + [HBM] * 2,
        out_specs=[HBM] * 2,
        scratch=[cells, cells, dma((2,))],
        aliases={at: 0, at + 1: 1},
    )
    return tuple(a.reshape(3, B, B, nz) for a in out)


def solution(mesh):
    placed = (P(None, "px", "py", None), P(None, "px", "py", None), P("px", "py", None), P(), P())
    return jax.shard_map(
        local,
        mesh=mesh,
        in_specs=placed,
        out_specs=(P(None, "px", "py", None), P(None, "px", "py", None)),
        check_vma=False,
    )
```

```python
import functools

import jax
import jax.numpy as jnp
from jax import lax
from jax.experimental import pallas as pl
from jax.experimental.pallas import tpu as pltpu
from jax.sharding import PartitionSpec as P

h = 32.0
B = 16
F32 = jnp.float32


def plane(i):
    return pl.ds(i * B, B)


def strided(j):
    return pl.ds(j, B, stride=B)


def lanes(v):
    return lax.broadcasted_iota(jnp.int32, v.shape, 1)


def behind_z(v):
    return v - jnp.where(lanes(v) == 0, 0.0, pltpu.roll(v, 1, 1))


def ahead_z(v):
    n = v.shape[1]
    return jnp.where(lanes(v) == n - 1, 0.0, pltpu.roll(v, n - 1, 1)) - v


def factor(w_of, first_block, p, u, v):
    d = None
    y = []
    for j in range(B):
        w = w_of(j)
        e = w + (jnp.where(first_block, 0.0, 1.0) if j == 0 else d)
        inv = 1.0 / (1.0 + e)
        d = e * inv
        p[plane(j)] = inv
        y.append(jnp.ones_like(inv) if j == 0 else y[-1] * last)
        last = inv
    uj = y[B - 1] * last
    vj = last
    u[plane(B - 1)] = uj
    v[plane(B - 1)] = vj
    for j in range(B - 2, -1, -1):
        inv = p[plane(j)]
        uj = inv * (y[j] + uj)
        vj = inv * vj
        u[plane(j)] = uj
        v[plane(j)] = vj


def eliminate(source_of, p, g):
    y = source_of(0)
    ys = [y]
    for j in range(1, B):
        y = source_of(j) + p[plane(j - 1)] * y
        ys.append(y)
    x = y * p[plane(B - 1)]
    end = x
    g[plane(B - 1)] = x
    for j in range(B - 2, -1, -1):
        x = p[plane(j)] * (ys[j] + x)
        g[plane(j)] = x
    return x, end


def boundary(me, rows, coefs, here, coef_here, outer):
    n = len(rows)
    left = [a for a, _ in outer]
    right = [b for _, b in outer]
    beta = delta = jnp.zeros_like(left[0])
    for s in range(n - 1):
        ff, fl, ll = coefs[s]
        t = fl / (1.0 - ff * beta)
        on = s < me
        left = [jnp.where(on, dl + t * (a + beta * gf), a) for a, (gf, dl) in zip(left, rows[s])]
        beta = jnp.where(on, ll + t * beta * fl, beta)
        m = n - 1 - s
        ff, fl, ll = coefs[m]
        t = fl / (1.0 - ll * delta)
        on = m > me
        right = [jnp.where(on, gf + t * (b + delta * dl), b) for b, (gf, dl) in zip(right, rows[m])]
        delta = jnp.where(on, ff + t * delta * fl, delta)
    ff, fl, ll = coef_here
    after_scale = 1.0 / (1.0 - delta * ll)
    t = fl * after_scale
    before_scale = 1.0 / (1.0 - beta * (ff + t * delta * fl))
    ends = []
    for a, b, (gf, dl) in zip(left, right, here):
        before = (a + beta * (gf + t * (b + delta * dl))) * before_scale
        ends.append((before, (b + delta * (dl + fl * before)) * after_scale))
    return ends


def merge(one, two):
    (ff1, fl1, ll1), rows1 = one
    (ff2, fl2, ll2), rows2 = two
    d = 1.0 / (1.0 - ll1 * ff2)
    t1, t2 = fl1 * d, fl2 * d
    rows = [
        (gf1 + t1 * (gf2 + ff2 * dl1), dl2 + t2 * (dl1 + ll1 * gf2))
        for (gf1, dl1), (gf2, dl2) in zip(rows1, rows2)
    ]
    return (ff1 + t1 * fl1 * ff2, t1 * fl2, ll2 + t2 * fl2 * ll1), rows


def solve_z(r, w):
    n = r.shape[1]
    lane = lanes(r)
    e = jnp.where(lane == n - 1, 0.0, 1.0)
    l = jnp.where(lane == 0, 0.0, 1.0)
    s = w + jnp.where(lane == n - 1, 1.0, 0.0)
    step = 1
    while step < n:
        inv = 1.0 / (s + (l + e))
        a, b = e * inv, l * inv
        r = r + (pltpu.roll(a * r, step, 1) + pltpu.roll(b * r, n - step, 1))
        s = s + (pltpu.roll(a * s, step, 1) + pltpu.roll(b * s, n - step, 1))
        g = a * l
        if 2 * step < n:
            e, l = pltpu.roll(g, n - step, 1), pltpu.roll(g, step, 1)
        step *= 2
    return r / s


def factors_kernel(w_in, a_out, b_out, scale):
    w = w_in[...]
    n = w.shape[1]
    lane = lanes(w)
    e = jnp.where(lane == n - 1, 0.0, 1.0)
    l = jnp.where(lane == 0, 0.0, 1.0)
    s = w + jnp.where(lane == n - 1, 1.0, 0.0)
    for k in range(a_out.shape[0]):
        step = 1 << k
        inv = 1.0 / (s + (l + e))
        a, b = e * inv, l * inv
        a_out[k] = a
        b_out[k] = b
        s = s + (pltpu.roll(a * s, step, 1) + pltpu.roll(b * s, n - step, 1))
        g = a * l
        e, l = pltpu.roll(g, n - step, 1), pltpu.roll(g, step, 1)
    scale[...] = 1.0 / s


def solve_factored(r, a, b, scale):
    n = r.shape[1]
    for k in range(a.shape[0]):
        step = 1 << k
        r = r + (pltpu.roll(a[k] * r, step, 1) + pltpu.roll(b[k] * r, n - step, 1))
    return r * scale[...]


def collect(r, order, own, others, got):
    refs = [own] + [others[order.index(s)] for s in range(1, len(order) + 1)]
    count = len(refs)
    blocks = [[] for _ in refs]
    for k in range(own.shape[0] // B):
        values = [ref[plane(k)] for ref in refs]
        bit = 1
        while bit < count:
            swap = lax.bitwise_and(r, bit) != 0
            values = [jnp.where(swap, values[m ^ bit], values[m]) for m in range(count)]
            bit *= 2
        for m, value in enumerate(values):
            got[m, plane(k)] = value
            blocks[m].append(value)
    return blocks


def rows_of(block, sources):
    return [(block[2 * k], block[2 * k + 1]) for k in range(sources)]


def stored(got, m, planes):
    return [got[m, plane(k)] for k in planes]


def loaded(msg, planes):
    return [msg[plane(k)] for k in planes]


def pick(values, index):
    out = values[0]
    for k in range(1, len(values)):
        out = jnp.where(index == k, values[k], out)
    return out


def place(pos, axis, near):
    here = pos[plane(axis)]
    return lax.shift_right_logical(here, near.bit_length() - 1), lax.bitwise_and(here, near - 1)


def cut_kernel(magn, hx_last, sem):
    load = pltpu.make_async_copy(magn.at[0, :, B - 1], hx_last, sem)
    load.start()
    load.wait()


def tables_kernel(
    me, eps_in, sig_in, material, elec_in, magn_in, w, c, p, u, v, flux, part, elec, magn, ez_first, pos, ids, eps, sig, sems
):
    loads = [(eps_in, eps), (sig_in, sig), (material, ids)]
    for field, to, k in ((elec_in, elec, 0), (magn_in, magn, 1), (elec_in, elec, 2), (magn_in, magn, 0)):
        loads.append((field.at[k], to.at[k]))
    loads += [(elec_in.at[1], elec.at[1]), (magn_in.at[2], magn.at[2])]
    loads = [pltpu.make_async_copy(a, b, sems.at[k]) for k, (a, b) in enumerate(loads)]
    for load in loads:
        load.start()
    for axis in range(2):
        pos[plane(axis)] = jnp.full((B, w.shape[1]), me[axis], jnp.int32)
    for load in loads[:3]:
        load.wait()
    ws = [eps[m] * (1.0 / (h * h)) + sig[m] * (0.5 / h) for m in range(eps.shape[0])]
    cs = [eps[m] * (1.0 / (h * h)) - sig[m] * (0.5 / h) for m in range(eps.shape[0])]
    for i in range(B):
        cell = ids[plane(i)]
        wi = jnp.full(cell.shape, ws[0], F32)
        ci = jnp.full(cell.shape, cs[0], F32)
        for m in range(1, len(ws)):
            wi = jnp.where(cell == m, ws[m], wi)
            ci = jnp.where(cell == m, cs[m], ci)
        w[plane(i)] = wi
        c[plane(i)] = ci
    factor(lambda i: w[plane(i)], me[0] == 0, p, u, v)
    for load in loads[3:7]:
        load.wait()
    row = lax.broadcasted_iota(jnp.int32, (B, w.shape[1]), 0)
    for i in range(B):
        q = magn[1, plane(i)] * (1.0 / h) - ahead_z(elec[0, plane(i)])
        flux[plane(i)] = q
        if i > 0:
            q = q - flux[plane(i - 1)]
        here = magn[0, plane(i)]
        before = jnp.where(row == 0, 0.0, pltpu.roll(here, 1, 0))
        part[plane(i)] = c[plane(i)] * elec[2, plane(i)] + (q - (here - before) * (1.0 / h))
    for k in range(ez_first.shape[0] // B):
        ez_first[plane(k)] = elec.at[2][strided(0)]
    for load in loads[7:]:
        load.wait()


def first_x_kernel(pos, part, hx_prev, flux, p, u, v, elec, magn, g, msg):
    row = lax.broadcasted_iota(jnp.int32, hx_prev.shape, 0)
    scale = jnp.where(pos[plane(1)] == 0, 0.0, jnp.where(row == 0, 1.0 / h, 0.0))

    def source(i):
        return part[plane(i)] + hx_prev[pl.ds(i, 1)] * scale

    first, last = eliminate(source, p, g)
    msg[plane(0)] = first
    msg[plane(1)] = last - flux[plane(B - 1)]
    msg[plane(2)] = u[plane(0)]
    msg[plane(3)] = v[plane(0)]
    msg[plane(4)] = v[plane(B - 1)]
    msg[plane(5)] = elec[1, plane(0)]
    msg[plane(6)] = magn[2, plane(B - 1)]


def merged(blocks):
    while len(blocks) > 1:
        blocks = [merge(a, b) for a, b in zip(blocks[::2], blocks[1::2])]
    return blocks[0]


def merge_kernel(axis, near, order, sources, halos, pos, *refs):
    got, msg = refs[-2:]
    blocks = collect(place(pos, axis, near)[1], order, refs[0], refs[1:near], got)
    at = 2 * sources
    coefs, rows = merged([(b[at : at + 3], rows_of(b, sources)) for b in blocks])
    for k, value in enumerate([v for pair in rows for v in pair] + list(coefs)):
        msg[plane(k)] = value
    if halos:
        msg[plane(5)] = blocks[0][5]
        msg[plane(6)] = blocks[-1][6]


def merge_rows_kernel(axis, near, order, pos, coefs, *refs):
    got, msg = refs[-2:]
    blocks = collect(place(pos, axis, near)[1], order, refs[0], refs[1:near], got)
    _, rows = merged([(stored(coefs, m, (2, 3, 4)), rows_of(b, 1)) for m, b in enumerate(blocks)])
    msg[plane(0)], msg[plane(1)] = rows[0]


def solved_ends(q, r, sources, near_rows, near_coefs, far_rows, far_coefs, own_near, own_far):
    zero = jnp.zeros_like(far_coefs[0][0])
    outer = boundary(q, far_rows, far_coefs, *own_far, [(zero, zero)] * sources)
    return boundary(r, near_rows, near_coefs, *own_near, outer)


def first_z_kernel(n, pos, ef, mf, ez_next, w, c, p, u, v, r_top, src_top, curl, flux_y, flux_a, part_a, src, r):
    factor(lambda j: w[strided(j)], pos[plane(1)] == 0, p, u, v)
    inside = jnp.where(pos[pl.ds(B, 1)] == n - 1, 0.0, 1.0)
    row = lax.broadcasted_iota(jnp.int32, (B, w.shape[1]), 0)
    for i in range(B):
        ez = ef[2, plane(i)]
        after = jnp.where(row == B - 1, ez_next[pl.ds(i, 1)] * inside, pltpu.roll(ez, B - 1, 0))
        ri = mf[0, plane(i)] * (1.0 / h) - (after - ez)
        r[plane(i)] = ri
        gain = mf[2, plane(i)]
        if i > 0:
            gain = gain - mf[2, plane(i - 1)]
        src[plane(i)] = c[plane(i)] * ef[1, plane(i)] + (behind_z(ri) - gain * (1.0 / h))
        part_a[plane(i)] = c[plane(i)] * ef[0, plane(i)] - behind_z(mf[1, plane(i)]) * (1.0 / h)
        if i < B - 1:
            rise = ef[1, plane(i + 1)] - ef[1, plane(i)]
            flux_a[plane(i)] = mf[2, plane(i)] * (1.0 / h) - rise
    flux_a[plane(B - 1)] = mf[2, plane(B - 1)] * (1.0 / h) + ef[1, plane(B - 1)]
    r_top[...] = r[plane(0)]
    src_top[...] = src[plane(0)]
    x = solve_z(src[...], w[...])
    rise = ahead_z(x)
    mx = r[...] + rise
    curl[...] = c[...] * x + behind_z(mx)
    flux_y[...] = -(mx + rise)


def both_y_kernel(near, far, order, pos, got_near, own_near, *refs):
    others, refs = refs[:far], refs[far:]
    (g_b, u_x, v_x, flux_b, w, c, r_top, src_top, curl_in, flux_y_in, flux_a_in, part_a, p_y, u_y, v_y) = refs[:15]
    got_far, rise_y, curl, flux_y, flux_a, g_a, g_c, msg, part, fz = refs[15:]
    top = plane(0)
    q, r = place(pos, 0, near)
    far_blocks = collect(q, order, others[0], others[1:], got_far)
    near_blocks = [stored(got_near, m, range(7)) for m in range(near)]
    after_group = jnp.where(q < far - 1, pick([b[5] for b in far_blocks], q + 1), 0.0)
    ey_next = jnp.where(r < near - 1, pick([b[5] for b in near_blocks], r + 1), after_group)
    before_group = jnp.where(q > 0, pick([b[6] for b in far_blocks], q - 1), 0.0)
    hz_prev = jnp.where(r > 0, pick([b[6] for b in near_blocks], r - 1), before_group)
    curl[...] = curl_in[...]
    flux_y[...] = flux_y_in[...]
    flux_a[...] = flux_a_in[...]

    x = solve_z(src_top[...] + hz_prev * (1.0 / h), w[top])
    rise = ahead_z(x)
    mx = r_top[...] + rise
    curl[top] = c[top] * x + behind_z(mx)
    flux_y[top] = -(mx + rise)

    flux_a[plane(B - 1)] = flux_a[plane(B - 1)] - ey_next

    def source_a(j):
        f = flux_a[strided(j)]
        if j > 0:
            f = f - flux_a[strided(j - 1)]
        return part_a[strided(j)] + f

    first_a, last_a = eliminate(source_a, p_y, g_a)
    last_a = last_a - flux_a[strided(B - 1)]

    own, own_group = loaded(own_near, range(5)), loaded(others[0], range(5))
    ((before, after),) = solved_ends(
        q,
        r,
        1,
        [rows_of(b, 1) for b in near_blocks],
        [b[2:5] for b in near_blocks],
        [rows_of(b, 1) for b in far_blocks],
        [b[2:5] for b in far_blocks],
        (rows_of(own, 1), own[2:5]),
        (rows_of(own_group, 1), own_group[2:5]),
    )
    for i in range(B):
        fz[plane(i)] = g_b[plane(i)] + (u_x[plane(i)] * before + v_x[plane(i)] * after)
    my_before = jnp.where(pos[plane(0)] == 0, 0.0, fz[top] - before)
    for i in range(B):
        here = fz[plane(i)]
        rise = (fz[plane(i + 1)] if i < B - 1 else after) - here
        my = flux_b[plane(i)] + rise
        rise_y[plane(i)] = my + rise
        part[plane(i)] = c[plane(i)] * here + (my - my_before)
        my_before = my

    def source_c(j):
        f = flux_y[strided(j)]
        if j > 0:
            f = f - flux_y[strided(j - 1)]
        return part[strided(j)] + f

    first_c, last_c = eliminate(source_c, p_y, g_c)
    last_c = last_c - flux_y[strided(B - 1)]
    sent = [first_a, last_a, first_c, last_c, u_y[plane(0)], v_y[plane(0)], v_y[plane(B - 1)]]
    for k, value in enumerate(sent):
        msg[plane(k)] = value


def second_x_kernel(near, far, order, pos, got_near, own_near, *refs):
    others, refs = refs[:far], refs[far:]
    g_a, u, v, flux_a, c, curl, p_x, part, flux2, g2, ends_c, msg, got_far, fx = refs
    q, r = place(pos, 1, near)
    far_blocks = collect(q, order, others[0], others[1:], got_far)
    near_blocks = [stored(got_near, m, range(7)) for m in range(near)]
    own, own_group = loaded(own_near, range(7)), loaded(others[0], range(7))
    (before, after), (before_c, after_c) = solved_ends(
        q,
        r,
        2,
        [rows_of(b, 2) for b in near_blocks],
        [b[4:7] for b in near_blocks],
        [rows_of(b, 2) for b in far_blocks],
        [b[4:7] for b in far_blocks],
        (rows_of(own, 2), own[4:7]),
        (rows_of(own_group, 2), own_group[4:7]),
    )
    ends_c[plane(0)] = before_c
    ends_c[plane(1)] = after_c
    for j in range(B):
        fx[plane(j)] = g_a[plane(j)] + (u[plane(j)] * before + v[plane(j)] * after)
    mz_before = jnp.where(pos[plane(1)] == 0, 0.0, fx[plane(0)] - before)
    for j in range(B):
        here = fx[plane(j)]
        rise = (fx[plane(j + 1)] if j < B - 1 else after) - here
        mz = flux_a[strided(j)] + rise
        part[strided(j)] = c[strided(j)] * here + (mz - mz_before)
        flux2[strided(j)] = -(mz + rise)
        mz_before = mz

    def source(i):
        f = flux2[plane(i)]
        if i > 0:
            f = f - flux2[plane(i - 1)]
        return curl[plane(i)] + f

    first, last = eliminate(source, p_x, g2)
    msg[plane(0)] = first
    msg[plane(1)] = last - flux2[plane(B - 1)]


def second_y_kernel(ends_c, g_c, u, v, flux_y, elec, magn, full_z, new_x, sems):
    stores = [(full_z, elec.at[2]), (new_x, magn.at[0])]
    stores = [pltpu.make_async_copy(a, b, sems.at[k]) for k, (a, b) in enumerate(stores)]
    before, after = ends_c[plane(0)], ends_c[plane(1)]
    here = None
    for j in range(B):
        ahead = g_c[plane(j)] + (u[plane(j)] * before + v[plane(j)] * after)
        full_z[strided(j)] = ahead
        if j > 0:
            new_x[strided(j - 1)] = -h * (flux_y[strided(j - 1)] + (ahead - here))
        here = ahead
    new_x[strided(B - 1)] = -h * (flux_y[strided(B - 1)] + (after - here))
    for store in stores:
        store.start()
    for store in stores:
        store.wait()


def second_z_kernel(part, rise_y, z_a, z_b, z_scale, _, __, elec, magn, full_x, new_y, sems):
    stores = [(full_x, elec.at[0]), (new_y, magn.at[1])]
    stores = [pltpu.make_async_copy(a, b, sems.at[k]) for k, (a, b) in enumerate(stores)]
    a = rise_y[...]
    x = solve_factored(part[...] - behind_z(a), z_a, z_b, z_scale)
    full_x[...] = x
    stores[0].start()
    new_y[...] = h * (a - ahead_z(x))
    stores[1].start()
    for store in stores:
        store.wait()


def last_kernel(near, far, order, pos, coefs_near, coefs_far, own_b, group_b, got_near, own_near, *refs):
    others, refs = refs[:far], refs[far:]
    g, u, v, flux2, _, _, elec, magn, got_far, full_y, new_z, sems = refs
    q, r = place(pos, 0, near)
    far_blocks = collect(q, order, others[0], others[1:], got_far)
    ((before, after),) = solved_ends(
        q,
        r,
        1,
        [rows_of(stored(got_near, m, range(2)), 1) for m in range(near)],
        [stored(coefs_near, m, (2, 3, 4)) for m in range(near)],
        [rows_of(b, 1) for b in far_blocks],
        [stored(coefs_far, m, (2, 3, 4)) for m in range(far)],
        (rows_of(loaded(own_near, range(2)), 1), loaded(own_b, (2, 3, 4))),
        (rows_of(loaded(others[0], range(2)), 1), loaded(group_b, (2, 3, 4))),
    )
    stores = [(full_y, elec.at[1]), (new_z, magn.at[2])]
    stores = [pltpu.make_async_copy(a, b, sems.at[k]) for k, (a, b) in enumerate(stores)]
    for i in range(B):
        full_y[plane(i)] = g[plane(i)] + (u[plane(i)] * before + v[plane(i)] * after)
    stores[0].start()
    for i in range(B):
        rise = (full_y[plane(i + 1)] if i < B - 1 else after) - full_y[plane(i)]
        new_z[plane(i)] = -h * (flux2[plane(i)] + rise)
    stores[1].start()
    for store in stores:
        store.wait()


VMEM = pl.BlockSpec(memory_space=pltpu.VMEM)
SMEM = pl.BlockSpec(memory_space=pltpu.SMEM)
HBM = pl.BlockSpec(memory_space=pltpu.HBM)


def call(kernel, ins, outs, specs=None, out_specs=None, scratch=(), aliases=None, flops=1_000_000):
    shapes = [jax.ShapeDtypeStruct(s, F32) if isinstance(s, tuple) else s for s in outs]
    return pl.pallas_call(
        kernel,
        out_shape=shapes,
        in_specs=specs or [VMEM] * len(ins),
        out_specs=out_specs or [VMEM] * len(outs),
        scratch_shapes=[pltpu.VMEM(s, F32) if isinstance(s, tuple) else s for s in scratch],
        input_output_aliases=aliases or {},
        compiler_params=pltpu.CompilerParams(vmem_limit_bytes=24 * 1024 * 1024),
        cost_estimate=pl.CostEstimate(flops=flops, bytes_accessed=1_000_000, transcendentals=0),
    )(*ins)


def shared(value, axis, n, order, near=1, bent=()):
    masks = [near * s + (near // 2 if s in bent else 0) for s in order]
    return [value] + [lax.ppermute(value, axis, [(i, i ^ mask) for i in range(n)]) for mask in masks]


def split(n):
    near = 1 << (n.bit_length() // 2)
    return near, n // near


def local(electric, magnetic, material, permittivity, conductivity):
    nx, ny = lax.axis_size("px"), lax.axis_size("py")
    near_x, far_x = split(nx)
    near_y, far_y = split(ny)
    nz = material.shape[2]
    cells = (B * B, nz)
    me = jnp.stack([lax.axis_index("px"), lax.axis_index("py")]).astype(jnp.int32)
    in_hbm = lambda a: pltpu.with_memory_space_constraint(a, pltpu.HBM)
    elec = in_hbm(electric.reshape(3, *cells))
    magn = in_hbm(magnetic.reshape(3, *cells))
    ids = in_hbm(material.reshape(cells))
    dma = pltpu.SemaphoreType.DMA
    orders = [(1, 2, 3), (2, 1, 3), (2, 1, 3), (1, 3, 2)]
    counts = (near_x, far_x, near_y, far_y)
    px_near, px_far, py_near, py_far = [
        tuple(s for s in order if s < count) for order, count in zip(orders, counts)
    ]

    (hx_last,) = call(
        cut_kernel, [in_hbm(magnetic)], [(B, nz)], specs=[HBM], scratch=[dma(())], flops=1000
    )
    hx_prev = lax.ppermute(hx_last, "py", [(i, (i + 1) % ny) for i in range(ny)])
    w, c, p_x, u_x, v_x, flux_b, part_b, ef, mf, ez_first, pos = call(
        tables_kernel,
        [me, in_hbm(permittivity), in_hbm(conductivity), ids, elec, magn],
        [cells] * 7 + [(3, *cells)] * 2 + [(8 * B, nz), jax.ShapeDtypeStruct((2 * B, nz), jnp.int32)],
        specs=[SMEM] + [HBM] * 5,
        scratch=[pltpu.VMEM(cells, jnp.int32)] + [pltpu.SMEM(permittivity.shape, F32)] * 2 + [dma((9,))],
    )
    g_b, own_b = call(
        first_x_kernel,
        [pos, part_b, hx_prev, flux_b, p_x, u_x, v_x, ef, mf],
        [cells, (7 * B, nz)],
    )
    ins = shared(own_b, "px", nx, px_near)
    ez_next = lax.ppermute(ez_first, "py", [((i + 1) % ny, i) for i in range(ny)])
    near_b, group_b = call(
        functools.partial(merge_kernel, 0, near_x, px_near, 1, True),
        [pos] + ins,
        [(near_x, 7 * B, nz), (7 * B, nz)],
    )
    ins = shared(group_b, "px", nx, px_far, near_x, (1, 3))
    p_y, u_y, v_y, r_top, src_top, curl, flux_y, flux_a, part_a = call(
        functools.partial(first_z_kernel, ny),
        [pos, ef, mf, ez_next, w, c],
        [cells] * 3 + [(B, nz)] * 2 + [cells] * 4,
        scratch=[cells] * 2,
        flops=8_000_000,
    )
    ins = [pos, near_b, own_b] + ins + [g_b, u_x, v_x, flux_b, w, c, r_top, src_top]
    far_b, rise_y, curl, flux_y, flux_a, g_a, g_c, own_ac = call(
        functools.partial(both_y_kernel, near_x, far_x, px_far),
        ins + [curl, flux_y, flux_a, part_a, p_y, u_y, v_y],
        [(far_x, 7 * B, nz)] + [cells] * 6 + [(7 * B, nz)],
        scratch=[cells] * 2,
    )
    ins = shared(own_ac, "py", ny, py_near)
    near_ac, msg = call(
        functools.partial(merge_kernel, 1, near_y, py_near, 2, False), [pos] + ins, [(near_y, 7 * B, nz), (7 * B, nz)]
    )
    msg, w = lax.optimization_barrier((msg, w))
    ins = shared(msg, "py", ny, py_far, near_y, (2,))
    steps = (nz - 1).bit_length()
    z_factors = call(factors_kernel, [w], [(steps, *cells)] * 2 + [cells], flops=8_000_000)
    ins, z_factors = lax.optimization_barrier((ins, z_factors))
    part_x, flux2, g2, ends_c, own_a = call(
        functools.partial(second_x_kernel, near_y, far_y, py_far),
        [pos, near_ac, own_ac] + ins + [g_a, u_y, v_y, flux_a, c, curl, p_x],
        [cells] * 3 + [(2 * B, nz)] * 2,
        scratch=[(far_y, 7 * B, nz), cells],
    )
    ins = shared(own_a, "px", nx, px_near)
    whole = pltpu.HBM((3, *cells), F32)
    elec, magn = call(
        second_y_kernel,
        [ends_c, g_c, u_y, v_y, flux_y],
        [whole, whole],
        out_specs=[HBM] * 2,
        scratch=[cells] * 2 + [dma((2,))],
    )
    near_a, msg = call(
        functools.partial(merge_rows_kernel, 0, near_x, px_near),
        [pos, near_b] + ins,
        [(near_x, 2 * B, nz), (2 * B, nz)],
    )
    msg, elec = lax.optimization_barrier((msg, elec))
    ins = shared(msg, "px", nx, px_far, near_x, (1, 3))
    elec, magn = call(
        second_z_kernel,
        [part_x, rise_y, *z_factors, elec, magn],
        [whole] * 2,
        specs=[VMEM] * 5 + [HBM] * 2,
        out_specs=[HBM] * 2,
        scratch=[cells] * 2 + [dma((2,))],
        aliases={5: 0, 6: 1},
        flops=4_000_000,
    )
    ins = [pos, near_b, far_b, own_b, group_b, near_a, own_a] + ins + [g2, u_x, v_x, flux2]
    at = len(ins)
    out = call(
        functools.partial(last_kernel, near_x, far_x, px_far),
        ins + [elec, magn],
        [whole] * 2,
        specs=[VMEM] * at + [HBM] * 2,
        out_specs=[HBM] * 2,
        scratch=[(far_x, 2 * B, nz), cells, cells, dma((2,))],
        aliases={at: 0, at + 1: 1},
    )
    return tuple(a.reshape(3, B, B, nz) for a in out)


def solution(mesh):
    placed = (P(None, "px", "py", None), P(None, "px", "py", None), P("px", "py", None), P(), P())
    return jax.shard_map(
        local,
        mesh=mesh,
        in_specs=placed,
        out_specs=(P(None, "px", "py", None), P(None, "px", "py", None)),
        check_vma=False,
    )
```

```python
import functools

import jax
import jax.numpy as jnp
from jax import lax
from jax.experimental import pallas as pl
from jax.experimental.pallas import tpu as pltpu
from jax.sharding import PartitionSpec as P

h = 32.0
B = 16
F32 = jnp.float32


def plane(i):
    return pl.ds(i * B, B)


def strided(j):
    return pl.ds(j, B, stride=B)


def lanes(v):
    return lax.broadcasted_iota(jnp.int32, v.shape, 1)


def behind_z(v):
    return v - jnp.where(lanes(v) == 0, 0.0, pltpu.roll(v, 1, 1))


def ahead_z(v):
    n = v.shape[1]
    return jnp.where(lanes(v) == n - 1, 0.0, pltpu.roll(v, n - 1, 1)) - v


def factor(w_of, first_block, p, u, v):
    d = None
    y = []
    for j in range(B):
        w = w_of(j)
        e = w + (jnp.where(first_block, 0.0, 1.0) if j == 0 else d)
        inv = 1.0 / (1.0 + e)
        d = e * inv
        p[plane(j)] = inv
        y.append(jnp.ones_like(inv) if j == 0 else y[-1] * last)
        last = inv
    uj = y[B - 1] * last
    vj = last
    u[plane(B - 1)] = uj
    v[plane(B - 1)] = vj
    for j in range(B - 2, -1, -1):
        inv = p[plane(j)]
        uj = inv * (y[j] + uj)
        vj = inv * vj
        u[plane(j)] = uj
        v[plane(j)] = vj


def eliminate(source_of, p, g):
    y = source_of(0)
    ys = [y]
    for j in range(1, B):
        y = source_of(j) + p[plane(j - 1)] * y
        ys.append(y)
    x = y * p[plane(B - 1)]
    end = x
    g[plane(B - 1)] = x
    for j in range(B - 2, -1, -1):
        x = p[plane(j)] * (ys[j] + x)
        g[plane(j)] = x
    return x, end


def boundary(me, rows, coefs, here, coef_here, outer):
    n = len(rows)
    left = [a for a, _ in outer]
    right = [b for _, b in outer]
    beta = delta = jnp.zeros_like(left[0])
    for s in range(n - 1):
        ff, fl, ll = coefs[s]
        t = fl / (1.0 - ff * beta)
        on = s < me
        left = [jnp.where(on, dl + t * (a + beta * gf), a) for a, (gf, dl) in zip(left, rows[s])]
        beta = jnp.where(on, ll + t * beta * fl, beta)
        m = n - 1 - s
        ff, fl, ll = coefs[m]
        t = fl / (1.0 - ll * delta)
        on = m > me
        right = [jnp.where(on, gf + t * (b + delta * dl), b) for b, (gf, dl) in zip(right, rows[m])]
        delta = jnp.where(on, ff + t * delta * fl, delta)
    ff, fl, ll = coef_here
    after_scale = 1.0 / (1.0 - delta * ll)
    t = fl * after_scale
    before_scale = 1.0 / (1.0 - beta * (ff + t * delta * fl))
    ends = []
    for a, b, (gf, dl) in zip(left, right, here):
        before = (a + beta * (gf + t * (b + delta * dl))) * before_scale
        ends.append((before, (b + delta * (dl + fl * before)) * after_scale))
    return ends


def merge(one, two):
    (ff1, fl1, ll1), rows1 = one
    (ff2, fl2, ll2), rows2 = two
    d = 1.0 / (1.0 - ll1 * ff2)
    t1, t2 = fl1 * d, fl2 * d
    rows = [
        (gf1 + t1 * (gf2 + ff2 * dl1), dl2 + t2 * (dl1 + ll1 * gf2))
        for (gf1, dl1), (gf2, dl2) in zip(rows1, rows2)
    ]
    return (ff1 + t1 * fl1 * ff2, t1 * fl2, ll2 + t2 * fl2 * ll1), rows


def solve_z(r, w):
    n = r.shape[1]
    lane = lanes(r)
    e = jnp.where(lane == n - 1, 0.0, 1.0)
    l = jnp.where(lane == 0, 0.0, 1.0)
    s = w + jnp.where(lane == n - 1, 1.0, 0.0)
    step = 1
    while step < n:
        inv = 1.0 / (s + (l + e))
        a, b = e * inv, l * inv
        r = r + (pltpu.roll(a * r, step, 1) + pltpu.roll(b * r, n - step, 1))
        s = s + (pltpu.roll(a * s, step, 1) + pltpu.roll(b * s, n - step, 1))
        g = a * l
        if 2 * step < n:
            e, l = pltpu.roll(g, n - step, 1), pltpu.roll(g, step, 1)
        step *= 2
    return r / s


def factors_kernel(w_in, a_out, b_out, scale):
    w = w_in[...]
    n = w.shape[1]
    lane = lanes(w)
    e = jnp.where(lane == n - 1, 0.0, 1.0)
    l = jnp.where(lane == 0, 0.0, 1.0)
    s = w + jnp.where(lane == n - 1, 1.0, 0.0)
    for k in range(a_out.shape[0]):
        step = 1 << k
        inv = 1.0 / (s + (l + e))
        a, b = e * inv, l * inv
        a_out[k] = a
        b_out[k] = b
        s = s + (pltpu.roll(a * s, step, 1) + pltpu.roll(b * s, n - step, 1))
        g = a * l
        e, l = pltpu.roll(g, n - step, 1), pltpu.roll(g, step, 1)
    scale[...] = 1.0 / s


def solve_factored(r, a, b, scale):
    n = r.shape[1]
    for k in range(a.shape[0]):
        step = 1 << k
        r = r + (pltpu.roll(a[k] * r, step, 1) + pltpu.roll(b[k] * r, n - step, 1))
    return r * scale[...]


def collect(r, order, own, others, got):
    refs = [own] + [others[order.index(s)] for s in range(1, len(order) + 1)]
    return ordered(r, [loaded(ref, range(ref.shape[0] // B)) for ref in refs], got)


def ordered(r, found, got):
    count = len(found)
    blocks = [[] for _ in found]
    for k in range(len(found[0])):
        values = [planes[k] for planes in found]
        bit = 1
        while bit < count:
            swap = lax.bitwise_and(r, bit) != 0
            values = [jnp.where(swap, values[m ^ bit], values[m]) for m in range(count)]
            bit *= 2
        for m, value in enumerate(values):
            got[m, plane(k)] = value
            blocks[m].append(value)
    return blocks


def rows_of(block, sources):
    return [(block[2 * k], block[2 * k + 1]) for k in range(sources)]


def stored(got, m, planes):
    return [got[m, plane(k)] for k in planes]


def loaded(msg, planes):
    return [msg[plane(k)] for k in planes]


def pick(values, index):
    out = values[0]
    for k in range(1, len(values)):
        out = jnp.where(index == k, values[k], out)
    return out


def place(pos, axis, near):
    here = pos[plane(axis)]
    return lax.shift_right_logical(here, near.bit_length() - 1), lax.bitwise_and(here, near - 1)


def cut_kernel(elec, magn, hx_last, ez_first, sems):
    loads = [(magn.at[0, :, B - 1], hx_last), (elec.at[2, :, 0], ez_first)]
    loads = [pltpu.make_async_copy(a, b, sems.at[k]) for k, (a, b) in enumerate(loads)]
    for load in loads:
        load.start()
    for load in loads:
        load.wait()


def tables_kernel(
    me, eps_in, sig_in, material, elec_in, magn_in, w, c, p, u, v, flux, part, elec, magn, pos, early, ids, eps, sig, sems
):
    loads = [(eps_in, eps), (sig_in, sig), (material, ids)]
    for field, to, k in ((elec_in, elec, 0), (magn_in, magn, 1), (elec_in, elec, 2), (magn_in, magn, 0)):
        loads.append((field.at[k], to.at[k]))
    loads += [(elec_in.at[1], elec.at[1]), (magn_in.at[2], magn.at[2])]
    loads = [pltpu.make_async_copy(a, b, sems.at[k]) for k, (a, b) in enumerate(loads)]
    for load in loads:
        load.start()
    for axis in range(2):
        pos[plane(axis)] = jnp.full((B, w.shape[1]), me[axis], jnp.int32)
    for load in loads[:3]:
        load.wait()
    ws = [eps[m] * (1.0 / (h * h)) + sig[m] * (0.5 / h) for m in range(eps.shape[0])]
    cs = [eps[m] * (1.0 / (h * h)) - sig[m] * (0.5 / h) for m in range(eps.shape[0])]
    for i in range(B):
        cell = ids[plane(i)]
        wi = jnp.full(cell.shape, ws[0], F32)
        ci = jnp.full(cell.shape, cs[0], F32)
        for m in range(1, len(ws)):
            wi = jnp.where(cell == m, ws[m], wi)
            ci = jnp.where(cell == m, cs[m], ci)
        w[plane(i)] = wi
        c[plane(i)] = ci
    factor(lambda i: w[plane(i)], me[0] == 0, p, u, v)
    for load in loads[3:7]:
        load.wait()
    row = lax.broadcasted_iota(jnp.int32, (B, w.shape[1]), 0)
    for i in range(B):
        q = magn[1, plane(i)] * (1.0 / h) - ahead_z(elec[0, plane(i)])
        flux[plane(i)] = q
        if i > 0:
            q = q - flux[plane(i - 1)]
        here = magn[0, plane(i)]
        before = jnp.where(row == 0, 0.0, pltpu.roll(here, 1, 0))
        part[plane(i)] = c[plane(i)] * elec[2, plane(i)] + (q - (here - before) * (1.0 / h))
    for load in loads[7:]:
        load.wait()
    sent = [u[plane(0)], v[plane(0)], v[plane(B - 1)], elec[1, plane(0)], magn[2, plane(B - 1)]]
    for k in range(early.shape[0] // B):
        early[plane(k)] = sent[min(k, 4)]


def first_x_kernel(pos, part, hx_prev, flux, p, early, g, own, ends):
    row = lax.broadcasted_iota(jnp.int32, hx_prev.shape, 0)
    scale = jnp.where(pos[plane(1)] == 0, 0.0, jnp.where(row == 0, 1.0 / h, 0.0))

    def source(i):
        return part[plane(i)] + hx_prev[pl.ds(i, 1)] * scale

    first, last = eliminate(source, p, g)
    ends[plane(0)] = first
    ends[plane(1)] = last - flux[plane(B - 1)]
    own[pl.ds(0, 2 * B)] = ends[...]
    own[pl.ds(2 * B, 5 * B)] = early[pl.ds(0, 5 * B)]


def merged(blocks):
    while len(blocks) > 1:
        blocks = [merge(a, b) for a, b in zip(blocks[::2], blocks[1::2])]
    return blocks[0]


def merge_kernel(axis, near, order, sources, pos, *refs):
    got, msg = refs[-2:]
    blocks = collect(place(pos, axis, near)[1], order, refs[0], refs[1:near], got)
    at = 2 * sources
    coefs, rows = merged([(b[at : at + 3], rows_of(b, sources)) for b in blocks])
    for k, value in enumerate([v for pair in rows for v in pair] + list(coefs)):
        msg[plane(k)] = value


def merge_first_kernel(near, pos, own, *refs):
    got, msg = refs[-2:]
    early, nearest, ends = refs[: near - 2], refs[near - 2], refs[near - 1 : -2]
    found = [loaded(own, range(7)), loaded(nearest, range(7))]
    found += [loaded(a, range(2)) + loaded(b, range(5)) for a, b in zip(ends, early)]
    blocks = ordered(place(pos, 0, near)[1], found, got)
    coefs, rows = merged([(b[2:5], rows_of(b, 1)) for b in blocks])
    for k, value in enumerate([*rows[0], *coefs, blocks[0][5], blocks[-1][6]]):
        msg[plane(k)] = value


def merge_rows_kernel(axis, near, order, pos, coefs, *refs):
    got, msg = refs[-2:]
    blocks = collect(place(pos, axis, near)[1], order, refs[0], refs[1:near], got)
    _, rows = merged([(stored(coefs, m, (2, 3, 4)), rows_of(b, 1)) for m, b in enumerate(blocks)])
    msg[plane(0)], msg[plane(1)] = rows[0]


def solved_ends(q, r, sources, near_rows, near_coefs, far_rows, far_coefs, own_near, own_far):
    zero = jnp.zeros_like(far_coefs[0][0])
    outer = boundary(q, far_rows, far_coefs, *own_far, [(zero, zero)] * sources)
    return boundary(r, near_rows, near_coefs, *own_near, outer)


def first_z_kernel(n, pos, ef, mf, ez_next, w, c, p, u, v, r_top, src_top, curl, flux_y, flux_a, part_a, src, r):
    factor(lambda j: w[strided(j)], pos[plane(1)] == 0, p, u, v)
    inside = jnp.where(pos[pl.ds(B, 1)] == n - 1, 0.0, 1.0)
    row = lax.broadcasted_iota(jnp.int32, (B, w.shape[1]), 0)
    for i in range(B):
        ez = ef[2, plane(i)]
        after = jnp.where(row == B - 1, ez_next[pl.ds(i, 1)] * inside, pltpu.roll(ez, B - 1, 0))
        ri = mf[0, plane(i)] * (1.0 / h) - (after - ez)
        r[plane(i)] = ri
        gain = mf[2, plane(i)]
        if i > 0:
            gain = gain - mf[2, plane(i - 1)]
        src[plane(i)] = c[plane(i)] * ef[1, plane(i)] + (behind_z(ri) - gain * (1.0 / h))
        part_a[plane(i)] = c[plane(i)] * ef[0, plane(i)] - behind_z(mf[1, plane(i)]) * (1.0 / h)
        if i < B - 1:
            rise = ef[1, plane(i + 1)] - ef[1, plane(i)]
            flux_a[plane(i)] = mf[2, plane(i)] * (1.0 / h) - rise
    flux_a[plane(B - 1)] = mf[2, plane(B - 1)] * (1.0 / h) + ef[1, plane(B - 1)]
    r_top[...] = r[plane(0)]
    src_top[...] = src[plane(0)]
    x = solve_z(src[...], w[...])
    rise = ahead_z(x)
    mx = r[...] + rise
    curl[...] = c[...] * x + behind_z(mx)
    flux_y[...] = -(mx + rise)


def both_y_kernel(near, far, order, pos, got_near, own_near, *refs):
    others, refs = refs[:far], refs[far:]
    (g_b, u_x, v_x, flux_b, w, c, r_top, src_top, curl_in, flux_y_in, flux_a_in, part_a, p_y, u_y, v_y) = refs[:15]
    got_far, rise_y, curl, flux_y, flux_a, g_a, g_c, msg, part, fz = refs[15:]
    top = plane(0)
    q, r = place(pos, 0, near)
    far_blocks = collect(q, order, others[0], others[1:], got_far)
    near_blocks = [stored(got_near, m, range(7)) for m in range(near)]
    after_group = jnp.where(q < far - 1, pick([b[5] for b in far_blocks], q + 1), 0.0)
    ey_next = jnp.where(r < near - 1, pick([b[5] for b in near_blocks], r + 1), after_group)
    before_group = jnp.where(q > 0, pick([b[6] for b in far_blocks], q - 1), 0.0)
    hz_prev = jnp.where(r > 0, pick([b[6] for b in near_blocks], r - 1), before_group)
    curl[...] = curl_in[...]
    flux_y[...] = flux_y_in[...]
    flux_a[...] = flux_a_in[...]

    x = solve_z(src_top[...] + hz_prev * (1.0 / h), w[top])
    rise = ahead_z(x)
    mx = r_top[...] + rise
    curl[top] = c[top] * x + behind_z(mx)
    flux_y[top] = -(mx + rise)

    flux_a[plane(B - 1)] = flux_a[plane(B - 1)] - ey_next

    def source_a(j):
        f = flux_a[strided(j)]
        if j > 0:
            f = f - flux_a[strided(j - 1)]
        return part_a[strided(j)] + f

    first_a, last_a = eliminate(source_a, p_y, g_a)
    last_a = last_a - flux_a[strided(B - 1)]

    own, own_group = loaded(own_near, range(5)), loaded(others[0], range(5))
    ((before, after),) = solved_ends(
        q,
        r,
        1,
        [rows_of(b, 1) for b in near_blocks],
        [b[2:5] for b in near_blocks],
        [rows_of(b, 1) for b in far_blocks],
        [b[2:5] for b in far_blocks],
        (rows_of(own, 1), own[2:5]),
        (rows_of(own_group, 1), own_group[2:5]),
    )
    for i in range(B):
        fz[plane(i)] = g_b[plane(i)] + (u_x[plane(i)] * before + v_x[plane(i)] * after)
    my_before = jnp.where(pos[plane(0)] == 0, 0.0, fz[top] - before)
    for i in range(B):
        here = fz[plane(i)]
        rise = (fz[plane(i + 1)] if i < B - 1 else after) - here
        my = flux_b[plane(i)] + rise
        rise_y[plane(i)] = my + rise
        part[plane(i)] = c[plane(i)] * here + (my - my_before)
        my_before = my

    def source_c(j):
        f = flux_y[strided(j)]
        if j > 0:
            f = f - flux_y[strided(j - 1)]
        return part[strided(j)] + f

    first_c, last_c = eliminate(source_c, p_y, g_c)
    last_c = last_c - flux_y[strided(B - 1)]
    sent = [first_a, last_a, first_c, last_c, u_y[plane(0)], v_y[plane(0)], v_y[plane(B - 1)]]
    for k, value in enumerate(sent):
        msg[plane(k)] = value


def second_x_kernel(near, far, order, pos, got_near, own_near, *refs):
    others, refs = refs[:far], refs[far:]
    g_a, u, v, flux_a, c, curl, p_x, part, flux2, g2, ends_c, msg, got_far, fx = refs
    q, r = place(pos, 1, near)
    far_blocks = collect(q, order, others[0], others[1:], got_far)
    near_blocks = [stored(got_near, m, range(7)) for m in range(near)]
    own, own_group = loaded(own_near, range(7)), loaded(others[0], range(7))
    (before, after), (before_c, after_c) = solved_ends(
        q,
        r,
        2,
        [rows_of(b, 2) for b in near_blocks],
        [b[4:7] for b in near_blocks],
        [rows_of(b, 2) for b in far_blocks],
        [b[4:7] for b in far_blocks],
        (rows_of(own, 2), own[4:7]),
        (rows_of(own_group, 2), own_group[4:7]),
    )
    ends_c[plane(0)] = before_c
    ends_c[plane(1)] = after_c
    for j in range(B):
        fx[plane(j)] = g_a[plane(j)] + (u[plane(j)] * before + v[plane(j)] * after)
    mz_before = jnp.where(pos[plane(1)] == 0, 0.0, fx[plane(0)] - before)
    for j in range(B):
        here = fx[plane(j)]
        rise = (fx[plane(j + 1)] if j < B - 1 else after) - here
        mz = flux_a[strided(j)] + rise
        part[strided(j)] = c[strided(j)] * here + (mz - mz_before)
        flux2[strided(j)] = -(mz + rise)
        mz_before = mz

    def source(i):
        f = flux2[plane(i)]
        if i > 0:
            f = f - flux2[plane(i - 1)]
        return curl[plane(i)] + f

    first, last = eliminate(source, p_x, g2)
    msg[plane(0)] = first
    msg[plane(1)] = last - flux2[plane(B - 1)]


def second_y_kernel(ends_c, g_c, u, v, flux_y, elec, magn, full_z, new_x, sems):
    stores = [(full_z, elec.at[2]), (new_x, magn.at[0])]
    stores = [pltpu.make_async_copy(a, b, sems.at[k]) for k, (a, b) in enumerate(stores)]
    before, after = ends_c[plane(0)], ends_c[plane(1)]
    here = None
    for j in range(B):
        ahead = g_c[plane(j)] + (u[plane(j)] * before + v[plane(j)] * after)
        full_z[strided(j)] = ahead
        if j > 0:
            new_x[strided(j - 1)] = -h * (flux_y[strided(j - 1)] + (ahead - here))
        here = ahead
    new_x[strided(B - 1)] = -h * (flux_y[strided(B - 1)] + (after - here))
    for store in stores:
        store.start()
    for store in stores:
        store.wait()


def second_z_kernel(part, rise_y, z_a, z_b, z_scale, _, __, elec, magn, full_x, new_y, sems):
    stores = [(full_x, elec.at[0]), (new_y, magn.at[1])]
    stores = [pltpu.make_async_copy(a, b, sems.at[k]) for k, (a, b) in enumerate(stores)]
    a = rise_y[...]
    x = solve_factored(part[...] - behind_z(a), z_a, z_b, z_scale)
    full_x[...] = x
    stores[0].start()
    new_y[...] = h * (a - ahead_z(x))
    stores[1].start()
    for store in stores:
        store.wait()


def last_kernel(near, far, order, pos, coefs_near, coefs_far, own_b, group_b, got_near, own_near, *refs):
    others, refs = refs[:far], refs[far:]
    g, u, v, flux2, _, _, elec, magn, got_far, full_y, new_z, sems = refs
    q, r = place(pos, 0, near)
    far_blocks = collect(q, order, others[0], others[1:], got_far)
    ((before, after),) = solved_ends(
        q,
        r,
        1,
        [rows_of(stored(got_near, m, range(2)), 1) for m in range(near)],
        [stored(coefs_near, m, (2, 3, 4)) for m in range(near)],
        [rows_of(b, 1) for b in far_blocks],
        [stored(coefs_far, m, (2, 3, 4)) for m in range(far)],
        (rows_of(loaded(own_near, range(2)), 1), loaded(own_b, (2, 3, 4))),
        (rows_of(loaded(others[0], range(2)), 1), loaded(group_b, (2, 3, 4))),
    )
    stores = [(full_y, elec.at[1]), (new_z, magn.at[2])]
    stores = [pltpu.make_async_copy(a, b, sems.at[k]) for k, (a, b) in enumerate(stores)]
    for i in range(B):
        full_y[plane(i)] = g[plane(i)] + (u[plane(i)] * before + v[plane(i)] * after)
    stores[0].start()
    for i in range(B):
        rise = (full_y[plane(i + 1)] if i < B - 1 else after) - full_y[plane(i)]
        new_z[plane(i)] = -h * (flux2[plane(i)] + rise)
    stores[1].start()
    for store in stores:
        store.wait()


VMEM = pl.BlockSpec(memory_space=pltpu.VMEM)
SMEM = pl.BlockSpec(memory_space=pltpu.SMEM)
HBM = pl.BlockSpec(memory_space=pltpu.HBM)


def call(kernel, ins, outs, specs=None, out_specs=None, scratch=(), aliases=None, flops=1_000_000):
    shapes = [jax.ShapeDtypeStruct(s, F32) if isinstance(s, tuple) else s for s in outs]
    return pl.pallas_call(
        kernel,
        out_shape=shapes,
        in_specs=specs or [VMEM] * len(ins),
        out_specs=out_specs or [VMEM] * len(outs),
        scratch_shapes=[pltpu.VMEM(s, F32) if isinstance(s, tuple) else s for s in scratch],
        input_output_aliases=aliases or {},
        compiler_params=pltpu.CompilerParams(vmem_limit_bytes=24 * 1024 * 1024),
        cost_estimate=pl.CostEstimate(flops=flops, bytes_accessed=1_000_000, transcendentals=0),
    )(*ins)


def shared(value, axis, n, order, near=1, bent=()):
    masks = [near * s + (near // 2 if s in bent else 0) for s in order]
    return [value] + [lax.ppermute(value, axis, [(i, i ^ mask) for i in range(n)]) for mask in masks]


def split(n):
    near = 1 << (n.bit_length() // 2)
    return near, n // near


def local(electric, magnetic, material, permittivity, conductivity):
    nx, ny = lax.axis_size("px"), lax.axis_size("py")
    near_x, far_x = split(nx)
    near_y, far_y = split(ny)
    nz = material.shape[2]
    cells = (B * B, nz)
    me = jnp.stack([lax.axis_index("px"), lax.axis_index("py")]).astype(jnp.int32)
    in_hbm = lambda a: pltpu.with_memory_space_constraint(a, pltpu.HBM)
    elec = in_hbm(electric.reshape(3, *cells))
    magn = in_hbm(magnetic.reshape(3, *cells))
    ids = in_hbm(material.reshape(cells))
    dma = pltpu.SemaphoreType.DMA
    orders = [(1, 2, 3), (2, 1, 3), (2, 1, 3), (1, 3, 2)]
    counts = (near_x, far_x, near_y, far_y)
    px_near, px_far, py_near, py_far = [
        tuple(s for s in order if s < count) for order, count in zip(orders, counts)
    ]

    hx_last, ez_first = call(
        cut_kernel,
        [in_hbm(electric), in_hbm(magnetic)],
        [(B, nz)] * 2,
        specs=[HBM] * 2,
        scratch=[dma((2,))],
        flops=1000,
    )
    hx_prev = lax.ppermute(hx_last, "py", [(i, (i + 1) % ny) for i in range(ny)])
    ez_next = lax.ppermute(ez_first, "py", [((i + 1) % ny, i) for i in range(ny)])
    w, c, p_x, u_x, v_x, flux_b, part_b, ef, mf, pos, early = call(
        tables_kernel,
        [me, in_hbm(permittivity), in_hbm(conductivity), ids, elec, magn],
        [cells] * 7 + [(3, *cells)] * 2 + [jax.ShapeDtypeStruct((2 * B, nz), jnp.int32), (7 * B, nz)],
        specs=[SMEM] + [HBM] * 5,
        scratch=[pltpu.VMEM(cells, jnp.int32)] + [pltpu.SMEM(permittivity.shape, F32)] * 2 + [dma((9,))],
    )
    beyond = tuple(range(2, near_x))
    sent = shared(early, "px", nx, beyond)
    hx_prev, ez_next = lax.optimization_barrier((hx_prev, ez_next))
    g_b, own_b, ends = call(
        first_x_kernel,
        [pos, part_b, hx_prev, flux_b, p_x, early],
        [cells, (7 * B, nz), (2 * B, nz)],
    )
    ins = [own_b] + sent[1:] + shared(own_b, "px", nx, (1,))[1:] + shared(ends, "px", nx, beyond)[1:]
    near_b, group_b = call(
        functools.partial(merge_first_kernel, near_x),
        [pos] + ins,
        [(near_x, 7 * B, nz), (7 * B, nz)],
    )
    ins = shared(group_b, "px", nx, px_far, near_x, (1, 3))
    p_y, u_y, v_y, r_top, src_top, curl, flux_y, flux_a, part_a = call(
        functools.partial(first_z_kernel, ny),
        [pos, ef, mf, ez_next, w, c],
        [cells] * 3 + [(B, nz)] * 2 + [cells] * 4,
        scratch=[cells] * 2,
        flops=8_000_000,
    )
    ins = [pos, near_b, own_b] + ins + [g_b, u_x, v_x, flux_b, w, c, r_top, src_top]
    far_b, rise_y, curl, flux_y, flux_a, g_a, g_c, own_ac = call(
        functools.partial(both_y_kernel, near_x, far_x, px_far),
        ins + [curl, flux_y, flux_a, part_a, p_y, u_y, v_y],
        [(far_x, 7 * B, nz)] + [cells] * 6 + [(7 * B, nz)],
        scratch=[cells] * 2,
    )
    ins = shared(own_ac, "py", ny, py_near)
    near_ac, msg = call(
        functools.partial(merge_kernel, 1, near_y, py_near, 2), [pos] + ins, [(near_y, 7 * B, nz), (7 * B, nz)]
    )
    msg, w = lax.optimization_barrier((msg, w))
    ins = shared(msg, "py", ny, py_far, near_y, (2,))
    steps = (nz - 1).bit_length()
    z_factors = call(factors_kernel, [w], [(steps, *cells)] * 2 + [cells], flops=8_000_000)
    ins, z_factors = lax.optimization_barrier((ins, z_factors))
    part_x, flux2, g2, ends_c, own_a = call(
        functools.partial(second_x_kernel, near_y, far_y, py_far),
        [pos, near_ac, own_ac] + ins + [g_a, u_y, v_y, flux_a, c, curl, p_x],
        [cells] * 3 + [(2 * B, nz)] * 2,
        scratch=[(far_y, 7 * B, nz), cells],
    )
    ins = shared(own_a, "px", nx, px_near)
    whole = pltpu.HBM((3, *cells), F32)
    elec, magn = call(
        second_y_kernel,
        [ends_c, g_c, u_y, v_y, flux_y],
        [whole, whole],
        out_specs=[HBM] * 2,
        scratch=[cells] * 2 + [dma((2,))],
    )
    near_a, msg = call(
        functools.partial(merge_rows_kernel, 0, near_x, px_near),
        [pos, near_b] + ins,
        [(near_x, 2 * B, nz), (2 * B, nz)],
    )
    msg, elec = lax.optimization_barrier((msg, elec))
    ins = shared(msg, "px", nx, px_far, near_x, (1, 3))
    elec, magn = call(
        second_z_kernel,
        [part_x, rise_y, *z_factors, elec, magn],
        [whole] * 2,
        specs=[VMEM] * 5 + [HBM] * 2,
        out_specs=[HBM] * 2,
        scratch=[cells] * 2 + [dma((2,))],
        aliases={5: 0, 6: 1},
        flops=4_000_000,
    )
    ins = [pos, near_b, far_b, own_b, group_b, near_a, own_a] + ins + [g2, u_x, v_x, flux2]
    at = len(ins)
    out = call(
        functools.partial(last_kernel, near_x, far_x, px_far),
        ins + [elec, magn],
        [whole] * 2,
        specs=[VMEM] * at + [HBM] * 2,
        out_specs=[HBM] * 2,
        scratch=[(far_x, 2 * B, nz), cells, cells, dma((2,))],
        aliases={at: 0, at + 1: 1},
    )
    return tuple(a.reshape(3, B, B, nz) for a in out)


def solution(mesh):
    placed = (P(None, "px", "py", None), P(None, "px", "py", None), P("px", "py", None), P(), P())
    return jax.shard_map(
        local,
        mesh=mesh,
        in_specs=placed,
        out_specs=(P(None, "px", "py", None), P(None, "px", "py", None)),
        check_vma=False,
    )
```

```python
import functools

import jax
import jax.numpy as jnp
from jax import lax
from jax.experimental import pallas as pl
from jax.experimental.pallas import tpu as pltpu
from jax.sharding import PartitionSpec as P

h = 32.0
B = 16
F32 = jnp.float32


def plane(i):
    return pl.ds(i * B, B)


def strided(j):
    return pl.ds(j, B, stride=B)


def lanes(v):
    return lax.broadcasted_iota(jnp.int32, v.shape, 1)


def behind_z(v):
    return v - jnp.where(lanes(v) == 0, 0.0, pltpu.roll(v, 1, 1))


def ahead_z(v):
    n = v.shape[1]
    return jnp.where(lanes(v) == n - 1, 0.0, pltpu.roll(v, n - 1, 1)) - v


def factor(w_of, first_block, p, u, v):
    d = None
    y = []
    for j in range(B):
        w = w_of(j)
        e = w + (jnp.where(first_block, 0.0, 1.0) if j == 0 else d)
        inv = 1.0 / (1.0 + e)
        d = e * inv
        p[plane(j)] = inv
        y.append(jnp.ones_like(inv) if j == 0 else y[-1] * last)
        last = inv
    uj = y[B - 1] * last
    vj = last
    u[plane(B - 1)] = uj
    v[plane(B - 1)] = vj
    for j in range(B - 2, -1, -1):
        inv = p[plane(j)]
        uj = inv * (y[j] + uj)
        vj = inv * vj
        u[plane(j)] = uj
        v[plane(j)] = vj


def eliminate(source_of, p, g):
    y = source_of(0)
    ys = [y]
    for j in range(1, B):
        y = source_of(j) + p[plane(j - 1)] * y
        ys.append(y)
    x = y * p[plane(B - 1)]
    end = x
    g[plane(B - 1)] = x
    for j in range(B - 2, -1, -1):
        x = p[plane(j)] * (ys[j] + x)
        g[plane(j)] = x
    return x, end


def boundary(me, rows, coefs, here, coef_here, outer):
    n = len(rows)
    left = [a for a, _ in outer]
    right = [b for _, b in outer]
    beta = delta = jnp.zeros_like(left[0])
    for s in range(n - 1):
        ff, fl, ll = coefs[s]
        t = fl / (1.0 - ff * beta)
        on = s < me
        left = [jnp.where(on, dl + t * (a + beta * gf), a) for a, (gf, dl) in zip(left, rows[s])]
        beta = jnp.where(on, ll + t * beta * fl, beta)
        m = n - 1 - s
        ff, fl, ll = coefs[m]
        t = fl / (1.0 - ll * delta)
        on = m > me
        right = [jnp.where(on, gf + t * (b + delta * dl), b) for b, (gf, dl) in zip(right, rows[m])]
        delta = jnp.where(on, ff + t * delta * fl, delta)
    ff, fl, ll = coef_here
    after_scale = 1.0 / (1.0 - delta * ll)
    t = fl * after_scale
    before_scale = 1.0 / (1.0 - beta * (ff + t * delta * fl))
    ends = []
    for a, b, (gf, dl) in zip(left, right, here):
        before = (a + beta * (gf + t * (b + delta * dl))) * before_scale
        ends.append((before, (b + delta * (dl + fl * before)) * after_scale))
    return ends


def merge(one, two):
    (ff1, fl1, ll1), rows1 = one
    (ff2, fl2, ll2), rows2 = two
    d = 1.0 / (1.0 - ll1 * ff2)
    t1, t2 = fl1 * d, fl2 * d
    rows = [
        (gf1 + t1 * (gf2 + ff2 * dl1), dl2 + t2 * (dl1 + ll1 * gf2))
        for (gf1, dl1), (gf2, dl2) in zip(rows1, rows2)
    ]
    return (ff1 + t1 * fl1 * ff2, t1 * fl2, ll2 + t2 * fl2 * ll1), rows


def solve_z(r, w):
    n = r.shape[1]
    lane = lanes(r)
    e = jnp.where(lane == n - 1, 0.0, 1.0)
    l = jnp.where(lane == 0, 0.0, 1.0)
    s = w + jnp.where(lane == n - 1, 1.0, 0.0)
    step = 1
    while step < n:
        inv = 1.0 / (s + (l + e))
        a, b = e * inv, l * inv
        r = r + (pltpu.roll(a * r, step, 1) + pltpu.roll(b * r, n - step, 1))
        s = s + (pltpu.roll(a * s, step, 1) + pltpu.roll(b * s, n - step, 1))
        g = a * l
        if 2 * step < n:
            e, l = pltpu.roll(g, n - step, 1), pltpu.roll(g, step, 1)
        step *= 2
    return r / s


def factors_kernel(w_in, a_out, b_out, scale):
    w = w_in[...]
    n = w.shape[1]
    lane = lanes(w)
    e = jnp.where(lane == n - 1, 0.0, 1.0)
    l = jnp.where(lane == 0, 0.0, 1.0)
    s = w + jnp.where(lane == n - 1, 1.0, 0.0)
    for k in range(a_out.shape[0]):
        step = 1 << k
        inv = 1.0 / (s + (l + e))
        a, b = e * inv, l * inv
        a_out[k] = a
        b_out[k] = b
        s = s + (pltpu.roll(a * s, step, 1) + pltpu.roll(b * s, n - step, 1))
        g = a * l
        e, l = pltpu.roll(g, n - step, 1), pltpu.roll(g, step, 1)
    scale[...] = 1.0 / s


def solve_factored(r, a, b, scale):
    n = r.shape[1]
    for k in range(a.shape[0]):
        step = 1 << k
        r = r + (pltpu.roll(a[k] * r, step, 1) + pltpu.roll(b[k] * r, n - step, 1))
    return r * scale[...]


def collect(r, order, own, others, got):
    refs = [own] + [others[order.index(s)] for s in range(1, len(order) + 1)]
    return ordered(r, [loaded(ref, range(got.shape[1] // B)) for ref in refs], got)


def ordered(r, found, got):
    count = len(found)
    blocks = [[] for _ in found]
    for k in range(got.shape[1] // B):
        values = [planes[k] for planes in found]
        bit = 1
        while bit < count:
            swap = lax.bitwise_and(r, bit) != 0
            values = [jnp.where(swap, values[m ^ bit], values[m]) for m in range(count)]
            bit *= 2
        for m, value in enumerate(values):
            got[m, plane(k)] = value
            blocks[m].append(value)
    return blocks


def rows_of(block, sources):
    return [(block[2 * k], block[2 * k + 1]) for k in range(sources)]


def stored(got, m, planes):
    return [got[m, plane(k)] for k in planes]


def loaded(msg, planes):
    return [msg[plane(k)] for k in planes]


def pick(values, index):
    out = values[0]
    for k in range(1, len(values)):
        out = jnp.where(index == k, values[k], out)
    return out


def place(pos, axis, near):
    here = pos[plane(axis)]
    return lax.shift_right_logical(here, near.bit_length() - 1), lax.bitwise_and(here, near - 1)


def cut_kernel(magn, hx_last, sem):
    load = pltpu.make_async_copy(magn.at[0, :, B - 1], hx_last, sem)
    load.start()
    load.wait()


def tables_kernel(
    me, eps_in, sig_in, material, elec_in, magn_in, w, c, p, u, v, flux, part, elec, magn, ez_first, pos, ids, eps, sig, sems
):
    loads = [(eps_in, eps), (sig_in, sig), (material, ids)]
    for field, to, k in ((elec_in, elec, 0), (magn_in, magn, 1), (elec_in, elec, 2), (magn_in, magn, 0)):
        loads.append((field.at[k], to.at[k]))
    loads += [(elec_in.at[1], elec.at[1]), (magn_in.at[2], magn.at[2])]
    loads = [pltpu.make_async_copy(a, b, sems.at[k]) for k, (a, b) in enumerate(loads)]
    for load in loads:
        load.start()
    for axis in range(2):
        pos[plane(axis)] = jnp.full((B, w.shape[1]), me[axis], jnp.int32)
    for load in loads[:3]:
        load.wait()
    ws = [eps[m] * (1.0 / (h * h)) + sig[m] * (0.5 / h) for m in range(eps.shape[0])]
    cs = [eps[m] * (1.0 / (h * h)) - sig[m] * (0.5 / h) for m in range(eps.shape[0])]
    for i in range(B):
        cell = ids[plane(i)]
        wi = jnp.full(cell.shape, ws[0], F32)
        ci = jnp.full(cell.shape, cs[0], F32)
        for m in range(1, len(ws)):
            wi = jnp.where(cell == m, ws[m], wi)
            ci = jnp.where(cell == m, cs[m], ci)
        w[plane(i)] = wi
        c[plane(i)] = ci
    factor(lambda i: w[plane(i)], me[0] == 0, p, u, v)
    for load in loads[3:7]:
        load.wait()
    row = lax.broadcasted_iota(jnp.int32, (B, w.shape[1]), 0)
    for i in range(B):
        q = magn[1, plane(i)] * (1.0 / h) - ahead_z(elec[0, plane(i)])
        flux[plane(i)] = q
        if i > 0:
            q = q - flux[plane(i - 1)]
        here = magn[0, plane(i)]
        before = jnp.where(row == 0, 0.0, pltpu.roll(here, 1, 0))
        part[plane(i)] = c[plane(i)] * elec[2, plane(i)] + (q - (here - before) * (1.0 / h))
    for k in range(ez_first.shape[0] // B):
        ez_first[plane(k)] = elec.at[2][strided(0)]
    for load in loads[7:]:
        load.wait()


def first_x_kernel(pos, part, hx_prev, flux, p, u, v, elec, magn, g, msg, inner, outer):
    row = lax.broadcasted_iota(jnp.int32, hx_prev.shape, 0)
    scale = jnp.where(pos[plane(1)] == 0, 0.0, jnp.where(row == 0, 1.0 / h, 0.0))

    def source(i):
        return part[plane(i)] + hx_prev[pl.ds(i, 1)] * scale

    first, last = eliminate(source, p, g)
    msg[plane(0)] = first
    msg[plane(1)] = last - flux[plane(B - 1)]
    msg[plane(2)] = u[plane(0)]
    msg[plane(3)] = v[plane(0)]
    msg[plane(4)] = v[plane(B - 1)]
    msg[plane(5)] = elec[1, plane(0)]
    msg[plane(6)] = magn[2, plane(B - 1)]
    even = lax.bitwise_and(pos[plane(0)], 1) == 0
    for sent, halo in ((inner, (6, 5)), (outer, (5, 6))):
        sent[pl.ds(0, 5 * B)] = msg[pl.ds(0, 5 * B)]
        sent[plane(5)] = jnp.where(even, msg[plane(halo[0])], msg[plane(halo[1])])


def merged(blocks):
    while len(blocks) > 1:
        blocks = [merge(a, b) for a, b in zip(blocks[::2], blocks[1::2])]
    return blocks[0]


def merge_kernel(axis, near, order, sources, pos, *refs):
    got, msg = refs[-2:]
    blocks = collect(place(pos, axis, near)[1], order, refs[0], refs[1:near], got)
    at = 2 * sources
    coefs, rows = merged([(b[at : at + 3], rows_of(b, sources)) for b in blocks])
    for k, value in enumerate([v for pair in rows for v in pair] + list(coefs)):
        msg[plane(k)] = value


def merge_first_kernel(near, pos, own, *refs):
    got, msg, halos = refs[-3:]
    r = place(pos, 0, near)[1]
    blocks = ordered(r, [loaded(ref, range(5)) for ref in (own, *refs[: near - 1])], got)
    coefs, rows = merged([(b[2:5], rows_of(b, 1)) for b in blocks])
    for k, value in enumerate([*rows[0], *coefs, jnp.where(r == 0, own[plane(5)], own[plane(6)])]):
        msg[plane(k)] = value
    inner, outer = refs[0][plane(5)], refs[near - 2][plane(5)]
    odd = lax.bitwise_and(r, 1) == 1
    halos[plane(0)] = jnp.where(odd, outer, inner)
    halos[plane(1)] = jnp.where(odd, inner, outer)


def merge_rows_kernel(axis, near, order, pos, coefs, *refs):
    got, msg = refs[-2:]
    blocks = collect(place(pos, axis, near)[1], order, refs[0], refs[1:near], got)
    _, rows = merged([(stored(coefs, m, (2, 3, 4)), rows_of(b, 1)) for m, b in enumerate(blocks)])
    msg[plane(0)], msg[plane(1)] = rows[0]


def solved_ends(q, r, sources, near_rows, near_coefs, far_rows, far_coefs, own_near, own_far):
    zero = jnp.zeros_like(far_coefs[0][0])
    outer = boundary(q, far_rows, far_coefs, *own_far, [(zero, zero)] * sources)
    return boundary(r, near_rows, near_coefs, *own_near, outer)


def first_z_kernel(n, pos, ef, mf, ez_next, w, c, p, u, v, r_top, src_top, curl, flux_y, flux_a, part_a, src, r):
    factor(lambda j: w[strided(j)], pos[plane(1)] == 0, p, u, v)
    inside = jnp.where(pos[pl.ds(B, 1)] == n - 1, 0.0, 1.0)
    row = lax.broadcasted_iota(jnp.int32, (B, w.shape[1]), 0)
    for i in range(B):
        ez = ef[2, plane(i)]
        after = jnp.where(row == B - 1, ez_next[pl.ds(i, 1)] * inside, pltpu.roll(ez, B - 1, 0))
        ri = mf[0, plane(i)] * (1.0 / h) - (after - ez)
        r[plane(i)] = ri
        gain = mf[2, plane(i)]
        if i > 0:
            gain = gain - mf[2, plane(i - 1)]
        src[plane(i)] = c[plane(i)] * ef[1, plane(i)] + (behind_z(ri) - gain * (1.0 / h))
        part_a[plane(i)] = c[plane(i)] * ef[0, plane(i)] - behind_z(mf[1, plane(i)]) * (1.0 / h)
        if i < B - 1:
            rise = ef[1, plane(i + 1)] - ef[1, plane(i)]
            flux_a[plane(i)] = mf[2, plane(i)] * (1.0 / h) - rise
    flux_a[plane(B - 1)] = mf[2, plane(B - 1)] * (1.0 / h) + ef[1, plane(B - 1)]
    r_top[...] = r[plane(0)]
    src_top[...] = src[plane(0)]
    x = solve_z(src[...], w[...])
    rise = ahead_z(x)
    mx = r[...] + rise
    curl[...] = c[...] * x + behind_z(mx)
    flux_y[...] = -(mx + rise)


def both_y_kernel(near, far, order, pos, got_near, own_near, *refs):
    others, refs = refs[:far], refs[far:]
    (halos, g_b, u_x, v_x, flux_b, w, c, r_top, src_top, curl_in, flux_y_in, flux_a_in, part_a, p_y, u_y, v_y) = refs[:16]
    got_far, rise_y, curl, flux_y, flux_a, g_a, g_c, msg, part, fz = refs[16:]
    top = plane(0)
    q, r = place(pos, 0, near)
    far_blocks = collect(q, order, others[0], others[1:], got_far)
    near_blocks = [stored(got_near, m, range(5)) for m in range(near)]
    ends = [b[5] for b in far_blocks]
    after_group = jnp.where(q < far - 1, pick(ends, q + 1), 0.0)
    ey_next = jnp.where(r < near - 1, halos[plane(0)], after_group)
    before_group = jnp.where(q > 0, pick(ends, q - 1), 0.0)
    hz_prev = jnp.where(r > 0, halos[plane(1)], before_group)
    curl[...] = curl_in[...]
    flux_y[...] = flux_y_in[...]
    flux_a[...] = flux_a_in[...]

    x = solve_z(src_top[...] + hz_prev * (1.0 / h), w[top])
    rise = ahead_z(x)
    mx = r_top[...] + rise
    curl[top] = c[top] * x + behind_z(mx)
    flux_y[top] = -(mx + rise)

    flux_a[plane(B - 1)] = flux_a[plane(B - 1)] - ey_next

    def source_a(j):
        f = flux_a[strided(j)]
        if j > 0:
            f = f - flux_a[strided(j - 1)]
        return part_a[strided(j)] + f

    first_a, last_a = eliminate(source_a, p_y, g_a)
    last_a = last_a - flux_a[strided(B - 1)]

    own, own_group = loaded(own_near, range(5)), loaded(others[0], range(5))
    ((before, after),) = solved_ends(
        q,
        r,
        1,
        [rows_of(b, 1) for b in near_blocks],
        [b[2:5] for b in near_blocks],
        [rows_of(b, 1) for b in far_blocks],
        [b[2:5] for b in far_blocks],
        (rows_of(own, 1), own[2:5]),
        (rows_of(own_group, 1), own_group[2:5]),
    )
    for i in range(B):
        fz[plane(i)] = g_b[plane(i)] + (u_x[plane(i)] * before + v_x[plane(i)] * after)
    my_before = jnp.where(pos[plane(0)] == 0, 0.0, fz[top] - before)
    for i in range(B):
        here = fz[plane(i)]
        rise = (fz[plane(i + 1)] if i < B - 1 else after) - here
        my = flux_b[plane(i)] + rise
        rise_y[plane(i)] = my + rise
        part[plane(i)] = c[plane(i)] * here + (my - my_before)
        my_before = my

    def source_c(j):
        f = flux_y[strided(j)]
        if j > 0:
            f = f - flux_y[strided(j - 1)]
        return part[strided(j)] + f

    first_c, last_c = eliminate(source_c, p_y, g_c)
    last_c = last_c - flux_y[strided(B - 1)]
    sent = [first_a, last_a, first_c, last_c, u_y[plane(0)], v_y[plane(0)], v_y[plane(B - 1)]]
    for k, value in enumerate(sent):
        msg[plane(k)] = value


def second_x_kernel(near, far, order, pos, got_near, own_near, *refs):
    others, refs = refs[:far], refs[far:]
    g_a, u, v, flux_a, c, curl, p_x, part, flux2, g2, ends_c, msg, got_far, fx = refs
    q, r = place(pos, 1, near)
    far_blocks = collect(q, order, others[0], others[1:], got_far)
    near_blocks = [stored(got_near, m, range(7)) for m in range(near)]
    own, own_group = loaded(own_near, range(7)), loaded(others[0], range(7))
    (before, after), (before_c, after_c) = solved_ends(
        q,
        r,
        2,
        [rows_of(b, 2) for b in near_blocks],
        [b[4:7] for b in near_blocks],
        [rows_of(b, 2) for b in far_blocks],
        [b[4:7] for b in far_blocks],
        (rows_of(own, 2), own[4:7]),
        (rows_of(own_group, 2), own_group[4:7]),
    )
    ends_c[plane(0)] = before_c
    ends_c[plane(1)] = after_c
    for j in range(B):
        fx[plane(j)] = g_a[plane(j)] + (u[plane(j)] * before + v[plane(j)] * after)
    mz_before = jnp.where(pos[plane(1)] == 0, 0.0, fx[plane(0)] - before)
    for j in range(B):
        here = fx[plane(j)]
        rise = (fx[plane(j + 1)] if j < B - 1 else after) - here
        mz = flux_a[strided(j)] + rise
        part[strided(j)] = c[strided(j)] * here + (mz - mz_before)
        flux2[strided(j)] = -(mz + rise)
        mz_before = mz

    def source(i):
        f = flux2[plane(i)]
        if i > 0:
            f = f - flux2[plane(i - 1)]
        return curl[plane(i)] + f

    first, last = eliminate(source, p_x, g2)
    msg[plane(0)] = first
    msg[plane(1)] = last - flux2[plane(B - 1)]


def second_y_kernel(ends_c, g_c, u, v, flux_y, elec, magn, full_z, new_x, sems):
    stores = [(full_z, elec.at[2]), (new_x, magn.at[0])]
    stores = [pltpu.make_async_copy(a, b, sems.at[k]) for k, (a, b) in enumerate(stores)]
    before, after = ends_c[plane(0)], ends_c[plane(1)]
    here = None
    for j in range(B):
        ahead = g_c[plane(j)] + (u[plane(j)] * before + v[plane(j)] * after)
        full_z[strided(j)] = ahead
        if j > 0:
            new_x[strided(j - 1)] = -h * (flux_y[strided(j - 1)] + (ahead - here))
        here = ahead
    new_x[strided(B - 1)] = -h * (flux_y[strided(B - 1)] + (after - here))
    for store in stores:
        store.start()
    for store in stores:
        store.wait()


def second_z_kernel(part, rise_y, z_a, z_b, z_scale, _, __, elec, magn, full_x, new_y, sems):
    stores = [(full_x, elec.at[0]), (new_y, magn.at[1])]
    stores = [pltpu.make_async_copy(a, b, sems.at[k]) for k, (a, b) in enumerate(stores)]
    a = rise_y[...]
    x = solve_factored(part[...] - behind_z(a), z_a, z_b, z_scale)
    full_x[...] = x
    stores[0].start()
    new_y[...] = h * (a - ahead_z(x))
    stores[1].start()
    for store in stores:
        store.wait()


def last_kernel(near, far, order, pos, coefs_near, coefs_far, own_b, group_b, got_near, own_near, *refs):
    others, refs = refs[:far], refs[far:]
    g, u, v, flux2, _, _, elec, magn, got_far, full_y, new_z, sems = refs
    q, r = place(pos, 0, near)
    far_blocks = collect(q, order, others[0], others[1:], got_far)
    ((before, after),) = solved_ends(
        q,
        r,
        1,
        [rows_of(stored(got_near, m, range(2)), 1) for m in range(near)],
        [stored(coefs_near, m, (2, 3, 4)) for m in range(near)],
        [rows_of(b, 1) for b in far_blocks],
        [stored(coefs_far, m, (2, 3, 4)) for m in range(far)],
        (rows_of(loaded(own_near, range(2)), 1), loaded(own_b, (2, 3, 4))),
        (rows_of(loaded(others[0], range(2)), 1), loaded(group_b, (2, 3, 4))),
    )
    stores = [(full_y, elec.at[1]), (new_z, magn.at[2])]
    stores = [pltpu.make_async_copy(a, b, sems.at[k]) for k, (a, b) in enumerate(stores)]
    for i in range(B):
        full_y[plane(i)] = g[plane(i)] + (u[plane(i)] * before + v[plane(i)] * after)
    stores[0].start()
    for i in range(B):
        rise = (full_y[plane(i + 1)] if i < B - 1 else after) - full_y[plane(i)]
        new_z[plane(i)] = -h * (flux2[plane(i)] + rise)
    stores[1].start()
    for store in stores:
        store.wait()


VMEM = pl.BlockSpec(memory_space=pltpu.VMEM)
SMEM = pl.BlockSpec(memory_space=pltpu.SMEM)
HBM = pl.BlockSpec(memory_space=pltpu.HBM)


def call(kernel, ins, outs, specs=None, out_specs=None, scratch=(), aliases=None, flops=1_000_000):
    shapes = [jax.ShapeDtypeStruct(s, F32) if isinstance(s, tuple) else s for s in outs]
    return pl.pallas_call(
        kernel,
        out_shape=shapes,
        in_specs=specs or [VMEM] * len(ins),
        out_specs=out_specs or [VMEM] * len(outs),
        scratch_shapes=[pltpu.VMEM(s, F32) if isinstance(s, tuple) else s for s in scratch],
        input_output_aliases=aliases or {},
        compiler_params=pltpu.CompilerParams(vmem_limit_bytes=24 * 1024 * 1024),
        cost_estimate=pl.CostEstimate(flops=flops, bytes_accessed=1_000_000, transcendentals=0),
    )(*ins)


def shared(value, axis, n, order, near=1, bent=(), by=0):
    masks = [near * s + (by if s in bent else 0) for s in order]
    return [value] + [lax.ppermute(value, axis, [(i, i ^ mask) for i in range(n)]) for mask in masks]


def split(n):
    near = 1 << (n.bit_length() // 2)
    return near, n // near


def local(electric, magnetic, material, permittivity, conductivity):
    nx, ny = lax.axis_size("px"), lax.axis_size("py")
    near_x, far_x = split(nx)
    near_y, far_y = split(ny)
    nz = material.shape[2]
    cells = (B * B, nz)
    me = jnp.stack([lax.axis_index("px"), lax.axis_index("py")]).astype(jnp.int32)
    in_hbm = lambda a: pltpu.with_memory_space_constraint(a, pltpu.HBM)
    elec = in_hbm(electric.reshape(3, *cells))
    magn = in_hbm(magnetic.reshape(3, *cells))
    ids = in_hbm(material.reshape(cells))
    dma = pltpu.SemaphoreType.DMA
    orders = [(1, 2, 3), (2, 1, 3), (2, 1, 3), (1, 3, 2)]
    counts = (near_x, far_x, near_y, far_y)
    px_near, px_far, py_near, py_far = [
        tuple(s for s in order if s < count) for order, count in zip(orders, counts)
    ]

    (hx_last,) = call(
        cut_kernel, [in_hbm(magnetic)], [(B, nz)], specs=[HBM], scratch=[dma(())], flops=1000
    )
    hx_prev = lax.ppermute(hx_last, "py", [(i, (i + 1) % ny) for i in range(ny)])
    w, c, p_x, u_x, v_x, flux_b, part_b, ef, mf, ez_first, pos = call(
        tables_kernel,
        [me, in_hbm(permittivity), in_hbm(conductivity), ids, elec, magn],
        [cells] * 7 + [(3, *cells)] * 2 + [(8 * B, nz), jax.ShapeDtypeStruct((2 * B, nz), jnp.int32)],
        specs=[SMEM] + [HBM] * 5,
        scratch=[pltpu.VMEM(cells, jnp.int32)] + [pltpu.SMEM(permittivity.shape, F32)] * 2 + [dma((9,))],
    )
    g_b, own_b, inner, outer = call(
        first_x_kernel,
        [pos, part_b, hx_prev, flux_b, p_x, u_x, v_x, ef, mf],
        [cells, (7 * B, nz), (6 * B, nz), (6 * B, nz)],
    )
    ins = [own_b] + [shared(outer if k == 3 else inner, "px", nx, (k,))[1] for k in px_near]
    ez_next = lax.ppermute(ez_first, "py", [((i + 1) % ny, i) for i in range(ny)])
    near_b, group_b, halos = call(
        functools.partial(merge_first_kernel, near_x),
        [pos] + ins,
        [(near_x, 5 * B, nz), (6 * B, nz), (2 * B, nz)],
    )
    ins = shared(group_b, "px", nx, px_far, near_x, (1, 3), near_x - 1)
    p_y, u_y, v_y, r_top, src_top, curl, flux_y, flux_a, part_a = call(
        functools.partial(first_z_kernel, ny),
        [pos, ef, mf, ez_next, w, c],
        [cells] * 3 + [(B, nz)] * 2 + [cells] * 4,
        scratch=[cells] * 2,
        flops=8_000_000,
    )
    ins = [pos, near_b, own_b] + ins + [halos, g_b, u_x, v_x, flux_b, w, c, r_top, src_top]
    far_b, rise_y, curl, flux_y, flux_a, g_a, g_c, own_ac = call(
        functools.partial(both_y_kernel, near_x, far_x, px_far),
        ins + [curl, flux_y, flux_a, part_a, p_y, u_y, v_y],
        [(far_x, 6 * B, nz)] + [cells] * 6 + [(7 * B, nz)],
        scratch=[cells] * 2,
    )
    ins = shared(own_ac, "py", ny, py_near)
    near_ac, msg = call(
        functools.partial(merge_kernel, 1, near_y, py_near, 2), [pos] + ins, [(near_y, 7 * B, nz), (7 * B, nz)]
    )
    msg, w = lax.optimization_barrier((msg, w))
    ins = shared(msg, "py", ny, py_far, near_y, (2,), near_y // 2)
    steps = (nz - 1).bit_length()
    z_factors = call(factors_kernel, [w], [(steps, *cells)] * 2 + [cells], flops=8_000_000)
    ins, z_factors = lax.optimization_barrier((ins, z_factors))
    part_x, flux2, g2, ends_c, own_a = call(
        functools.partial(second_x_kernel, near_y, far_y, py_far),
        [pos, near_ac, own_ac] + ins + [g_a, u_y, v_y, flux_a, c, curl, p_x],
        [cells] * 3 + [(2 * B, nz)] * 2,
        scratch=[(far_y, 7 * B, nz), cells],
    )
    ins = shared(own_a, "px", nx, px_near)
    whole = pltpu.HBM((3, *cells), F32)
    elec, magn = call(
        second_y_kernel,
        [ends_c, g_c, u_y, v_y, flux_y],
        [whole, whole],
        out_specs=[HBM] * 2,
        scratch=[cells] * 2 + [dma((2,))],
    )
    near_a, msg = call(
        functools.partial(merge_rows_kernel, 0, near_x, px_near),
        [pos, near_b] + ins,
        [(near_x, 2 * B, nz), (2 * B, nz)],
    )
    msg, elec = lax.optimization_barrier((msg, elec))
    ins = shared(msg, "px", nx, px_far, near_x, (1, 3), near_x // 2)
    elec, magn = call(
        second_z_kernel,
        [part_x, rise_y, *z_factors, elec, magn],
        [whole] * 2,
        specs=[VMEM] * 5 + [HBM] * 2,
        out_specs=[HBM] * 2,
        scratch=[cells] * 2 + [dma((2,))],
        aliases={5: 0, 6: 1},
        flops=4_000_000,
    )
    ins = [pos, near_b, far_b, own_b, group_b, near_a, own_a] + ins + [g2, u_x, v_x, flux2]
    at = len(ins)
    out = call(
        functools.partial(last_kernel, near_x, far_x, px_far),
        ins + [elec, magn],
        [whole] * 2,
        specs=[VMEM] * at + [HBM] * 2,
        out_specs=[HBM] * 2,
        scratch=[(far_x, 2 * B, nz), cells, cells, dma((2,))],
        aliases={at: 0, at + 1: 1},
    )
    return tuple(a.reshape(3, B, B, nz) for a in out)


def solution(mesh):
    placed = (P(None, "px", "py", None), P(None, "px", "py", None), P("px", "py", None), P(), P())
    return jax.shard_map(
        local,
        mesh=mesh,
        in_specs=placed,
        out_specs=(P(None, "px", "py", None), P(None, "px", "py", None)),
        check_vma=False,
    )
```

```python
import functools

import jax
import jax.numpy as jnp
from jax import lax
from jax.experimental import pallas as pl
from jax.experimental.pallas import tpu as pltpu
from jax.sharding import PartitionSpec as P

h = 32.0
B = 16
F32 = jnp.float32


def plane(i):
    return pl.ds(i * B, B)


def strided(j):
    return pl.ds(j, B, stride=B)


def lanes(v):
    return lax.broadcasted_iota(jnp.int32, v.shape, 1)


def behind_z(v):
    return v - jnp.where(lanes(v) == 0, 0.0, pltpu.roll(v, 1, 1))


def ahead_z(v):
    n = v.shape[1]
    return jnp.where(lanes(v) == n - 1, 0.0, pltpu.roll(v, n - 1, 1)) - v


def factor(w_of, first_block, p, u, v):
    d = None
    y = []
    for j in range(B):
        w = w_of(j)
        e = w + (jnp.where(first_block, 0.0, 1.0) if j == 0 else d)
        inv = 1.0 / (1.0 + e)
        d = e * inv
        p[plane(j)] = inv
        y.append(jnp.ones_like(inv) if j == 0 else y[-1] * last)
        last = inv
    uj = y[B - 1] * last
    vj = last
    u[plane(B - 1)] = uj
    v[plane(B - 1)] = vj
    for j in range(B - 2, -1, -1):
        inv = p[plane(j)]
        uj = inv * (y[j] + uj)
        vj = inv * vj
        u[plane(j)] = uj
        v[plane(j)] = vj


def eliminate(source_of, p, g):
    y = source_of(0)
    ys = [y]
    for j in range(1, B):
        y = source_of(j) + p[plane(j - 1)] * y
        ys.append(y)
    x = y * p[plane(B - 1)]
    end = x
    g[plane(B - 1)] = x
    for j in range(B - 2, -1, -1):
        x = p[plane(j)] * (ys[j] + x)
        g[plane(j)] = x
    return x, end


def boundary(me, rows, coefs, here, coef_here, outer):
    n = len(rows)
    left = [a for a, _ in outer]
    right = [b for _, b in outer]
    beta = delta = jnp.zeros_like(left[0])
    for s in range(n - 1):
        ff, fl, ll = coefs[s]
        t = fl / (1.0 - ff * beta)
        on = s < me
        left = [jnp.where(on, dl + t * (a + beta * gf), a) for a, (gf, dl) in zip(left, rows[s])]
        beta = jnp.where(on, ll + t * beta * fl, beta)
        m = n - 1 - s
        ff, fl, ll = coefs[m]
        t = fl / (1.0 - ll * delta)
        on = m > me
        right = [jnp.where(on, gf + t * (b + delta * dl), b) for b, (gf, dl) in zip(right, rows[m])]
        delta = jnp.where(on, ff + t * delta * fl, delta)
    ff, fl, ll = coef_here
    after_scale = 1.0 / (1.0 - delta * ll)
    t = fl * after_scale
    before_scale = 1.0 / (1.0 - beta * (ff + t * delta * fl))
    ends = []
    for a, b, (gf, dl) in zip(left, right, here):
        before = (a + beta * (gf + t * (b + delta * dl))) * before_scale
        ends.append((before, (b + delta * (dl + fl * before)) * after_scale))
    return ends


def merge(one, two):
    (ff1, fl1, ll1), rows1 = one
    (ff2, fl2, ll2), rows2 = two
    d = 1.0 / (1.0 - ll1 * ff2)
    t1, t2 = fl1 * d, fl2 * d
    rows = [
        (gf1 + t1 * (gf2 + ff2 * dl1), dl2 + t2 * (dl1 + ll1 * gf2))
        for (gf1, dl1), (gf2, dl2) in zip(rows1, rows2)
    ]
    return (ff1 + t1 * fl1 * ff2, t1 * fl2, ll2 + t2 * fl2 * ll1), rows


def solve_z(r, w):
    n = r.shape[1]
    lane = lanes(r)
    e = jnp.where(lane == n - 1, 0.0, 1.0)
    l = jnp.where(lane == 0, 0.0, 1.0)
    s = w + jnp.where(lane == n - 1, 1.0, 0.0)
    step = 1
    while step < n:
        inv = 1.0 / (s + (l + e))
        a, b = e * inv, l * inv
        r = r + (pltpu.roll(a * r, step, 1) + pltpu.roll(b * r, n - step, 1))
        s = s + (pltpu.roll(a * s, step, 1) + pltpu.roll(b * s, n - step, 1))
        g = a * l
        if 2 * step < n:
            e, l = pltpu.roll(g, n - step, 1), pltpu.roll(g, step, 1)
        step *= 2
    return r / s


def factors_kernel(w_in, a_out, b_out, scale):
    w = w_in[...]
    n = w.shape[1]
    lane = lanes(w)
    e = jnp.where(lane == n - 1, 0.0, 1.0)
    l = jnp.where(lane == 0, 0.0, 1.0)
    s = w + jnp.where(lane == n - 1, 1.0, 0.0)
    for k in range(a_out.shape[0]):
        step = 1 << k
        inv = 1.0 / (s + (l + e))
        a, b = e * inv, l * inv
        a_out[k] = a
        b_out[k] = b
        s = s + (pltpu.roll(a * s, step, 1) + pltpu.roll(b * s, n - step, 1))
        g = a * l
        e, l = pltpu.roll(g, n - step, 1), pltpu.roll(g, step, 1)
    scale[...] = 1.0 / s


def solve_factored(r, a, b, scale):
    n = r.shape[1]
    for k in range(a.shape[0]):
        step = 1 << k
        r = r + (pltpu.roll(a[k] * r, step, 1) + pltpu.roll(b[k] * r, n - step, 1))
    return r * scale[...]


def collect(r, order, own, others, got):
    refs = [own] + [others[order.index(s)] for s in range(1, len(order) + 1)]
    return ordered(r, [loaded(ref, range(got.shape[1] // B)) for ref in refs], got)


def ordered(r, found, got):
    count = len(found)
    blocks = [[] for _ in found]
    for k in range(got.shape[1] // B):
        values = [planes[k] for planes in found]
        bit = 1
        while bit < count:
            swap = lax.bitwise_and(r, bit) != 0
            values = [jnp.where(swap, values[m ^ bit], values[m]) for m in range(count)]
            bit *= 2
        for m, value in enumerate(values):
            got[m, plane(k)] = value
            blocks[m].append(value)
    return blocks


def rows_of(block, sources):
    return [(block[2 * k], block[2 * k + 1]) for k in range(sources)]


def stored(got, m, planes):
    return [got[m, plane(k)] for k in planes]


def loaded(msg, planes):
    return [msg[plane(k)] for k in planes]


def pick(values, index):
    out = values[0]
    for k in range(1, len(values)):
        out = jnp.where(index == k, values[k], out)
    return out


def place(pos, axis, near):
    here = pos[plane(axis)]
    return lax.shift_right_logical(here, near.bit_length() - 1), lax.bitwise_and(here, near - 1)


def cut_kernel(magn, hx_last, sem):
    load = pltpu.make_async_copy(magn.at[0, :, B - 1], hx_last, sem)
    load.start()
    load.wait()


def tables_kernel(
    me, eps_in, sig_in, material, elec_in, magn_in, w, c, p, u, v, flux, part, elec, magn, ez_first, pos, ids, eps, sig, sems
):
    loads = [(eps_in, eps), (sig_in, sig), (material, ids)]
    for field, to, k in ((elec_in, elec, 0), (magn_in, magn, 1), (elec_in, elec, 2), (magn_in, magn, 0)):
        loads.append((field.at[k], to.at[k]))
    loads += [(elec_in.at[1], elec.at[1]), (magn_in.at[2], magn.at[2])]
    loads = [pltpu.make_async_copy(a, b, sems.at[k]) for k, (a, b) in enumerate(loads)]
    for load in loads:
        load.start()
    for axis in range(2):
        pos[plane(axis)] = jnp.full((B, w.shape[1]), me[axis], jnp.int32)
    for load in loads[:3]:
        load.wait()
    ws = [eps[m] * (1.0 / (h * h)) + sig[m] * (0.5 / h) for m in range(eps.shape[0])]
    cs = [eps[m] * (1.0 / (h * h)) - sig[m] * (0.5 / h) for m in range(eps.shape[0])]
    for i in range(B):
        cell = ids[plane(i)]
        wi = jnp.full(cell.shape, ws[0], F32)
        ci = jnp.full(cell.shape, cs[0], F32)
        for m in range(1, len(ws)):
            wi = jnp.where(cell == m, ws[m], wi)
            ci = jnp.where(cell == m, cs[m], ci)
        w[plane(i)] = wi
        c[plane(i)] = ci
    factor(lambda i: w[plane(i)], me[0] == 0, p, u, v)
    for load in loads[3:7]:
        load.wait()
    row = lax.broadcasted_iota(jnp.int32, (B, w.shape[1]), 0)
    for i in range(B):
        q = magn[1, plane(i)] * (1.0 / h) - ahead_z(elec[0, plane(i)])
        flux[plane(i)] = q
        if i > 0:
            q = q - flux[plane(i - 1)]
        here = magn[0, plane(i)]
        before = jnp.where(row == 0, 0.0, pltpu.roll(here, 1, 0))
        part[plane(i)] = c[plane(i)] * elec[2, plane(i)] + (q - (here - before) * (1.0 / h))
    for k in range(ez_first.shape[0] // B):
        ez_first[plane(k)] = elec.at[2][strided(0)]
    for load in loads[7:]:
        load.wait()


def first_x_kernel(pos, part, hx_prev, flux, p, u, v, elec, magn, g, msg, inner, outer):
    row = lax.broadcasted_iota(jnp.int32, hx_prev.shape, 0)
    scale = jnp.where(pos[plane(1)] == 0, 0.0, jnp.where(row == 0, 1.0 / h, 0.0))

    def source(i):
        return part[plane(i)] + hx_prev[pl.ds(i, 1)] * scale

    first, last = eliminate(source, p, g)
    msg[plane(0)] = first
    msg[plane(1)] = last - flux[plane(B - 1)]
    msg[plane(2)] = u[plane(0)]
    msg[plane(3)] = v[plane(0)]
    msg[plane(4)] = v[plane(B - 1)]
    msg[plane(5)] = elec[1, plane(0)]
    msg[plane(6)] = magn[2, plane(B - 1)]
    even = lax.bitwise_and(pos[plane(0)], 1) == 0
    for sent, halo in ((inner, (6, 5)), (outer, (5, 6))):
        sent[pl.ds(0, 5 * B)] = msg[pl.ds(0, 5 * B)]
        sent[plane(5)] = jnp.where(even, msg[plane(halo[0])], msg[plane(halo[1])])


def merged(blocks):
    while len(blocks) > 1:
        blocks = [merge(a, b) for a, b in zip(blocks[::2], blocks[1::2])]
    return blocks[0]


def merge_kernel(axis, near, order, sources, pos, *refs):
    got, msg = refs[-2:]
    blocks = collect(place(pos, axis, near)[1], order, refs[0], refs[1:near], got)
    at = 2 * sources
    coefs, rows = merged([(b[at : at + 3], rows_of(b, sources)) for b in blocks])
    for k, value in enumerate([v for pair in rows for v in pair] + list(coefs)):
        msg[plane(k)] = value


def merge_first_kernel(near, pos, own, *refs):
    got, msg, halos = refs[-3:]
    r = place(pos, 0, near)[1]
    blocks = ordered(r, [loaded(ref, range(5)) for ref in (own, *refs[: near - 1])], got)
    coefs, rows = merged([(b[2:5], rows_of(b, 1)) for b in blocks])
    for k, value in enumerate([*rows[0], *coefs, jnp.where(r == 0, own[plane(5)], own[plane(6)])]):
        msg[plane(k)] = value
    inner, outer = refs[0][plane(5)], refs[near - 2][plane(5)]
    odd = lax.bitwise_and(r, 1) == 1
    halos[plane(0)] = jnp.where(odd, outer, inner)
    halos[plane(1)] = jnp.where(odd, inner, outer)


def merge_rows_kernel(axis, near, order, pos, coefs, *refs):
    got, msg = refs[-2:]
    blocks = collect(place(pos, axis, near)[1], order, refs[0], refs[1:near], got)
    _, rows = merged([(stored(coefs, m, (2, 3, 4)), rows_of(b, 1)) for m, b in enumerate(blocks)])
    msg[plane(0)], msg[plane(1)] = rows[0]


def solved_ends(q, r, sources, near_rows, near_coefs, far_rows, far_coefs, own_near, own_far):
    zero = jnp.zeros_like(far_coefs[0][0])
    outer = boundary(q, far_rows, far_coefs, *own_far, [(zero, zero)] * sources)
    return boundary(r, near_rows, near_coefs, *own_near, outer)


def first_z_kernel(n, pos, ef, mf, ez_next, w, c, p, u, v, r_top, src_top, curl, flux_y, flux_a, part_a, src, r):
    factor(lambda j: w[strided(j)], pos[plane(1)] == 0, p, u, v)
    inside = jnp.where(pos[pl.ds(B, 1)] == n - 1, 0.0, 1.0)
    row = lax.broadcasted_iota(jnp.int32, (B, w.shape[1]), 0)
    for i in range(B):
        ez = ef[2, plane(i)]
        after = jnp.where(row == B - 1, ez_next[pl.ds(i, 1)] * inside, pltpu.roll(ez, B - 1, 0))
        ri = mf[0, plane(i)] * (1.0 / h) - (after - ez)
        r[plane(i)] = ri
        gain = mf[2, plane(i)]
        if i > 0:
            gain = gain - mf[2, plane(i - 1)]
        src[plane(i)] = c[plane(i)] * ef[1, plane(i)] + (behind_z(ri) - gain * (1.0 / h))
        part_a[plane(i)] = c[plane(i)] * ef[0, plane(i)] - behind_z(mf[1, plane(i)]) * (1.0 / h)
        if i < B - 1:
            rise = ef[1, plane(i + 1)] - ef[1, plane(i)]
            flux_a[plane(i)] = mf[2, plane(i)] * (1.0 / h) - rise
    flux_a[plane(B - 1)] = mf[2, plane(B - 1)] * (1.0 / h) + ef[1, plane(B - 1)]
    r_top[...] = r[plane(0)]
    src_top[...] = src[plane(0)]
    x = solve_z(src[...], w[...])
    rise = ahead_z(x)
    mx = r[...] + rise
    curl[...] = c[...] * x + behind_z(mx)
    flux_y[...] = -(mx + rise)


def both_y_kernel(near, far, order, pos, got_near, own_near, *refs):
    others, refs = refs[:far], refs[far:]
    (halos, g_b, u_x, v_x, flux_b, w, c, r_top, src_top, curl_in, flux_y_in, flux_a_in, part_a, p_y, u_y, v_y) = refs[:16]
    got_far, rise_y, curl, flux_y, flux_a, g_a, g_c, msg, part, fz = refs[16:]
    top = plane(0)
    q, r = place(pos, 0, near)
    far_blocks = collect(q, order, others[0], others[1:], got_far)
    near_blocks = [stored(got_near, m, range(5)) for m in range(near)]
    ends = [b[5] for b in far_blocks]
    after_group = jnp.where(q < far - 1, pick(ends, q + 1), 0.0)
    ey_next = jnp.where(r < near - 1, halos[plane(0)], after_group)
    before_group = jnp.where(q > 0, pick(ends, q - 1), 0.0)
    hz_prev = jnp.where(r > 0, halos[plane(1)], before_group)
    curl[...] = curl_in[...]
    flux_y[...] = flux_y_in[...]
    flux_a[...] = flux_a_in[...]

    x = solve_z(src_top[...] + hz_prev * (1.0 / h), w[top])
    rise = ahead_z(x)
    mx = r_top[...] + rise
    curl[top] = c[top] * x + behind_z(mx)
    flux_y[top] = -(mx + rise)

    flux_a[plane(B - 1)] = flux_a[plane(B - 1)] - ey_next

    def source_a(j):
        f = flux_a[strided(j)]
        if j > 0:
            f = f - flux_a[strided(j - 1)]
        return part_a[strided(j)] + f

    first_a, last_a = eliminate(source_a, p_y, g_a)
    last_a = last_a - flux_a[strided(B - 1)]

    own, own_group = loaded(own_near, range(5)), loaded(others[0], range(5))
    ((before, after),) = solved_ends(
        q,
        r,
        1,
        [rows_of(b, 1) for b in near_blocks],
        [b[2:5] for b in near_blocks],
        [rows_of(b, 1) for b in far_blocks],
        [b[2:5] for b in far_blocks],
        (rows_of(own, 1), own[2:5]),
        (rows_of(own_group, 1), own_group[2:5]),
    )
    for i in range(B):
        fz[plane(i)] = g_b[plane(i)] + (u_x[plane(i)] * before + v_x[plane(i)] * after)
    my_before = jnp.where(pos[plane(0)] == 0, 0.0, fz[top] - before)
    for i in range(B):
        here = fz[plane(i)]
        rise = (fz[plane(i + 1)] if i < B - 1 else after) - here
        my = flux_b[plane(i)] + rise
        rise_y[plane(i)] = my + rise
        part[plane(i)] = c[plane(i)] * here + (my - my_before)
        my_before = my

    def source_c(j):
        f = flux_y[strided(j)]
        if j > 0:
            f = f - flux_y[strided(j - 1)]
        return part[strided(j)] + f

    first_c, last_c = eliminate(source_c, p_y, g_c)
    last_c = last_c - flux_y[strided(B - 1)]
    sent = [first_a, last_a, first_c, last_c, u_y[plane(0)], v_y[plane(0)], v_y[plane(B - 1)]]
    for k, value in enumerate(sent):
        msg[plane(k)] = value


def second_x_kernel(near, far, order, pos, got_near, own_near, *refs):
    others, refs = refs[:far], refs[far:]
    g_a, u, v, flux_a, c, curl, p_x, part, flux2, g2, ends_c, msg, got_far, fx = refs
    q, r = place(pos, 1, near)
    far_blocks = collect(q, order, others[0], others[1:], got_far)
    near_blocks = [stored(got_near, m, range(7)) for m in range(near)]
    own, own_group = loaded(own_near, range(7)), loaded(others[0], range(7))
    (before, after), (before_c, after_c) = solved_ends(
        q,
        r,
        2,
        [rows_of(b, 2) for b in near_blocks],
        [b[4:7] for b in near_blocks],
        [rows_of(b, 2) for b in far_blocks],
        [b[4:7] for b in far_blocks],
        (rows_of(own, 2), own[4:7]),
        (rows_of(own_group, 2), own_group[4:7]),
    )
    ends_c[plane(0)] = before_c
    ends_c[plane(1)] = after_c
    for j in range(B):
        fx[plane(j)] = g_a[plane(j)] + (u[plane(j)] * before + v[plane(j)] * after)
    mz_before = jnp.where(pos[plane(1)] == 0, 0.0, fx[plane(0)] - before)
    for j in range(B):
        here = fx[plane(j)]
        rise = (fx[plane(j + 1)] if j < B - 1 else after) - here
        mz = flux_a[strided(j)] + rise
        part[strided(j)] = c[strided(j)] * here + (mz - mz_before)
        flux2[strided(j)] = -(mz + rise)
        mz_before = mz

    def source(i):
        f = flux2[plane(i)]
        if i > 0:
            f = f - flux2[plane(i - 1)]
        return curl[plane(i)] + f

    first, last = eliminate(source, p_x, g2)
    msg[plane(0)] = first
    msg[plane(1)] = last - flux2[plane(B - 1)]


def second_y_kernel(ends_c, g_c, u, v, flux_y, elec, magn, full_z, new_x, sems):
    stores = [(full_z, elec.at[2]), (new_x, magn.at[0])]
    stores = [pltpu.make_async_copy(a, b, sems.at[k]) for k, (a, b) in enumerate(stores)]
    before, after = ends_c[plane(0)], ends_c[plane(1)]
    here = None
    for j in range(B):
        ahead = g_c[plane(j)] + (u[plane(j)] * before + v[plane(j)] * after)
        full_z[strided(j)] = ahead
        if j > 0:
            new_x[strided(j - 1)] = -h * (flux_y[strided(j - 1)] + (ahead - here))
        here = ahead
    new_x[strided(B - 1)] = -h * (flux_y[strided(B - 1)] + (after - here))
    for store in stores:
        store.start()
    for store in stores:
        store.wait()


def second_z_kernel(part, rise_y, z_a, z_b, z_scale, _, __, elec, magn, full_x, new_y, sems):
    stores = [(full_x, elec.at[0]), (new_y, magn.at[1])]
    stores = [pltpu.make_async_copy(a, b, sems.at[k]) for k, (a, b) in enumerate(stores)]
    a = rise_y[...]
    x = solve_factored(part[...] - behind_z(a), z_a, z_b, z_scale)
    full_x[...] = x
    stores[0].start()
    new_y[...] = h * (a - ahead_z(x))
    stores[1].start()
    for store in stores:
        store.wait()


def last_kernel(near, far, order, pos, coefs_near, coefs_far, own_b, group_b, got_near, own_near, *refs):
    others, refs = refs[:far], refs[far:]
    g, u, v, flux2, _, _, elec, magn, got_far, full_y, new_z, sems = refs
    q, r = place(pos, 0, near)
    far_blocks = collect(q, order, others[0], others[1:], got_far)
    ((before, after),) = solved_ends(
        q,
        r,
        1,
        [rows_of(stored(got_near, m, range(2)), 1) for m in range(near)],
        [stored(coefs_near, m, (2, 3, 4)) for m in range(near)],
        [rows_of(b, 1) for b in far_blocks],
        [stored(coefs_far, m, (2, 3, 4)) for m in range(far)],
        (rows_of(loaded(own_near, range(2)), 1), loaded(own_b, (2, 3, 4))),
        (rows_of(loaded(others[0], range(2)), 1), loaded(group_b, (2, 3, 4))),
    )
    stores = [(full_y, elec.at[1]), (new_z, magn.at[2])]
    stores = [pltpu.make_async_copy(a, b, sems.at[k]) for k, (a, b) in enumerate(stores)]
    for i in range(B):
        full_y[plane(i)] = g[plane(i)] + (u[plane(i)] * before + v[plane(i)] * after)
    stores[0].start()
    for i in range(B):
        rise = (full_y[plane(i + 1)] if i < B - 1 else after) - full_y[plane(i)]
        new_z[plane(i)] = -h * (flux2[plane(i)] + rise)
    stores[1].start()
    for store in stores:
        store.wait()


VMEM = pl.BlockSpec(memory_space=pltpu.VMEM)
SMEM = pl.BlockSpec(memory_space=pltpu.SMEM)
HBM = pl.BlockSpec(memory_space=pltpu.HBM)


def call(kernel, ins, outs, specs=None, out_specs=None, scratch=(), aliases=None, flops=1_000_000):
    shapes = [jax.ShapeDtypeStruct(s, F32) if isinstance(s, tuple) else s for s in outs]
    return pl.pallas_call(
        kernel,
        out_shape=shapes,
        in_specs=specs or [VMEM] * len(ins),
        out_specs=out_specs or [VMEM] * len(outs),
        scratch_shapes=[pltpu.VMEM(s, F32) if isinstance(s, tuple) else s for s in scratch],
        input_output_aliases=aliases or {},
        compiler_params=pltpu.CompilerParams(vmem_limit_bytes=24 * 1024 * 1024),
        cost_estimate=pl.CostEstimate(flops=flops, bytes_accessed=1_000_000, transcendentals=0),
    )(*ins)


def shared(value, axis, n, order, near=1, bent=(), by=0):
    masks = [near * s + (by if s in bent else 0) for s in order]
    return [value] + [lax.ppermute(value, axis, [(i, i ^ mask) for i in range(n)]) for mask in masks]


def split(n):
    near = 1 << (n.bit_length() // 2)
    return near, n // near


def local(electric, magnetic, material, permittivity, conductivity):
    nx, ny = lax.axis_size("px"), lax.axis_size("py")
    near_x, far_x = split(nx)
    near_y, far_y = split(ny)
    nz = material.shape[2]
    cells = (B * B, nz)
    me = jnp.stack([lax.axis_index("px"), lax.axis_index("py")]).astype(jnp.int32)
    in_hbm = lambda a: pltpu.with_memory_space_constraint(a, pltpu.HBM)
    elec = in_hbm(electric.reshape(3, *cells))
    magn = in_hbm(magnetic.reshape(3, *cells))
    ids = in_hbm(material.reshape(cells))
    dma = pltpu.SemaphoreType.DMA
    orders = [(1, 2, 3), (2, 1, 3), (2, 1, 3), (1, 2, 3)]
    counts = (near_x, far_x, near_y, far_y)
    px_near, px_far, py_near, py_far = [
        tuple(s for s in order if s < count) for order, count in zip(orders, counts)
    ]

    (hx_last,) = call(
        cut_kernel, [in_hbm(magnetic)], [(B, nz)], specs=[HBM], scratch=[dma(())], flops=1000
    )
    hx_prev = lax.ppermute(hx_last, "py", [(i, (i + 1) % ny) for i in range(ny)])
    w, c, p_x, u_x, v_x, flux_b, part_b, ef, mf, ez_first, pos = call(
        tables_kernel,
        [me, in_hbm(permittivity), in_hbm(conductivity), ids, elec, magn],
        [cells] * 7 + [(3, *cells)] * 2 + [(8 * B, nz), jax.ShapeDtypeStruct((2 * B, nz), jnp.int32)],
        specs=[SMEM] + [HBM] * 5,
        scratch=[pltpu.VMEM(cells, jnp.int32)] + [pltpu.SMEM(permittivity.shape, F32)] * 2 + [dma((9,))],
    )
    g_b, own_b, inner, outer = call(
        first_x_kernel,
        [pos, part_b, hx_prev, flux_b, p_x, u_x, v_x, ef, mf],
        [cells, (7 * B, nz), (6 * B, nz), (6 * B, nz)],
    )
    ins = [own_b] + [shared(outer if k == 3 else inner, "px", nx, (k,))[1] for k in px_near]
    ez_next = lax.ppermute(ez_first, "py", [((i + 1) % ny, i) for i in range(ny)])
    near_b, group_b, halos = call(
        functools.partial(merge_first_kernel, near_x),
        [pos] + ins,
        [(near_x, 5 * B, nz), (6 * B, nz), (2 * B, nz)],
    )
    ins = shared(group_b, "px", nx, px_far, near_x, (1, 3), near_x - 1)
    p_y, u_y, v_y, r_top, src_top, curl, flux_y, flux_a, part_a = call(
        functools.partial(first_z_kernel, ny),
        [pos, ef, mf, ez_next, w, c],
        [cells] * 3 + [(B, nz)] * 2 + [cells] * 4,
        scratch=[cells] * 2,
        flops=8_000_000,
    )
    ins = [pos, near_b, own_b] + ins + [halos, g_b, u_x, v_x, flux_b, w, c, r_top, src_top]
    far_b, rise_y, curl, flux_y, flux_a, g_a, g_c, own_ac = call(
        functools.partial(both_y_kernel, near_x, far_x, px_far),
        ins + [curl, flux_y, flux_a, part_a, p_y, u_y, v_y],
        [(far_x, 6 * B, nz)] + [cells] * 6 + [(7 * B, nz)],
        scratch=[cells] * 2,
    )
    ins = shared(own_ac, "py", ny, py_near)
    near_ac, msg = call(
        functools.partial(merge_kernel, 1, near_y, py_near, 2), [pos] + ins, [(near_y, 7 * B, nz), (7 * B, nz)]
    )
    msg, w = lax.optimization_barrier((msg, w))
    ins = shared(msg, "py", ny, py_far, near_y, (2,), near_y // 2)
    steps = (nz - 1).bit_length()
    z_factors = call(factors_kernel, [w], [(steps, *cells)] * 2 + [cells], flops=8_000_000)
    ins, z_factors = lax.optimization_barrier((ins, z_factors))
    part_x, flux2, g2, ends_c, own_a = call(
        functools.partial(second_x_kernel, near_y, far_y, py_far),
        [pos, near_ac, own_ac] + ins + [g_a, u_y, v_y, flux_a, c, curl, p_x],
        [cells] * 3 + [(2 * B, nz)] * 2,
        scratch=[(far_y, 7 * B, nz), cells],
    )
    ins = shared(own_a, "px", nx, px_near)
    whole = pltpu.HBM((3, *cells), F32)
    elec, magn = call(
        second_y_kernel,
        [ends_c, g_c, u_y, v_y, flux_y],
        [whole, whole],
        out_specs=[HBM] * 2,
        scratch=[cells] * 2 + [dma((2,))],
    )
    near_a, msg = call(
        functools.partial(merge_rows_kernel, 0, near_x, px_near),
        [pos, near_b] + ins,
        [(near_x, 2 * B, nz), (2 * B, nz)],
    )
    msg, elec = lax.optimization_barrier((msg, elec))
    ins = shared(msg, "px", nx, px_far, near_x, (1, 3), near_x // 2)
    elec, magn = call(
        second_z_kernel,
        [part_x, rise_y, *z_factors, elec, magn],
        [whole] * 2,
        specs=[VMEM] * 5 + [HBM] * 2,
        out_specs=[HBM] * 2,
        scratch=[cells] * 2 + [dma((2,))],
        aliases={5: 0, 6: 1},
        flops=4_000_000,
    )
    ins = [pos, near_b, far_b, own_b, group_b, near_a, own_a] + ins + [g2, u_x, v_x, flux2]
    at = len(ins)
    out = call(
        functools.partial(last_kernel, near_x, far_x, px_far),
        ins + [elec, magn],
        [whole] * 2,
        specs=[VMEM] * at + [HBM] * 2,
        out_specs=[HBM] * 2,
        scratch=[(far_x, 2 * B, nz), cells, cells, dma((2,))],
        aliases={at: 0, at + 1: 1},
    )
    return tuple(a.reshape(3, B, B, nz) for a in out)


def solution(mesh):
    placed = (P(None, "px", "py", None), P(None, "px", "py", None), P("px", "py", None), P(), P())
    return jax.shard_map(
        local,
        mesh=mesh,
        in_specs=placed,
        out_specs=(P(None, "px", "py", None), P(None, "px", "py", None)),
        check_vma=False,
    )
```

```python
import functools

import jax
import jax.numpy as jnp
from jax import lax
from jax.experimental import pallas as pl
from jax.experimental.pallas import tpu as pltpu
from jax.sharding import PartitionSpec as P

h = 32.0
B = 16
F32 = jnp.float32


def plane(i):
    return pl.ds(i * B, B)


def strided(j):
    return pl.ds(j, B, stride=B)


def lanes(v):
    return lax.broadcasted_iota(jnp.int32, v.shape, 1)


def behind_z(v):
    return v - jnp.where(lanes(v) == 0, 0.0, pltpu.roll(v, 1, 1))


def ahead_z(v):
    n = v.shape[1]
    return jnp.where(lanes(v) == n - 1, 0.0, pltpu.roll(v, n - 1, 1)) - v


def factor(w_of, first_block, p, u, v):
    d = None
    y = []
    for j in range(B):
        w = w_of(j)
        e = w + (jnp.where(first_block, 0.0, 1.0) if j == 0 else d)
        inv = 1.0 / (1.0 + e)
        d = e * inv
        p[plane(j)] = inv
        y.append(jnp.ones_like(inv) if j == 0 else y[-1] * last)
        last = inv
    uj = y[B - 1] * last
    vj = last
    u[plane(B - 1)] = uj
    v[plane(B - 1)] = vj
    for j in range(B - 2, -1, -1):
        inv = p[plane(j)]
        uj = inv * (y[j] + uj)
        vj = inv * vj
        u[plane(j)] = uj
        v[plane(j)] = vj


def eliminate(source_of, p, g):
    y = source_of(0)
    ys = [y]
    for j in range(1, B):
        y = source_of(j) + p[plane(j - 1)] * y
        ys.append(y)
    x = y * p[plane(B - 1)]
    end = x
    g[plane(B - 1)] = x
    for j in range(B - 2, -1, -1):
        x = p[plane(j)] * (ys[j] + x)
        g[plane(j)] = x
    return x, end


def boundary(me, rows, coefs, here, coef_here, outer):
    n = len(rows)
    left = [a for a, _ in outer]
    right = [b for _, b in outer]
    beta = delta = jnp.zeros_like(left[0])
    for s in range(n - 1):
        ff, fl, ll = coefs[s]
        t = fl / (1.0 - ff * beta)
        on = s < me
        left = [jnp.where(on, dl + t * (a + beta * gf), a) for a, (gf, dl) in zip(left, rows[s])]
        beta = jnp.where(on, ll + t * beta * fl, beta)
        m = n - 1 - s
        ff, fl, ll = coefs[m]
        t = fl / (1.0 - ll * delta)
        on = m > me
        right = [jnp.where(on, gf + t * (b + delta * dl), b) for b, (gf, dl) in zip(right, rows[m])]
        delta = jnp.where(on, ff + t * delta * fl, delta)
    ff, fl, ll = coef_here
    after_scale = 1.0 / (1.0 - delta * ll)
    t = fl * after_scale
    before_scale = 1.0 / (1.0 - beta * (ff + t * delta * fl))
    ends = []
    for a, b, (gf, dl) in zip(left, right, here):
        before = (a + beta * (gf + t * (b + delta * dl))) * before_scale
        ends.append((before, (b + delta * (dl + fl * before)) * after_scale))
    return ends


def merge(one, two):
    (ff1, fl1, ll1), rows1 = one
    (ff2, fl2, ll2), rows2 = two
    d = 1.0 / (1.0 - ll1 * ff2)
    t1, t2 = fl1 * d, fl2 * d
    rows = [
        (gf1 + t1 * (gf2 + ff2 * dl1), dl2 + t2 * (dl1 + ll1 * gf2))
        for (gf1, dl1), (gf2, dl2) in zip(rows1, rows2)
    ]
    return (ff1 + t1 * fl1 * ff2, t1 * fl2, ll2 + t2 * fl2 * ll1), rows


def solve_z(r, w):
    n = r.shape[1]
    lane = lanes(r)
    e = jnp.where(lane == n - 1, 0.0, 1.0)
    l = jnp.where(lane == 0, 0.0, 1.0)
    s = w + jnp.where(lane == n - 1, 1.0, 0.0)
    step = 1
    while step < n:
        inv = 1.0 / (s + (l + e))
        a, b = e * inv, l * inv
        r = r + (pltpu.roll(a * r, step, 1) + pltpu.roll(b * r, n - step, 1))
        s = s + (pltpu.roll(a * s, step, 1) + pltpu.roll(b * s, n - step, 1))
        g = a * l
        if 2 * step < n:
            e, l = pltpu.roll(g, n - step, 1), pltpu.roll(g, step, 1)
        step *= 2
    return r / s


def factors_kernel(w_in, a_out, b_out, scale):
    w = w_in[...]
    n = w.shape[1]
    lane = lanes(w)
    e = jnp.where(lane == n - 1, 0.0, 1.0)
    l = jnp.where(lane == 0, 0.0, 1.0)
    s = w + jnp.where(lane == n - 1, 1.0, 0.0)
    for k in range(a_out.shape[0]):
        step = 1 << k
        inv = 1.0 / (s + (l + e))
        a, b = e * inv, l * inv
        a_out[k] = a
        b_out[k] = b
        s = s + (pltpu.roll(a * s, step, 1) + pltpu.roll(b * s, n - step, 1))
        g = a * l
        e, l = pltpu.roll(g, n - step, 1), pltpu.roll(g, step, 1)
    scale[...] = 1.0 / s


def solve_factored(r, a, b, scale):
    n = r.shape[1]
    for k in range(a.shape[0]):
        step = 1 << k
        r = r + (pltpu.roll(a[k] * r, step, 1) + pltpu.roll(b[k] * r, n - step, 1))
    return r * scale[...]


def collect(r, order, own, others, got):
    refs = [own] + [others[order.index(s)] for s in range(1, len(order) + 1)]
    return ordered(r, [loaded(ref, range(got.shape[1] // B)) for ref in refs], got)


def ordered(r, found, got):
    count = len(found)
    blocks = [[] for _ in found]
    for k in range(got.shape[1] // B):
        values = [planes[k] for planes in found]
        bit = 1
        while bit < count:
            swap = lax.bitwise_and(r, bit) != 0
            values = [jnp.where(swap, values[m ^ bit], values[m]) for m in range(count)]
            bit *= 2
        for m, value in enumerate(values):
            got[m, plane(k)] = value
            blocks[m].append(value)
    return blocks


def rows_of(block, sources):
    return [(block[2 * k], block[2 * k + 1]) for k in range(sources)]


def stored(got, m, planes):
    return [got[m, plane(k)] for k in planes]


def loaded(msg, planes):
    return [msg[plane(k)] for k in planes]


def pick(values, index):
    out = values[0]
    for k in range(1, len(values)):
        out = jnp.where(index == k, values[k], out)
    return out


def place(pos, axis, near):
    here = pos[plane(axis)]
    return lax.shift_right_logical(here, near.bit_length() - 1), lax.bitwise_and(here, near - 1)


def cut_kernel(magn, hx_last, sem):
    load = pltpu.make_async_copy(magn.at[0, :, B - 1], hx_last, sem)
    load.start()
    load.wait()


def tables_kernel(
    me, eps_in, sig_in, material, elec_in, magn_in, w, c, p, u, v, flux, part, elec, magn, ez_first, pos, ids, eps, sig, sems
):
    loads = [(eps_in, eps), (sig_in, sig), (material, ids)]
    for field, to, k in ((elec_in, elec, 0), (magn_in, magn, 1), (elec_in, elec, 2), (magn_in, magn, 0)):
        loads.append((field.at[k], to.at[k]))
    loads += [(elec_in.at[1], elec.at[1]), (magn_in.at[2], magn.at[2])]
    loads = [pltpu.make_async_copy(a, b, sems.at[k]) for k, (a, b) in enumerate(loads)]
    for load in loads:
        load.start()
    for axis in range(2):
        pos[plane(axis)] = jnp.full((B, w.shape[1]), me[axis], jnp.int32)
    for load in loads[:3]:
        load.wait()
    ws = [eps[m] * (1.0 / (h * h)) + sig[m] * (0.5 / h) for m in range(eps.shape[0])]
    cs = [eps[m] * (1.0 / (h * h)) - sig[m] * (0.5 / h) for m in range(eps.shape[0])]
    for i in range(B):
        cell = ids[plane(i)]
        wi = jnp.full(cell.shape, ws[0], F32)
        ci = jnp.full(cell.shape, cs[0], F32)
        for m in range(1, len(ws)):
            wi = jnp.where(cell == m, ws[m], wi)
            ci = jnp.where(cell == m, cs[m], ci)
        w[plane(i)] = wi
        c[plane(i)] = ci
    factor(lambda i: w[plane(i)], me[0] == 0, p, u, v)
    for load in loads[3:7]:
        load.wait()
    row = lax.broadcasted_iota(jnp.int32, (B, w.shape[1]), 0)
    for i in range(B):
        q = magn[1, plane(i)] * (1.0 / h) - ahead_z(elec[0, plane(i)])
        flux[plane(i)] = q
        if i > 0:
            q = q - flux[plane(i - 1)]
        here = magn[0, plane(i)]
        before = jnp.where(row == 0, 0.0, pltpu.roll(here, 1, 0))
        part[plane(i)] = c[plane(i)] * elec[2, plane(i)] + (q - (here - before) * (1.0 / h))
    for k in range(ez_first.shape[0] // B):
        ez_first[plane(k)] = elec.at[2][strided(0)]
    for load in loads[7:]:
        load.wait()


def first_x_kernel(pos, part, hx_prev, flux, p, u, v, elec, magn, g, msg, inner, outer):
    row = lax.broadcasted_iota(jnp.int32, hx_prev.shape, 0)
    scale = jnp.where(pos[plane(1)] == 0, 0.0, jnp.where(row == 0, 1.0 / h, 0.0))

    def source(i):
        return part[plane(i)] + hx_prev[pl.ds(i, 1)] * scale

    first, last = eliminate(source, p, g)
    msg[plane(0)] = first
    msg[plane(1)] = last - flux[plane(B - 1)]
    msg[plane(2)] = u[plane(0)]
    msg[plane(3)] = v[plane(0)]
    msg[plane(4)] = v[plane(B - 1)]
    msg[plane(5)] = elec[1, plane(0)]
    msg[plane(6)] = magn[2, plane(B - 1)]
    even = lax.bitwise_and(pos[plane(0)], 1) == 0
    for sent, halo in ((inner, (6, 5)), (outer, (5, 6))):
        sent[pl.ds(0, 5 * B)] = msg[pl.ds(0, 5 * B)]
        sent[plane(5)] = jnp.where(even, msg[plane(halo[0])], msg[plane(halo[1])])


def merged(blocks):
    while len(blocks) > 1:
        blocks = [merge(a, b) for a, b in zip(blocks[::2], blocks[1::2])]
    return blocks[0]


def merge_kernel(axis, near, order, sources, pos, *refs):
    got, msg = refs[-2:]
    blocks = collect(place(pos, axis, near)[1], order, refs[0], refs[1:near], got)
    at = 2 * sources
    coefs, rows = merged([(b[at : at + 3], rows_of(b, sources)) for b in blocks])
    for k, value in enumerate([v for pair in rows for v in pair] + list(coefs)):
        msg[plane(k)] = value


def merge_first_kernel(near, pos, own, *refs):
    got, msg, halos = refs[-3:]
    r = place(pos, 0, near)[1]
    blocks = ordered(r, [loaded(ref, range(5)) for ref in (own, *refs[: near - 1])], got)
    coefs, rows = merged([(b[2:5], rows_of(b, 1)) for b in blocks])
    for k, value in enumerate([*rows[0], *coefs, jnp.where(r == 0, own[plane(5)], own[plane(6)])]):
        msg[plane(k)] = value
    inner, outer = refs[0][plane(5)], refs[near - 2][plane(5)]
    odd = lax.bitwise_and(r, 1) == 1
    halos[plane(0)] = jnp.where(odd, outer, inner)
    halos[plane(1)] = jnp.where(odd, inner, outer)


def merge_rows_kernel(axis, near, order, pos, coefs, *refs):
    got, msg = refs[-2:]
    blocks = collect(place(pos, axis, near)[1], order, refs[0], refs[1:near], got)
    _, rows = merged([(stored(coefs, m, (2, 3, 4)), rows_of(b, 1)) for m, b in enumerate(blocks)])
    msg[plane(0)], msg[plane(1)] = rows[0]


def solved_ends(q, r, sources, near_rows, near_coefs, far_rows, far_coefs, own_near, own_far):
    zero = jnp.zeros_like(far_coefs[0][0])
    outer = boundary(q, far_rows, far_coefs, *own_far, [(zero, zero)] * sources)
    return boundary(r, near_rows, near_coefs, *own_near, outer)


def first_z_kernel(n, pos, ef, mf, ez_next, w, c, p, u, v, r_top, src_top, curl, flux_y, flux_a, part_a, src, r):
    factor(lambda j: w[strided(j)], pos[plane(1)] == 0, p, u, v)
    inside = jnp.where(pos[pl.ds(B, 1)] == n - 1, 0.0, 1.0)
    row = lax.broadcasted_iota(jnp.int32, (B, w.shape[1]), 0)
    for i in range(B):
        ez = ef[2, plane(i)]
        after = jnp.where(row == B - 1, ez_next[pl.ds(i, 1)] * inside, pltpu.roll(ez, B - 1, 0))
        ri = mf[0, plane(i)] * (1.0 / h) - (after - ez)
        r[plane(i)] = ri
        gain = mf[2, plane(i)]
        if i > 0:
            gain = gain - mf[2, plane(i - 1)]
        src[plane(i)] = c[plane(i)] * ef[1, plane(i)] + (behind_z(ri) - gain * (1.0 / h))
        part_a[plane(i)] = c[plane(i)] * ef[0, plane(i)] - behind_z(mf[1, plane(i)]) * (1.0 / h)
        if i < B - 1:
            rise = ef[1, plane(i + 1)] - ef[1, plane(i)]
            flux_a[plane(i)] = mf[2, plane(i)] * (1.0 / h) - rise
    flux_a[plane(B - 1)] = mf[2, plane(B - 1)] * (1.0 / h) + ef[1, plane(B - 1)]
    r_top[...] = r[plane(0)]
    src_top[...] = src[plane(0)]
    x = solve_z(src[...], w[...])
    rise = ahead_z(x)
    mx = r[...] + rise
    curl[...] = c[...] * x + behind_z(mx)
    flux_y[...] = -(mx + rise)


def both_y_kernel(near, far, order, pos, got_near, own_near, *refs):
    others, refs = refs[:far], refs[far:]
    (halos, g_b, u_x, v_x, flux_b, w, c, r_top, src_top, curl_in, flux_y_in, flux_a_in, part_a, p_y, u_y, v_y) = refs[:16]
    got_far, rise_y, curl, flux_y, flux_a, g_a, g_c, msg, part, fz = refs[16:]
    top = plane(0)
    q, r = place(pos, 0, near)
    far_blocks = collect(q, order, others[0], others[1:], got_far)
    near_blocks = [stored(got_near, m, range(5)) for m in range(near)]
    ends = [b[5] for b in far_blocks]
    after_group = jnp.where(q < far - 1, pick(ends, q + 1), 0.0)
    ey_next = jnp.where(r < near - 1, halos[plane(0)], after_group)
    before_group = jnp.where(q > 0, pick(ends, q - 1), 0.0)
    hz_prev = jnp.where(r > 0, halos[plane(1)], before_group)
    curl[...] = curl_in[...]
    flux_y[...] = flux_y_in[...]
    flux_a[...] = flux_a_in[...]

    x = solve_z(src_top[...] + hz_prev * (1.0 / h), w[top])
    rise = ahead_z(x)
    mx = r_top[...] + rise
    curl[top] = c[top] * x + behind_z(mx)
    flux_y[top] = -(mx + rise)

    flux_a[plane(B - 1)] = flux_a[plane(B - 1)] - ey_next

    def source_a(j):
        f = flux_a[strided(j)]
        if j > 0:
            f = f - flux_a[strided(j - 1)]
        return part_a[strided(j)] + f

    first_a, last_a = eliminate(source_a, p_y, g_a)
    last_a = last_a - flux_a[strided(B - 1)]

    own, own_group = loaded(own_near, range(5)), loaded(others[0], range(5))
    ((before, after),) = solved_ends(
        q,
        r,
        1,
        [rows_of(b, 1) for b in near_blocks],
        [b[2:5] for b in near_blocks],
        [rows_of(b, 1) for b in far_blocks],
        [b[2:5] for b in far_blocks],
        (rows_of(own, 1), own[2:5]),
        (rows_of(own_group, 1), own_group[2:5]),
    )
    for i in range(B):
        fz[plane(i)] = g_b[plane(i)] + (u_x[plane(i)] * before + v_x[plane(i)] * after)
    my_before = jnp.where(pos[plane(0)] == 0, 0.0, fz[top] - before)
    for i in range(B):
        here = fz[plane(i)]
        rise = (fz[plane(i + 1)] if i < B - 1 else after) - here
        my = flux_b[plane(i)] + rise
        rise_y[plane(i)] = my + rise
        part[plane(i)] = c[plane(i)] * here + (my - my_before)
        my_before = my

    def source_c(j):
        f = flux_y[strided(j)]
        if j > 0:
            f = f - flux_y[strided(j - 1)]
        return part[strided(j)] + f

    first_c, last_c = eliminate(source_c, p_y, g_c)
    last_c = last_c - flux_y[strided(B - 1)]
    sent = [first_a, last_a, first_c, last_c, u_y[plane(0)], v_y[plane(0)], v_y[plane(B - 1)]]
    for k, value in enumerate(sent):
        msg[plane(k)] = value


def second_x_kernel(near, far, order, pos, got_near, own_near, *refs):
    others, refs = refs[:far], refs[far:]
    g_a, u, v, flux_a, c, curl, p_x, part, flux2, g2, ends_c, msg, got_far, fx = refs
    q, r = place(pos, 1, near)
    far_blocks = collect(q, order, others[0], others[1:], got_far)
    near_blocks = [stored(got_near, m, range(7)) for m in range(near)]
    own, own_group = loaded(own_near, range(7)), loaded(others[0], range(7))
    (before, after), (before_c, after_c) = solved_ends(
        q,
        r,
        2,
        [rows_of(b, 2) for b in near_blocks],
        [b[4:7] for b in near_blocks],
        [rows_of(b, 2) for b in far_blocks],
        [b[4:7] for b in far_blocks],
        (rows_of(own, 2), own[4:7]),
        (rows_of(own_group, 2), own_group[4:7]),
    )
    ends_c[plane(0)] = before_c
    ends_c[plane(1)] = after_c
    for j in range(B):
        fx[plane(j)] = g_a[plane(j)] + (u[plane(j)] * before + v[plane(j)] * after)
    mz_before = jnp.where(pos[plane(1)] == 0, 0.0, fx[plane(0)] - before)
    for j in range(B):
        here = fx[plane(j)]
        rise = (fx[plane(j + 1)] if j < B - 1 else after) - here
        mz = flux_a[strided(j)] + rise
        part[strided(j)] = c[strided(j)] * here + (mz - mz_before)
        flux2[strided(j)] = -(mz + rise)
        mz_before = mz

    def source(i):
        f = flux2[plane(i)]
        if i > 0:
            f = f - flux2[plane(i - 1)]
        return curl[plane(i)] + f

    first, last = eliminate(source, p_x, g2)
    msg[plane(0)] = first
    msg[plane(1)] = last - flux2[plane(B - 1)]


def second_y_kernel(ends_c, g_c, u, v, flux_y, elec, magn, full_z, new_x, sems):
    stores = [(full_z, elec.at[2]), (new_x, magn.at[0])]
    stores = [pltpu.make_async_copy(a, b, sems.at[k]) for k, (a, b) in enumerate(stores)]
    before, after = ends_c[plane(0)], ends_c[plane(1)]
    here = None
    for j in range(B):
        ahead = g_c[plane(j)] + (u[plane(j)] * before + v[plane(j)] * after)
        full_z[strided(j)] = ahead
        if j > 0:
            new_x[strided(j - 1)] = -h * (flux_y[strided(j - 1)] + (ahead - here))
        here = ahead
    new_x[strided(B - 1)] = -h * (flux_y[strided(B - 1)] + (after - here))
    for store in stores:
        store.start()
    for store in stores:
        store.wait()


def second_z_kernel(part, rise_y, z_a, z_b, z_scale, _, __, elec, magn, full_x, new_y, sems):
    stores = [(full_x, elec.at[0]), (new_y, magn.at[1])]
    stores = [pltpu.make_async_copy(a, b, sems.at[k]) for k, (a, b) in enumerate(stores)]
    a = rise_y[...]
    x = solve_factored(part[...] - behind_z(a), z_a, z_b, z_scale)
    full_x[...] = x
    stores[0].start()
    new_y[...] = h * (a - ahead_z(x))
    stores[1].start()
    for store in stores:
        store.wait()


def last_kernel(near, far, order, pos, coefs_near, coefs_far, own_b, group_b, got_near, own_near, *refs):
    others, refs = refs[:far], refs[far:]
    g, u, v, flux2, _, _, elec, magn, got_far, full_y, new_z, sems = refs
    q, r = place(pos, 0, near)
    far_blocks = collect(q, order, others[0], others[1:], got_far)
    ((before, after),) = solved_ends(
        q,
        r,
        1,
        [rows_of(stored(got_near, m, range(2)), 1) for m in range(near)],
        [stored(coefs_near, m, (2, 3, 4)) for m in range(near)],
        [rows_of(b, 1) for b in far_blocks],
        [stored(coefs_far, m, (2, 3, 4)) for m in range(far)],
        (rows_of(loaded(own_near, range(2)), 1), loaded(own_b, (2, 3, 4))),
        (rows_of(loaded(others[0], range(2)), 1), loaded(group_b, (2, 3, 4))),
    )
    def store(value, field, k, part, sem):
        rows = pl.ds(part * 4 * B, 4 * B)
        copy = pltpu.make_async_copy(value.at[rows], field.at[k, rows], sems.at[sem])
        copy.start()
        return copy

    stores = []
    for i in range(B):
        full_y[plane(i)] = g[plane(i)] + (u[plane(i)] * before + v[plane(i)] * after)
        if i % 4 == 3:
            stores.append(store(full_y, elec, 1, i // 4, i // 4))
    for i in range(B):
        rise = (full_y[plane(i + 1)] if i < B - 1 else after) - full_y[plane(i)]
        new_z[plane(i)] = -h * (flux2[plane(i)] + rise)
        if i % 4 == 3:
            stores.append(store(new_z, magn, 2, i // 4, 4 + i // 4))
    for copy in stores:
        copy.wait()


VMEM = pl.BlockSpec(memory_space=pltpu.VMEM)
SMEM = pl.BlockSpec(memory_space=pltpu.SMEM)
HBM = pl.BlockSpec(memory_space=pltpu.HBM)


def call(kernel, ins, outs, specs=None, out_specs=None, scratch=(), aliases=None, flops=1_000_000):
    shapes = [jax.ShapeDtypeStruct(s, F32) if isinstance(s, tuple) else s for s in outs]
    return pl.pallas_call(
        kernel,
        out_shape=shapes,
        in_specs=specs or [VMEM] * len(ins),
        out_specs=out_specs or [VMEM] * len(outs),
        scratch_shapes=[pltpu.VMEM(s, F32) if isinstance(s, tuple) else s for s in scratch],
        input_output_aliases=aliases or {},
        compiler_params=pltpu.CompilerParams(vmem_limit_bytes=24 * 1024 * 1024),
        cost_estimate=pl.CostEstimate(flops=flops, bytes_accessed=1_000_000, transcendentals=0),
    )(*ins)


def shared(value, axis, n, order, near=1, bent=(), by=0):
    masks = [near * s + (by if s in bent else 0) for s in order]
    return [value] + [lax.ppermute(value, axis, [(i, i ^ mask) for i in range(n)]) for mask in masks]


def split(n):
    near = 1 << (n.bit_length() // 2)
    return near, n // near


def local(electric, magnetic, material, permittivity, conductivity):
    nx, ny = lax.axis_size("px"), lax.axis_size("py")
    near_x, far_x = split(nx)
    near_y, far_y = split(ny)
    nz = material.shape[2]
    cells = (B * B, nz)
    me = jnp.stack([lax.axis_index("px"), lax.axis_index("py")]).astype(jnp.int32)
    in_hbm = lambda a: pltpu.with_memory_space_constraint(a, pltpu.HBM)
    elec = in_hbm(electric.reshape(3, *cells))
    magn = in_hbm(magnetic.reshape(3, *cells))
    ids = in_hbm(material.reshape(cells))
    dma = pltpu.SemaphoreType.DMA
    orders = [(1, 2, 3), (2, 1, 3), (2, 1, 3), (1, 2, 3)]
    counts = (near_x, far_x, near_y, far_y)
    px_near, px_far, py_near, py_far = [
        tuple(s for s in order if s < count) for order, count in zip(orders, counts)
    ]

    (hx_last,) = call(
        cut_kernel, [in_hbm(magnetic)], [(B, nz)], specs=[HBM], scratch=[dma(())], flops=1000
    )
    hx_prev = lax.ppermute(hx_last, "py", [(i, (i + 1) % ny) for i in range(ny)])
    w, c, p_x, u_x, v_x, flux_b, part_b, ef, mf, ez_first, pos = call(
        tables_kernel,
        [me, in_hbm(permittivity), in_hbm(conductivity), ids, elec, magn],
        [cells] * 7 + [(3, *cells)] * 2 + [(8 * B, nz), jax.ShapeDtypeStruct((2 * B, nz), jnp.int32)],
        specs=[SMEM] + [HBM] * 5,
        scratch=[pltpu.VMEM(cells, jnp.int32)] + [pltpu.SMEM(permittivity.shape, F32)] * 2 + [dma((9,))],
    )
    g_b, own_b, inner, outer = call(
        first_x_kernel,
        [pos, part_b, hx_prev, flux_b, p_x, u_x, v_x, ef, mf],
        [cells, (7 * B, nz), (6 * B, nz), (6 * B, nz)],
    )
    ins = [own_b] + [shared(outer if k == 3 else inner, "px", nx, (k,))[1] for k in px_near]
    ez_next = lax.ppermute(ez_first, "py", [((i + 1) % ny, i) for i in range(ny)])
    near_b, group_b, halos = call(
        functools.partial(merge_first_kernel, near_x),
        [pos] + ins,
        [(near_x, 5 * B, nz), (6 * B, nz), (2 * B, nz)],
    )
    ins = shared(group_b, "px", nx, px_far, near_x, (1, 3), near_x - 1)
    p_y, u_y, v_y, r_top, src_top, curl, flux_y, flux_a, part_a = call(
        functools.partial(first_z_kernel, ny),
        [pos, ef, mf, ez_next, w, c],
        [cells] * 3 + [(B, nz)] * 2 + [cells] * 4,
        scratch=[cells] * 2,
        flops=8_000_000,
    )
    ins = [pos, near_b, own_b] + ins + [halos, g_b, u_x, v_x, flux_b, w, c, r_top, src_top]
    far_b, rise_y, curl, flux_y, flux_a, g_a, g_c, own_ac = call(
        functools.partial(both_y_kernel, near_x, far_x, px_far),
        ins + [curl, flux_y, flux_a, part_a, p_y, u_y, v_y],
        [(far_x, 6 * B, nz)] + [cells] * 6 + [(7 * B, nz)],
        scratch=[cells] * 2,
    )
    ins = shared(own_ac, "py", ny, py_near)
    near_ac, msg = call(
        functools.partial(merge_kernel, 1, near_y, py_near, 2), [pos] + ins, [(near_y, 7 * B, nz), (7 * B, nz)]
    )
    msg, w = lax.optimization_barrier((msg, w))
    ins = shared(msg, "py", ny, py_far, near_y, (2,), near_y // 2)
    steps = (nz - 1).bit_length()
    z_factors = call(factors_kernel, [w], [(steps, *cells)] * 2 + [cells], flops=8_000_000)
    ins, z_factors = lax.optimization_barrier((ins, z_factors))
    part_x, flux2, g2, ends_c, own_a = call(
        functools.partial(second_x_kernel, near_y, far_y, py_far),
        [pos, near_ac, own_ac] + ins + [g_a, u_y, v_y, flux_a, c, curl, p_x],
        [cells] * 3 + [(2 * B, nz)] * 2,
        scratch=[(far_y, 7 * B, nz), cells],
    )
    ins = shared(own_a, "px", nx, px_near)
    whole = pltpu.HBM((3, *cells), F32)
    elec, magn = call(
        second_y_kernel,
        [ends_c, g_c, u_y, v_y, flux_y],
        [whole, whole],
        out_specs=[HBM] * 2,
        scratch=[cells] * 2 + [dma((2,))],
    )
    near_a, msg = call(
        functools.partial(merge_rows_kernel, 0, near_x, px_near),
        [pos, near_b] + ins,
        [(near_x, 2 * B, nz), (2 * B, nz)],
    )
    msg, elec = lax.optimization_barrier((msg, elec))
    ins = shared(msg, "px", nx, px_far, near_x, (1, 3), near_x // 2)
    elec, magn = call(
        second_z_kernel,
        [part_x, rise_y, *z_factors, elec, magn],
        [whole] * 2,
        specs=[VMEM] * 5 + [HBM] * 2,
        out_specs=[HBM] * 2,
        scratch=[cells] * 2 + [dma((2,))],
        aliases={5: 0, 6: 1},
        flops=4_000_000,
    )
    ins = [pos, near_b, far_b, own_b, group_b, near_a, own_a] + ins + [g2, u_x, v_x, flux2]
    at = len(ins)
    out = call(
        functools.partial(last_kernel, near_x, far_x, px_far),
        ins + [elec, magn],
        [whole] * 2,
        specs=[VMEM] * at + [HBM] * 2,
        out_specs=[HBM] * 2,
        scratch=[(far_x, 2 * B, nz), cells, cells, dma((8,))],
        aliases={at: 0, at + 1: 1},
    )
    return tuple(a.reshape(3, B, B, nz) for a in out)


def solution(mesh):
    placed = (P(None, "px", "py", None), P(None, "px", "py", None), P("px", "py", None), P(), P())
    return jax.shard_map(
        local,
        mesh=mesh,
        in_specs=placed,
        out_specs=(P(None, "px", "py", None), P(None, "px", "py", None)),
        check_vma=False,
    )
```

```python
import functools

import jax
import jax.numpy as jnp
from jax import lax
from jax.experimental import pallas as pl
from jax.experimental.pallas import tpu as pltpu
from jax.sharding import PartitionSpec as P

h = 32.0
B = 16
F32 = jnp.float32


def plane(i):
    return pl.ds(i * B, B)


def strided(j):
    return pl.ds(j, B, stride=B)


def lanes(v):
    return lax.broadcasted_iota(jnp.int32, v.shape, 1)


def behind_z(v):
    return v - jnp.where(lanes(v) == 0, 0.0, pltpu.roll(v, 1, 1))


def ahead_z(v):
    n = v.shape[1]
    return jnp.where(lanes(v) == n - 1, 0.0, pltpu.roll(v, n - 1, 1)) - v


def factor(w_of, first_block, p, u, v):
    d = None
    y = []
    for j in range(B):
        w = w_of(j)
        e = w + (jnp.where(first_block, 0.0, 1.0) if j == 0 else d)
        inv = 1.0 / (1.0 + e)
        d = e * inv
        p[plane(j)] = inv
        y.append(jnp.ones_like(inv) if j == 0 else y[-1] * last)
        last = inv
    uj = y[B - 1] * last
    vj = last
    u[plane(B - 1)] = uj
    v[plane(B - 1)] = vj
    for j in range(B - 2, -1, -1):
        inv = p[plane(j)]
        uj = inv * (y[j] + uj)
        vj = inv * vj
        u[plane(j)] = uj
        v[plane(j)] = vj


def eliminate(source_of, p, g):
    y = source_of(0)
    ys = [y]
    for j in range(1, B):
        y = source_of(j) + p[plane(j - 1)] * y
        ys.append(y)
    x = y * p[plane(B - 1)]
    end = x
    g[plane(B - 1)] = x
    for j in range(B - 2, -1, -1):
        x = p[plane(j)] * (ys[j] + x)
        g[plane(j)] = x
    return x, end


def boundary(me, rows, coefs, here, coef_here, outer):
    n = len(rows)
    left = [a for a, _ in outer]
    right = [b for _, b in outer]
    beta = delta = jnp.zeros_like(left[0])
    for s in range(n - 1):
        ff, fl, ll = coefs[s]
        t = fl / (1.0 - ff * beta)
        on = s < me
        left = [jnp.where(on, dl + t * (a + beta * gf), a) for a, (gf, dl) in zip(left, rows[s])]
        beta = jnp.where(on, ll + t * beta * fl, beta)
        m = n - 1 - s
        ff, fl, ll = coefs[m]
        t = fl / (1.0 - ll * delta)
        on = m > me
        right = [jnp.where(on, gf + t * (b + delta * dl), b) for b, (gf, dl) in zip(right, rows[m])]
        delta = jnp.where(on, ff + t * delta * fl, delta)
    ff, fl, ll = coef_here
    after_scale = 1.0 / (1.0 - delta * ll)
    t = fl * after_scale
    before_scale = 1.0 / (1.0 - beta * (ff + t * delta * fl))
    ends = []
    for a, b, (gf, dl) in zip(left, right, here):
        before = (a + beta * (gf + t * (b + delta * dl))) * before_scale
        ends.append((before, (b + delta * (dl + fl * before)) * after_scale))
    return ends


def merge(one, two):
    (ff1, fl1, ll1), rows1 = one
    (ff2, fl2, ll2), rows2 = two
    d = 1.0 / (1.0 - ll1 * ff2)
    t1, t2 = fl1 * d, fl2 * d
    rows = [
        (gf1 + t1 * (gf2 + ff2 * dl1), dl2 + t2 * (dl1 + ll1 * gf2))
        for (gf1, dl1), (gf2, dl2) in zip(rows1, rows2)
    ]
    return (ff1 + t1 * fl1 * ff2, t1 * fl2, ll2 + t2 * fl2 * ll1), rows


def solve_z(r, w):
    n = r.shape[1]
    lane = lanes(r)
    e = jnp.where(lane == n - 1, 0.0, 1.0)
    l = jnp.where(lane == 0, 0.0, 1.0)
    s = w + jnp.where(lane == n - 1, 1.0, 0.0)
    step = 1
    while step < n:
        inv = 1.0 / (s + (l + e))
        a, b = e * inv, l * inv
        r = r + (pltpu.roll(a * r, step, 1) + pltpu.roll(b * r, n - step, 1))
        s = s + (pltpu.roll(a * s, step, 1) + pltpu.roll(b * s, n - step, 1))
        g = a * l
        if 2 * step < n:
            e, l = pltpu.roll(g, n - step, 1), pltpu.roll(g, step, 1)
        step *= 2
    return r / s


def factors_kernel(w_in, a_out, b_out, scale):
    w = w_in[...]
    n = w.shape[1]
    lane = lanes(w)
    e = jnp.where(lane == n - 1, 0.0, 1.0)
    l = jnp.where(lane == 0, 0.0, 1.0)
    s = w + jnp.where(lane == n - 1, 1.0, 0.0)
    for k in range(a_out.shape[0]):
        step = 1 << k
        inv = 1.0 / (s + (l + e))
        a, b = e * inv, l * inv
        a_out[k] = a
        b_out[k] = b
        s = s + (pltpu.roll(a * s, step, 1) + pltpu.roll(b * s, n - step, 1))
        g = a * l
        e, l = pltpu.roll(g, n - step, 1), pltpu.roll(g, step, 1)
    scale[...] = 1.0 / s


def solve_factored(r, a, b, scale):
    n = r.shape[1]
    for k in range(a.shape[0]):
        step = 1 << k
        r = r + (pltpu.roll(a[k] * r, step, 1) + pltpu.roll(b[k] * r, n - step, 1))
    return r * scale[...]


def collect(r, order, own, others, got):
    refs = [own] + [others[order.index(s)] for s in range(1, len(order) + 1)]
    return ordered(r, [loaded(ref, range(got.shape[1] // B)) for ref in refs], got)


def ordered(r, found, got):
    count = len(found)
    blocks = [[] for _ in found]
    for k in range(got.shape[1] // B):
        values = [planes[k] for planes in found]
        bit = 1
        while bit < count:
            swap = lax.bitwise_and(r, bit) != 0
            values = [jnp.where(swap, values[m ^ bit], values[m]) for m in range(count)]
            bit *= 2
        for m, value in enumerate(values):
            got[m, plane(k)] = value
            blocks[m].append(value)
    return blocks


def rows_of(block, sources):
    return [(block[2 * k], block[2 * k + 1]) for k in range(sources)]


def stored(got, m, planes):
    return [got[m, plane(k)] for k in planes]


def loaded(msg, planes):
    return [msg[plane(k)] for k in planes]


def pick(values, index):
    out = values[0]
    for k in range(1, len(values)):
        out = jnp.where(index == k, values[k], out)
    return out


def place(pos, axis, near):
    here = pos[plane(axis)]
    return lax.shift_right_logical(here, near.bit_length() - 1), lax.bitwise_and(here, near - 1)


def cut_kernel(magn, hx_last, sem):
    load = pltpu.make_async_copy(magn.at[0, :, B - 1], hx_last, sem)
    load.start()
    load.wait()


def tables_kernel(
    me, eps_in, sig_in, material, elec_in, magn_in, w, c, p, u, v, flux, part, elec, magn, ez_first, pos, ids, eps, sig, sems
):
    loads = [(eps_in, eps), (sig_in, sig), (material, ids)]
    for field, to, k in ((elec_in, elec, 0), (magn_in, magn, 1), (elec_in, elec, 2), (magn_in, magn, 0)):
        loads.append((field.at[k], to.at[k]))
    loads += [(elec_in.at[1], elec.at[1]), (magn_in.at[2], magn.at[2])]
    loads = [pltpu.make_async_copy(a, b, sems.at[k]) for k, (a, b) in enumerate(loads)]
    for load in loads:
        load.start()
    for axis in range(2):
        pos[plane(axis)] = jnp.full((B, w.shape[1]), me[axis], jnp.int32)
    for load in loads[:3]:
        load.wait()
    ws = [eps[m] * (1.0 / (h * h)) + sig[m] * (0.5 / h) for m in range(eps.shape[0])]
    cs = [eps[m] * (1.0 / (h * h)) - sig[m] * (0.5 / h) for m in range(eps.shape[0])]
    for i in range(B):
        cell = ids[plane(i)]
        wi = jnp.full(cell.shape, ws[0], F32)
        ci = jnp.full(cell.shape, cs[0], F32)
        for m in range(1, len(ws)):
            wi = jnp.where(cell == m, ws[m], wi)
            ci = jnp.where(cell == m, cs[m], ci)
        w[plane(i)] = wi
        c[plane(i)] = ci
    factor(lambda i: w[plane(i)], me[0] == 0, p, u, v)
    for load in loads[3:7]:
        load.wait()
    row = lax.broadcasted_iota(jnp.int32, (B, w.shape[1]), 0)
    for i in range(B):
        q = magn[1, plane(i)] * (1.0 / h) - ahead_z(elec[0, plane(i)])
        flux[plane(i)] = q
        if i > 0:
            q = q - flux[plane(i - 1)]
        here = magn[0, plane(i)]
        before = jnp.where(row == 0, 0.0, pltpu.roll(here, 1, 0))
        part[plane(i)] = c[plane(i)] * elec[2, plane(i)] + (q - (here - before) * (1.0 / h))
    for k in range(ez_first.shape[0] // B):
        ez_first[plane(k)] = elec.at[2][strided(0)]
    for load in loads[7:]:
        load.wait()


def first_x_kernel(pos, part, hx_prev, flux, p, u, v, elec, magn, g, msg, inner, outer):
    row = lax.broadcasted_iota(jnp.int32, hx_prev.shape, 0)
    scale = jnp.where(pos[plane(1)] == 0, 0.0, jnp.where(row == 0, 1.0 / h, 0.0))

    def source(i):
        return part[plane(i)] + hx_prev[pl.ds(i, 1)] * scale

    first, last = eliminate(source, p, g)
    msg[plane(0)] = first
    msg[plane(1)] = last - flux[plane(B - 1)]
    msg[plane(2)] = u[plane(0)]
    msg[plane(3)] = v[plane(0)]
    msg[plane(4)] = v[plane(B - 1)]
    msg[plane(5)] = elec[1, plane(0)]
    msg[plane(6)] = magn[2, plane(B - 1)]
    even = lax.bitwise_and(pos[plane(0)], 1) == 0
    for sent, halo in ((inner, (6, 5)), (outer, (5, 6))):
        sent[pl.ds(0, 5 * B)] = msg[pl.ds(0, 5 * B)]
        sent[plane(5)] = jnp.where(even, msg[plane(halo[0])], msg[plane(halo[1])])


def merged(blocks):
    while len(blocks) > 1:
        blocks = [merge(a, b) for a, b in zip(blocks[::2], blocks[1::2])]
    return blocks[0]


def merge_kernel(axis, near, order, sources, pos, *refs):
    got, msg = refs[-2:]
    blocks = collect(place(pos, axis, near)[1], order, refs[0], refs[1:near], got)
    at = 2 * sources
    coefs, rows = merged([(b[at : at + 3], rows_of(b, sources)) for b in blocks])
    for k, value in enumerate([v for pair in rows for v in pair] + list(coefs)):
        msg[plane(k)] = value


def merge_first_kernel(near, pos, own, *refs):
    got, msg, halos = refs[-3:]
    r = place(pos, 0, near)[1]
    blocks = ordered(r, [loaded(ref, range(5)) for ref in (own, *refs[: near - 1])], got)
    coefs, rows = merged([(b[2:5], rows_of(b, 1)) for b in blocks])
    for k, value in enumerate([*rows[0], *coefs, jnp.where(r == 0, own[plane(5)], own[plane(6)])]):
        msg[plane(k)] = value
    inner, outer = refs[0][plane(5)], refs[near - 2][plane(5)]
    odd = lax.bitwise_and(r, 1) == 1
    halos[plane(0)] = jnp.where(odd, outer, inner)
    halos[plane(1)] = jnp.where(odd, inner, outer)


def merge_rows_kernel(axis, near, order, pos, coefs, *refs):
    got, msg = refs[-2:]
    blocks = collect(place(pos, axis, near)[1], order, refs[0], refs[1:near], got)
    _, rows = merged([(stored(coefs, m, (2, 3, 4)), rows_of(b, 1)) for m, b in enumerate(blocks)])
    msg[plane(0)], msg[plane(1)] = rows[0]


def solved_ends(q, r, sources, near_rows, near_coefs, far_rows, far_coefs, own_near, own_far):
    zero = jnp.zeros_like(far_coefs[0][0])
    outer = boundary(q, far_rows, far_coefs, *own_far, [(zero, zero)] * sources)
    return boundary(r, near_rows, near_coefs, *own_near, outer)


def first_z_kernel(n, pos, ef, mf, ez_next, w, c, p, u, v, r_top, src_top, curl, flux_y, flux_a, part_a, src, r):
    factor(lambda j: w[strided(j)], pos[plane(1)] == 0, p, u, v)
    inside = jnp.where(pos[pl.ds(B, 1)] == n - 1, 0.0, 1.0)
    row = lax.broadcasted_iota(jnp.int32, (B, w.shape[1]), 0)
    for i in range(B):
        ez = ef[2, plane(i)]
        after = jnp.where(row == B - 1, ez_next[pl.ds(i, 1)] * inside, pltpu.roll(ez, B - 1, 0))
        ri = mf[0, plane(i)] * (1.0 / h) - (after - ez)
        r[plane(i)] = ri
        gain = mf[2, plane(i)]
        if i > 0:
            gain = gain - mf[2, plane(i - 1)]
        src[plane(i)] = c[plane(i)] * ef[1, plane(i)] + (behind_z(ri) - gain * (1.0 / h))
        part_a[plane(i)] = c[plane(i)] * ef[0, plane(i)] - behind_z(mf[1, plane(i)]) * (1.0 / h)
        if i < B - 1:
            rise = ef[1, plane(i + 1)] - ef[1, plane(i)]
            flux_a[plane(i)] = mf[2, plane(i)] * (1.0 / h) - rise
    flux_a[plane(B - 1)] = mf[2, plane(B - 1)] * (1.0 / h) + ef[1, plane(B - 1)]
    r_top[...] = r[plane(0)]
    src_top[...] = src[plane(0)]
    x = solve_z(src[...], w[...])
    rise = ahead_z(x)
    mx = r[...] + rise
    curl[...] = c[...] * x + behind_z(mx)
    flux_y[...] = -(mx + rise)


def both_y_kernel(near, far, order, pos, got_near, own_near, *refs):
    others, refs = refs[:far], refs[far:]
    (halos, g_b, u_x, v_x, flux_b, w, c, r_top, src_top, curl_in, flux_y_in, flux_a_in, part_a, p_y, u_y, v_y) = refs[:16]
    got_far, rise_y, curl, flux_y, flux_a, g_a, g_c, msg, part, fz = refs[16:]
    top = plane(0)
    q, r = place(pos, 0, near)
    far_blocks = collect(q, order, others[0], others[1:], got_far)
    near_blocks = [stored(got_near, m, range(5)) for m in range(near)]
    ends = [b[5] for b in far_blocks]
    after_group = jnp.where(q < far - 1, pick(ends, q + 1), 0.0)
    ey_next = jnp.where(r < near - 1, halos[plane(0)], after_group)
    before_group = jnp.where(q > 0, pick(ends, q - 1), 0.0)
    hz_prev = jnp.where(r > 0, halos[plane(1)], before_group)
    curl[...] = curl_in[...]
    flux_y[...] = flux_y_in[...]
    flux_a[...] = flux_a_in[...]

    x = solve_z(src_top[...] + hz_prev * (1.0 / h), w[top])
    rise = ahead_z(x)
    mx = r_top[...] + rise
    curl[top] = c[top] * x + behind_z(mx)
    flux_y[top] = -(mx + rise)

    flux_a[plane(B - 1)] = flux_a[plane(B - 1)] - ey_next

    def source_a(j):
        f = flux_a[strided(j)]
        if j > 0:
            f = f - flux_a[strided(j - 1)]
        return part_a[strided(j)] + f

    first_a, last_a = eliminate(source_a, p_y, g_a)
    last_a = last_a - flux_a[strided(B - 1)]

    own, own_group = loaded(own_near, range(5)), loaded(others[0], range(5))
    ((before, after),) = solved_ends(
        q,
        r,
        1,
        [rows_of(b, 1) for b in near_blocks],
        [b[2:5] for b in near_blocks],
        [rows_of(b, 1) for b in far_blocks],
        [b[2:5] for b in far_blocks],
        (rows_of(own, 1), own[2:5]),
        (rows_of(own_group, 1), own_group[2:5]),
    )
    for i in range(B):
        fz[plane(i)] = g_b[plane(i)] + (u_x[plane(i)] * before + v_x[plane(i)] * after)
    my_before = jnp.where(pos[plane(0)] == 0, 0.0, fz[top] - before)
    for i in range(B):
        here = fz[plane(i)]
        rise = (fz[plane(i + 1)] if i < B - 1 else after) - here
        my = flux_b[plane(i)] + rise
        rise_y[plane(i)] = my + rise
        part[plane(i)] = c[plane(i)] * here + (my - my_before)
        my_before = my

    def source_c(j):
        f = flux_y[strided(j)]
        if j > 0:
            f = f - flux_y[strided(j - 1)]
        return part[strided(j)] + f

    first_c, last_c = eliminate(source_c, p_y, g_c)
    last_c = last_c - flux_y[strided(B - 1)]
    sent = [first_a, last_a, first_c, last_c, u_y[plane(0)], v_y[plane(0)], v_y[plane(B - 1)]]
    for k, value in enumerate(sent):
        msg[plane(k)] = value


def second_x_kernel(near, far, order, pos, got_near, own_near, *refs):
    others, refs = refs[:far], refs[far:]
    g_a, u, v, flux_a, c, curl, p_x, part, flux2, g2, ends_c, msg, got_far, fx = refs
    q, r = place(pos, 1, near)
    far_blocks = collect(q, order, others[0], others[1:], got_far)
    near_blocks = [stored(got_near, m, range(7)) for m in range(near)]
    own, own_group = loaded(own_near, range(7)), loaded(others[0], range(7))
    (before, after), (before_c, after_c) = solved_ends(
        q,
        r,
        2,
        [rows_of(b, 2) for b in near_blocks],
        [b[4:7] for b in near_blocks],
        [rows_of(b, 2) for b in far_blocks],
        [b[4:7] for b in far_blocks],
        (rows_of(own, 2), own[4:7]),
        (rows_of(own_group, 2), own_group[4:7]),
    )
    ends_c[plane(0)] = before_c
    ends_c[plane(1)] = after_c
    for j in range(B):
        fx[plane(j)] = g_a[plane(j)] + (u[plane(j)] * before + v[plane(j)] * after)
    mz_before = jnp.where(pos[plane(1)] == 0, 0.0, fx[plane(0)] - before)
    for j in range(B):
        here = fx[plane(j)]
        rise = (fx[plane(j + 1)] if j < B - 1 else after) - here
        mz = flux_a[strided(j)] + rise
        part[strided(j)] = c[strided(j)] * here + (mz - mz_before)
        flux2[strided(j)] = -(mz + rise)
        mz_before = mz

    def source(i):
        f = flux2[plane(i)]
        if i > 0:
            f = f - flux2[plane(i - 1)]
        return curl[plane(i)] + f

    first, last = eliminate(source, p_x, g2)
    msg[plane(0)] = first
    msg[plane(1)] = last - flux2[plane(B - 1)]


def second_y_kernel(ends_c, g_c, u, v, flux_y, elec, magn, full_z, new_x, sems):
    stores = [(full_z, elec.at[2]), (new_x, magn.at[0])]
    stores = [pltpu.make_async_copy(a, b, sems.at[k]) for k, (a, b) in enumerate(stores)]
    before, after = ends_c[plane(0)], ends_c[plane(1)]
    here = None
    for j in range(B):
        ahead = g_c[plane(j)] + (u[plane(j)] * before + v[plane(j)] * after)
        full_z[strided(j)] = ahead
        if j > 0:
            new_x[strided(j - 1)] = -h * (flux_y[strided(j - 1)] + (ahead - here))
        here = ahead
    new_x[strided(B - 1)] = -h * (flux_y[strided(B - 1)] + (after - here))
    for store in stores:
        store.start()
    for store in stores:
        store.wait()


def second_z_kernel(part, rise_y, z_a, z_b, z_scale, _, __, elec, magn, full_x, new_y, sems):
    stores = [(full_x, elec.at[0]), (new_y, magn.at[1])]
    stores = [pltpu.make_async_copy(a, b, sems.at[k]) for k, (a, b) in enumerate(stores)]
    a = rise_y[...]
    x = solve_factored(part[...] - behind_z(a), z_a, z_b, z_scale)
    full_x[...] = x
    stores[0].start()
    new_y[...] = h * (a - ahead_z(x))
    stores[1].start()
    for store in stores:
        store.wait()


def last_kernel(near, far, order, pos, coefs_near, coefs_far, own_b, group_b, got_near, own_near, *refs):
    others, refs = refs[:far], refs[far:]
    g, u, v, flux2, _, _, elec, magn, got_far, full_y, new_z, sems = refs
    q, r = place(pos, 0, near)
    far_blocks = collect(q, order, others[0], others[1:], got_far)
    ((before, after),) = solved_ends(
        q,
        r,
        1,
        [rows_of(stored(got_near, m, range(2)), 1) for m in range(near)],
        [stored(coefs_near, m, (2, 3, 4)) for m in range(near)],
        [rows_of(b, 1) for b in far_blocks],
        [stored(coefs_far, m, (2, 3, 4)) for m in range(far)],
        (rows_of(loaded(own_near, range(2)), 1), loaded(own_b, (2, 3, 4))),
        (rows_of(loaded(others[0], range(2)), 1), loaded(group_b, (2, 3, 4))),
    )
    stores = [(full_y, elec.at[1]), (new_z, magn.at[2])]
    stores = [pltpu.make_async_copy(a, b, sems.at[k]) for k, (a, b) in enumerate(stores)]
    for i in range(B):
        full_y[plane(i)] = g[plane(i)] + (u[plane(i)] * before + v[plane(i)] * after)
    stores[0].start()
    for i in range(B):
        rise = (full_y[plane(i + 1)] if i < B - 1 else after) - full_y[plane(i)]
        new_z[plane(i)] = -h * (flux2[plane(i)] + rise)
    stores[1].start()
    for store in stores:
        store.wait()


VMEM = pl.BlockSpec(memory_space=pltpu.VMEM)
SMEM = pl.BlockSpec(memory_space=pltpu.SMEM)
HBM = pl.BlockSpec(memory_space=pltpu.HBM)


def call(kernel, ins, outs, specs=None, out_specs=None, scratch=(), aliases=None, flops=1_000_000):
    shapes = [jax.ShapeDtypeStruct(s, F32) if isinstance(s, tuple) else s for s in outs]
    return pl.pallas_call(
        kernel,
        out_shape=shapes,
        in_specs=specs or [VMEM] * len(ins),
        out_specs=out_specs or [VMEM] * len(outs),
        scratch_shapes=[pltpu.VMEM(s, F32) if isinstance(s, tuple) else s for s in scratch],
        input_output_aliases=aliases or {},
        compiler_params=pltpu.CompilerParams(vmem_limit_bytes=24 * 1024 * 1024),
        cost_estimate=pl.CostEstimate(flops=flops, bytes_accessed=1_000_000, transcendentals=0),
    )(*ins)


def shared(value, axis, n, order, near=1, bent=(), by=0):
    masks = [near * s + (by if s in bent else 0) for s in order]
    return [value] + [lax.ppermute(value, axis, [(i, i ^ mask) for i in range(n)]) for mask in masks]


def split(n):
    near = 1 << (n.bit_length() // 2)
    return near, n // near


def local(electric, magnetic, material, permittivity, conductivity):
    nx, ny = lax.axis_size("px"), lax.axis_size("py")
    near_x, far_x = split(nx)
    near_y, far_y = split(ny)
    nz = material.shape[2]
    cells = (B * B, nz)
    me = jnp.stack([lax.axis_index("px"), lax.axis_index("py")]).astype(jnp.int32)
    in_hbm = lambda a: pltpu.with_memory_space_constraint(a, pltpu.HBM)
    elec = in_hbm(electric.reshape(3, *cells))
    magn = in_hbm(magnetic.reshape(3, *cells))
    ids = in_hbm(material.reshape(cells))
    dma = pltpu.SemaphoreType.DMA
    orders = [(1, 2, 3), (2, 1, 3), (2, 1, 3), (1, 2, 3)]
    counts = (near_x, far_x, near_y, far_y)
    px_near, px_far, py_near, py_far = [
        tuple(s for s in order if s < count) for order, count in zip(orders, counts)
    ]

    (hx_last,) = call(
        cut_kernel, [in_hbm(magnetic)], [(B, nz)], specs=[HBM], scratch=[dma(())], flops=1000
    )
    hx_prev = lax.ppermute(hx_last, "py", [(i, (i + 1) % ny) for i in range(ny)])
    w, c, p_x, u_x, v_x, flux_b, part_b, ef, mf, ez_first, pos = call(
        tables_kernel,
        [me, in_hbm(permittivity), in_hbm(conductivity), ids, elec, magn],
        [cells] * 7 + [(3, *cells)] * 2 + [(6 * B, nz), jax.ShapeDtypeStruct((2 * B, nz), jnp.int32)],
        specs=[SMEM] + [HBM] * 5,
        scratch=[pltpu.VMEM(cells, jnp.int32)] + [pltpu.SMEM(permittivity.shape, F32)] * 2 + [dma((9,))],
    )
    g_b, own_b, inner, outer = call(
        first_x_kernel,
        [pos, part_b, hx_prev, flux_b, p_x, u_x, v_x, ef, mf],
        [cells, (7 * B, nz), (6 * B, nz), (6 * B, nz)],
    )
    ins = [own_b] + [shared(outer if k == 3 else inner, "px", nx, (k,))[1] for k in px_near]
    ez_next = lax.ppermute(ez_first, "py", [((i + 1) % ny, i) for i in range(ny)])
    near_b, group_b, halos = call(
        functools.partial(merge_first_kernel, near_x),
        [pos] + ins,
        [(near_x, 5 * B, nz), (6 * B, nz), (2 * B, nz)],
    )
    ins = shared(group_b, "px", nx, px_far, near_x, (1, 3), near_x - 1)
    p_y, u_y, v_y, r_top, src_top, curl, flux_y, flux_a, part_a = call(
        functools.partial(first_z_kernel, ny),
        [pos, ef, mf, ez_next, w, c],
        [cells] * 3 + [(B, nz)] * 2 + [cells] * 4,
        scratch=[cells] * 2,
        flops=8_000_000,
    )
    ins = [pos, near_b, own_b] + ins + [halos, g_b, u_x, v_x, flux_b, w, c, r_top, src_top]
    far_b, rise_y, curl, flux_y, flux_a, g_a, g_c, own_ac = call(
        functools.partial(both_y_kernel, near_x, far_x, px_far),
        ins + [curl, flux_y, flux_a, part_a, p_y, u_y, v_y],
        [(far_x, 6 * B, nz)] + [cells] * 6 + [(7 * B, nz)],
        scratch=[cells] * 2,
    )
    ins = shared(own_ac, "py", ny, py_near)
    near_ac, msg = call(
        functools.partial(merge_kernel, 1, near_y, py_near, 2), [pos] + ins, [(near_y, 7 * B, nz), (7 * B, nz)]
    )
    msg, w = lax.optimization_barrier((msg, w))
    ins = shared(msg, "py", ny, py_far, near_y, (2,), near_y // 2)
    steps = (nz - 1).bit_length()
    z_factors = call(factors_kernel, [w], [(steps, *cells)] * 2 + [cells], flops=8_000_000)
    ins, z_factors = lax.optimization_barrier((ins, z_factors))
    part_x, flux2, g2, ends_c, own_a = call(
        functools.partial(second_x_kernel, near_y, far_y, py_far),
        [pos, near_ac, own_ac] + ins + [g_a, u_y, v_y, flux_a, c, curl, p_x],
        [cells] * 3 + [(2 * B, nz)] * 2,
        scratch=[(far_y, 7 * B, nz), cells],
    )
    ins = shared(own_a, "px", nx, px_near)
    whole = pltpu.HBM((3, *cells), F32)
    elec, magn = call(
        second_y_kernel,
        [ends_c, g_c, u_y, v_y, flux_y],
        [whole, whole],
        out_specs=[HBM] * 2,
        scratch=[cells] * 2 + [dma((2,))],
    )
    near_a, msg = call(
        functools.partial(merge_rows_kernel, 0, near_x, px_near),
        [pos, near_b] + ins,
        [(near_x, 2 * B, nz), (2 * B, nz)],
    )
    msg, elec = lax.optimization_barrier((msg, elec))
    ins = shared(msg, "px", nx, px_far, near_x, (1, 3), near_x // 2)
    elec, magn = call(
        second_z_kernel,
        [part_x, rise_y, *z_factors, elec, magn],
        [whole] * 2,
        specs=[VMEM] * 5 + [HBM] * 2,
        out_specs=[HBM] * 2,
        scratch=[cells] * 2 + [dma((2,))],
        aliases={5: 0, 6: 1},
        flops=4_000_000,
    )
    ins = [pos, near_b, far_b, own_b, group_b, near_a, own_a] + ins + [g2, u_x, v_x, flux2]
    at = len(ins)
    out = call(
        functools.partial(last_kernel, near_x, far_x, px_far),
        ins + [elec, magn],
        [whole] * 2,
        specs=[VMEM] * at + [HBM] * 2,
        out_specs=[HBM] * 2,
        scratch=[(far_x, 2 * B, nz), cells, cells, dma((2,))],
        aliases={at: 0, at + 1: 1},
    )
    return tuple(a.reshape(3, B, B, nz) for a in out)


def solution(mesh):
    placed = (P(None, "px", "py", None), P(None, "px", "py", None), P("px", "py", None), P(), P())
    return jax.shard_map(
        local,
        mesh=mesh,
        in_specs=placed,
        out_specs=(P(None, "px", "py", None), P(None, "px", "py", None)),
        check_vma=False,
    )
```

```python
import functools

import jax
import jax.numpy as jnp
from jax import lax
from jax.experimental import pallas as pl
from jax.experimental.pallas import tpu as pltpu
from jax.sharding import PartitionSpec as P

h = 32.0
B = 16
F32 = jnp.float32


def plane(i):
    return pl.ds(i * B, B)


def strided(j):
    return pl.ds(j, B, stride=B)


def lanes(v):
    return lax.broadcasted_iota(jnp.int32, v.shape, 1)


def behind_z(v):
    return v - jnp.where(lanes(v) == 0, 0.0, pltpu.roll(v, 1, 1))


def ahead_z(v):
    n = v.shape[1]
    return jnp.where(lanes(v) == n - 1, 0.0, pltpu.roll(v, n - 1, 1)) - v


def factor(w_of, first_block, p, u, v):
    d = None
    y = []
    for j in range(B):
        w = w_of(j)
        e = w + (jnp.where(first_block, 0.0, 1.0) if j == 0 else d)
        inv = 1.0 / (1.0 + e)
        d = e * inv
        p[plane(j)] = inv
        y.append(jnp.ones_like(inv) if j == 0 else y[-1] * last)
        last = inv
    uj = y[B - 1] * last
    vj = last
    u[plane(B - 1)] = uj
    v[plane(B - 1)] = vj
    for j in range(B - 2, -1, -1):
        inv = p[plane(j)]
        uj = inv * (y[j] + uj)
        vj = inv * vj
        u[plane(j)] = uj
        v[plane(j)] = vj


def eliminate(source_of, p, g):
    y = source_of(0)
    ys = [y]
    for j in range(1, B):
        y = source_of(j) + p[plane(j - 1)] * y
        ys.append(y)
    x = y * p[plane(B - 1)]
    end = x
    g[plane(B - 1)] = x
    for j in range(B - 2, -1, -1):
        x = p[plane(j)] * (ys[j] + x)
        g[plane(j)] = x
    return x, end


def boundary(me, rows, coefs, here, coef_here, outer):
    n = len(rows)
    left = [a for a, _ in outer]
    right = [b for _, b in outer]
    beta = delta = jnp.zeros_like(left[0])
    for s in range(n - 1):
        ff, fl, ll = coefs[s]
        t = fl / (1.0 - ff * beta)
        on = s < me
        left = [jnp.where(on, dl + t * (a + beta * gf), a) for a, (gf, dl) in zip(left, rows[s])]
        beta = jnp.where(on, ll + t * beta * fl, beta)
        m = n - 1 - s
        ff, fl, ll = coefs[m]
        t = fl / (1.0 - ll * delta)
        on = m > me
        right = [jnp.where(on, gf + t * (b + delta * dl), b) for b, (gf, dl) in zip(right, rows[m])]
        delta = jnp.where(on, ff + t * delta * fl, delta)
    ff, fl, ll = coef_here
    after_scale = 1.0 / (1.0 - delta * ll)
    t = fl * after_scale
    before_scale = 1.0 / (1.0 - beta * (ff + t * delta * fl))
    ends = []
    for a, b, (gf, dl) in zip(left, right, here):
        before = (a + beta * (gf + t * (b + delta * dl))) * before_scale
        ends.append((before, (b + delta * (dl + fl * before)) * after_scale))
    return ends


def merge(one, two):
    (ff1, fl1, ll1), rows1 = one
    (ff2, fl2, ll2), rows2 = two
    d = 1.0 / (1.0 - ll1 * ff2)
    t1, t2 = fl1 * d, fl2 * d
    rows = [
        (gf1 + t1 * (gf2 + ff2 * dl1), dl2 + t2 * (dl1 + ll1 * gf2))
        for (gf1, dl1), (gf2, dl2) in zip(rows1, rows2)
    ]
    return (ff1 + t1 * fl1 * ff2, t1 * fl2, ll2 + t2 * fl2 * ll1), rows


def solve_z(r, w):
    n = r.shape[1]
    lane = lanes(r)
    e = jnp.where(lane == n - 1, 0.0, 1.0)
    l = jnp.where(lane == 0, 0.0, 1.0)
    s = w + jnp.where(lane == n - 1, 1.0, 0.0)
    step = 1
    while step < n:
        inv = 1.0 / (s + (l + e))
        a, b = e * inv, l * inv
        r = r + (pltpu.roll(a * r, step, 1) + pltpu.roll(b * r, n - step, 1))
        s = s + (pltpu.roll(a * s, step, 1) + pltpu.roll(b * s, n - step, 1))
        g = a * l
        if 2 * step < n:
            e, l = pltpu.roll(g, n - step, 1), pltpu.roll(g, step, 1)
        step *= 2
    return r / s


def factors_kernel(w_in, a_out, b_out, scale):
    w = w_in[...]
    n = w.shape[1]
    lane = lanes(w)
    e = jnp.where(lane == n - 1, 0.0, 1.0)
    l = jnp.where(lane == 0, 0.0, 1.0)
    s = w + jnp.where(lane == n - 1, 1.0, 0.0)
    for k in range(a_out.shape[0]):
        step = 1 << k
        inv = 1.0 / (s + (l + e))
        a, b = e * inv, l * inv
        a_out[k] = a
        b_out[k] = b
        s = s + (pltpu.roll(a * s, step, 1) + pltpu.roll(b * s, n - step, 1))
        g = a * l
        e, l = pltpu.roll(g, n - step, 1), pltpu.roll(g, step, 1)
    scale[...] = 1.0 / s


def solve_factored(r, a, b, scale):
    n = r.shape[1]
    for k in range(a.shape[0]):
        step = 1 << k
        r = r + (pltpu.roll(a[k] * r, step, 1) + pltpu.roll(b[k] * r, n - step, 1))
    return r * scale[...]


def collect(r, order, own, others, got):
    refs = [own] + [others[order.index(s)] for s in range(1, len(order) + 1)]
    return ordered(r, [loaded(ref, range(got.shape[1] // B)) for ref in refs], got)


def ordered(r, found, got):
    count = len(found)
    blocks = [[] for _ in found]
    for k in range(got.shape[1] // B):
        values = [planes[k] for planes in found]
        bit = 1
        while bit < count:
            swap = lax.bitwise_and(r, bit) != 0
            values = [jnp.where(swap, values[m ^ bit], values[m]) for m in range(count)]
            bit *= 2
        for m, value in enumerate(values):
            got[m, plane(k)] = value
            blocks[m].append(value)
    return blocks


def rows_of(block, sources):
    return [(block[2 * k], block[2 * k + 1]) for k in range(sources)]


def stored(got, m, planes):
    return [got[m, plane(k)] for k in planes]


def loaded(msg, planes):
    return [msg[plane(k)] for k in planes]


def pick(values, index):
    out = values[0]
    for k in range(1, len(values)):
        out = jnp.where(index == k, values[k], out)
    return out


def place(pos, axis, near):
    here = pos[plane(axis)]
    return lax.shift_right_logical(here, near.bit_length() - 1), lax.bitwise_and(here, near - 1)


def cut_kernel(magn, hx_last, sem):
    load = pltpu.make_async_copy(magn.at[0, :, B - 1], hx_last, sem)
    load.start()
    load.wait()


def tables_kernel(
    me, eps_in, sig_in, material, elec_in, magn_in, w, c, p, u, v, flux, part, elec, magn, ez_first, pos, ids, eps, sig, sems
):
    loads = [(eps_in, eps), (sig_in, sig), (material, ids)]
    for field, to, k in ((elec_in, elec, 0), (magn_in, magn, 1), (elec_in, elec, 2), (magn_in, magn, 0)):
        loads.append((field.at[k], to.at[k]))
    loads += [(elec_in.at[1], elec.at[1]), (magn_in.at[2], magn.at[2])]
    loads = [pltpu.make_async_copy(a, b, sems.at[k]) for k, (a, b) in enumerate(loads)]
    for load in loads:
        load.start()
    for axis in range(2):
        pos[plane(axis)] = jnp.full((B, w.shape[1]), me[axis], jnp.int32)
    for load in loads[:3]:
        load.wait()
    ws = [eps[m] * (1.0 / (h * h)) + sig[m] * (0.5 / h) for m in range(eps.shape[0])]
    cs = [eps[m] * (1.0 / (h * h)) - sig[m] * (0.5 / h) for m in range(eps.shape[0])]
    for i in range(B):
        cell = ids[plane(i)]
        wi = jnp.full(cell.shape, ws[0], F32)
        ci = jnp.full(cell.shape, cs[0], F32)
        for m in range(1, len(ws)):
            wi = jnp.where(cell == m, ws[m], wi)
            ci = jnp.where(cell == m, cs[m], ci)
        w[plane(i)] = wi
        c[plane(i)] = ci
    factor(lambda i: w[plane(i)], me[0] == 0, p, u, v)
    for load in loads[3:7]:
        load.wait()
    row = lax.broadcasted_iota(jnp.int32, (B, w.shape[1]), 0)
    for i in range(B):
        q = magn[1, plane(i)] * (1.0 / h) - ahead_z(elec[0, plane(i)])
        flux[plane(i)] = q
        if i > 0:
            q = q - flux[plane(i - 1)]
        here = magn[0, plane(i)]
        before = jnp.where(row == 0, 0.0, pltpu.roll(here, 1, 0))
        part[plane(i)] = c[plane(i)] * elec[2, plane(i)] + (q - (here - before) * (1.0 / h))
    for k in range(ez_first.shape[0] // B):
        ez_first[plane(k)] = elec.at[2][strided(0)]
    for load in loads[7:]:
        load.wait()


def first_x_kernel(pos, part, hx_prev, flux, p, u, v, elec, magn, g, msg, inner, outer):
    row = lax.broadcasted_iota(jnp.int32, hx_prev.shape, 0)
    scale = jnp.where(pos[plane(1)] == 0, 0.0, jnp.where(row == 0, 1.0 / h, 0.0))

    def source(i):
        return part[plane(i)] + hx_prev[pl.ds(i, 1)] * scale

    first, last = eliminate(source, p, g)
    msg[plane(0)] = first
    msg[plane(1)] = last - flux[plane(B - 1)]
    msg[plane(2)] = u[plane(0)]
    msg[plane(3)] = v[plane(0)]
    msg[plane(4)] = v[plane(B - 1)]
    msg[plane(5)] = elec[1, plane(0)]
    msg[plane(6)] = magn[2, plane(B - 1)]
    even = lax.bitwise_and(pos[plane(0)], 1) == 0
    for sent, halo in ((inner, (6, 5)), (outer, (5, 6))):
        sent[pl.ds(0, 5 * B)] = msg[pl.ds(0, 5 * B)]
        sent[plane(5)] = jnp.where(even, msg[plane(halo[0])], msg[plane(halo[1])])


def merged(blocks):
    while len(blocks) > 1:
        blocks = [merge(a, b) for a, b in zip(blocks[::2], blocks[1::2])]
    return blocks[0]


def merge_kernel(axis, near, order, sources, pos, *refs):
    got, msg = refs[-2:]
    blocks = collect(place(pos, axis, near)[1], order, refs[0], refs[1:near], got)
    at = 2 * sources
    coefs, rows = merged([(b[at : at + 3], rows_of(b, sources)) for b in blocks])
    for k, value in enumerate([v for pair in rows for v in pair] + list(coefs)):
        msg[plane(k)] = value


def merge_first_kernel(near, pos, own, *refs):
    got, msg, halos = refs[-3:]
    r = place(pos, 0, near)[1]
    blocks = ordered(r, [loaded(ref, range(5)) for ref in (own, *refs[: near - 1])], got)
    coefs, rows = merged([(b[2:5], rows_of(b, 1)) for b in blocks])
    for k, value in enumerate([*rows[0], *coefs, jnp.where(r == 0, own[plane(5)], own[plane(6)])]):
        msg[plane(k)] = value
    inner, outer = refs[0][plane(5)], refs[near - 2][plane(5)]
    odd = lax.bitwise_and(r, 1) == 1
    halos[plane(0)] = jnp.where(odd, outer, inner)
    halos[plane(1)] = jnp.where(odd, inner, outer)


def merge_rows_kernel(axis, near, order, pos, coefs, *refs):
    got, msg = refs[-2:]
    blocks = collect(place(pos, axis, near)[1], order, refs[0], refs[1:near], got)
    _, rows = merged([(stored(coefs, m, (2, 3, 4)), rows_of(b, 1)) for m, b in enumerate(blocks)])
    msg[plane(0)], msg[plane(1)] = rows[0]


def solved_ends(q, r, sources, near_rows, near_coefs, far_rows, far_coefs, own_near, own_far):
    zero = jnp.zeros_like(far_coefs[0][0])
    outer = boundary(q, far_rows, far_coefs, *own_far, [(zero, zero)] * sources)
    return boundary(r, near_rows, near_coefs, *own_near, outer)


def first_z_kernel(n, pos, ef, mf, ez_next, w, c, p, u, v, r_top, src_top, curl, flux_y, flux_a, part_a, src, r):
    factor(lambda j: w[strided(j)], pos[plane(1)] == 0, p, u, v)
    inside = jnp.where(pos[pl.ds(B, 1)] == n - 1, 0.0, 1.0)
    row = lax.broadcasted_iota(jnp.int32, (B, w.shape[1]), 0)
    for i in range(B):
        ez = ef[2, plane(i)]
        after = jnp.where(row == B - 1, ez_next[pl.ds(i, 1)] * inside, pltpu.roll(ez, B - 1, 0))
        ri = mf[0, plane(i)] * (1.0 / h) - (after - ez)
        r[plane(i)] = ri
        gain = mf[2, plane(i)]
        if i > 0:
            gain = gain - mf[2, plane(i - 1)]
        src[plane(i)] = c[plane(i)] * ef[1, plane(i)] + (behind_z(ri) - gain * (1.0 / h))
        part_a[plane(i)] = c[plane(i)] * ef[0, plane(i)] - behind_z(mf[1, plane(i)]) * (1.0 / h)
        if i < B - 1:
            rise = ef[1, plane(i + 1)] - ef[1, plane(i)]
            flux_a[plane(i)] = mf[2, plane(i)] * (1.0 / h) - rise
    flux_a[plane(B - 1)] = mf[2, plane(B - 1)] * (1.0 / h) + ef[1, plane(B - 1)]
    r_top[...] = r[plane(0)]
    src_top[...] = src[plane(0)]
    x = solve_z(src[...], w[...])
    rise = ahead_z(x)
    mx = r[...] + rise
    curl[...] = c[...] * x + behind_z(mx)
    flux_y[...] = -(mx + rise)


def both_y_kernel(near, far, order, pos, got_near, own_near, *refs):
    others, refs = refs[:far], refs[far:]
    (halos, g_b, u_x, v_x, flux_b, w, c, r_top, src_top, curl_in, flux_y_in, flux_a_in, part_a, p_y, u_y, v_y) = refs[:16]
    got_far, rise_y, curl, flux_y, flux_a, g_a, g_c, msg, part, fz = refs[16:]
    top = plane(0)
    q, r = place(pos, 0, near)
    far_blocks = collect(q, order, others[0], others[1:], got_far)
    near_blocks = [stored(got_near, m, range(5)) for m in range(near)]
    ends = [b[5] for b in far_blocks]
    after_group = jnp.where(q < far - 1, pick(ends, q + 1), 0.0)
    ey_next = jnp.where(r < near - 1, halos[plane(0)], after_group)
    before_group = jnp.where(q > 0, pick(ends, q - 1), 0.0)
    hz_prev = jnp.where(r > 0, halos[plane(1)], before_group)
    curl[...] = curl_in[...]
    flux_y[...] = flux_y_in[...]
    flux_a[...] = flux_a_in[...]

    x = solve_z(src_top[...] + hz_prev * (1.0 / h), w[top])
    rise = ahead_z(x)
    mx = r_top[...] + rise
    curl[top] = c[top] * x + behind_z(mx)
    flux_y[top] = -(mx + rise)

    flux_a[plane(B - 1)] = flux_a[plane(B - 1)] - ey_next

    def source_a(j):
        f = flux_a[strided(j)]
        if j > 0:
            f = f - flux_a[strided(j - 1)]
        return part_a[strided(j)] + f

    first_a, last_a = eliminate(source_a, p_y, g_a)
    last_a = last_a - flux_a[strided(B - 1)]

    own, own_group = loaded(own_near, range(5)), loaded(others[0], range(5))
    ((before, after),) = solved_ends(
        q,
        r,
        1,
        [rows_of(b, 1) for b in near_blocks],
        [b[2:5] for b in near_blocks],
        [rows_of(b, 1) for b in far_blocks],
        [b[2:5] for b in far_blocks],
        (rows_of(own, 1), own[2:5]),
        (rows_of(own_group, 1), own_group[2:5]),
    )
    for i in range(B):
        fz[plane(i)] = g_b[plane(i)] + (u_x[plane(i)] * before + v_x[plane(i)] * after)
    my_before = jnp.where(pos[plane(0)] == 0, 0.0, fz[top] - before)
    for i in range(B):
        here = fz[plane(i)]
        rise = (fz[plane(i + 1)] if i < B - 1 else after) - here
        my = flux_b[plane(i)] + rise
        rise_y[plane(i)] = my + rise
        part[plane(i)] = c[plane(i)] * here + (my - my_before)
        my_before = my

    def source_c(j):
        f = flux_y[strided(j)]
        if j > 0:
            f = f - flux_y[strided(j - 1)]
        return part[strided(j)] + f

    first_c, last_c = eliminate(source_c, p_y, g_c)
    last_c = last_c - flux_y[strided(B - 1)]
    sent = [first_a, last_a, first_c, last_c, u_y[plane(0)], v_y[plane(0)], v_y[plane(B - 1)]]
    for k, value in enumerate(sent):
        msg[plane(k)] = value


def second_x_kernel(near, far, order, pos, got_near, own_near, *refs):
    others, refs = refs[:far], refs[far:]
    g_a, u, v, flux_a, c, curl, p_x, part, flux2, g2, ends_c, msg, got_far, fx = refs
    q, r = place(pos, 1, near)
    far_blocks = collect(q, order, others[0], others[1:], got_far)
    near_blocks = [stored(got_near, m, range(7)) for m in range(near)]
    own, own_group = loaded(own_near, range(7)), loaded(others[0], range(7))
    (before, after), (before_c, after_c) = solved_ends(
        q,
        r,
        2,
        [rows_of(b, 2) for b in near_blocks],
        [b[4:7] for b in near_blocks],
        [rows_of(b, 2) for b in far_blocks],
        [b[4:7] for b in far_blocks],
        (rows_of(own, 2), own[4:7]),
        (rows_of(own_group, 2), own_group[4:7]),
    )
    ends_c[plane(0)] = before_c
    ends_c[plane(1)] = after_c
    for j in range(B):
        fx[plane(j)] = g_a[plane(j)] + (u[plane(j)] * before + v[plane(j)] * after)
    mz_before = jnp.where(pos[plane(1)] == 0, 0.0, fx[plane(0)] - before)
    for j in range(B):
        here = fx[plane(j)]
        rise = (fx[plane(j + 1)] if j < B - 1 else after) - here
        mz = flux_a[strided(j)] + rise
        part[strided(j)] = c[strided(j)] * here + (mz - mz_before)
        flux2[strided(j)] = -(mz + rise)
        mz_before = mz

    def source(i):
        f = flux2[plane(i)]
        if i > 0:
            f = f - flux2[plane(i - 1)]
        return curl[plane(i)] + f

    first, last = eliminate(source, p_x, g2)
    msg[plane(0)] = first
    msg[plane(1)] = last - flux2[plane(B - 1)]


def second_y_kernel(ends_c, g_c, u, v, flux_y, elec, magn, full_z, new_x, sems):
    stores = [(full_z, elec.at[2]), (new_x, magn.at[0])]
    stores = [pltpu.make_async_copy(a, b, sems.at[k]) for k, (a, b) in enumerate(stores)]
    before, after = ends_c[plane(0)], ends_c[plane(1)]
    here = None
    for j in range(B):
        ahead = g_c[plane(j)] + (u[plane(j)] * before + v[plane(j)] * after)
        full_z[strided(j)] = ahead
        if j > 0:
            new_x[strided(j - 1)] = -h * (flux_y[strided(j - 1)] + (ahead - here))
        here = ahead
    new_x[strided(B - 1)] = -h * (flux_y[strided(B - 1)] + (after - here))
    for store in stores:
        store.start()
    for store in stores:
        store.wait()


def second_z_kernel(part, rise_y, z_a, z_b, z_scale, _, __, elec, magn, full_x, new_y, sems):
    stores = [(full_x, elec.at[0]), (new_y, magn.at[1])]
    stores = [pltpu.make_async_copy(a, b, sems.at[k]) for k, (a, b) in enumerate(stores)]
    a = rise_y[...]
    x = solve_factored(part[...] - behind_z(a), z_a, z_b, z_scale)
    full_x[...] = x
    stores[0].start()
    new_y[...] = h * (a - ahead_z(x))
    stores[1].start()
    for store in stores:
        store.wait()


def last_kernel(near, far, order, pos, coefs_near, coefs_far, own_b, group_b, got_near, own_near, *refs):
    others, refs = refs[:far], refs[far:]
    g, u, v, flux2, _, _, elec, magn, got_far, full_y, new_z, sems = refs
    q, r = place(pos, 0, near)
    far_blocks = collect(q, order, others[0], others[1:], got_far)
    ((before, after),) = solved_ends(
        q,
        r,
        1,
        [rows_of(stored(got_near, m, range(2)), 1) for m in range(near)],
        [stored(coefs_near, m, (2, 3, 4)) for m in range(near)],
        [rows_of(b, 1) for b in far_blocks],
        [stored(coefs_far, m, (2, 3, 4)) for m in range(far)],
        (rows_of(loaded(own_near, range(2)), 1), loaded(own_b, (2, 3, 4))),
        (rows_of(loaded(others[0], range(2)), 1), loaded(group_b, (2, 3, 4))),
    )
    stores = [(full_y, elec.at[1]), (new_z, magn.at[2])]
    stores = [pltpu.make_async_copy(a, b, sems.at[k]) for k, (a, b) in enumerate(stores)]
    for i in range(B):
        full_y[plane(i)] = g[plane(i)] + (u[plane(i)] * before + v[plane(i)] * after)
    stores[0].start()
    for i in range(B):
        rise = (full_y[plane(i + 1)] if i < B - 1 else after) - full_y[plane(i)]
        new_z[plane(i)] = -h * (flux2[plane(i)] + rise)
    stores[1].start()
    for store in stores:
        store.wait()


VMEM = pl.BlockSpec(memory_space=pltpu.VMEM)
SMEM = pl.BlockSpec(memory_space=pltpu.SMEM)
HBM = pl.BlockSpec(memory_space=pltpu.HBM)


def call(kernel, ins, outs, specs=None, out_specs=None, scratch=(), aliases=None, flops=1_000_000):
    shapes = [jax.ShapeDtypeStruct(s, F32) if isinstance(s, tuple) else s for s in outs]
    return pl.pallas_call(
        kernel,
        out_shape=shapes,
        in_specs=specs or [VMEM] * len(ins),
        out_specs=out_specs or [VMEM] * len(outs),
        scratch_shapes=[pltpu.VMEM(s, F32) if isinstance(s, tuple) else s for s in scratch],
        input_output_aliases=aliases or {},
        compiler_params=pltpu.CompilerParams(vmem_limit_bytes=24 * 1024 * 1024),
        cost_estimate=pl.CostEstimate(flops=flops, bytes_accessed=1_000_000, transcendentals=0),
    )(*ins)


def shared(value, axis, n, order, near=1, bent=(), by=0):
    masks = [near * s + (by if s in bent else 0) for s in order]
    return [value] + [lax.ppermute(value, axis, [(i, i ^ mask) for i in range(n)]) for mask in masks]


def split(n):
    near = 1 << (n.bit_length() // 2)
    return near, n // near


def local(electric, magnetic, material, permittivity, conductivity):
    nx, ny = lax.axis_size("px"), lax.axis_size("py")
    near_x, far_x = split(nx)
    near_y, far_y = split(ny)
    nz = material.shape[2]
    cells = (B * B, nz)
    me = jnp.stack([lax.axis_index("px"), lax.axis_index("py")]).astype(jnp.int32)
    in_hbm = lambda a: pltpu.with_memory_space_constraint(a, pltpu.HBM)
    elec = in_hbm(electric.reshape(3, *cells))
    magn = in_hbm(magnetic.reshape(3, *cells))
    ids = in_hbm(material.reshape(cells))
    dma = pltpu.SemaphoreType.DMA
    orders = [(1, 2, 3), (1, 2, 3), (2, 1, 3), (1, 2, 3)]
    counts = (near_x, far_x, near_y, far_y)
    px_near, px_far, py_near, py_far = [
        tuple(s for s in order if s < count) for order, count in zip(orders, counts)
    ]

    (hx_last,) = call(
        cut_kernel, [in_hbm(magnetic)], [(B, nz)], specs=[HBM], scratch=[dma(())], flops=1000
    )
    hx_prev = lax.ppermute(hx_last, "py", [(i, (i + 1) % ny) for i in range(ny)])
    w, c, p_x, u_x, v_x, flux_b, part_b, ef, mf, ez_first, pos = call(
        tables_kernel,
        [me, in_hbm(permittivity), in_hbm(conductivity), ids, elec, magn],
        [cells] * 7 + [(3, *cells)] * 2 + [(8 * B, nz), jax.ShapeDtypeStruct((2 * B, nz), jnp.int32)],
        specs=[SMEM] + [HBM] * 5,
        scratch=[pltpu.VMEM(cells, jnp.int32)] + [pltpu.SMEM(permittivity.shape, F32)] * 2 + [dma((9,))],
    )
    g_b, own_b, inner, outer = call(
        first_x_kernel,
        [pos, part_b, hx_prev, flux_b, p_x, u_x, v_x, ef, mf],
        [cells, (7 * B, nz), (6 * B, nz), (6 * B, nz)],
    )
    ins = [own_b] + [shared(outer if k == 3 else inner, "px", nx, (k,))[1] for k in px_near]
    ez_next = lax.ppermute(ez_first, "py", [((i + 1) % ny, i) for i in range(ny)])
    near_b, group_b, halos = call(
        functools.partial(merge_first_kernel, near_x),
        [pos] + ins,
        [(near_x, 5 * B, nz), (6 * B, nz), (2 * B, nz)],
    )
    ins = shared(group_b, "px", nx, px_far, near_x, (1, 3), near_x - 1)
    p_y, u_y, v_y, r_top, src_top, curl, flux_y, flux_a, part_a = call(
        functools.partial(first_z_kernel, ny),
        [pos, ef, mf, ez_next, w, c],
        [cells] * 3 + [(B, nz)] * 2 + [cells] * 4,
        scratch=[cells] * 2,
        flops=8_000_000,
    )
    ins = [pos, near_b, own_b] + ins + [halos, g_b, u_x, v_x, flux_b, w, c, r_top, src_top]
    far_b, rise_y, curl, flux_y, flux_a, g_a, g_c, own_ac = call(
        functools.partial(both_y_kernel, near_x, far_x, px_far),
        ins + [curl, flux_y, flux_a, part_a, p_y, u_y, v_y],
        [(far_x, 6 * B, nz)] + [cells] * 6 + [(7 * B, nz)],
        scratch=[cells] * 2,
    )
    ins = shared(own_ac, "py", ny, py_near)
    near_ac, msg = call(
        functools.partial(merge_kernel, 1, near_y, py_near, 2), [pos] + ins, [(near_y, 7 * B, nz), (7 * B, nz)]
    )
    msg, w = lax.optimization_barrier((msg, w))
    ins = shared(msg, "py", ny, py_far, near_y, (2,), near_y // 2)
    steps = (nz - 1).bit_length()
    z_factors = call(factors_kernel, [w], [(steps, *cells)] * 2 + [cells], flops=8_000_000)
    ins, z_factors = lax.optimization_barrier((ins, z_factors))
    part_x, flux2, g2, ends_c, own_a = call(
        functools.partial(second_x_kernel, near_y, far_y, py_far),
        [pos, near_ac, own_ac] + ins + [g_a, u_y, v_y, flux_a, c, curl, p_x],
        [cells] * 3 + [(2 * B, nz)] * 2,
        scratch=[(far_y, 7 * B, nz), cells],
    )
    ins = shared(own_a, "px", nx, px_near)
    whole = pltpu.HBM((3, *cells), F32)
    elec, magn = call(
        second_y_kernel,
        [ends_c, g_c, u_y, v_y, flux_y],
        [whole, whole],
        out_specs=[HBM] * 2,
        scratch=[cells] * 2 + [dma((2,))],
    )
    near_a, msg = call(
        functools.partial(merge_rows_kernel, 0, near_x, px_near),
        [pos, near_b] + ins,
        [(near_x, 2 * B, nz), (2 * B, nz)],
    )
    msg, elec = lax.optimization_barrier((msg, elec))
    ins = shared(msg, "px", nx, px_far, near_x, (1, 3), near_x // 2)
    elec, magn = call(
        second_z_kernel,
        [part_x, rise_y, *z_factors, elec, magn],
        [whole] * 2,
        specs=[VMEM] * 5 + [HBM] * 2,
        out_specs=[HBM] * 2,
        scratch=[cells] * 2 + [dma((2,))],
        aliases={5: 0, 6: 1},
        flops=4_000_000,
    )
    ins = [pos, near_b, far_b, own_b, group_b, near_a, own_a] + ins + [g2, u_x, v_x, flux2]
    at = len(ins)
    out = call(
        functools.partial(last_kernel, near_x, far_x, px_far),
        ins + [elec, magn],
        [whole] * 2,
        specs=[VMEM] * at + [HBM] * 2,
        out_specs=[HBM] * 2,
        scratch=[(far_x, 2 * B, nz), cells, cells, dma((2,))],
        aliases={at: 0, at + 1: 1},
    )
    return tuple(a.reshape(3, B, B, nz) for a in out)


def solution(mesh):
    placed = (P(None, "px", "py", None), P(None, "px", "py", None), P("px", "py", None), P(), P())
    return jax.shard_map(
        local,
        mesh=mesh,
        in_specs=placed,
        out_specs=(P(None, "px", "py", None), P(None, "px", "py", None)),
        check_vma=False,
    )
```
